32 devices in a mesh: dp: 2 (over y), seq: 4 (over z), head: 4 (over x, core).
Axes of the slice: x: 2, y: 2, z: 4, core: 2. Of those that a mesh axis runs over, the one named last changes fastest.
Arguments:
- tokens: bfloat16 [2, 2048, 1536], P('dp', 'seq'), may hold values from -6 to 6
- cotangent: bfloat16 [2, 2048, 1536], P('dp', 'seq'), may hold values from -6 to 6
- doc_lengths: int32 [2, 2], P('dp'), may hold values from 0 to 2048, as said below
- queries_master: float32 [1536, 1536], P(('dp', 'seq'), 'head'), may hold values from -0.15625 to 0.15625
- queries_moment: float32 [1536, 1536], P(('dp', 'seq'), 'head'), may hold values from -512 to 512
- queries_square: float32 [1536, 1536], P(('dp', 'seq'), 'head'), may hold values from 9216 to 36864
- keyvalue_master: float32 [1536, 512], P(('dp', 'seq')), may hold values from -0.15625 to 0.15625
- keyvalue_moment: float32 [1536, 512], P(('dp', 'seq')), may hold values from -1024 to 1024
- keyvalue_square: float32 [1536, 512], P(('dp', 'seq')), may hold values from 36864 to 147456
- mixing_master: float32 [1536, 1536], P('head', ('dp', 'seq')), may hold values from -2.5 to 2.5
- mixing_moment: float32 [1536, 1536], P('head', ('dp', 'seq')), may hold values from -24 to 24
- mixing_square: float32 [1536, 1536], P('head', ('dp', 'seq')), may hold values from 16 to 64
- expand_master: float32 [1536, 2, 8960], P(('dp', 'seq'), None, 'head'), may hold values from -0.15625 to 0.15625
- expand_moment: float32 [1536, 2, 8960], P(('dp', 'seq'), None, 'head'), may hold values from -96 to 96
- expand_square: float32 [1536, 2, 8960], P(('dp', 'seq'), None, 'head'), may hold values from 256 to 1024
- shrink_master: float32 [8960, 1536], P('head', ('dp', 'seq')), may hold values from -0.0625 to 0.0625
- shrink_moment: float32 [8960, 1536], P('head', ('dp', 'seq')), may hold values from -192 to 192
- shrink_square: float32 [8960, 1536], P('head', ('dp', 'seq')), may hold values from 1024 to 4096
- scalars_master: float32 [5120], P(('dp', 'seq')), as said below
- scalars_moment: float32 [5120], P(('dp', 'seq')), may hold values from -384 to 384
- scalars_square: float32 [5120], P(('dp', 'seq')), may hold values from 4096 to 201326592
Outputs:
- layer_out: bfloat16 [2, 2048, 1536], P('dp', 'seq')
- input_grad: bfloat16 [2, 2048, 1536], P('dp', 'seq')
- queries_grad: float32 [1536, 1536], P(('dp', 'seq'), 'head')
- queries_first: float32 [1536, 1536], P(('dp', 'seq'), 'head')
- queries_second: float32 [1536, 1536], P(('dp', 'seq'), 'head')
- queries_weight: float32 [1536, 1536], P(('dp', 'seq'), 'head')
- queries_copy: bfloat16 [1536, 1536], P(('dp', 'seq'), 'head')
- keyvalue_grad: float32 [1536, 512], P(('dp', 'seq'))
- keyvalue_first: float32 [1536, 512], P(('dp', 'seq'))
- keyvalue_second: float32 [1536, 512], P(('dp', 'seq'))
- keyvalue_weight: float32 [1536, 512], P(('dp', 'seq'))
- keyvalue_copy: bfloat16 [1536, 512], P(('dp', 'seq'))
- mixing_grad: float32 [1536, 1536], P('head', ('dp', 'seq'))
- mixing_first: float32 [1536, 1536], P('head', ('dp', 'seq'))
- mixing_second: float32 [1536, 1536], P('head', ('dp', 'seq'))
- mixing_weight: float32 [1536, 1536], P('head', ('dp', 'seq'))
- mixing_copy: bfloat16 [1536, 1536], P('head', ('dp', 'seq'))
- expand_grad: float32 [1536, 2, 8960], P(('dp', 'seq'), None, 'head')
- expand_first: float32 [1536, 2, 8960], P(('dp', 'seq'), None, 'head')
- expand_second: float32 [1536, 2, 8960], P(('dp', 'seq'), None, 'head')
- expand_weight: float32 [1536, 2, 8960], P(('dp', 'seq'), None, 'head')
- expand_copy: bfloat16 [1536, 2, 8960], P(('dp', 'seq'), None, 'head')
- shrink_grad: float32 [8960, 1536], P('head', ('dp', 'seq'))
- shrink_first: float32 [8960, 1536], P('head', ('dp', 'seq'))
- shrink_second: float32 [8960, 1536], P('head', ('dp', 'seq'))
- shrink_weight: float32 [8960, 1536], P('head', ('dp', 'seq'))
- shrink_copy: bfloat16 [8960, 1536], P('head', ('dp', 'seq'))
- scalars_grad: float32 [5120], P(('dp', 'seq'))
- scalars_first: float32 [5120], P(('dp', 'seq'))
- scalars_second: float32 [5120], P(('dp', 'seq'))
- scalars_weight: float32 [5120], P(('dp', 'seq'))
- scalars_copy: bfloat16 [5120], P(('dp', 'seq'))
The draws below stay inside these ranges and needn't reach their ends.
Inputs may be any that keep to these rules, and one draw needn't show every extreme that they name: `doc_lengths`: row b lists the lengths of batch b's packed sequences in order: multiples of 1024 that sum to 2048, followed by zeros; the first is longer than half of 2048; in one batch, picked from the seed, a single sequence fills all 2048 rows. `scalars_master`: the gains come first, each within 0.7 to 1.3; the biases follow.
All inputs are finite; a program needn't handle non-finite values.
Results may differ from the reference program's by a relative error of at most 0.025.
Values may be sent and summed in bfloat16 or wider, within the bound.
A program may use at most 256 MiB of HBM per device.

```python
import math
import jax
import jax.numpy as jnp
from jax import lax

D = 1536
H = 12
KV = 2
HD = 128
FF = 8960
TOK_DEV = 512
SEG = 1024
STEP = 5
BATCHES = 2
STREAM = 2048
UNITS = 2
SMALL = 5120
N_SEQ = 4


def one_row(row_key, forced):
    drawn_units = jax.random.randint(jax.random.fold_in(row_key, 1), (), UNITS // 2 + 1, UNITS + 1)
    first_units = jnp.where(forced, UNITS, drawn_units)
    cut_bits = jax.random.randint(jax.random.fold_in(row_key, 2), (UNITS,), 0, 2)
    unit_index = jnp.arange(UNITS, dtype=jnp.int32)
    begins = jnp.where(unit_index == 0, 1, jnp.where(unit_index < first_units, 0, jnp.where(unit_index == first_units, 1, cut_bits)))
    doc_index = jnp.cumsum(begins) - 1
    counts = jnp.sum((doc_index[None, :] == unit_index[:, None]).astype(jnp.int32), axis=1)
    return (counts * SEG).astype(jnp.int32)


def draw_doc_lengths(key, part):
    key = jax.random.fold_in(key, 11)
    row_keys = jax.random.split(key, BATCHES)
    picked = jax.random.randint(jax.random.fold_in(key, 5), (), 0, BATCHES)
    forced = jnp.arange(BATCHES, dtype=jnp.int32) == picked
    return jax.vmap(one_row)(row_keys, forced).astype(jnp.int32)


def draw_scalars_master(key, part):
    key = jax.random.fold_in(key, 23)
    gain_part = 1.0 + 0.3 * jax.random.uniform(jax.random.fold_in(key, 1), (2 * D,), jnp.float32, -1.0, 1.0)
    biases = 0.5 * jax.random.normal(jax.random.fold_in(key, 2), (H * HD + 2 * KV * HD,), jnp.float32)
    return jnp.concatenate([gain_part, biases]).astype(jnp.float32)


def draw_scalars_square(key, part):
    key = jax.random.fold_in(key, 31)
    spread = jax.random.uniform(key, (SMALL,), jnp.float32, 0.0, 1.0)
    level = 1.0 * BATCHES * STREAM
    factor = jnp.exp(spread * math.log(4.0))
    return (level * factor).astype(jnp.float32)


def levels(key, shape, cuts, least, top_value):
    def one(axis_at, blocks):
        steps = jax.random.uniform(jax.random.fold_in(jax.random.fold_in(key, 6), axis_at), (blocks,), jnp.float32, least / len(cuts), top_value / len(cuts))
        return jnp.repeat(jnp.exp(steps), shape[axis_at] // blocks).reshape((-1,) + (1,) * (len(shape) - axis_at - 1))

    level = one(*cuts[0])
    for cut in cuts[1:]:
        level = level * one(*cut)
    return level


def scatter_about(key, dims, width, most, pieces=(), kind=jnp.bfloat16):
    values = jax.random.normal(key, dims, jnp.float32) * width
    if len(pieces) > 0:
        values = levels(key, dims, pieces, -0.22, 0.18) * values
    return jnp.clip(values, min=-most, max=most).astype(kind)


def setup_inputs(seed: int = 0) -> dict:
    key_list = jax.random.split(jax.random.key(seed), 22)
    tokens = scatter_about(key_list[0], (BATCHES, STREAM, D), 1.0, 6.0, ((0, 2), (1, 4)))
    cotangent = scatter_about(key_list[1], (BATCHES, STREAM, D), 1.0, 6.0, ((0, 2), (1, 4)))
    doc_lengths = draw_doc_lengths(jax.random.fold_in(key_list[21], 71), 0)
    queries_master = scatter_about(key_list[3], (D, H * HD), D ** -0.5, 0.15625, ((0, 8), (1, 4)), jnp.float32)
    queries_moment = scatter_about(key_list[4], (D, H * HD), (1.5 * (BATCHES * STREAM) ** 0.5), 512.0, ((0, 8), (1, 4)), jnp.float32)
    queries_square = jnp.clip(jnp.exp(math.log(36864.0) - 1.3862944 * jax.random.uniform(key_list[5], (D, H * HD), jnp.float32) ** levels(key_list[5], (D, H * HD), ((0, 8), (1, 4)), -0.2, 0.2)), 9216.0, 36864.0)
    keyvalue_master = scatter_about(key_list[6], (D, 2 * KV * HD), D ** -0.5, 0.15625, ((0, 8),), jnp.float32)
    keyvalue_moment = scatter_about(key_list[7], (D, 2 * KV * HD), (3 * (BATCHES * STREAM) ** 0.5), 1024.0, ((0, 8),), jnp.float32)
    keyvalue_square = jnp.clip(jnp.exp(math.log(147456.0) - 1.3862944 * jax.random.uniform(key_list[8], (D, 2 * KV * HD), jnp.float32) ** levels(key_list[8], (D, 2 * KV * HD), ((0, 8),), -0.2, 0.2)), 36864.0, 147456.0)
    mixing_master = scatter_about(key_list[9], (H * HD, D), (max(1, 8 * H * HD // STREAM)) ** -0.5, 2.5, ((0, 4), (1, 8)), jnp.float32)
    mixing_moment = scatter_about(key_list[10], (H * HD, D), 4.0, 24.0, ((0, 4), (1, 8)), jnp.float32)
    mixing_square = jnp.clip(jnp.exp(math.log(64.0) - 1.3862944 * jax.random.uniform(key_list[11], (H * HD, D), jnp.float32) ** levels(key_list[11], (H * HD, D), ((0, 4), (1, 8)), -0.2, 0.2)), 16.0, 64.0)
    expand_master = scatter_about(key_list[12], (D, 2, FF), D ** -0.5, 0.15625, ((0, 8), (2, 4)), jnp.float32)
    expand_moment = scatter_about(key_list[13], (D, 2, FF), (0.25 * (BATCHES * STREAM) ** 0.5), 96.0, ((0, 8), (2, 4)), jnp.float32)
    expand_square = jnp.clip(jnp.exp(math.log(1024.0) - 1.3862944 * jax.random.uniform(key_list[14], (D, 2, FF), jnp.float32) ** levels(key_list[14], (D, 2, FF), ((0, 8), (2, 4)), -0.2, 0.2)), 256.0, 1024.0)
    shrink_master = scatter_about(key_list[15], (FF, D), FF ** -0.5, 0.0625, ((0, 4), (1, 8)), jnp.float32)
    shrink_moment = scatter_about(key_list[16], (FF, D), (0.5 * (BATCHES * STREAM) ** 0.5), 192.0, ((0, 4), (1, 8)), jnp.float32)
    shrink_square = jnp.clip(jnp.exp(math.log(4096.0) - 1.3862944 * jax.random.uniform(key_list[17], (FF, D), jnp.float32) ** levels(key_list[17], (FF, D), ((0, 4), (1, 8)), -0.2, 0.2)), 1024.0, 4096.0)
    scalars_master = draw_scalars_master(jax.random.fold_in(key_list[21], 71), 0)
    scalars_moment = scatter_about(key_list[19], (SMALL,), ((BATCHES * STREAM) ** 0.5), 384.0, ((0, 8),), jnp.float32)
    scalars_square = draw_scalars_square(jax.random.fold_in(key_list[21], 71), 0)
    return {"tokens": tokens, "cotangent": cotangent, "doc_lengths": doc_lengths, "queries_master": queries_master, "queries_moment": queries_moment, "queries_square": queries_square, "keyvalue_master": keyvalue_master, "keyvalue_moment": keyvalue_moment, "keyvalue_square": keyvalue_square, "mixing_master": mixing_master, "mixing_moment": mixing_moment, "mixing_square": mixing_square, "expand_master": expand_master, "expand_moment": expand_moment, "expand_square": expand_square, "shrink_master": shrink_master, "shrink_moment": shrink_moment, "shrink_square": shrink_square, "scalars_master": scalars_master, "scalars_moment": scalars_moment, "scalars_square": scalars_square}


norm_eps = 1e-06
rope_base = 1000000.0
beta_first = 0.5
beta_second = 0.5
adam_eps = 1e-08
masked_low = -1e+30
learn_rates = (0.02, 0.02, 0.3, 0.02, 0.01, 0.2)
decay_rates = (0.1, 0.1, 0.1, 0.1, 0.1, 0.0)

@jax.custom_vjp
def low(v):
    return lax.optimization_barrier(v.astype(jnp.bfloat16)).astype(jnp.float32)

@jax.custom_vjp
def low_back(v):
    return v

def low_keep(v):
    return (low(v), None)

def low_pass(kept, grad):
    return (grad,)

def back_keep(v):
    return (v, None)

def back_low(kept, grad):
    return (low(grad),)
low.defvjp(low_keep, low_pass)
low_back.defvjp(back_keep, back_low)

def folded_places(row_ids, shard_rows, seq_count):
    owner_index = row_ids // shard_rows
    inside = row_ids % shard_rows
    halves = shard_rows // 2
    block_index = jnp.where(inside < halves, owner_index, 2 * seq_count - 1 - owner_index)
    return (block_index * halves + inside % halves).astype(jnp.int32)

def doc_starts(places, lengths):
    endings = jnp.cumsum(lengths).astype(jnp.int32)
    taken_lengths = jnp.where(endings[None, :] <= places[:, None], lengths[None, :], 0)
    return lax.optimization_barrier(jnp.sum(taken_lengths, axis=1)).astype(jnp.int32)

def rotate(values, places):
    halves = values.shape[-1] // 2
    powers = jnp.arange(halves, dtype=jnp.float32) * (-2.0 / values.shape[-1])
    frequency = jnp.power(jnp.float32(rope_base), powers)
    angles = places.astype(jnp.float32)[:, None] * frequency[None, :]
    cosine = jnp.cos(angles)[:, None, :]
    sine_term = jnp.sin(angles)[:, None, :]
    first_half = values[..., :halves]
    second_half = values[..., halves:]
    return jnp.concatenate([first_half * cosine - second_half * sine_term, second_half * cosine + first_half * sine_term], axis=-1)

def matmul(left, right):
    return jnp.dot(left, right, precision=lax.Precision.HIGHEST)

def rms_norm(values, gain_vector):
    return values * lax.rsqrt(lax.optimization_barrier(jnp.mean(values * values, axis=-1, keepdims=True)) + norm_eps) * gain_vector

def layer(inputs, query_weight, keyvalue_weight, mixing_weight, expand_weight, shrink_weight, scalars, places, starts):
    gain_one = scalars[:D]
    gain_two = scalars[D:2 * D]
    bias_query = scalars[2 * D:2 * D + H * HD]
    bias_keyvalue = scalars[2 * D + H * HD:]
    within = places - starts
    normed = low(rms_norm(inputs, gain_one))
    query_pre = low_back(matmul(normed, query_weight) + bias_query)
    queries = low(rotate(query_pre.reshape(STREAM, H, HD), within))
    keyvalue_pre = matmul(normed, keyvalue_weight) + bias_keyvalue
    key_pre = low_back(keyvalue_pre[:, :KV * HD])
    key_rows = low(rotate(key_pre.reshape(STREAM, KV, HD), within))
    value_rows = low(low_back(keyvalue_pre[:, KV * HD:])).reshape(STREAM, KV, HD)
    group_size = H // KV
    keys_wide = jnp.repeat(key_rows, group_size, axis=1)
    values_wide = jnp.repeat(value_rows, group_size, axis=1)
    score_scale = 1.0 / math.sqrt(HD)
    block_rows = min(512, STREAM)

    def attend(blocks):
        query_block, query_places, query_starts = blocks
        scores = jnp.einsum('qhd,khd->hqk', query_block, keys_wide, precision=lax.Precision.HIGHEST) * score_scale
        scores = low_back(scores)
        visible = (places[None, :] <= query_places[:, None]) & (places[None, :] >= query_starts[:, None])
        scores = jnp.where(visible[None, :, :], scores, masked_low)
        attn_probs = low(jax.nn.softmax(scores, axis=-1))
        return jnp.einsum('hqk,khd->qhd', attn_probs, values_wide, precision=lax.Precision.HIGHEST)
    block_count = STREAM // block_rows
    blocks = (queries.reshape(block_count, block_rows, H, HD), places.reshape(block_count, block_rows), starts.reshape(block_count, block_rows))
    attended = lax.map(jax.checkpoint(attend), blocks).reshape(STREAM, H * HD)
    attended = low(low_back(attended))
    branch = low_back(matmul(attended, mixing_weight))
    hidden = inputs + branch
    normed_two = low(rms_norm(hidden, gain_two))
    gate_value = low_back(matmul(normed_two, expand_weight[:, 0, :]))
    up_value = low_back(matmul(normed_two, expand_weight[:, 1, :]))
    activation = low(low_back(jax.nn.silu(gate_value) * up_value))
    return hidden + matmul(activation, shrink_weight)

def adamw(master, moment, square, grad_rows, rate_value, decay_value):
    first_new = beta_first * moment + (1.0 - beta_first) * grad_rows
    second_new = beta_second * square + (1.0 - beta_second) * grad_rows * grad_rows
    fix_first = 1.0 - beta_first ** STEP
    fix_second = 1.0 - beta_second ** STEP
    weight = master - rate_value * (first_new / fix_first / (jnp.sqrt(second_new / fix_second) + adam_eps) + decay_value * master)
    return (grad_rows, first_new, second_new, weight, weight.astype(jnp.bfloat16))

def reference(tokens, cotangent, doc_lengths, queries_master, queries_moment, queries_square, keyvalue_master, keyvalue_moment, keyvalue_square, mixing_master, mixing_moment, mixing_square, expand_master, expand_moment, expand_square, shrink_master, shrink_moment, shrink_square, scalars_master, scalars_moment, scalars_square):
    masters = (queries_master, keyvalue_master, mixing_master, expand_master, shrink_master, scalars_master)
    params = tuple((master.astype(jnp.bfloat16).astype(jnp.float32) for master in masters))
    places = folded_places(jnp.arange(STREAM, dtype=jnp.int32), TOK_DEV, N_SEQ)

    def one_batch(totals, batch_rows):
        token_rows, cot_rows, lengths = batch_rows
        starts = doc_starts(places, lengths)

        def forward(inputs, *weights):
            return layer(inputs, *weights, places, starts)
        result, pullback = jax.vjp(forward, token_rows.astype(jnp.float32), *params)
        grads = pullback(cot_rows.astype(jnp.float32))
        totals = tuple((total_grad + grad_part for total_grad, grad_part in zip(totals, grads[1:])))
        return (totals, (result.astype(jnp.bfloat16), grads[0].astype(jnp.bfloat16)))
    zero_grads = tuple((jnp.zeros(param.shape, jnp.float32) for param in params))
    totals, (layer_out, input_grad) = lax.scan(one_batch, zero_grads, (tokens, cotangent, doc_lengths))
    query_out = adamw(queries_master, queries_moment, queries_square, totals[0], learn_rates[0], decay_rates[0])
    keyvalue_out = adamw(keyvalue_master, keyvalue_moment, keyvalue_square, totals[1], learn_rates[1], decay_rates[1])
    mixing_out = adamw(mixing_master, mixing_moment, mixing_square, totals[2], learn_rates[2], decay_rates[2])
    expand_out = adamw(expand_master, expand_moment, expand_square, totals[3], learn_rates[3], decay_rates[3])
    shrink_out = adamw(shrink_master, shrink_moment, shrink_square, totals[4], learn_rates[4], decay_rates[4])
    scalars_out = adamw(scalars_master, scalars_moment, scalars_square, totals[5], learn_rates[5], decay_rates[5])
    return (layer_out, input_grad, query_out[0], query_out[1], query_out[2], query_out[3], query_out[4], keyvalue_out[0], keyvalue_out[1], keyvalue_out[2], keyvalue_out[3], keyvalue_out[4], mixing_out[0], mixing_out[1], mixing_out[2], mixing_out[3], mixing_out[4], expand_out[0], expand_out[1], expand_out[2], expand_out[3], expand_out[4], shrink_out[0], shrink_out[1], shrink_out[2], shrink_out[3], shrink_out[4], scalars_out[0], scalars_out[1], scalars_out[2], scalars_out[3], scalars_out[4])
```

```python
import functools
import math

import jax
import jax.numpy as jnp
from jax import lax
from jax.experimental import pallas as pl
from jax.experimental.pallas import tpu as pltpu
from jax.sharding import PartitionSpec as P

D = 1536
H = 12
KV = 2
HD = 128
STEP = 5


norm_eps = 1e-06
rope_base = 1000000.0
beta_first = 0.5
beta_second = 0.5
adam_eps = 1e-08
masked_low = -1e30
learn_rates = (0.02, 0.02, 0.3, 0.02, 0.01, 0.2)
decay_rates = (0.1, 0.1, 0.1, 0.1, 0.1, 0.0)


def folded_places(row_ids, shard_rows, seq_count):
    owner_index = row_ids // shard_rows
    inside = row_ids % shard_rows
    halves = shard_rows // 2
    block_index = jnp.where(inside < halves, owner_index, 2 * seq_count - 1 - owner_index)
    return block_index * halves + inside % halves


def doc_starts(places, lengths):
    endings = jnp.cumsum(lengths)
    taken_lengths = jnp.where(endings[None, :] <= places[:, None], lengths[None, :], 0)
    return jnp.sum(taken_lengths, axis=1)


def rotate(values, places):
    halves = values.shape[-1] // 2
    powers = jnp.arange(halves, dtype=jnp.float32) * (-2.0 / values.shape[-1])
    frequency = jnp.power(jnp.float32(rope_base), powers)
    angles = places.astype(jnp.float32)[:, None] * frequency[None, :]
    cosine = jnp.cos(angles)[:, None, :]
    sine_term = jnp.sin(angles)[:, None, :]
    first_half = values[..., :halves]
    second_half = values[..., halves:]
    return jnp.concatenate(
        [
            first_half * cosine - second_half * sine_term,
            second_half * cosine + first_half * sine_term,
        ],
        axis=-1,
    )


def norm_back(grad_rows, values, scale_rows, gain_vector):
    unit_rows = values * scale_rows
    scaled = grad_rows * gain_vector
    mean_term = jnp.mean(scaled * unit_rows, axis=-1, keepdims=True)
    return (scale_rows * (scaled - unit_rows * mean_term), jnp.sum(grad_rows * unit_rows, axis=0))


def adamw(master, moment, square, grad_rows, rate_value, decay_value):
    first_new = beta_first * moment + (1.0 - beta_first) * grad_rows
    second_new = beta_second * square + (1.0 - beta_second) * grad_rows * grad_rows
    fix_first = 1.0 - beta_first**STEP
    fix_second = 1.0 - beta_second**STEP
    weight = master - rate_value * (
        first_new / fix_first / (jnp.sqrt(second_new / fix_second) + adam_eps)
        + decay_value * master
    )
    return (grad_rows, first_new, second_new, weight, weight.astype(jnp.bfloat16))


def shift(values, axis, steps):
    size = lax.axis_size(axis)
    return lax.ppermute(values, axis, [(i, (i + steps) % size) for i in range(size)])


def swap(values, axis, bit):
    size = lax.axis_size(axis)
    return lax.ppermute(values, axis, [(i, i ^ bit) for i in range(size)])


def dot_nn(left, right):
    return jnp.dot(left, right, preferred_element_type=jnp.float32)


def dot_nt(left, right):
    return lax.dot_general(left, right, (((1,), (1,)), ((), ())), preferred_element_type=jnp.float32)


def dot_tn(left, right):
    return lax.dot_general(left, right, (((0,), (0,)), ((), ())), preferred_element_type=jnp.float32)


def low(values):
    return values.astype(jnp.bfloat16)


def wide(values):
    return values.astype(jnp.float32)


def halve(values, which):
    size = values.shape[0] // 2
    mine = lax.dynamic_slice_in_dim(values, which * size, size, 0)
    other = lax.dynamic_slice_in_dim(values, (1 - which) * size, size, 0)
    return mine, other


def head_scatter(values):
    index = lax.axis_index("head")
    mine, other = halve(values, index % 2)
    values = mine + wide(swap(low(other), "head", 1))
    mine, other = halve(values, index // 2)
    return mine + wide(swap(low(other), "head", 2))


def head_gather(values, dim=0):
    index = lax.axis_index("head")
    for bit, which in ((2, index // 2), (1, index % 2)):
        got = swap(values, "head", bit)
        values = jnp.where(
            which == 0,
            jnp.concatenate([values, got], dim),
            jnp.concatenate([got, values], dim),
        )
    return values


def seq_sum(blocks):
    total = blocks[0]
    for s in range(1, len(blocks)):
        total = total + wide(shift(low(blocks[s]), "seq", -s))
    return total


def place(blocks):
    size = lax.axis_size("seq")
    dp_index, seq_index = lax.axis_index("dp"), lax.axis_index("seq")
    first = next(iter(blocks.values()))
    out = jnp.zeros((2 * size,) + first.shape, first.dtype)
    for (a, k), block in blocks.items():
        owner = lax.rem(dp_index + a, 2) * size + lax.rem(seq_index + size - k, size)
        out = lax.dynamic_update_slice(out, block[None], (owner,) + (0,) * first.ndim)
    return out


def weight_gather(block):
    size = lax.axis_size("seq")
    blocks = {}
    for k in range(size):
        if k > 0:
            block = shift(block, "seq", 1)
        blocks[0, k] = block
        blocks[1, k] = swap(block, "dp", 1)
    out = place(blocks)
    return out.reshape((-1,) + out.shape[2:])


def weight_exchange(packs):
    size = lax.axis_size("seq")
    seq_index = lax.axis_index("seq")
    blocks = {}
    for k in range(size):
        block = lax.dynamic_index_in_dim(packs, lax.rem(seq_index + k, size), 0, False)
        if k > 0:
            block = shift(block, "seq", k)
        blocks[0, k] = block
        blocks[1, k] = swap(block, "dp", 1)
    out = place(blocks)
    return out.reshape((-1,) + out.shape[2:])


def grad_exchange(parts, scatter):
    size = lax.axis_size("seq")
    dp_index, seq_index = lax.axis_index("dp"), lax.axis_index("seq")
    parts = parts.reshape(2, size, -1, parts.shape[1])
    total = jnp.zeros(parts.shape[2:], jnp.float32)
    out = jnp.zeros(parts.shape[1:], jnp.bfloat16)
    for k in range(size - 1, -1, -1):
        target = lax.rem(seq_index + k, size)
        pair = lax.dynamic_index_in_dim(parts, target, 1, False)
        mine = lax.dynamic_index_in_dim(pair, dp_index, 0, False)
        other = lax.dynamic_index_in_dim(pair, 1 - dp_index, 0, False)
        block = wide(mine) + wide(swap(low(other), "dp", 1))
        if k > 0:
            block = wide(shift(low(block), "seq", k))
        if scatter:
            total = total + block
        else:
            source = lax.rem(seq_index + size - k, size)
            out = lax.dynamic_update_slice(out, low(block)[None], (source, 0, 0))
    return total if scatter else out


def visible_blocks(starts_ref, block_rows, half):
    size = lax.axis_size("seq")
    index = lax.axis_index("seq")
    place_block = jnp.where(half == 0, index, 2 * size - 1 - index)
    return starts_ref[half] // block_rows, place_block


def key_offset(block, size, block_rows):
    owner = jnp.where(block < size, block, 2 * size - 1 - block)
    return owner * (2 * block_rows) + jnp.where(block < size, 0, block_rows)


def attention_forward(starts_ref, q_ref, k_ref, v_ref, o_ref, lse_ref):
    local_rows, heads = q_ref.shape[0], q_ref.shape[1] // HD
    block_rows = local_rows // 2
    size = lax.axis_size("seq")
    scale = 1.0 / math.sqrt(HD)
    stacked = heads * block_rows
    for half in range(2):
        begin, last = visible_blocks(starts_ref, block_rows, half)
        rows = pl.ds(half * block_rows, block_rows)
        q = jnp.concatenate([q_ref[rows, i * HD : (i + 1) * HD] for i in range(heads)], axis=0)

        def step(block, carried, diagonal, q=q):
            running_max, running_sum, running_out = carried
            keys = pl.ds(pl.multiple_of(key_offset(block, size, block_rows), block_rows), block_rows)
            scores = dot_nt(q, k_ref[keys, :]) * scale
            if diagonal:
                row = lax.broadcasted_iota(jnp.int32, (block_rows, block_rows), 0)
                col = lax.broadcasted_iota(jnp.int32, (block_rows, block_rows), 1)
                seen = jnp.concatenate([jnp.where(col <= row, 0.0, masked_low)] * heads, axis=0)
                scores = scores + seen
            new_max = jnp.maximum(running_max, jnp.max(scores, axis=-1, keepdims=True))
            probs = jnp.exp(scores - new_max)
            fade = jnp.exp(running_max - new_max)
            running_sum = running_sum * fade + jnp.sum(probs, axis=-1, keepdims=True)
            running_out = running_out * fade + dot_nn(low(probs), v_ref[keys, :])
            return new_max, running_sum, running_out

        carried = (
            jnp.full((stacked, 1), masked_low, jnp.float32),
            jnp.zeros((stacked, 1), jnp.float32),
            jnp.zeros((stacked, HD), jnp.float32),
        )
        carried = lax.fori_loop(begin, last, functools.partial(step, diagonal=False), carried)
        running_max, running_sum, running_out = step(last, carried, True)
        out = running_out / running_sum
        lse = running_max + jnp.log(running_sum)
        for i in range(heads):
            part = slice(i * block_rows, (i + 1) * block_rows)
            o_ref[rows, i * HD : (i + 1) * HD] = out[part]
            lse_ref[rows, i : i + 1] = lse[part]


def attention_backward(
    starts_ref, q_ref, k_ref, v_ref, do_ref, o_ref, lse_ref, dq_ref, dk_ref, dv_ref
):
    local_rows, heads = q_ref.shape[0], q_ref.shape[1] // HD
    block_rows = local_rows // 2
    size = lax.axis_size("seq")
    scale = 1.0 / math.sqrt(HD)
    stacked = heads * block_rows
    dk_ref[...] = jnp.zeros_like(dk_ref)
    dv_ref[...] = jnp.zeros_like(dv_ref)
    for half in range(2):
        begin, last = visible_blocks(starts_ref, block_rows, half)
        rows = pl.ds(half * block_rows, block_rows)

        def stack(ref):
            return jnp.concatenate([ref[rows, i * HD : (i + 1) * HD] for i in range(heads)], axis=0)

        q, do = stack(q_ref), stack(do_ref)
        delta = jnp.sum(wide(do) * stack(o_ref), axis=-1, keepdims=True)
        lse = jnp.concatenate([lse_ref[rows, i : i + 1] for i in range(heads)], axis=0)

        def step(block, dq, diagonal, q=q, do=do, delta=delta, lse=lse):
            keys = pl.ds(pl.multiple_of(key_offset(block, size, block_rows), block_rows), block_rows)
            k, v = k_ref[keys, :], v_ref[keys, :]
            scores = dot_nt(q, k) * scale
            if diagonal:
                row = lax.broadcasted_iota(jnp.int32, (block_rows, block_rows), 0)
                col = lax.broadcasted_iota(jnp.int32, (block_rows, block_rows), 1)
                seen = jnp.concatenate([jnp.where(col <= row, 0.0, masked_low)] * heads, axis=0)
                scores = scores + seen
            probs = jnp.exp(scores - lse)
            score_grad = low(probs * (dot_nt(do, v) - delta))
            dk_ref[keys, :] += dot_tn(score_grad, q) * scale
            dv_ref[keys, :] += dot_tn(low(probs), do)
            return dq + dot_nn(score_grad, k)

        dq = jnp.zeros((stacked, HD), jnp.float32)
        dq = lax.fori_loop(begin, last, functools.partial(step, diagonal=False), dq)
        dq = step(last, dq, True) * scale
        for i in range(heads):
            dq_ref[rows, i * HD : (i + 1) * HD] = dq[i * block_rows : (i + 1) * block_rows]


def in_vmem(kernel, outs, scalars, *arrays):
    return pl.pallas_call(
        kernel,
        out_shape=outs,
        in_specs=[pl.BlockSpec(memory_space=pltpu.SMEM)]
        + [pl.BlockSpec(memory_space=pltpu.VMEM)] * len(arrays),
        out_specs=[pl.BlockSpec(memory_space=pltpu.VMEM)] * len(outs),
        compiler_params=pltpu.CompilerParams(vmem_limit_bytes=40 * 1024 * 1024),
        cost_estimate=pl.CostEstimate(
            flops=12 * 10**9, bytes_accessed=8 * 10**6, transcendentals=10**7
        ),
    )(scalars, *arrays)


def local(
    tokens,
    cotangent,
    doc_lengths,
    queries_master,
    queries_moment,
    queries_square,
    keyvalue_master,
    keyvalue_moment,
    keyvalue_square,
    mixing_master,
    mixing_moment,
    mixing_square,
    expand_master,
    expand_moment,
    expand_square,
    shrink_master,
    shrink_moment,
    shrink_square,
    scalars_master,
    scalars_moment,
    scalars_square,
):
    local_rows, width = tokens.shape[1], tokens.shape[2]
    seq_count = lax.axis_size("seq")
    head_count = lax.axis_size("head")
    head_index = lax.axis_index("head")
    seq_index = lax.axis_index("seq")
    local_heads = H // head_count
    wide_heads = local_heads * HD
    kv_head = head_index * local_heads // (H // KV)
    core = head_index % 2
    quarter = local_rows // 4
    row_begin = (head_index % 2) * (2 * quarter) + (head_index // 2) * quarter
    hidden_units = expand_master.shape[2]
    units = 64 * -(-hidden_units // (64 * seq_count))
    more = ((0, 0), (0, units * seq_count - hidden_units))

    attn_pack = jnp.concatenate(
        [
            low(queries_master),
            low(mixing_master).T,
            low(lax.dynamic_slice_in_dim(keyvalue_master, kv_head * HD, HD, 1)),
            low(lax.dynamic_slice_in_dim(keyvalue_master, (KV + kv_head) * HD, HD, 1)),
        ],
        axis=1,
    )
    expand_low = low(expand_master)

    def cut(values):
        values = jnp.pad(values, more)
        return values.reshape(values.shape[0], seq_count, units).transpose(1, 0, 2)

    ff_packs = jnp.concatenate(
        [cut(expand_low[:, 0]), cut(expand_low[:, 1]), cut(low(shrink_master).T)], axis=2
    )
    scalar_values = wide(lax.all_gather(low(scalars_master), ("dp", "seq"), axis=0, tiled=True))
    attn_weight = weight_gather(attn_pack)
    ff_weight = weight_exchange(ff_packs)
    query_weight = attn_weight[:, :wide_heads]
    mixing_t = attn_weight[:, wide_heads : 2 * wide_heads]
    key_value_weight = attn_weight[:, 2 * wide_heads :]
    expand_weight = ff_weight[:, : 2 * units]
    shrink_t = ff_weight[:, 2 * units :]

    cot_rows = cotangent[0]
    cot_own = lax.dynamic_slice_in_dim(cot_rows, row_begin, quarter, 0)
    cot_blocks = [cot_rows]
    moving = cot_own
    for s in range(1, seq_count):
        moving = shift(moving, "seq", 1)
        cot_blocks.append(head_gather(moving))

    gain_one = scalar_values[:width]
    gain_two = scalar_values[width : 2 * width]
    bias_query = lax.dynamic_slice_in_dim(
        scalar_values, 2 * width + head_index * wide_heads, wide_heads
    )
    bias_keyvalue = scalar_values[2 * width + H * HD :]
    key_bias = lax.dynamic_slice_in_dim(bias_keyvalue, kv_head * HD, HD)
    value_bias = lax.dynamic_slice_in_dim(bias_keyvalue, (KV + kv_head) * HD, HD)
    x_rows = wide(tokens[0])
    lengths = doc_lengths[0]
    places = folded_places(
        seq_index * local_rows + jnp.arange(local_rows, dtype=jnp.int32), local_rows, seq_count
    )
    starts = doc_starts(places, lengths)
    half_starts = jnp.stack([starts[0], starts[local_rows // 2]])
    within = places - starts
    scale_one = lax.rsqrt(jnp.mean(x_rows * x_rows, axis=-1, keepdims=True) + norm_eps)
    normed = low(x_rows * scale_one * gain_one)
    query_pre = dot_nn(normed, query_weight) + bias_query
    queries = low(rotate(query_pre.reshape(local_rows, local_heads, HD), within)).reshape(
        local_rows, wide_heads
    )
    key_value_pre = dot_nn(normed, key_value_weight)
    key_rows = low(rotate((key_value_pre[:, :HD] + key_bias)[:, None, :], within)[:, 0, :])
    value_rows = low(key_value_pre[:, HD:] + value_bias)
    moving = jnp.concatenate([key_rows, value_rows], axis=1)
    all_rows = jnp.zeros((seq_count,) + moving.shape, moving.dtype)
    for s in range(seq_count):
        if s > 0:
            moving = shift(moving, "seq", 1)
        owner = lax.rem(seq_index + seq_count - s, seq_count)
        all_rows = lax.dynamic_update_slice(all_rows, moving[None], (owner, 0, 0))
    all_rows = all_rows.reshape(-1, 2 * HD)
    all_keys, all_values = all_rows[:, :HD], all_rows[:, HD:]
    stream_rows = all_rows.shape[0]
    attended, log_total = in_vmem(
        attention_forward,
        [
            jax.ShapeDtypeStruct((local_rows, wide_heads), jnp.float32),
            jax.ShapeDtypeStruct((local_rows, local_heads), jnp.float32),
        ],
        half_starts,
        queries,
        all_keys,
        all_values,
    )
    attended_low = low(attended)
    x_own = lax.dynamic_slice_in_dim(x_rows, row_begin, quarter, 0)
    hidden = x_own + head_scatter(dot_nt(attended_low, mixing_t))
    scale_two = lax.rsqrt(jnp.mean(hidden * hidden, axis=-1, keepdims=True) + norm_eps)
    normed_two = low(hidden * scale_two * gain_two)

    normed_blocks, grad_blocks, act_blocks, back_parts, out_parts = [], [], [], [], []
    moving = normed_two
    for s in range(seq_count):
        if s > 0:
            moving = shift(moving, "seq", 1)
        block = head_gather(moving)
        both = dot_nn(block, expand_weight)
        gate_value, up_value = both[:, :units], both[:, units:]
        gate_sigmoid = jax.nn.sigmoid(gate_value)
        activation = low(gate_value * gate_sigmoid * up_value)
        act_grad = wide(low(dot_nn(cot_blocks[s], shrink_t)))
        gate_grad = low(act_grad * up_value * gate_sigmoid * (1.0 + gate_value * (1.0 - gate_sigmoid)))
        up_grad = low(act_grad * gate_value * gate_sigmoid)
        both_grad = jnp.concatenate([gate_grad, up_grad], axis=1)
        back_parts.append(head_scatter(dot_nt(both_grad, expand_weight)))
        out_parts.append(head_scatter(dot_nt(activation, shrink_t)))
        normed_blocks.append(block)
        grad_blocks.append(both_grad)
        act_blocks.append(activation)
    norm_two_grad = seq_sum(back_parts)
    back_two, gain_two_grad = norm_back(norm_two_grad, hidden, scale_two, gain_two)
    hidden_grad = wide(lax.dynamic_slice_in_dim(cot_rows, row_begin, quarter, 0)) + back_two
    branch_grad = head_gather(low(hidden_grad))
    feedforward = seq_sum(out_parts)
    layer_out = head_gather(low(hidden + feedforward))
    expand_part = dot_tn(jnp.concatenate(normed_blocks), jnp.concatenate(grad_blocks))
    shrink_part = dot_tn(jnp.concatenate(cot_blocks), jnp.concatenate(act_blocks))
    ff_grads = grad_exchange(low(jnp.concatenate([expand_part, shrink_part], axis=1)), False)

    attended_grad = low(dot_nn(branch_grad, mixing_t))
    query_sum, key_sum, value_sum = in_vmem(
        attention_backward,
        [
            jax.ShapeDtypeStruct((local_rows, wide_heads), jnp.float32),
            jax.ShapeDtypeStruct((stream_rows, HD), jnp.float32),
            jax.ShapeDtypeStruct((stream_rows, HD), jnp.float32),
        ],
        half_starts,
        queries,
        all_keys,
        all_values,
        attended_grad,
        attended,
        log_total,
    )
    mine = jnp.where(core == 0, key_sum, value_sum)
    other = jnp.where(core == 0, value_sum, key_sum)
    mine = mine + wide(swap(low(other), "head", 1))
    mine = mine.reshape(seq_count, local_rows, HD)
    own_sum = seq_sum(
        [
            lax.dynamic_index_in_dim(mine, lax.rem(seq_index + seq_count - s, seq_count), 0, False)
            for s in range(seq_count)
        ]
    )
    own_sum = low(jnp.where(core == 0, rotate(own_sum[:, None, :], -within)[:, 0, :], own_sum))
    query_grad = low(
        rotate(query_sum.reshape(local_rows, local_heads, HD), -within).reshape(
            local_rows, wide_heads
        )
    )
    own_weight = lax.dynamic_slice_in_dim(key_value_weight, core * HD, HD, 1)
    norm_one_grad = head_scatter(dot_nt(query_grad, query_weight) + dot_nt(own_sum, own_weight))
    scale_own = lax.dynamic_slice_in_dim(scale_one, row_begin, quarter, 0)
    back_one, gain_one_grad = norm_back(norm_one_grad, x_own, scale_own, gain_one)
    input_grad = head_gather(low(hidden_grad + back_one))
    attn_part = jnp.concatenate(
        [
            dot_tn(normed, query_grad),
            dot_tn(branch_grad, attended_low),
            dot_tn(normed, own_sum),
        ],
        axis=1,
    )
    attn_grads = grad_exchange(attn_part, True)
    kv_block = low(attn_grads[:, 2 * wide_heads :])
    small = jnp.zeros((scalars_master.shape[0] * 2 * seq_count,), jnp.float32)
    small = lax.dynamic_update_slice(small, jnp.concatenate([gain_one_grad, gain_two_grad]), (0,))
    small = lax.dynamic_update_slice(
        small, jnp.sum(wide(query_grad), axis=0), (2 * width + head_index * wide_heads,)
    )
    kv_column = core * KV * HD + kv_head * HD
    small = lax.dynamic_update_slice(
        small, jnp.sum(wide(own_sum), axis=0), (2 * width + H * HD + kv_column,)
    )
    small = lax.psum(small, "head")
    shared_scalars = lax.psum_scatter(small, ("dp", "seq"), scatter_dimension=0, tiled=True)
    gathered = head_gather(kv_block, 1)
    shared_keyvalue = wide(gathered)

    def joined(part):
        part = ff_grads[:, :, part * units : (part + 1) * units].transpose(1, 0, 2)
        return wide(part.reshape(part.shape[0], -1)[:, :hidden_units])

    grads = (
        attn_grads[:, :wide_heads],
        shared_keyvalue,
        attn_grads[:, wide_heads : 2 * wide_heads].T,
        jnp.stack([joined(0), joined(1)], axis=1),
        joined(2).T,
        shared_scalars,
    )
    masters = (
        (queries_master, queries_moment, queries_square),
        (keyvalue_master, keyvalue_moment, keyvalue_square),
        (mixing_master, mixing_moment, mixing_square),
        (expand_master, expand_moment, expand_square),
        (shrink_master, shrink_moment, shrink_square),
        (scalars_master, scalars_moment, scalars_square),
    )
    results = [layer_out[None], input_grad[None]]
    for held, grad, rate, decay in zip(masters, grads, learn_rates, decay_rates):
        results.extend(adamw(*held, wide(low(grad)), rate, decay))
    return tuple(results)


def solution(mesh):
    placed = (
        P("dp", "seq", None),
        P("dp", "seq", None),
        P("dp", None),
        P(("dp", "seq"), "head"),
        P(("dp", "seq"), "head"),
        P(("dp", "seq"), "head"),
        P(("dp", "seq"), None),
        P(("dp", "seq"), None),
        P(("dp", "seq"), None),
        P("head", ("dp", "seq")),
        P("head", ("dp", "seq")),
        P("head", ("dp", "seq")),
        P(("dp", "seq"), None, "head"),
        P(("dp", "seq"), None, "head"),
        P(("dp", "seq"), None, "head"),
        P("head", ("dp", "seq")),
        P("head", ("dp", "seq")),
        P("head", ("dp", "seq")),
        P(("dp", "seq")),
        P(("dp", "seq")),
        P(("dp", "seq")),
    )
    return jax.shard_map(
        local,
        mesh=mesh,
        in_specs=placed,
        out_specs=(
            P("dp", "seq", None),
            P("dp", "seq", None),
            P(("dp", "seq"), "head"),
            P(("dp", "seq"), "head"),
            P(("dp", "seq"), "head"),
            P(("dp", "seq"), "head"),
            P(("dp", "seq"), "head"),
            P(("dp", "seq"), None),
            P(("dp", "seq"), None),
            P(("dp", "seq"), None),
            P(("dp", "seq"), None),
            P(("dp", "seq"), None),
            P("head", ("dp", "seq")),
            P("head", ("dp", "seq")),
            P("head", ("dp", "seq")),
            P("head", ("dp", "seq")),
            P("head", ("dp", "seq")),
            P(("dp", "seq"), None, "head"),
            P(("dp", "seq"), None, "head"),
            P(("dp", "seq"), None, "head"),
            P(("dp", "seq"), None, "head"),
            P(("dp", "seq"), None, "head"),
            P("head", ("dp", "seq")),
            P("head", ("dp", "seq")),
            P("head", ("dp", "seq")),
            P("head", ("dp", "seq")),
            P("head", ("dp", "seq")),
            P(("dp", "seq")),
            P(("dp", "seq")),
            P(("dp", "seq")),
            P(("dp", "seq")),
            P(("dp", "seq")),
        ),
        check_vma=False,
    )
```

```python
import functools
import math

import jax
import jax.numpy as jnp
from jax import lax
from jax.experimental import pallas as pl
from jax.experimental.pallas import tpu as pltpu
from jax.sharding import PartitionSpec as P

D = 1536
H = 12
KV = 2
HD = 128
STEP = 5


norm_eps = 1e-06
rope_base = 1000000.0
beta_first = 0.5
beta_second = 0.5
adam_eps = 1e-08
masked_low = -1e30
learn_rates = (0.02, 0.02, 0.3, 0.02, 0.01, 0.2)
decay_rates = (0.1, 0.1, 0.1, 0.1, 0.1, 0.0)


def folded_places(row_ids, shard_rows, seq_count):
    owner_index = row_ids // shard_rows
    inside = row_ids % shard_rows
    halves = shard_rows // 2
    block_index = jnp.where(inside < halves, owner_index, 2 * seq_count - 1 - owner_index)
    return block_index * halves + inside % halves


def doc_starts(places, lengths):
    endings = jnp.cumsum(lengths)
    taken_lengths = jnp.where(endings[None, :] <= places[:, None], lengths[None, :], 0)
    return jnp.sum(taken_lengths, axis=1)


def rotate(values, places):
    halves = values.shape[-1] // 2
    powers = jnp.arange(halves, dtype=jnp.float32) * (-2.0 / values.shape[-1])
    frequency = jnp.power(jnp.float32(rope_base), powers)
    angles = places.astype(jnp.float32)[:, None] * frequency[None, :]
    cosine = jnp.cos(angles)[:, None, :]
    sine_term = jnp.sin(angles)[:, None, :]
    first_half = values[..., :halves]
    second_half = values[..., halves:]
    return jnp.concatenate(
        [
            first_half * cosine - second_half * sine_term,
            second_half * cosine + first_half * sine_term,
        ],
        axis=-1,
    )


def norm_back(grad_rows, values, scale_rows, gain_vector):
    unit_rows = values * scale_rows
    scaled = grad_rows * gain_vector
    mean_term = jnp.mean(scaled * unit_rows, axis=-1, keepdims=True)
    return (scale_rows * (scaled - unit_rows * mean_term), jnp.sum(grad_rows * unit_rows, axis=0))


def adamw(master, moment, square, grad_rows, rate_value, decay_value):
    first_new = beta_first * moment + (1.0 - beta_first) * grad_rows
    second_new = beta_second * square + (1.0 - beta_second) * grad_rows * grad_rows
    fix_first = 1.0 - beta_first**STEP
    fix_second = 1.0 - beta_second**STEP
    weight = master - rate_value * (
        first_new / fix_first / (jnp.sqrt(second_new / fix_second) + adam_eps)
        + decay_value * master
    )
    return (grad_rows, first_new, second_new, weight, weight.astype(jnp.bfloat16))


def shift(values, axis, steps):
    size = lax.axis_size(axis)
    return lax.ppermute(values, axis, [(i, (i + steps) % size) for i in range(size)])


def swap(values, axis, bit):
    size = lax.axis_size(axis)
    return lax.ppermute(values, axis, [(i, i ^ bit) for i in range(size)])


def dot_nn(left, right):
    return jnp.dot(left, right, preferred_element_type=jnp.float32)


def dot_nt(left, right):
    return lax.dot_general(left, right, (((1,), (1,)), ((), ())), preferred_element_type=jnp.float32)


def dot_tn(left, right):
    return lax.dot_general(left, right, (((0,), (0,)), ((), ())), preferred_element_type=jnp.float32)


def low(values):
    return values.astype(jnp.bfloat16)


def wide(values):
    return values.astype(jnp.float32)


def halve(values, which):
    size = values.shape[0] // 2
    mine = lax.dynamic_slice_in_dim(values, which * size, size, 0)
    other = lax.dynamic_slice_in_dim(values, (1 - which) * size, size, 0)
    return mine, other


def head_scatter(values):
    index = lax.axis_index("head")
    mine, other = halve(values, index % 2)
    values = mine + wide(swap(low(other), "head", 1))
    mine, other = halve(values, index // 2)
    return mine + wide(swap(low(other), "head", 2))


def head_gather(values, dim=0):
    index = lax.axis_index("head")
    for bit, which in ((2, index // 2), (1, index % 2)):
        got = swap(values, "head", bit)
        values = jnp.where(
            which == 0,
            jnp.concatenate([values, got], dim),
            jnp.concatenate([got, values], dim),
        )
    return values


def seq_sum(blocks):
    total = blocks[0]
    for s in range(1, len(blocks)):
        total = total + wide(shift(low(blocks[s]), "seq", -s))
    return total


def place(blocks):
    size = lax.axis_size("seq")
    dp_index, seq_index = lax.axis_index("dp"), lax.axis_index("seq")
    first = next(iter(blocks.values()))
    out = jnp.zeros((2 * size,) + first.shape, first.dtype)
    for (a, k), block in blocks.items():
        owner = lax.rem(dp_index + a, 2) * size + lax.rem(seq_index + size - k, size)
        out = lax.dynamic_update_slice(out, block[None], (owner,) + (0,) * first.ndim)
    return out


def weight_gather(block):
    size = lax.axis_size("seq")
    blocks = {}
    for k in range(size):
        if k > 0:
            block = shift(block, "seq", 1)
        blocks[0, k] = block
        blocks[1, k] = swap(block, "dp", 1)
    out = place(blocks)
    return out.reshape((-1,) + out.shape[2:])


def weight_exchange(packs):
    size = lax.axis_size("seq")
    seq_index = lax.axis_index("seq")
    blocks = {}
    for k in range(size):
        block = lax.dynamic_index_in_dim(packs, lax.rem(seq_index + k, size), 0, False)
        if k > 0:
            block = shift(block, "seq", k)
        blocks[0, k] = block
        blocks[1, k] = swap(block, "dp", 1)
    out = place(blocks)
    return out.reshape((-1,) + out.shape[2:])


def grad_exchange(parts, scatter):
    size = lax.axis_size("seq")
    dp_index, seq_index = lax.axis_index("dp"), lax.axis_index("seq")
    parts = parts.reshape(2, size, -1, parts.shape[1])
    total = jnp.zeros(parts.shape[2:], jnp.float32)
    out = jnp.zeros(parts.shape[1:], jnp.bfloat16)
    for k in range(size - 1, -1, -1):
        target = lax.rem(seq_index + k, size)
        pair = lax.dynamic_index_in_dim(parts, target, 1, False)
        mine = lax.dynamic_index_in_dim(pair, dp_index, 0, False)
        other = lax.dynamic_index_in_dim(pair, 1 - dp_index, 0, False)
        block = wide(mine) + wide(swap(low(other), "dp", 1))
        if k > 0:
            block = wide(shift(low(block), "seq", k))
        if scatter:
            total = total + block
        else:
            source = lax.rem(seq_index + size - k, size)
            out = lax.dynamic_update_slice(out, low(block)[None], (source, 0, 0))
    return total if scatter else out


def hidden_before(starts_ref, half, block, block_rows):
    return jnp.where(block * block_rows >= starts_ref[half], 0.0, masked_low)


def last_block(half):
    index = lax.axis_index("seq")
    return index if half == 0 else 2 * lax.axis_size("seq") - 1 - index


def key_offset(block, size, block_rows):
    owner = jnp.where(block < size, block, 2 * size - 1 - block)
    return owner * (2 * block_rows) + jnp.where(block < size, 0, block_rows)


def seen_bias(block_rows, heads):
    row = lax.broadcasted_iota(jnp.int32, (block_rows, block_rows), 0)
    col = lax.broadcasted_iota(jnp.int32, (block_rows, block_rows), 1)
    return jnp.concatenate([jnp.where(col <= row, 0.0, masked_low)] * heads, axis=0)


def stacked_heads(ref, half):
    block_rows, heads = ref.shape[0] // 2, ref.shape[1] // HD
    rows = pl.ds(half * block_rows, block_rows)
    return jnp.concatenate([ref[rows, i * HD : (i + 1) * HD] for i in range(heads)], axis=0)


def attention_forward(starts_ref, q_ref, k_ref, v_ref, o_ref, lse_ref, halves=(0, 1)):
    local_rows, heads = q_ref.shape[0], q_ref.shape[1] // HD
    block_rows = local_rows // 2
    size = lax.axis_size("seq")
    scale = 1.0 / math.sqrt(HD)
    stacked = heads * block_rows
    for half in halves:
        last = last_block(half)
        rows = pl.ds(half * block_rows, block_rows)
        q = stacked_heads(q_ref, half)

        def step(block, carried, diagonal, q=q, half=half):
            running_max, running_sum, running_out = carried
            keys = pl.ds(pl.multiple_of(key_offset(block, size, block_rows), block_rows), block_rows)
            scores = dot_nt(q, k_ref[keys, :]) * scale
            if diagonal:
                scores = scores + seen_bias(block_rows, heads)
            else:
                scores = scores + hidden_before(starts_ref, half, block, block_rows)
            new_max = jnp.maximum(running_max, jnp.max(scores, axis=-1, keepdims=True))
            probs = jnp.exp(scores - new_max)
            fade = jnp.exp(running_max - new_max)
            running_sum = running_sum * fade + jnp.sum(probs, axis=-1, keepdims=True)
            running_out = running_out * fade + dot_nn(low(probs), v_ref[keys, :])
            return new_max, running_sum, running_out

        carried = (
            jnp.full((stacked, 1), masked_low, jnp.float32),
            jnp.zeros((stacked, 1), jnp.float32),
            jnp.zeros((stacked, HD), jnp.float32),
        )
        carried = lax.fori_loop(0, last, functools.partial(step, diagonal=False), carried)
        running_max, running_sum, running_out = step(last, carried, True)
        out = running_out / running_sum
        lse = running_max + jnp.log(running_sum)
        for i in range(heads):
            part = slice(i * block_rows, (i + 1) * block_rows)
            o_ref[rows, i * HD : (i + 1) * HD] = out[part]
            lse_ref[rows, i : i + 1] = lse[part]


def attention_backward(
    starts_ref, q_ref, k_ref, v_ref, do_ref, o_ref, lse_ref, dq_ref, dk_ref, dv_ref, halves=(0, 1)
):
    local_rows, heads = q_ref.shape[0], q_ref.shape[1] // HD
    block_rows = local_rows // 2
    size = lax.axis_size("seq")
    scale = 1.0 / math.sqrt(HD)
    stacked = heads * block_rows
    for half in halves:
        if half == 0:
            dk_ref[...] = jnp.zeros_like(dk_ref)
            dv_ref[...] = jnp.zeros_like(dv_ref)
        last = last_block(half)
        rows = pl.ds(half * block_rows, block_rows)
        q, do = stacked_heads(q_ref, half), stacked_heads(do_ref, half)
        delta = jnp.sum(wide(do) * stacked_heads(o_ref, half), axis=-1, keepdims=True)
        lse = jnp.concatenate([lse_ref[rows, i : i + 1] for i in range(heads)], axis=0)

        def step(block, dq, diagonal, q=q, do=do, delta=delta, lse=lse, half=half):
            keys = pl.ds(pl.multiple_of(key_offset(block, size, block_rows), block_rows), block_rows)
            k, v = k_ref[keys, :], v_ref[keys, :]
            scores = dot_nt(q, k) * scale
            if diagonal:
                scores = scores + seen_bias(block_rows, heads)
            else:
                scores = scores + hidden_before(starts_ref, half, block, block_rows)
            probs = jnp.exp(scores - lse)
            score_grad = low(probs * (dot_nt(do, v) - delta))
            dk_ref[keys, :] += dot_tn(score_grad, q) * scale
            dv_ref[keys, :] += dot_tn(low(probs), do)
            return dq + dot_nn(score_grad, k)

        dq = jnp.zeros((stacked, HD), jnp.float32)
        dq = lax.fori_loop(0, last, functools.partial(step, diagonal=False), dq)
        dq = step(last, dq, True) * scale
        for i in range(heads):
            dq_ref[rows, i * HD : (i + 1) * HD] = dq[i * block_rows : (i + 1) * block_rows]


def in_vmem(kernel, outs, scalars, *arrays):
    return pl.pallas_call(
        kernel,
        out_shape=outs,
        in_specs=[pl.BlockSpec(memory_space=pltpu.SMEM)]
        + [pl.BlockSpec(memory_space=pltpu.VMEM)] * len(arrays),
        out_specs=[pl.BlockSpec(memory_space=pltpu.VMEM)] * len(outs),
        compiler_params=pltpu.CompilerParams(vmem_limit_bytes=40 * 1024 * 1024),
        cost_estimate=pl.CostEstimate(
            flops=12 * 10**9, bytes_accessed=8 * 10**6, transcendentals=10**7
        ),
    )(scalars, *arrays)


class Links:
    def __init__(self, send_sems, recv_sems):
        self.send_sems, self.recv_sems, self.started = send_sems, recv_sems, []

    def to(self, source, target, **where):
        number = len(self.started)
        copy = pltpu.make_async_remote_copy(
            src_ref=source,
            dst_ref=target,
            send_sem=self.send_sems.at[number],
            recv_sem=self.recv_sems.at[number],
            device_id=where,
            device_id_type=pl.DeviceIdType.MESH,
        )
        copy.start()
        self.started.append(copy)
        return copy

    def finish(self):
        for copy in self.started:
            copy.wait_send()


def greet(partners):
    barrier = pltpu.get_barrier_semaphore()
    for where in partners:
        pl.semaphore_signal(
            barrier, inc=1, device_id=where, device_id_type=pl.DeviceIdType.MESH
        )
    pl.semaphore_wait(barrier, len(partners))


def at_rows(ref, block, size):
    return ref.at[pl.ds(pl.multiple_of(block * size, size), size), :]


def rows_of(begin, size):
    return pl.ds(pl.multiple_of(begin, size), size)


def turn(values, cosine, sine_term):
    return values * cosine + pltpu.roll(values, HD // 2, 1) * sine_term


def vector_of(scal_ref, begin, size):
    per = scal_ref.shape[2] // 128
    tiles = []
    for i in range(size // 128):
        tile = begin // 128 + i
        if isinstance(tile, int):
            owner, column = tile // per, tile % per * 128
        else:
            owner, column = lax.div(tile, per), pl.multiple_of(lax.rem(tile, per) * 128, 128)
        tiles.append(scal_ref[owner, 0:1, pl.ds(column, 128)])
    return jnp.concatenate(tiles, axis=1)


def front_kernel(
    starts_ref, scal_in, pack, ff_packs, x_ref, cot_ref, cos_ref, sin_ref,
    scal_ref, attn_w, ff_w, cot_all, normed_ref, q_ref, k_all, v_all, att_ref, lse_ref, hid_ref, nt_ref,
    send_c, recv_c, send_x, recv_x, kept, send_sems, recv_sems, local_sems,
):
    rows, width = x_ref.shape
    quarter, half = rows // 4, rows // 2
    block_rows = pack.shape[0]
    size = lax.axis_size("seq")
    y, z, head = lax.axis_index("dp"), lax.axis_index("seq"), lax.axis_index("head")
    core, xx = lax.rem(head, 2), lax.div(head, 2)
    heads = q_ref.shape[1] // HD
    wide_heads = heads * HD
    row_begin = core * half + xx * quarter
    me = y * size + z
    ahead = [lax.rem(z + k, size) for k in range(size)]
    behind = [lax.rem(z + size - k, size) for k in range(size)]
    to_y, to_x, to_core = {"dp": 1 - y}, {"head": head + 2 - 4 * xx}, {"head": head + 1 - 2 * core}
    greet([{"seq": ahead[k]} for k in range(1, size)] + [to_y, to_x, to_core])
    links = Links(send_sems, recv_sems)

    own_scal = pltpu.make_async_copy(scal_in, scal_ref.at[me], local_sems.at[0])
    own_scal.start()
    own_pack = pltpu.make_async_copy(pack, at_rows(attn_w, me, block_rows), local_sems.at[1])
    own_pack.start()
    own_cot = pltpu.make_async_copy(cot_ref, at_rows(cot_all, z, rows), local_sems.at[2])
    own_cot.start()
    own_ff = pltpu.make_async_copy(ff_packs.at[z], at_rows(ff_w, me, block_rows), local_sems.at[3])
    own_ff.start()
    scal_z = [links.to(scal_in, scal_ref.at[me], seq=ahead[k]) for k in range(1, size)]
    scal_y = [links.to(scal_in, scal_ref.at[me], **to_y)]
    attn_z = [
        links.to(pack, at_rows(attn_w, me, block_rows), seq=ahead[k]) for k in range(1, size)
    ]
    attn_y = [links.to(pack, at_rows(attn_w, me, block_rows), **to_y)]
    for k in range(1, size):
        scal_z[k - 1].wait_recv()
        owner = y * size + behind[k]
        scal_y.append(links.to(scal_ref.at[owner], scal_ref.at[owner], **to_y))
    for copy in scal_y:
        copy.wait_recv()
    own_scal.wait()
    gain_one = vector_of(scal_ref, 0, width)

    def norm_rows(i, unused):
        part = rows_of(i * quarter, quarter)
        values = wide(x_ref[part, :])
        scale = lax.rsqrt(jnp.mean(values * values, axis=-1, keepdims=True) + norm_eps)
        normed_ref[part, :] = low(values * scale * gain_one)
        return unused

    lax.fori_loop(0, 4, norm_rows, 0)
    for k in range(1, size):
        attn_z[k - 1].wait_recv()
        block = at_rows(attn_w, y * size + behind[k], block_rows)
        attn_y.append(links.to(block, block, **to_y))
    ff_z = [
        links.to(ff_packs.at[ahead[k]], at_rows(ff_w, me, block_rows), seq=ahead[k])
        for k in range(1, size)
    ]
    ff_y = [links.to(ff_packs.at[z], at_rows(ff_w, me, block_rows), **to_y)]
    own_pack.wait()
    for copy in attn_y:
        copy.wait_recv()

    base = 2 * width + H * HD
    kv_head = lax.div(head * heads, H // KV)
    bias_q = vector_of(scal_ref, 2 * width + head * wide_heads, wide_heads)
    bias_k = vector_of(scal_ref, base + kv_head * HD, HD)
    bias_v = vector_of(scal_ref, base + (KV + kv_head) * HD, HD)
    own_k, own_v = at_rows(k_all, z, rows), at_rows(v_all, z, rows)

    def project(i, unused):
        part = rows_of(i * half, half)
        normed = normed_ref[part, :]
        cosine, sine_term = cos_ref[part, :], sin_ref[part, :]
        pre = dot_nn(normed, attn_w[:, 2 * wide_heads : 2 * wide_heads + 2 * HD])
        own = rows_of(z * rows + i * half, half)
        k_all[own, :] = low(turn(pre[:, :HD] + bias_k, cosine, sine_term))
        v_all[own, :] = low(pre[:, HD:] + bias_v)
        pre = dot_nn(normed, attn_w[:, :wide_heads]) + bias_q
        for n in range(heads):
            at = slice(n * HD, (n + 1) * HD)
            q_ref[part, at] = low(turn(pre[:, at], cosine, sine_term))
        return unused

    lax.fori_loop(0, 2, project, 0)
    kv_send = [0] * (size - 1)
    first = len(links.started)
    for k in range(1, size):
        for which, ref in ((0, own_k), (1, own_v)):
            copy = pltpu.make_async_remote_copy(
                src_ref=ref, dst_ref=ref,
                send_sem=send_sems.at[first + k - 1], recv_sem=recv_sems.at[first + k - 1],
                device_id={"seq": ahead[k]}, device_id_type=pl.DeviceIdType.MESH,
            )
            pl.when(core == which)(copy.start)
        links.started.append(copy)
        kv_send[k - 1] = copy
    cot_own = cot_ref.at[rows_of(row_begin, quarter), :]
    cot_z = [
        links.to(cot_own, cot_all.at[rows_of(z * rows + row_begin, quarter), :], seq=ahead[k])
        for k in range(1, size)
    ]
    first = len(links.started)
    for k in range(1, size):
        kv_send[k - 1].wait_recv()
        for which, ref in ((0, k_all), (1, v_all)):
            block = at_rows(ref, behind[k], rows)
            copy = pltpu.make_async_remote_copy(
                src_ref=block, dst_ref=block,
                send_sem=send_sems.at[first + k - 1], recv_sem=recv_sems.at[first + k - 1],
                device_id=to_core, device_id_type=pl.DeviceIdType.MESH,
            )
            pl.when(core == which)(copy.start)
        links.started.append(copy)
        kv_send.append(copy)
    for copy in kv_send[size - 1 :]:
        copy.wait_recv()
    attention_forward(starts_ref, q_ref, k_all, v_all, att_ref, lse_ref)

    mixing = attn_w.at[:, wide_heads : 2 * wide_heads]

    def branch_part(begin, size_rows):
        return dot_nt(low(att_ref[rows_of(begin, size_rows), :]), mixing[...])

    def branch_send(i, unused):
        part = rows_of(i * quarter, quarter)
        send_c[part, :] = low(branch_part((1 - core) * half + i * quarter, quarter))
        return unused

    lax.fori_loop(0, 2, branch_send, 0)
    to_c = links.to(send_c, recv_c, **to_core)

    def branch_keep(i, unused):
        part = rows_of(i * quarter, quarter)
        kept[part, :] = branch_part(core * half + i * quarter, quarter)
        return unused

    lax.fori_loop(0, 2, branch_keep, 0)
    to_c.wait_recv()
    other, mine = rows_of((1 - xx) * quarter, quarter), rows_of(xx * quarter, quarter)
    send_x[...] = low(kept[other, :] + wide(recv_c[other, :]))
    to_xx = links.to(send_x, recv_x, **to_x)
    for k in range(1, size):
        ff_z[k - 1].wait_recv()
        block = at_rows(ff_w, y * size + behind[k], block_rows)
        ff_y.append(links.to(block, block, **to_y))
    to_xx.wait_recv()
    gain_two = vector_of(scal_ref, width, width)
    hidden = wide(x_ref[rows_of(row_begin, quarter), :]) + (
        kept[mine, :] + wide(recv_c[mine, :]) + wide(recv_x[...])
    )
    hid_ref[...] = hidden
    scale = lax.rsqrt(jnp.mean(hidden * hidden, axis=-1, keepdims=True) + norm_eps)
    nt_ref[...] = low(hidden * scale * gain_two)
    cot_x, cot_core = [], []
    for k in range(1, size):
        cot_z[k - 1].wait_recv()
        block = cot_all.at[rows_of(behind[k] * rows + row_begin, quarter), :]
        cot_x.append(links.to(block, block, **to_x))
        cot_core.append(links.to(block, block, **to_core))
    for k in range(1, size):
        cot_x[k - 1].wait_recv()
        begin = behind[k] * rows + core * half + (1 - xx) * quarter
        block = cot_all.at[rows_of(begin, quarter), :]
        cot_core.append(links.to(block, block, **to_core))
    for copy in cot_core + ff_y:
        copy.wait_recv()
    links.finish()
    own_cot.wait()
    own_ff.wait()


def front(starts, scal_in, pack, ff_packs, x_rows, cot_rows, cosine, sine_term, wide_heads):
    rows, width = x_rows.shape
    size = lax.axis_size("seq")
    quarter, half, count = rows // 4, rows // 2, 2 * size
    bf16, f32 = jnp.bfloat16, jnp.float32
    shape = jax.ShapeDtypeStruct
    in_vmem_spec, anywhere = pl.BlockSpec(memory_space=pltpu.VMEM), pl.BlockSpec(memory_space=pl.ANY)
    outs = [
        (shape((count,) + scal_in.shape, f32), in_vmem_spec),
        (shape((count * pack.shape[0], pack.shape[1]), bf16), in_vmem_spec),
        (shape((count * pack.shape[0], ff_packs.shape[2]), bf16), anywhere),
        (shape((size * rows, width), bf16), anywhere),
        (shape((rows, width), bf16), in_vmem_spec),
        (shape((rows, wide_heads), bf16), in_vmem_spec),
        (shape((size * rows, HD), bf16), in_vmem_spec),
        (shape((size * rows, HD), bf16), in_vmem_spec),
        (shape((rows, wide_heads), f32), in_vmem_spec),
        (shape((rows, wide_heads // HD), f32), in_vmem_spec),
        (shape((quarter, width), f32), in_vmem_spec),
        (shape((quarter, width), bf16), in_vmem_spec),
    ]
    return pl.pallas_call(
        front_kernel,
        out_shape=[o[0] for o in outs],
        in_specs=[
            pl.BlockSpec(memory_space=pltpu.SMEM), in_vmem_spec, in_vmem_spec, anywhere,
            in_vmem_spec, anywhere, in_vmem_spec, in_vmem_spec,
        ],
        out_specs=[o[1] for o in outs],
        scratch_shapes=[
            pltpu.VMEM((half, width), bf16),
            pltpu.VMEM((half, width), bf16),
            pltpu.VMEM((quarter, width), bf16),
            pltpu.VMEM((quarter, width), bf16),
            pltpu.VMEM((half, width), f32),
            pltpu.SemaphoreType.DMA((48,)),
            pltpu.SemaphoreType.DMA((48,)),
            pltpu.SemaphoreType.DMA((4,)),
        ],
        compiler_params=pltpu.CompilerParams(
            collective_id=1, has_side_effects=True, vmem_limit_bytes=48 * 1024 * 1024
        ),
        cost_estimate=pl.CostEstimate(
            flops=6 * 10**9, bytes_accessed=30 * 10**6, transcendentals=10**7
        ),
    )(starts, scal_in, pack, ff_packs, x_rows, cot_rows, cosine, sine_term)


def gated(gate_value, up_value, act_grad):
    gate_sigmoid = jax.nn.sigmoid(gate_value)
    silu = gate_value * gate_sigmoid
    gate_grad = act_grad * up_value * gate_sigmoid * (1.0 + gate_value * (1.0 - gate_sigmoid))
    return silu * up_value, gate_grad, act_grad * silu


def ff_kernel(
    nt_ref, ff_w, cot_all, hid_ref, scal_ref,
    hg_ref, bg_ref, gain_ref, gw_ref, out_ref,
    nt_all, cot_v, w_v, both_v, act_v, send_c, recv_c, kept, send_x, recv_x, send_z, recv_z, total, grad_v, out_v,
    send_sems, recv_sems, local_sems,
):
    quarter, width = nt_ref.shape
    half, rows = 2 * quarter, 4 * quarter
    y, z, head = lax.axis_index("dp"), lax.axis_index("seq"), lax.axis_index("head")
    core, xx = lax.rem(head, 2), lax.div(head, 2)
    row_begin = core * half + xx * quarter
    x_begin = core * half + (1 - xx) * quarter
    wide_units = both_v.shape[1]
    main = wide_units // 256 * 128
    owners = [z, z + 1 - 2 * lax.rem(z, 2), lax.rem(z + 2, 4), 3 - z]
    to_x, to_core = {"head": head + 2 - 4 * xx}, {"head": head + 1 - 2 * core}
    load_w = pltpu.make_async_copy(ff_w, w_v, local_sems.at[0])
    load_w.start()
    load_cot = pltpu.make_async_copy(cot_all, cot_v, local_sems.at[1])
    load_cot.start()
    greet([{"seq": owners[d]} for d in (1, 2, 3)] + [to_x, to_core])
    links = Links(send_sems, recv_sems)

    def piece(owner, begin):
        return nt_all.at[rows_of(owner * rows + begin, quarter), :]

    nt_x = [links.to(nt_ref, piece(z, row_begin), **to_x)]
    nt_core = [links.to(nt_ref, piece(z, row_begin), **to_core)]
    nt_z = [links.to(nt_ref, piece(z, row_begin), seq=owners[1])]
    nt_z.append(links.to(nt_ref, piece(z, row_begin), seq=owners[2]))
    nt_all[rows_of(z * rows + row_begin, quarter), :] = nt_ref[...]
    load_w.wait()
    load_cot.wait()

    def act_grad_rows(i, unused):
        part = rows_of(i * half, half)
        act_v[part, :] = low(dot_nn(cot_v[part, :], w_v[:, wide_units:]))
        return unused

    def forward(s):
        block = piece(owners[s], row_begin)
        if s > 0:
            nt_z[s - 1].wait_recv()
            if s == 2:
                nt_z.append(links.to(block, block, seq=owners[1]))
            nt_x.append(links.to(block, block, **to_x))
            nt_core.append(links.to(block, block, **to_core))

    def forward_x(s):
        nt_x[s].wait_recv()
        block = piece(owners[s], x_begin)
        nt_core.append(links.to(block, block, **to_core))
        return nt_core[-1]

    lax.fori_loop(0, 4, act_grad_rows, 0)
    first_core = [nt_core[0], forward_x(0)]
    lax.fori_loop(4, 8, act_grad_rows, 0)

    def gates(begin):
        part = rows_of(begin, half)
        values = dot_nn(nt_all[part, :], w_v[:, :wide_units])
        act_grad = wide(act_v[part, :])
        act, gate_grad, up_grad = gated(
            values[:, :main], values[:, main : 2 * main], act_grad[:, :main]
        )
        act_v[part, :main] = low(act)
        both_v[part, :main] = low(gate_grad)
        both_v[part, main : 2 * main] = low(up_grad)
        last = values[:, 2 * main :]
        act, gate_grad, up_grad = gated(last, pltpu.roll(last, 64, 1), act_grad[:, main:])
        left = lax.broadcasted_iota(jnp.int32, last.shape, 1) < 64
        act_v[part, main:] = low(jnp.where(left, act, 0.0))
        both_v[part, 2 * main :] = low(jnp.where(left, gate_grad, pltpu.roll(up_grad, 64, 1)))

    def back_part(begin):
        return low(dot_nt(both_v[rows_of(begin, half), :], w_v[:, :wide_units]))

    mine, other = rows_of(xx * quarter, quarter), rows_of((1 - xx) * quarter, quarter)
    steps_c, steps_x, steps_z = [], [], [None]

    def finish_step(s):
        steps_x[s].wait_recv()
        value = wide(kept[s % 2, mine, :]) + wide(recv_c[s, mine, :]) + wide(recv_x[s])
        if s == 0:
            total[...] = value
        else:
            send_z[s - 1] = low(value)
            steps_z.append(links.to(send_z.at[s - 1], recv_z.at[s - 1], seq=owners[s]))

    core_pairs = [first_core]
    for s in range(4):
        for copy in core_pairs[s]:
            copy.wait_recv()
        base = owners[s] * rows
        gates(base + (1 - core) * half)
        if s >= 2:
            steps_c[s - 2].wait_send()
        send_c[s % 2] = back_part(base + (1 - core) * half)
        steps_c.append(links.to(send_c.at[s % 2], recv_c.at[s], **to_core))
        if s == 0:
            forward(1)
        if s < 3:
            own_core = nt_core[-1]
        gates(base + core * half)
        if s == 0:
            forward(2)
        value = back_part(base + core * half)
        if s > 0:
            finish_step(s - 1)
        kept[s % 2] = value
        steps_c[s].wait_recv()
        if s >= 2:
            steps_x[s - 2].wait_send()
        send_x[s % 2] = low(wide(kept[s % 2, other, :]) + wide(recv_c[s, other, :]))
        steps_x.append(links.to(send_x.at[s % 2], recv_x.at[s], **to_x))
        if s == 0:
            core_pairs.append([nt_core[2], forward_x(1)])
        if s == 1:
            forward(3)
            core_pairs.append([nt_core[3], forward_x(2)])
        if s == 2:
            core_pairs.append([nt_core[5], forward_x(3)])

    count = both_v.shape[0] // rows
    pair_rows = grad_v.shape[1]

    def weight_grads(first, stores):
        for i in range(2):
            begin = pl.multiple_of((first * 2 + i) * pair_rows, 128)
            if len(stores) >= 2:
                stores[-2].wait()
            slot = grad_v.at[i]
            columns = pl.ds(begin, pair_rows)
            slot[:, :wide_units] = low(dot_tn(nt_all[:, columns], both_v[...]))
            slot[:, wide_units:] = low(dot_tn(cot_v[:, columns], act_v[...]))
            store = pltpu.make_async_copy(
                slot, gw_ref.at[pl.ds(begin, pair_rows), :], local_sems.at[i]
            )
            store.start()
            stores.append(store)

    finish_step(3)
    stores = []
    weight_grads(1 - y, stores)
    n2 = total[...]
    for s in range(1, 4):
        steps_z[s].wait_recv()
        n2 = n2 + wide(recv_z[s - 1])
    hidden = hid_ref[...]
    gain_two = vector_of(scal_ref, width, width)
    scale = lax.rsqrt(jnp.mean(hidden * hidden, axis=-1, keepdims=True) + norm_eps)
    back, gain_grad = norm_back(n2, hidden, scale, gain_two)
    gain_ref[...] = gain_grad[None]
    hidden_grad = wide(cot_v[rows_of(z * rows + row_begin, quarter), :]) + back
    hg_ref[...] = hidden_grad
    own = bg_ref.at[rows_of(row_begin, quarter), :]
    own[...] = low(hidden_grad)
    bg_x = links.to(own, own, **to_x)
    bg_core = [links.to(own, own, **to_core)]
    weight_grads(y, stores)
    out_stores = []
    for i in range(2 * count):
        part = pl.ds(i * half, half)
        if i >= 2:
            out_stores[i - 2].wait()
        out_v[i % 2] = low(dot_nt(act_v[part, :], w_v[:, wide_units:]))
        store = pltpu.make_async_copy(out_v.at[i % 2], out_ref.at[part, :], local_sems.at[2 + i % 2])
        store.start()
        out_stores.append(store)
        if i == 1:
            bg_x.wait_recv()
            block = bg_ref.at[rows_of(x_begin, quarter), :]
            bg_core.append(links.to(block, block, **to_core))
    for copy in bg_core:
        copy.wait_recv()
    for store in stores[-2:] + out_stores[-2:]:
        store.wait()
    waited = {id(copy) for copy in (steps_c[0], steps_c[1], steps_x[0], steps_x[1])}
    for copy in links.started:
        if id(copy) not in waited:
            copy.wait_send()


def feed_forward(nt, ff_w, cot_all, hidden, scal, units):
    quarter, width = nt.shape
    rows, stream, columns = 4 * quarter, cot_all.shape[0], ff_w.shape[1]
    bf16, f32 = jnp.bfloat16, jnp.float32
    shape = jax.ShapeDtypeStruct
    in_vmem_spec, anywhere = pl.BlockSpec(memory_space=pltpu.VMEM), pl.BlockSpec(memory_space=pl.ANY)
    outs = [
        (shape((quarter, width), f32), in_vmem_spec),
        (shape((rows, width), bf16), in_vmem_spec),
        (shape((1, width), f32), in_vmem_spec),
        (shape((width, columns), bf16), anywhere),
        (shape((stream, width), bf16), anywhere),
    ]
    return pl.pallas_call(
        ff_kernel,
        out_shape=[o[0] for o in outs],
        in_specs=[in_vmem_spec, anywhere, anywhere, in_vmem_spec, in_vmem_spec],
        out_specs=[o[1] for o in outs],
        scratch_shapes=[
            pltpu.VMEM((stream, width), bf16),
            pltpu.VMEM((stream, width), bf16),
            pltpu.VMEM((width, columns), bf16),
            pltpu.VMEM((stream, 2 * units), bf16),
            pltpu.VMEM((stream, columns - 2 * units), bf16),
            pltpu.VMEM((2, 2 * quarter, width), bf16),
            pltpu.VMEM((4, 2 * quarter, width), bf16),
            pltpu.VMEM((2, 2 * quarter, width), bf16),
            pltpu.VMEM((2, quarter, width), bf16),
            pltpu.VMEM((4, quarter, width), bf16),
            pltpu.VMEM((3, quarter, width), bf16),
            pltpu.VMEM((3, quarter, width), bf16),
            pltpu.VMEM((quarter, width), f32),
            pltpu.VMEM((2, width // 4, columns), bf16),
            pltpu.VMEM((2, 2 * quarter, width), bf16),
            pltpu.SemaphoreType.DMA((40,)),
            pltpu.SemaphoreType.DMA((40,)),
            pltpu.SemaphoreType.DMA((4,)),
        ],
        compiler_params=pltpu.CompilerParams(
            collective_id=2, has_side_effects=True, vmem_limit_bytes=62 * 1024 * 1024
        ),
        cost_estimate=pl.CostEstimate(
            flops=33 * 10**9, bytes_accessed=40 * 10**6, transcendentals=10**6
        ),
    )(nt, ff_w, cot_all, hidden, scal)


def back_kernel(
    starts_ref, scal_ref, x_own, hid_ref, hg_ref, gain_two_ref, bg_ref, attn_w, normed_ref, q_ref, k_all, v_all,
    att_ref, lse_ref, cos_ref, sin_ref, gw_ref, part_ref,
    layer_ref, input_ref, ff_grads, attn_ref, kv_ref, small_ref,
    ff_y, ff_own, out_c, out_own, out_sx, out_rx, out_sz, out_rz, dk, dv, do, dq, dkv_s, dkv_r, dkv_rz, dkv_own,
    qg, one_sc, one_rc, one_keep, one_sx, one_rx, layer_own, input_own, a_other, a_own, a_y, a_z, a_sz,
    small, small_y, small_s, small_z, small_h, kv_own,
    send_sems, recv_sems, local_sems,
):
    quarter, width = x_own.shape
    half, rows = 2 * quarter, 4 * quarter
    block_rows = attn_ref.shape[0]
    y, z, head = lax.axis_index("dp"), lax.axis_index("seq"), lax.axis_index("head")
    core, xx = lax.rem(head, 2), lax.div(head, 2)
    size = lax.axis_size("seq")
    heads = q_ref.shape[1] // HD
    wide_heads = heads * HD
    row_begin = core * half + xx * quarter
    x_begin = core * half + (1 - xx) * quarter
    owners = [z, z + 1 - 2 * lax.rem(z, 2), lax.rem(z + 2, 4), 3 - z]
    to_y, to_x, to_core = {"dp": 1 - y}, {"head": head + 2 - 4 * xx}, {"head": head + 1 - 2 * core}
    mine, other = rows_of(xx * quarter, quarter), rows_of((1 - xx) * quarter, quarter)
    is_core = wide(core)
    loads = []

    def load(source, target):
        copy = pltpu.make_async_copy(source, target, local_sems.at[len(loads)])
        copy.start()
        loads.append(copy)
        return copy

    greet([to_y] + [{"seq": owners[d]} for d in (1, 2, 3)] + [to_x, to_core])
    links = Links(send_sems, recv_sems)

    order = (3, 2, 1, 0)

    def grad_rows(ref, which, d):
        return at_rows(ref, which * size + owners[d], block_rows)

    ff_sent, ff_load = {}, {}
    for d in order:
        ff_sent[d] = links.to(grad_rows(gw_ref, 1 - y, d), ff_y.at[d], **to_y)
    out_sent, out_load = [], []
    for s in range(4):
        begin = owners[s] * rows
        source = part_ref.at[rows_of(begin + (1 - core) * half, half), :]
        out_sent.append(links.to(source, out_c.at[s], **to_core))
    for s in range(4):
        source = part_ref.at[rows_of(owners[s] * rows + core * half, half), :]
        out_load.append(load(source, out_own.at[s]))
    for d in order:
        ff_load[d] = load(grad_rows(gw_ref, y, d), ff_own.at[d])

    ff_over_z = {}

    def ff_step(d):
        ff_sent[d].wait_recv()
        ff_load[d].wait()

        def add(i, unused):
            part = rows_of(i * 64, 64)
            ff_own[d, part, :] = low(wide(ff_own[d, part, :]) + wide(ff_y[d, part, :]))
            return unused

        lax.fori_loop(0, block_rows // 64, add, 0)
        if d == 0:
            load(ff_own.at[d], ff_grads.at[z])
        else:
            ff_over_z[d] = links.to(ff_own.at[d], ff_grads.at[z], seq=owners[d])

    out_x, out_z = [], {}

    def out_step_c(s):
        out_sent[s].wait_recv()
        out_load[s].wait()
        out_sx[s] = low(wide(out_own[s, other, :]) + wide(out_c[s, other, :]))
        out_x.append(links.to(out_sx.at[s], out_rx.at[s], **to_x))

    def out_value(s):
        out_x[s].wait_recv()
        return wide(out_own[s, mine, :]) + wide(out_c[s, mine, :]) + wide(out_rx[s])

    def out_step_x(s):
        out_sz[s - 1] = low(out_value(s))
        out_z[s] = links.to(out_sz.at[s - 1], out_rz.at[s - 1], seq=owners[s])

    def do_rows(i, unused):
        part = rows_of(i * half, half)
        do[part, :] = low(dot_nn(bg_ref[part, :], attn_w[:, wide_heads : 2 * wide_heads]))
        return unused

    lax.fori_loop(0, 2, do_rows, 0)
    attention_backward(starts_ref, q_ref, k_all, v_all, do, att_ref, lse_ref, dq, dk, dv, (0,))
    for s in (3, 2):
        pass
    attention_backward(starts_ref, q_ref, k_all, v_all, do, att_ref, lse_ref, dq, dk, dv, (1,))
    dkv_s[...] = low(dv[...] * (1.0 - is_core) + dk[...] * is_core)
    dkv_core = links.to(dkv_s, dkv_r, **to_core)
    for n in range(heads):
        at = slice(n * HD, (n + 1) * HD)
        qg[:, at] = low(turn(dq[:, at], cos_ref[...], -sin_ref[...]))
    for s in range(4):
        out_step_c(s)
    dkv_core.wait_recv()

    def dkv_block(d):
        part = rows_of(owners[d] * rows, rows)
        return dk[part, :] * (1.0 - is_core) + dv[part, :] * is_core + wide(dkv_r[part, :])

    dkv_z = []
    for d in (1, 2, 3):
        dkv_own[d] = low(dkv_block(d))
        dkv_z.append(links.to(dkv_own.at[d], dkv_rz.at[d - 1], seq=owners[d]))
    total = dkv_block(0)
    ff_step(3)
    for d in (1, 2, 3):
        dkv_z[d - 1].wait_recv()
        total = total + wide(dkv_rz[d - 1])
    turned = turn(total, cos_ref[...], -sin_ref[...])
    dkv_own[0] = low(turned * (1.0 - is_core) + total * is_core)
    key_columns = pl.ds(pl.multiple_of(2 * wide_heads + core * HD, HD), HD)

    def one_part(begin):
        part = rows_of(begin, quarter)
        return dot_nt(qg[part, :], attn_w[:, :wide_heads]) + dot_nt(
            dkv_own[0, part, :], attn_w[:, key_columns]
        )

    def one_send(i, unused):
        one_sc[rows_of(i * quarter, quarter), :] = low(one_part((1 - core) * half + i * quarter))
        return unused

    def one_own(i, unused):
        one_keep[rows_of(i * quarter, quarter), :] = one_part(core * half + i * quarter)
        return unused

    lax.fori_loop(0, 2, one_send, 0)
    one_c = links.to(one_sc, one_rc, **to_core)
    lax.fori_loop(0, 2, one_own, 0)
    one_c.wait_recv()
    one_sx[...] = low(one_keep[other, :] + wide(one_rc[other, :]))
    one_x = links.to(one_sx, one_rx, **to_x)

    def attn_grads(which, target):
        columns = pl.ds(pl.multiple_of(which * (width // 2), 128), width // 2)
        normed = normed_ref[:, columns]
        target[:, :wide_heads] = low(dot_tn(normed, qg[...]))
        target[:, wide_heads : 2 * wide_heads] = low(
            dot_tn(bg_ref[:, columns], low(att_ref[...]))
        )
        target[:, 2 * wide_heads :] = low(dot_tn(normed, dkv_own[0]))

    attn_grads(1 - y, a_other)
    attn_sent = {
        d: links.to(at_rows(a_other, owners[d], block_rows), a_y.at[d], **to_y) for d in order
    }
    attn_grads(y, a_own)
    ff_step(2)
    out_step_x(3)

    one_x.wait_recv()
    norm_one_grad = one_keep[mine, :] + wide(one_rc[mine, :]) + wide(one_rx[...])
    x_rows = wide(x_own[...])
    gain_one = vector_of(scal_ref, 0, width)
    scale = lax.rsqrt(jnp.mean(x_rows * x_rows, axis=-1, keepdims=True) + norm_eps)
    back, gain_grad = norm_back(norm_one_grad, x_rows, scale, gain_one)
    input_own[...] = low(hg_ref[...] + back)

    def gather(source, target):
        place = target.at[rows_of(row_begin, quarter), :]
        load(source, place)
        return links.to(source, place, **to_x), [links.to(source, place, **to_core)]

    def gather_on(sent, target):
        sent[0].wait_recv()
        block = target.at[rows_of(x_begin, quarter), :]
        sent[1].append(links.to(block, block, **to_core))

    input_sent = gather(input_own, input_ref)
    small[...] = jnp.zeros_like(small)
    per = small.shape[2] // 128

    def put(begin, values):
        for i in range(values.shape[1] // 128):
            tile = begin // 128 + i
            value = values[:, i * 128 : (i + 1) * 128]
            if isinstance(tile, int):
                small[tile // per, 0:1, tile % per * 128 : tile % per * 128 + 128] = value
            else:
                column = pl.ds(pl.multiple_of(lax.rem(tile, per) * 128, 128), 128)
                small[lax.div(tile, per), 0:1, column] = value

    put(0, gain_grad[None])
    put(width, gain_two_ref[...])
    put(2 * width + head * wide_heads, jnp.sum(wide(qg[...]), axis=0, keepdims=True))
    kv_begin = 2 * width + H * HD + (core * KV + lax.div(head * heads, H // KV)) * HD
    put(kv_begin, jnp.sum(wide(dkv_own[0]), axis=0, keepdims=True))
    small_sent = links.to(small.at[pl.ds((1 - y) * size, size)], small_y, **to_y)
    out_step_x(2)
    ff_step(1)
    out_step_x(1)
    gather_on(input_sent, input_ref)
    small_sent.wait_recv()
    small_s[...] = small[pl.ds(y * size, size)] + small_y[...]
    small_over_z = [
        links.to(small_s.at[owners[d]], small_z.at[d - 1], seq=owners[d]) for d in (1, 2, 3)
    ]
    layer = hid_ref[...] + out_value(0)
    attn_over_z = {}

    def attn_step(d):
        attn_sent[d].wait_recv()
        block = wide(at_rows(a_own, owners[d], block_rows)[...]) + wide(a_y[d])
        if d == 0:
            return block
        a_sz[d - 1] = low(block)
        attn_over_z[d] = links.to(a_sz.at[d - 1], a_z.at[d - 1], seq=owners[d])
        return None

    for d in (3, 2, 1):
        attn_step(d)
    for d in (3, 2, 1):
        out_z[d].wait_recv()
        layer = layer + wide(out_rz[d - 1])
    layer_own[...] = low(layer)
    layer_sent = gather(layer_own, layer_ref)
    ff_step(0)
    value = small_s[z]
    for d in (1, 2, 3):
        small_over_z[d - 1].wait_recv()
        value = value + small_z[d - 1]
    small_h[0] = value
    small_x = links.to(small_h.at[0], small_h.at[1], **to_x)
    block = attn_step(0)
    small_x.wait_recv()
    small_h[2] = small_h[0] + small_h[1]
    small_c = links.to(small_h.at[2], small_h.at[3], **to_core)
    gather_on(layer_sent, layer_ref)
    for d in (3, 2, 1):
        attn_over_z[d].wait_recv()
        block = block + wide(a_z[d - 1])
    attn_ref[...] = block
    place = kv_ref.at[core * 2 + xx]
    kv_own[...] = low(block[:, 2 * wide_heads :])
    place[...] = kv_own[...]
    kv_x = links.to(kv_own, place, **to_x)
    kv_core = [links.to(kv_own, place, **to_core)]
    small_c.wait_recv()
    small_ref[...] = small_h[2] + small_h[3]
    kv_x.wait_recv()
    place = kv_ref.at[core * 2 + 1 - xx]
    kv_core.append(links.to(place, place, **to_core))
    for copy in kv_core + input_sent[1] + layer_sent[1] + [ff_over_z[d] for d in (3, 2, 1)]:
        copy.wait_recv()
    links.finish()
    for copy in loads[8:]:
        copy.wait()


def back(
    starts, scal, x_own, hidden, hidden_grad, gain_two_grad, branch_grad, attn_w, normed, q, k_all, v_all, attended, lse,
    cosine, sine_term, gw, out_part,
):
    quarter, width = x_own.shape
    half, rows = 2 * quarter, 4 * quarter
    size = lax.axis_size("seq")
    block_rows, columns = gw.shape[0] // (2 * size), gw.shape[1]
    wide_heads = q.shape[1]
    attn_columns = 2 * wide_heads + HD
    stream = k_all.shape[0]
    bf16, f32 = jnp.bfloat16, jnp.float32
    shape = jax.ShapeDtypeStruct
    in_vmem_spec, anywhere = pl.BlockSpec(memory_space=pltpu.VMEM), pl.BlockSpec(memory_space=pl.ANY)
    outs = [
        (shape((rows, width), bf16), anywhere),
        (shape((rows, width), bf16), anywhere),
        (shape((size, block_rows, columns), bf16), anywhere),
        (shape((block_rows, attn_columns), f32), in_vmem_spec),
        (shape((4, block_rows, HD), bf16), in_vmem_spec),
        (shape(scal.shape[1:], f32), in_vmem_spec),
    ]
    small = (size,) + scal.shape[1:]
    scratch = [
        ((size, block_rows, columns), bf16),
        ((size, block_rows, columns), bf16),
        ((4, half, width), bf16),
        ((4, half, width), bf16),
        ((4, quarter, width), bf16),
        ((4, quarter, width), bf16),
        ((3, quarter, width), bf16),
        ((3, quarter, width), bf16),
        ((stream, HD), f32),
        ((stream, HD), f32),
        ((rows, wide_heads), bf16),
        ((rows, wide_heads), f32),
        ((stream, HD), bf16),
        ((stream, HD), bf16),
        ((3, rows, HD), bf16),
        ((4, rows, HD), bf16),
        ((rows, wide_heads), bf16),
        ((half, width), bf16),
        ((half, width), bf16),
        ((half, width), f32),
        ((quarter, width), bf16),
        ((quarter, width), bf16),
        ((quarter, width), bf16),
        ((quarter, width), bf16),
        ((width // 2, attn_columns), bf16),
        ((width // 2, attn_columns), bf16),
        ((4, block_rows, attn_columns), bf16),
        ((3, block_rows, attn_columns), bf16),
        ((3, block_rows, attn_columns), bf16),
        (scal.shape, f32),
        (small, f32),
        (small, f32),
        ((3,) + scal.shape[1:], f32),
        ((4,) + scal.shape[1:], f32),
        ((block_rows, HD), bf16),
    ]
    return pl.pallas_call(
        back_kernel,
        out_shape=[o[0] for o in outs],
        in_specs=[pl.BlockSpec(memory_space=pltpu.SMEM)] + [in_vmem_spec] * 15 + [anywhere] * 2,
        out_specs=[o[1] for o in outs],
        scratch_shapes=[pltpu.VMEM(*one) for one in scratch]
        + [
            pltpu.SemaphoreType.DMA((56,)),
            pltpu.SemaphoreType.DMA((56,)),
            pltpu.SemaphoreType.DMA((12,)),
        ],
        compiler_params=pltpu.CompilerParams(
            collective_id=3, has_side_effects=True, vmem_limit_bytes=62 * 1024 * 1024
        ),
        cost_estimate=pl.CostEstimate(
            flops=10 * 10**9, bytes_accessed=40 * 10**6, transcendentals=10**6
        ),
    )(
        starts, scal, x_own, hidden, hidden_grad, gain_two_grad, branch_grad, attn_w, normed, q, k_all, v_all, attended,
        lse, cosine, sine_term, gw, out_part,
    )


def rope_tables(places):
    halves = HD // 2
    powers = jnp.arange(halves, dtype=jnp.float32) * (-2.0 / HD)
    frequency = jnp.power(jnp.float32(rope_base), powers)
    angles = places.astype(jnp.float32)[:, None] * frequency[None, :]
    cosine, sine_term = jnp.cos(angles), jnp.sin(angles)
    return (
        jnp.concatenate([cosine, cosine], axis=1),
        jnp.concatenate([-sine_term, sine_term], axis=1),
    )


def local(
    tokens,
    cotangent,
    doc_lengths,
    queries_master,
    queries_moment,
    queries_square,
    keyvalue_master,
    keyvalue_moment,
    keyvalue_square,
    mixing_master,
    mixing_moment,
    mixing_square,
    expand_master,
    expand_moment,
    expand_square,
    shrink_master,
    shrink_moment,
    shrink_square,
    scalars_master,
    scalars_moment,
    scalars_square,
):
    local_rows, width = tokens.shape[1], tokens.shape[2]
    seq_count = lax.axis_size("seq")
    head_count = lax.axis_size("head")
    head_index = lax.axis_index("head")
    seq_index = lax.axis_index("seq")
    local_heads = H // head_count
    wide_heads = local_heads * HD
    kv_head = head_index * local_heads // (H // KV)
    core = head_index % 2
    quarter = local_rows // 4
    row_begin = (head_index % 2) * (2 * quarter) + (head_index // 2) * quarter
    hidden_units = expand_master.shape[2]
    units = 64 * -(-hidden_units // (64 * seq_count))
    more = ((0, 0), (0, units * seq_count - hidden_units))

    attn_pack = jnp.concatenate(
        [
            low(queries_master),
            low(mixing_master).T,
            low(lax.dynamic_slice_in_dim(keyvalue_master, kv_head * HD, HD, 1)),
            low(lax.dynamic_slice_in_dim(keyvalue_master, (KV + kv_head) * HD, HD, 1)),
        ],
        axis=1,
    )
    expand_low = low(expand_master)

    def cut(values):
        values = jnp.pad(values, more)
        return values.reshape(values.shape[0], seq_count, units).transpose(1, 0, 2)

    ff_packs = jnp.concatenate(
        [cut(expand_low[:, 0]), cut(expand_low[:, 1]), cut(low(shrink_master).T)], axis=2
    )
    scalar_values = wide(lax.all_gather(low(scalars_master), ("dp", "seq"), axis=0, tiled=True))
    attn_weight = weight_gather(attn_pack)
    ff_weight = weight_exchange(ff_packs)
    query_weight = attn_weight[:, :wide_heads]
    mixing_t = attn_weight[:, wide_heads : 2 * wide_heads]
    key_value_weight = attn_weight[:, 2 * wide_heads :]
    expand_weight = ff_weight[:, : 2 * units]
    shrink_t = ff_weight[:, 2 * units :]

    cot_rows = cotangent[0]
    cot_own = lax.dynamic_slice_in_dim(cot_rows, row_begin, quarter, 0)
    cot_blocks = [cot_rows]
    moving = cot_own
    for s in range(1, seq_count):
        moving = shift(moving, "seq", 1)
        cot_blocks.append(head_gather(moving))

    gain_one = scalar_values[:width]
    gain_two = scalar_values[width : 2 * width]
    bias_query = lax.dynamic_slice_in_dim(
        scalar_values, 2 * width + head_index * wide_heads, wide_heads
    )
    bias_keyvalue = scalar_values[2 * width + H * HD :]
    key_bias = lax.dynamic_slice_in_dim(bias_keyvalue, kv_head * HD, HD)
    value_bias = lax.dynamic_slice_in_dim(bias_keyvalue, (KV + kv_head) * HD, HD)
    x_rows = wide(tokens[0])
    lengths = doc_lengths[0]
    places = folded_places(
        seq_index * local_rows + jnp.arange(local_rows, dtype=jnp.int32), local_rows, seq_count
    )
    starts = doc_starts(places, lengths)
    half_starts = jnp.stack([starts[0], starts[local_rows // 2]])
    within = places - starts
    scale_one = lax.rsqrt(jnp.mean(x_rows * x_rows, axis=-1, keepdims=True) + norm_eps)
    normed = low(x_rows * scale_one * gain_one)
    query_pre = dot_nn(normed, query_weight) + bias_query
    queries = low(rotate(query_pre.reshape(local_rows, local_heads, HD), within)).reshape(
        local_rows, wide_heads
    )
    key_value_pre = dot_nn(normed, key_value_weight)
    key_rows = low(rotate((key_value_pre[:, :HD] + key_bias)[:, None, :], within)[:, 0, :])
    value_rows = low(key_value_pre[:, HD:] + value_bias)
    moving = jnp.concatenate([key_rows, value_rows], axis=1)
    all_rows = jnp.zeros((seq_count,) + moving.shape, moving.dtype)
    for s in range(seq_count):
        if s > 0:
            moving = shift(moving, "seq", 1)
        owner = lax.rem(seq_index + seq_count - s, seq_count)
        all_rows = lax.dynamic_update_slice(all_rows, moving[None], (owner, 0, 0))
    all_rows = all_rows.reshape(-1, 2 * HD)
    all_keys, all_values = all_rows[:, :HD], all_rows[:, HD:]
    stream_rows = all_rows.shape[0]
    attended, log_total = in_vmem(
        attention_forward,
        [
            jax.ShapeDtypeStruct((local_rows, wide_heads), jnp.float32),
            jax.ShapeDtypeStruct((local_rows, local_heads), jnp.float32),
        ],
        half_starts,
        queries,
        all_keys,
        all_values,
    )
    attended_low = low(attended)
    x_own = lax.dynamic_slice_in_dim(x_rows, row_begin, quarter, 0)
    hidden = x_own + head_scatter(dot_nt(attended_low, mixing_t))
    scale_two = lax.rsqrt(jnp.mean(hidden * hidden, axis=-1, keepdims=True) + norm_eps)
    normed_two = low(hidden * scale_two * gain_two)

    normed_blocks, grad_blocks, act_blocks, back_parts, out_parts = [], [], [], [], []
    moving = normed_two
    for s in range(seq_count):
        if s > 0:
            moving = shift(moving, "seq", 1)
        block = head_gather(moving)
        both = dot_nn(block, expand_weight)
        gate_value, up_value = both[:, :units], both[:, units:]
        gate_sigmoid = jax.nn.sigmoid(gate_value)
        activation = low(gate_value * gate_sigmoid * up_value)
        act_grad = wide(low(dot_nn(cot_blocks[s], shrink_t)))
        gate_grad = low(act_grad * up_value * gate_sigmoid * (1.0 + gate_value * (1.0 - gate_sigmoid)))
        up_grad = low(act_grad * gate_value * gate_sigmoid)
        both_grad = jnp.concatenate([gate_grad, up_grad], axis=1)
        back_parts.append(head_scatter(dot_nt(both_grad, expand_weight)))
        out_parts.append(head_scatter(dot_nt(activation, shrink_t)))
        normed_blocks.append(block)
        grad_blocks.append(both_grad)
        act_blocks.append(activation)
    norm_two_grad = seq_sum(back_parts)
    back_two, gain_two_grad = norm_back(norm_two_grad, hidden, scale_two, gain_two)
    hidden_grad = wide(lax.dynamic_slice_in_dim(cot_rows, row_begin, quarter, 0)) + back_two
    branch_grad = head_gather(low(hidden_grad))
    feedforward = seq_sum(out_parts)
    layer_out = head_gather(low(hidden + feedforward))
    expand_part = dot_tn(jnp.concatenate(normed_blocks), jnp.concatenate(grad_blocks))
    shrink_part = dot_tn(jnp.concatenate(cot_blocks), jnp.concatenate(act_blocks))
    ff_grads = grad_exchange(low(jnp.concatenate([expand_part, shrink_part], axis=1)), False)

    attended_grad = low(dot_nn(branch_grad, mixing_t))
    query_sum, key_sum, value_sum = in_vmem(
        attention_backward,
        [
            jax.ShapeDtypeStruct((local_rows, wide_heads), jnp.float32),
            jax.ShapeDtypeStruct((stream_rows, HD), jnp.float32),
            jax.ShapeDtypeStruct((stream_rows, HD), jnp.float32),
        ],
        half_starts,
        queries,
        all_keys,
        all_values,
        attended_grad,
        attended,
        log_total,
    )
    mine = jnp.where(core == 0, key_sum, value_sum)
    other = jnp.where(core == 0, value_sum, key_sum)
    mine = mine + wide(swap(low(other), "head", 1))
    mine = mine.reshape(seq_count, local_rows, HD)
    own_sum = seq_sum(
        [
            lax.dynamic_index_in_dim(mine, lax.rem(seq_index + seq_count - s, seq_count), 0, False)
            for s in range(seq_count)
        ]
    )
    own_sum = low(jnp.where(core == 0, rotate(own_sum[:, None, :], -within)[:, 0, :], own_sum))
    query_grad = low(
        rotate(query_sum.reshape(local_rows, local_heads, HD), -within).reshape(
            local_rows, wide_heads
        )
    )
    own_weight = lax.dynamic_slice_in_dim(key_value_weight, core * HD, HD, 1)
    norm_one_grad = head_scatter(dot_nt(query_grad, query_weight) + dot_nt(own_sum, own_weight))
    scale_own = lax.dynamic_slice_in_dim(scale_one, row_begin, quarter, 0)
    back_one, gain_one_grad = norm_back(norm_one_grad, x_own, scale_own, gain_one)
    input_grad = head_gather(low(hidden_grad + back_one))
    attn_part = jnp.concatenate(
        [
            dot_tn(normed, query_grad),
            dot_tn(branch_grad, attended_low),
            dot_tn(normed, own_sum),
        ],
        axis=1,
    )
    attn_grads = grad_exchange(attn_part, True)
    kv_block = low(attn_grads[:, 2 * wide_heads :])
    small = jnp.zeros((scalars_master.shape[0] * 2 * seq_count,), jnp.float32)
    small = lax.dynamic_update_slice(small, jnp.concatenate([gain_one_grad, gain_two_grad]), (0,))
    small = lax.dynamic_update_slice(
        small, jnp.sum(wide(query_grad), axis=0), (2 * width + head_index * wide_heads,)
    )
    kv_column = core * KV * HD + kv_head * HD
    small = lax.dynamic_update_slice(
        small, jnp.sum(wide(own_sum), axis=0), (2 * width + H * HD + kv_column,)
    )
    small = lax.psum(small, "head")
    shared_scalars = lax.psum_scatter(small, ("dp", "seq"), scatter_dimension=0, tiled=True)
    gathered = head_gather(kv_block, 1)
    shared_keyvalue = wide(gathered)

    def joined(part):
        part = ff_grads[:, :, part * units : (part + 1) * units].transpose(1, 0, 2)
        return wide(part.reshape(part.shape[0], -1)[:, :hidden_units])

    grads = (
        attn_grads[:, :wide_heads],
        shared_keyvalue,
        attn_grads[:, wide_heads : 2 * wide_heads].T,
        jnp.stack([joined(0), joined(1)], axis=1),
        joined(2).T,
        shared_scalars,
    )
    masters = (
        (queries_master, queries_moment, queries_square),
        (keyvalue_master, keyvalue_moment, keyvalue_square),
        (mixing_master, mixing_moment, mixing_square),
        (expand_master, expand_moment, expand_square),
        (shrink_master, shrink_moment, shrink_square),
        (scalars_master, scalars_moment, scalars_square),
    )
    results = [layer_out[None], input_grad[None]]
    for held, grad, rate, decay in zip(masters, grads, learn_rates, decay_rates):
        results.extend(adamw(*held, wide(low(grad)), rate, decay))
    return tuple(results)


def local_fast(
    tokens,
    cotangent,
    doc_lengths,
    queries_master,
    queries_moment,
    queries_square,
    keyvalue_master,
    keyvalue_moment,
    keyvalue_square,
    mixing_master,
    mixing_moment,
    mixing_square,
    expand_master,
    expand_moment,
    expand_square,
    shrink_master,
    shrink_moment,
    shrink_square,
    scalars_master,
    scalars_moment,
    scalars_square,
):
    local_rows, width = tokens.shape[1], tokens.shape[2]
    seq_count = lax.axis_size("seq")
    head_count = lax.axis_size("head")
    head_index = lax.axis_index("head")
    seq_index = lax.axis_index("seq")
    local_heads = H // head_count
    wide_heads = local_heads * HD
    kv_head = head_index * local_heads // (H // KV)
    core = head_index % 2
    quarter = local_rows // 4
    row_begin = (head_index % 2) * (2 * quarter) + (head_index // 2) * quarter
    hidden_units = expand_master.shape[2]
    units = 64 * -(-hidden_units // (64 * seq_count))
    more = ((0, 0), (0, units * seq_count - hidden_units))

    attn_pack = jnp.concatenate(
        [
            low(queries_master),
            low(mixing_master).T,
            low(lax.dynamic_slice_in_dim(keyvalue_master, kv_head * HD, HD, 1)),
            low(lax.dynamic_slice_in_dim(keyvalue_master, (KV + kv_head) * HD, HD, 1)),
        ],
        axis=1,
    )
    expand_low = low(expand_master)

    def cut(values):
        values = jnp.pad(values, more)
        return values.reshape(values.shape[0], seq_count, units).transpose(1, 0, 2)

    main = units // 128 * 128
    gate_cut, up_cut = cut(expand_low[:, 0]), cut(expand_low[:, 1])
    ff_packs = jnp.concatenate(
        [
            gate_cut[..., :main],
            up_cut[..., :main],
            gate_cut[..., main:],
            up_cut[..., main:],
            cut(low(shrink_master).T),
            jnp.zeros(gate_cut.shape[:2] + (64,), jnp.bfloat16),
        ],
        axis=2,
    )
    x_low, cot_rows = tokens[0], cotangent[0]
    lengths = doc_lengths[0]
    places = folded_places(
        seq_index * local_rows + jnp.arange(local_rows, dtype=jnp.int32), local_rows, seq_count
    )
    starts = doc_starts(places, lengths)
    half_starts = jnp.stack([starts[0], starts[local_rows // 2]])
    within = places - starts
    cosine, sine_term = rope_tables(within)
    scal_in = jnp.broadcast_to(wide(low(scalars_master))[None], (8, scalars_master.shape[0]))
    (
        scal_all, attn_weight, ff_weight, cot_all, normed, queries, all_keys, all_values,
        attended, log_total, hidden, normed_two,
    ) = front(
        half_starts, scal_in, attn_pack, ff_packs, x_low, cot_rows, cosine, sine_term, wide_heads
    )
    hidden_grad, branch_grad, gain_two_grad, ff_part, out_part = feed_forward(
        normed_two, ff_weight, cot_all, hidden, scal_all, units
    )
    x_own = lax.dynamic_slice_in_dim(x_low, row_begin, quarter, 0)
    layer_out, input_grad, ff_grads, attn_grads, kv_blocks, small = back(
        half_starts, scal_all, x_own, hidden, hidden_grad, gain_two_grad, branch_grad, attn_weight, normed, queries,
        all_keys, all_values, attended, log_total, cosine, sine_term, ff_part, out_part,
    )
    shared_keyvalue = wide(jnp.concatenate([kv_blocks[i] for i in range(4)], axis=1))
    shared_scalars = small[0]

    def joined(part):
        if part < 2:
            rest = 2 * main + part * (units - main)
            pieces = [
                ff_grads[:, :, part * main : (part + 1) * main],
                ff_grads[:, :, rest : rest + units - main],
            ]
            part = jnp.concatenate(pieces, axis=2)
        else:
            part = ff_grads[:, :, 2 * units : 3 * units]
        part = part.transpose(1, 0, 2)
        return wide(part.reshape(part.shape[0], -1)[:, :hidden_units])

    grads = (
        attn_grads[:, :wide_heads],
        shared_keyvalue,
        attn_grads[:, wide_heads : 2 * wide_heads].T,
        jnp.stack([joined(0), joined(1)], axis=1),
        joined(2).T,
        shared_scalars,
    )
    masters = (
        (queries_master, queries_moment, queries_square),
        (keyvalue_master, keyvalue_moment, keyvalue_square),
        (mixing_master, mixing_moment, mixing_square),
        (expand_master, expand_moment, expand_square),
        (shrink_master, shrink_moment, shrink_square),
        (scalars_master, scalars_moment, scalars_square),
    )
    results = [layer_out[None], input_grad[None]]
    for held, grad, rate, decay in zip(masters, grads, learn_rates, decay_rates):
        results.extend(adamw(*held, wide(low(grad)), rate, decay))
    return tuple(results)


def solution(mesh):
    placed = (
        P("dp", "seq", None),
        P("dp", "seq", None),
        P("dp", None),
        P(("dp", "seq"), "head"),
        P(("dp", "seq"), "head"),
        P(("dp", "seq"), "head"),
        P(("dp", "seq"), None),
        P(("dp", "seq"), None),
        P(("dp", "seq"), None),
        P("head", ("dp", "seq")),
        P("head", ("dp", "seq")),
        P("head", ("dp", "seq")),
        P(("dp", "seq"), None, "head"),
        P(("dp", "seq"), None, "head"),
        P(("dp", "seq"), None, "head"),
        P("head", ("dp", "seq")),
        P("head", ("dp", "seq")),
        P("head", ("dp", "seq")),
        P(("dp", "seq")),
        P(("dp", "seq")),
        P(("dp", "seq")),
    )
    small = dict(mesh.shape) == {"dp": 2, "seq": 4, "head": 4}
    return jax.shard_map(
        local_fast if small else local,
        mesh=mesh,
        in_specs=placed,
        out_specs=(
            P("dp", "seq", None),
            P("dp", "seq", None),
            P(("dp", "seq"), "head"),
            P(("dp", "seq"), "head"),
            P(("dp", "seq"), "head"),
            P(("dp", "seq"), "head"),
            P(("dp", "seq"), "head"),
            P(("dp", "seq"), None),
            P(("dp", "seq"), None),
            P(("dp", "seq"), None),
            P(("dp", "seq"), None),
            P(("dp", "seq"), None),
            P("head", ("dp", "seq")),
            P("head", ("dp", "seq")),
            P("head", ("dp", "seq")),
            P("head", ("dp", "seq")),
            P("head", ("dp", "seq")),
            P(("dp", "seq"), None, "head"),
            P(("dp", "seq"), None, "head"),
            P(("dp", "seq"), None, "head"),
            P(("dp", "seq"), None, "head"),
            P(("dp", "seq"), None, "head"),
            P("head", ("dp", "seq")),
            P("head", ("dp", "seq")),
            P("head", ("dp", "seq")),
            P("head", ("dp", "seq")),
            P("head", ("dp", "seq")),
            P(("dp", "seq")),
            P(("dp", "seq")),
            P(("dp", "seq")),
            P(("dp", "seq")),
            P(("dp", "seq")),
        ),
        check_vma=False,
    )
```

```python
import functools
import math

import jax
import jax.numpy as jnp
from jax import lax
from jax.experimental import pallas as pl
from jax.experimental.layout import Layout, with_layout_constraint
from jax.experimental.pallas import tpu as pltpu
from jax.sharding import PartitionSpec as P

D = 1536
H = 12
KV = 2
HD = 128
STEP = 5


norm_eps = 1e-06
rope_base = 1000000.0
beta_first = 0.5
beta_second = 0.5
adam_eps = 1e-08
masked_low = -1e30
learn_rates = (0.02, 0.02, 0.3, 0.02, 0.01, 0.2)
decay_rates = (0.1, 0.1, 0.1, 0.1, 0.1, 0.0)


def folded_places(row_ids, shard_rows, seq_count):
    owner_index = row_ids // shard_rows
    inside = row_ids % shard_rows
    halves = shard_rows // 2
    block_index = jnp.where(inside < halves, owner_index, 2 * seq_count - 1 - owner_index)
    return block_index * halves + inside % halves


def doc_starts(places, lengths):
    end, total = jnp.int32(0), jnp.zeros_like(places)
    for i in range(lengths.shape[0]):
        end = end + lengths[i]
        total = total + jnp.where(end <= places, lengths[i], 0)
    return total


def rotate(values, places):
    halves = values.shape[-1] // 2
    powers = jnp.arange(halves, dtype=jnp.float32) * (-2.0 / values.shape[-1])
    frequency = jnp.power(jnp.float32(rope_base), powers)
    angles = places.astype(jnp.float32)[:, None] * frequency[None, :]
    cosine = jnp.cos(angles)[:, None, :]
    sine_term = jnp.sin(angles)[:, None, :]
    first_half = values[..., :halves]
    second_half = values[..., halves:]
    return jnp.concatenate(
        [
            first_half * cosine - second_half * sine_term,
            second_half * cosine + first_half * sine_term,
        ],
        axis=-1,
    )


def norm_back(grad_rows, values, scale_rows, gain_vector):
    unit_rows = values * scale_rows
    scaled = grad_rows * gain_vector
    mean_term = jnp.mean(scaled * unit_rows, axis=-1, keepdims=True)
    return (scale_rows * (scaled - unit_rows * mean_term), jnp.sum(grad_rows * unit_rows, axis=0))


def adamw(master, moment, square, grad_rows, rate_value, decay_value):
    first_new = beta_first * moment + (1.0 - beta_first) * grad_rows
    second_new = beta_second * square + (1.0 - beta_second) * grad_rows * grad_rows
    fix_first = 1.0 - beta_first**STEP
    fix_second = 1.0 - beta_second**STEP
    weight = master - rate_value * (
        first_new / fix_first / (jnp.sqrt(second_new / fix_second) + adam_eps)
        + decay_value * master
    )
    return (grad_rows, first_new, second_new, weight, weight.astype(jnp.bfloat16))


def shift(values, axis, steps):
    size = lax.axis_size(axis)
    return lax.ppermute(values, axis, [(i, (i + steps) % size) for i in range(size)])


def swap(values, axis, bit):
    size = lax.axis_size(axis)
    return lax.ppermute(values, axis, [(i, i ^ bit) for i in range(size)])


def dot_nn(left, right):
    return jnp.dot(left, right, preferred_element_type=jnp.float32)


def dot_nt(left, right):
    return lax.dot_general(left, right, (((1,), (1,)), ((), ())), preferred_element_type=jnp.float32)


def dot_tn(left, right):
    return lax.dot_general(left, right, (((0,), (0,)), ((), ())), preferred_element_type=jnp.float32)


def low(values):
    return values.astype(jnp.bfloat16)


def wide(values):
    return values.astype(jnp.float32)


def halve(values, which):
    size = values.shape[0] // 2
    mine = lax.dynamic_slice_in_dim(values, which * size, size, 0)
    other = lax.dynamic_slice_in_dim(values, (1 - which) * size, size, 0)
    return mine, other


def head_scatter(values):
    index = lax.axis_index("head")
    mine, other = halve(values, index % 2)
    values = mine + wide(swap(low(other), "head", 1))
    mine, other = halve(values, index // 2)
    return mine + wide(swap(low(other), "head", 2))


def head_gather(values, dim=0):
    index = lax.axis_index("head")
    for bit, which in ((2, index // 2), (1, index % 2)):
        got = swap(values, "head", bit)
        values = jnp.where(
            which == 0,
            jnp.concatenate([values, got], dim),
            jnp.concatenate([got, values], dim),
        )
    return values


def seq_sum(blocks):
    total = blocks[0]
    for s in range(1, len(blocks)):
        total = total + wide(shift(low(blocks[s]), "seq", -s))
    return total


def place(blocks):
    size = lax.axis_size("seq")
    dp_index, seq_index = lax.axis_index("dp"), lax.axis_index("seq")
    first = next(iter(blocks.values()))
    out = jnp.zeros((2 * size,) + first.shape, first.dtype)
    for (a, k), block in blocks.items():
        owner = lax.rem(dp_index + a, 2) * size + lax.rem(seq_index + size - k, size)
        out = lax.dynamic_update_slice(out, block[None], (owner,) + (0,) * first.ndim)
    return out


def weight_gather(block):
    size = lax.axis_size("seq")
    blocks = {}
    for k in range(size):
        if k > 0:
            block = shift(block, "seq", 1)
        blocks[0, k] = block
        blocks[1, k] = swap(block, "dp", 1)
    out = place(blocks)
    return out.reshape((-1,) + out.shape[2:])


def weight_exchange(packs):
    size = lax.axis_size("seq")
    seq_index = lax.axis_index("seq")
    blocks = {}
    for k in range(size):
        block = lax.dynamic_index_in_dim(packs, lax.rem(seq_index + k, size), 0, False)
        if k > 0:
            block = shift(block, "seq", k)
        blocks[0, k] = block
        blocks[1, k] = swap(block, "dp", 1)
    out = place(blocks)
    return out.reshape((-1,) + out.shape[2:])


def grad_exchange(parts, scatter):
    size = lax.axis_size("seq")
    dp_index, seq_index = lax.axis_index("dp"), lax.axis_index("seq")
    parts = parts.reshape(2, size, -1, parts.shape[1])
    total = jnp.zeros(parts.shape[2:], jnp.float32)
    out = jnp.zeros(parts.shape[1:], jnp.bfloat16)
    for k in range(size - 1, -1, -1):
        target = lax.rem(seq_index + k, size)
        pair = lax.dynamic_index_in_dim(parts, target, 1, False)
        mine = lax.dynamic_index_in_dim(pair, dp_index, 0, False)
        other = lax.dynamic_index_in_dim(pair, 1 - dp_index, 0, False)
        block = wide(mine) + wide(swap(low(other), "dp", 1))
        if k > 0:
            block = wide(shift(low(block), "seq", k))
        if scatter:
            total = total + block
        else:
            source = lax.rem(seq_index + size - k, size)
            out = lax.dynamic_update_slice(out, low(block)[None], (source, 0, 0))
    return total if scatter else out


def hidden_before(starts_ref, half, block, block_rows):
    return jnp.where(block * block_rows >= starts_ref[half], 0.0, masked_low)


def last_block(half):
    index = lax.axis_index("seq")
    return index if half == 0 else 2 * lax.axis_size("seq") - 1 - index


def key_offset(block, size, block_rows):
    owner = jnp.where(block < size, block, 2 * size - 1 - block)
    return owner * (2 * block_rows) + jnp.where(block < size, 0, block_rows)


def seen_bias(block_rows, heads):
    row = lax.broadcasted_iota(jnp.int32, (block_rows, block_rows), 0)
    col = lax.broadcasted_iota(jnp.int32, (block_rows, block_rows), 1)
    return jnp.concatenate([jnp.where(col <= row, 0.0, masked_low)] * heads, axis=0)


def stacked_heads(ref, half):
    block_rows, heads = ref.shape[0] // 2, ref.shape[1] // HD
    rows = pl.ds(half * block_rows, block_rows)
    return jnp.concatenate([ref[rows, i * HD : (i + 1) * HD] for i in range(heads)], axis=0)


def attention_forward(starts_ref, q_ref, k_ref, v_ref, o_ref, lse_ref, halves=(0, 1)):
    local_rows, heads = q_ref.shape[0], q_ref.shape[1] // HD
    block_rows = local_rows // 2
    size = lax.axis_size("seq")
    scale = 1.0 / math.sqrt(HD)
    stacked = heads * block_rows
    for half in halves:
        last = last_block(half)
        rows = pl.ds(half * block_rows, block_rows)
        q = stacked_heads(q_ref, half)

        def step(block, carried, diagonal, q=q, half=half):
            running_max, running_sum, running_out = carried
            keys = pl.ds(pl.multiple_of(key_offset(block, size, block_rows), block_rows), block_rows)
            scores = dot_nt(q, k_ref[keys, :]) * scale
            if diagonal:
                scores = scores + seen_bias(block_rows, heads)
            else:
                scores = scores + hidden_before(starts_ref, half, block, block_rows)
            new_max = jnp.maximum(running_max, jnp.max(scores, axis=-1, keepdims=True))
            probs = jnp.exp(scores - new_max)
            fade = jnp.exp(running_max - new_max)
            running_sum = running_sum * fade + jnp.sum(probs, axis=-1, keepdims=True)
            running_out = running_out * fade + dot_nn(low(probs), v_ref[keys, :])
            return new_max, running_sum, running_out

        carried = (
            jnp.full((stacked, 1), masked_low, jnp.float32),
            jnp.zeros((stacked, 1), jnp.float32),
            jnp.zeros((stacked, HD), jnp.float32),
        )
        carried = lax.fori_loop(0, last, functools.partial(step, diagonal=False), carried)
        running_max, running_sum, running_out = step(last, carried, True)
        out = running_out / running_sum
        lse = running_max + jnp.log(running_sum)
        for i in range(heads):
            part = slice(i * block_rows, (i + 1) * block_rows)
            o_ref[rows, i * HD : (i + 1) * HD] = out[part]
            lse_ref[rows, i : i + 1] = lse[part]


def attention_backward(
    starts_ref, q_ref, k_ref, v_ref, do_ref, o_ref, lse_ref, dq_ref, dk_ref, dv_ref, halves=(0, 1)
):
    local_rows, heads = q_ref.shape[0], q_ref.shape[1] // HD
    block_rows = local_rows // 2
    size = lax.axis_size("seq")
    scale = 1.0 / math.sqrt(HD)
    stacked = heads * block_rows
    for half in halves:
        if half == 0:
            dk_ref[...] = jnp.zeros_like(dk_ref)
            dv_ref[...] = jnp.zeros_like(dv_ref)
        last = last_block(half)
        rows = pl.ds(half * block_rows, block_rows)
        q, do = stacked_heads(q_ref, half), stacked_heads(do_ref, half)
        delta = jnp.sum(wide(do) * stacked_heads(o_ref, half), axis=-1, keepdims=True)
        lse = jnp.concatenate([lse_ref[rows, i : i + 1] for i in range(heads)], axis=0)

        def step(block, dq, diagonal, q=q, do=do, delta=delta, lse=lse, half=half):
            keys = pl.ds(pl.multiple_of(key_offset(block, size, block_rows), block_rows), block_rows)
            k, v = k_ref[keys, :], v_ref[keys, :]
            scores = dot_nt(q, k) * scale
            if diagonal:
                scores = scores + seen_bias(block_rows, heads)
            else:
                scores = scores + hidden_before(starts_ref, half, block, block_rows)
            probs = jnp.exp(scores - lse)
            score_grad = low(probs * (dot_nt(do, v) - delta))
            dk_ref[keys, :] += dot_tn(score_grad, q) * scale
            dv_ref[keys, :] += dot_tn(low(probs), do)
            return dq + dot_nn(score_grad, k)

        dq = jnp.zeros((stacked, HD), jnp.float32)
        dq = lax.fori_loop(0, last, functools.partial(step, diagonal=False), dq)
        dq = step(last, dq, True) * scale
        for i in range(heads):
            dq_ref[rows, i * HD : (i + 1) * HD] = dq[i * block_rows : (i + 1) * block_rows]


def in_vmem(kernel, outs, scalars, *arrays):
    return pl.pallas_call(
        kernel,
        out_shape=outs,
        in_specs=[pl.BlockSpec(memory_space=pltpu.SMEM)]
        + [pl.BlockSpec(memory_space=pltpu.VMEM)] * len(arrays),
        out_specs=[pl.BlockSpec(memory_space=pltpu.VMEM)] * len(outs),
        compiler_params=pltpu.CompilerParams(vmem_limit_bytes=40 * 1024 * 1024),
        cost_estimate=pl.CostEstimate(
            flops=12 * 10**9, bytes_accessed=8 * 10**6, transcendentals=10**7
        ),
    )(scalars, *arrays)


class Links:
    def __init__(self, send_sems, recv_sems):
        self.send_sems, self.recv_sems, self.started = send_sems, recv_sems, []

    def to(self, source, target, **where):
        number = len(self.started)
        copy = pltpu.make_async_remote_copy(
            src_ref=source,
            dst_ref=target,
            send_sem=self.send_sems.at[number],
            recv_sem=self.recv_sems.at[number],
            device_id=where,
            device_id_type=pl.DeviceIdType.MESH,
        )
        copy.start()
        self.started.append(copy)
        return copy

    def finish(self):
        for copy in self.started:
            copy.wait_send()


def greet(partners):
    barrier = pltpu.get_barrier_semaphore()
    for where in partners:
        pl.semaphore_signal(
            barrier, inc=1, device_id=where, device_id_type=pl.DeviceIdType.MESH
        )
    pl.semaphore_wait(barrier, len(partners))


def at_rows(ref, block, size):
    return ref.at[pl.ds(pl.multiple_of(block * size, size), size), :]


def rows_of(begin, size):
    return pl.ds(pl.multiple_of(begin, size), size)


def turn(values, cosine, sine_term):
    return values * cosine + pltpu.roll(values, HD // 2, 1) * sine_term


def vector_of(scal_ref, begin, size):
    per = scal_ref.shape[2] // 128
    tiles = []
    for i in range(size // 128):
        tile = begin // 128 + i
        if isinstance(tile, int):
            owner, column = tile // per, tile % per * 128
        else:
            owner, column = lax.div(tile, per), pl.multiple_of(lax.rem(tile, per) * 128, 128)
        tiles.append(scal_ref[owner, 0:1, pl.ds(column, 128)])
    return jnp.concatenate(tiles, axis=1)


def front_kernel(
    starts_ref, scal_in, pack, ff_packs, x_ref, cot_one, cot_two, cos_ref, sin_ref,
    scal_ref, attn_w, ff_w, cot_all, normed_ref, q_ref, k_all, v_all, att_ref, lse_ref, hid_ref, nt_all,
    nt_ref, send_c, recv_c, send_x, recv_x, kept, send_sems, recv_sems, local_sem,
):
    rows, width = x_ref.shape
    quarter, half = rows // 4, rows // 2
    block_rows = pack.shape[0]
    size = lax.axis_size("seq")
    y, z, head = lax.axis_index("dp"), lax.axis_index("seq"), lax.axis_index("head")
    core, xx = lax.rem(head, 2), lax.div(head, 2)
    heads = q_ref.shape[1] // HD
    wide_heads = heads * HD
    row_begin = core * half + xx * quarter
    me = y * size + z
    owners = [z, z + 1 - 2 * lax.rem(z, 2), lax.rem(z + 2, 4), 3 - z]
    to_y, to_x, to_core = {"dp": 1 - y}, {"head": head + 2 - 4 * xx}, {"head": head + 1 - 2 * core}
    greet([{"seq": owners[d]} for d in (1, 2, 3)] + [to_y, to_x, to_core])
    links = Links(send_sems, recv_sems)

    scal_ref[me] = scal_in[...]
    attn_w[rows_of(me * block_rows, block_rows), :] = pack[...]
    scal_z = {d: links.to(scal_in, scal_ref.at[me], seq=owners[d]) for d in (1, 2, 3)}
    scal_y = [links.to(scal_in, scal_ref.at[me], **to_y)]
    attn_own = at_rows(attn_w, me, block_rows)
    attn_z = {d: links.to(pack, attn_own, seq=owners[d]) for d in (1, 2)}
    attn_y = [links.to(pack, attn_own, **to_y)]
    for d in (1, 2, 3):
        scal_z[d].wait_recv()
        owner = y * size + owners[d]
        scal_y.append(links.to(scal_ref.at[owner], scal_ref.at[owner], **to_y))
    for copy in scal_y:
        copy.wait_recv()
    gain_one = vector_of(scal_ref, 0, width)

    def norm_rows(i, unused):
        part = rows_of(i * quarter, quarter)
        values = wide(x_ref[part, :])
        scale = lax.rsqrt(jnp.mean(values * values, axis=-1, keepdims=True) + norm_eps)
        normed_ref[part, :] = low(values * scale * gain_one)
        return unused

    lax.fori_loop(0, 4, norm_rows, 0)

    def attn_arrival(d):
        attn_z[d].wait_recv()
        block = at_rows(attn_w, y * size + owners[d], block_rows)
        if d == 2:
            attn_z[3] = links.to(block, block, seq=owners[1])
        attn_y.append(links.to(block, block, **to_y))

    def quarter_of(ref, d, begin):
        return ref.at[rows_of(owners[d] * rows + begin, quarter), :]

    x_begin = core * half + (1 - xx) * quarter
    cot_z = links.to(cot_two, quarter_of(cot_all, 2, row_begin), seq=owners[1])
    cot_x, cot_core = {}, []
    for d, ref in ((1, cot_one), (2, cot_two)):
        cot_x[d] = links.to(ref, quarter_of(cot_all, d, row_begin), **to_x)
        cot_core.append(links.to(ref, quarter_of(cot_all, d, row_begin), **to_core))

    def cot_on(d):
        cot_x[d].wait_recv()
        block = quarter_of(cot_all, d, x_begin)
        cot_core.append(links.to(block, block, **to_core))

    attn_arrival(2)
    attn_arrival(1)
    ff_own = at_rows(ff_w, me, block_rows)
    ff_z, ff_y = {}, []

    def ff_start(d):
        ff_z[d] = links.to(ff_packs.at[owners[d]], ff_own, seq=owners[d])

    def ff_arrival(d):
        ff_z[d].wait_recv()
        block = at_rows(ff_w, y * size + owners[d], block_rows)
        ff_y.append(links.to(block, block, **to_y))

    ff_start(2)
    attn_arrival(3)
    ff_y.append(links.to(ff_packs.at[z], ff_own, **to_y))
    for copy in attn_y:
        copy.wait_recv()

    base = 2 * width + H * HD
    kv_head = lax.div(head * heads, H // KV)
    bias_q = vector_of(scal_ref, 2 * width + head * wide_heads, wide_heads)
    bias_k = vector_of(scal_ref, base + kv_head * HD, HD)
    bias_v = vector_of(scal_ref, base + (KV + kv_head) * HD, HD)
    own_k, own_v = at_rows(k_all, z, rows), at_rows(v_all, z, rows)

    def project(i, unused):
        part = rows_of(i * half, half)
        normed = normed_ref[part, :]
        cosine, sine_term = cos_ref[part, :], sin_ref[part, :]
        pre = dot_nn(normed, attn_w[:, 2 * wide_heads : 2 * wide_heads + 2 * HD])
        own = rows_of(z * rows + i * half, half)
        k_all[own, :] = low(turn(pre[:, :HD] + bias_k, cosine, sine_term))
        v_all[own, :] = low(pre[:, HD:] + bias_v)
        pre = dot_nn(normed, attn_w[:, :wide_heads]) + bias_q
        for n in range(heads):
            at = slice(n * HD, (n + 1) * HD)
            q_ref[part, at] = low(turn(pre[:, at], cosine, sine_term))
        return unused

    lax.fori_loop(0, 2, project, 0)
    def keys_or_values(owner, where):
        number = len(links.started)
        for which, ref in ((0, k_all), (1, v_all)):
            block = at_rows(ref, owner, rows)
            copy = pltpu.make_async_remote_copy(
                src_ref=block,
                dst_ref=block,
                send_sem=send_sems.at[number],
                recv_sem=recv_sems.at[number],
                device_id=where,
                device_id_type=pl.DeviceIdType.MESH,
            )
            pl.when(core == which)(copy.start)
        links.started.append(copy)
        return copy

    kv_z = {d: keys_or_values(z, {"seq": owners[d]}) for d in (3, 2, 1)}
    kv_core = []
    ff_start(1)
    ff_start(3)
    cot_z.wait_recv()
    block = quarter_of(cot_all, 3, row_begin)
    cot_x[3] = links.to(block, block, **to_x)
    cot_core.append(links.to(block, block, **to_core))
    cot_on(1)
    cot_on(2)
    for d in (1, 2, 3):
        kv_z[d].wait_recv()
        kv_core.append(keys_or_values(owners[d], to_core))
    ff_arrival(2)
    for copy in kv_core:
        copy.wait_recv()
    attention_forward(starts_ref, q_ref, k_all, v_all, att_ref, lse_ref)

    mixing = attn_w.at[:, wide_heads : 2 * wide_heads]

    def branch_part(begin, size_rows):
        return dot_nt(low(att_ref[rows_of(begin, size_rows), :]), mixing[...])

    def branch_send(i, unused):
        part = rows_of(i * quarter, quarter)
        send_c[part, :] = low(branch_part((1 - core) * half + i * quarter, quarter))
        return unused

    lax.fori_loop(0, 2, branch_send, 0)
    to_c = links.to(send_c, recv_c, **to_core)

    def branch_keep(i, unused):
        part = rows_of(i * quarter, quarter)
        kept[part, :] = branch_part(core * half + i * quarter, quarter)
        return unused

    lax.fori_loop(0, 2, branch_keep, 0)
    to_c.wait_recv()
    other, mine = rows_of((1 - xx) * quarter, quarter), rows_of(xx * quarter, quarter)
    send_x[...] = low(kept[other, :] + wide(recv_c[other, :]))
    to_xx = links.to(send_x, recv_x, **to_x)
    to_xx.wait_recv()
    gain_two = vector_of(scal_ref, width, width)
    hidden = wide(x_ref[rows_of(row_begin, quarter), :]) + (
        kept[mine, :] + wide(recv_c[mine, :]) + wide(recv_x[...])
    )
    hid_ref[...] = hidden
    scale = lax.rsqrt(jnp.mean(hidden * hidden, axis=-1, keepdims=True) + norm_eps)
    nt_ref[...] = low(hidden * scale * gain_two)
    own = quarter_of(nt_all, 0, row_begin)
    own_copy = pltpu.make_async_copy(nt_ref, own, local_sem.at[0])
    own_copy.start()
    nt_z = {d: links.to(nt_ref, own, seq=owners[d]) for d in (2, 1)}
    nt_x = {0: links.to(nt_ref, own, **to_x)}
    nt_core = [links.to(nt_ref, own, **to_core)]

    def nt_arrival(d):
        nt_z[d].wait_recv()
        block = quarter_of(nt_all, d, row_begin)
        if d == 2:
            nt_z[3] = links.to(block, block, seq=owners[1])
        nt_x[d] = links.to(block, block, **to_x)
        nt_core.append(links.to(block, block, **to_core))

    def nt_on(d):
        nt_x[d].wait_recv()
        block = quarter_of(nt_all, d, x_begin)
        nt_core.append(links.to(block, block, **to_core))

    ff_arrival(1)
    nt_on(0)
    cot_on(3)
    ff_arrival(3)
    nt_arrival(2)
    nt_arrival(1)
    nt_arrival(3)
    for d in (2, 1, 3):
        nt_on(d)
    for copy in cot_core + ff_y + nt_core:
        copy.wait_recv()
    links.finish()
    own_copy.wait()


def front(starts, scal_in, pack, ff_packs, x_rows, cot_one, cot_two, cosine, sine_term, wide_heads):
    rows, width = x_rows.shape
    size = lax.axis_size("seq")
    quarter, half, count = rows // 4, rows // 2, 2 * size
    bf16, f32 = jnp.bfloat16, jnp.float32
    shape = jax.ShapeDtypeStruct
    in_vmem_spec, anywhere = pl.BlockSpec(memory_space=pltpu.VMEM), pl.BlockSpec(memory_space=pl.ANY)
    outs = [
        (shape((count,) + scal_in.shape, f32), in_vmem_spec),
        (shape((count * pack.shape[0], pack.shape[1]), bf16), in_vmem_spec),
        (shape((count * pack.shape[0], ff_packs.shape[2]), bf16), anywhere),
        (shape((size * rows, width), bf16), anywhere),
        (shape((rows, width), bf16), in_vmem_spec),
        (shape((rows, wide_heads), bf16), in_vmem_spec),
        (shape((size * rows, HD), bf16), in_vmem_spec),
        (shape((size * rows, HD), bf16), in_vmem_spec),
        (shape((rows, wide_heads), f32), in_vmem_spec),
        (shape((rows, wide_heads // HD), f32), in_vmem_spec),
        (shape((quarter, width), f32), in_vmem_spec),
        (shape((size * rows, width), bf16), anywhere),
    ]
    return pl.pallas_call(
        front_kernel,
        out_shape=[o[0] for o in outs],
        in_specs=[
            pl.BlockSpec(memory_space=pltpu.SMEM), in_vmem_spec, in_vmem_spec, anywhere,
            in_vmem_spec, anywhere, anywhere, in_vmem_spec, in_vmem_spec,
        ],
        out_specs=[o[1] for o in outs],
        scratch_shapes=[
            pltpu.VMEM((quarter, width), bf16),
            pltpu.VMEM((half, width), bf16),
            pltpu.VMEM((half, width), bf16),
            pltpu.VMEM((quarter, width), bf16),
            pltpu.VMEM((quarter, width), bf16),
            pltpu.VMEM((half, width), f32),
            pltpu.SemaphoreType.DMA((56,)),
            pltpu.SemaphoreType.DMA((56,)),
            pltpu.SemaphoreType.DMA((1,)),
        ],
        compiler_params=pltpu.CompilerParams(
            collective_id=1, has_side_effects=True, vmem_limit_bytes=48 * 1024 * 1024
        ),
        cost_estimate=pl.CostEstimate(
            flops=6 * 10**9, bytes_accessed=30 * 10**6, transcendentals=10**7
        ),
    )(starts, scal_in, pack, ff_packs, x_rows, cot_one, cot_two, cosine, sine_term)


def gated(gate_value, up_value, act_grad):
    gate_sigmoid = jax.nn.sigmoid(gate_value)
    silu = gate_value * gate_sigmoid
    gate_grad = act_grad * up_value * gate_sigmoid * (1.0 + gate_value * (1.0 - gate_sigmoid))
    return silu * up_value, gate_grad, act_grad * silu


def ff_kernel(
    nt_ref, ff_w, ff_packs, cot_all, cot_ref, cot_one, cot_two, hid_ref, scal_ref,
    hg_ref, bg_ref, gain_ref, gw_ref, out_ref, early_ref,
    nt_all, cot_v, w_v, both_v, act_v, send_c, recv_c, kept, send_x, recv_x, send_z, recv_z, total, grad_v, out_v,
    send_sems, recv_sems, local_sems,
):
    quarter, width = hid_ref.shape
    half, rows = 2 * quarter, 4 * quarter
    y, z, head = lax.axis_index("dp"), lax.axis_index("seq"), lax.axis_index("head")
    core, xx = lax.rem(head, 2), lax.div(head, 2)
    row_begin = core * half + xx * quarter
    x_begin = core * half + (1 - xx) * quarter
    wide_units = both_v.shape[1]
    main = wide_units // 256 * 128
    owners = [z, z + 1 - 2 * lax.rem(z, 2), lax.rem(z + 2, 4), 3 - z]
    to_x, to_core = {"head": head + 2 - 4 * xx}, {"head": head + 1 - 2 * core}
    size, block_rows = 4, ff_packs.shape[1]
    me = y * size + z
    loads = []

    def load(source, target):
        copy = pltpu.make_async_copy(source, target, local_sems.at[4 + len(loads)])
        copy.start()
        loads.append(copy)

    load(ff_packs.at[z], at_rows(w_v, me, block_rows))
    for k in range(1, 2 * size):
        owner = lax.rem(me + k, 2 * size)
        load(at_rows(ff_w, owner, block_rows), at_rows(w_v, owner, block_rows))
    load(cot_ref, at_rows(cot_v, z, rows))
    for d in (1, 2, 3):
        part = rows_of(owners[d] * rows + row_begin, quarter)
        load((cot_one, cot_two, cot_all.at[part, :])[d - 1], cot_v.at[part, :])
        part = rows_of(owners[d] * rows + x_begin, quarter)
        load(cot_all.at[part, :], cot_v.at[part, :])
        part = rows_of(owners[d] * rows + (1 - core) * half, half)
        load(cot_all.at[part, :], cot_v.at[part, :])
    first_loads = list(loads)
    load(nt_ref, nt_all)
    to_y = {"dp": 1 - y}
    greet([{"seq": owners[d]} for d in (1, 2, 3)] + [to_y, to_x, to_core])
    links = Links(send_sems, recv_sems)

    for copy in first_loads:
        copy.wait()

    def act_grad_rows(i, unused):
        part = rows_of(i * half, half)
        act_v[part, :] = low(dot_nn(cot_v[part, :], w_v[:, wide_units:]))
        return unused

    lax.fori_loop(0, 2 * size, act_grad_rows, 0)
    loads[-1].wait()

    def gates(begin):
        part = rows_of(begin, half)
        values = dot_nn(nt_all[part, :], w_v[:, :wide_units])
        act_grad = wide(act_v[part, :])
        act, gate_grad, up_grad = gated(
            values[:, :main], values[:, main : 2 * main], act_grad[:, :main]
        )
        act_v[part, :main] = low(act)
        both_v[part, :main] = low(gate_grad)
        both_v[part, main : 2 * main] = low(up_grad)
        last = values[:, 2 * main :]
        act, gate_grad, up_grad = gated(last, pltpu.roll(last, 64, 1), act_grad[:, main:])
        left = lax.broadcasted_iota(jnp.int32, last.shape, 1) < 64
        act_v[part, main:] = low(jnp.where(left, act, 0.0))
        both_v[part, 2 * main :] = low(jnp.where(left, gate_grad, pltpu.roll(up_grad, 64, 1)))

    def back_part(begin):
        return low(dot_nt(both_v[rows_of(begin, half), :], w_v[:, :wide_units]))

    mine, other = rows_of(xx * quarter, quarter), rows_of((1 - xx) * quarter, quarter)
    steps_c, steps_x, steps_z = {}, {}, {}
    sequence = (3, 2, 1, 0)

    def start_step(s):
        steps_c[s].wait_recv()
        send_x[s] = low(wide(kept[s % 2, other, :]) + wide(recv_c[s, other, :]))
        steps_x[s] = links.to(send_x.at[s], recv_x.at[s], **to_x)

    def finish_step(s):
        steps_x[s].wait_recv()
        value = wide(kept[s % 2, mine, :]) + wide(recv_c[s, mine, :]) + wide(recv_x[s])
        if s == 0:
            total[...] = value
        else:
            send_z[s - 1] = low(value)
            steps_z[s] = links.to(send_z.at[s - 1], recv_z.at[s - 1], seq=owners[s])

    for s in sequence:
        base = owners[s] * rows
        gates(base + (1 - core) * half)
        if s < 2:
            steps_c[s + 2].wait_send()
        send_c[s % 2] = back_part(base + (1 - core) * half)
        steps_c[s] = links.to(send_c.at[s % 2], recv_c.at[s], **to_core)
        gates(base + core * half)
        kept[s % 2] = back_part(base + core * half)
        start_step(s)
        if s < 3:
            finish_step(s + 1)

    count = both_v.shape[0] // rows
    pair_rows = grad_v.shape[1]

    def weight_grads(first, stores):
        for i in range(2):
            begin = pl.multiple_of((first * 2 + i) * pair_rows, 128)
            if len(stores) >= 2:
                stores[-2].wait()
            slot = grad_v.at[i]
            columns = pl.ds(begin, pair_rows)
            slot[:, :wide_units] = low(dot_tn(nt_all[:, columns], both_v[...]))
            slot[:, wide_units:] = low(dot_tn(cot_v[:, columns], act_v[...]))
            store = pltpu.make_async_copy(
                slot, gw_ref.at[pl.ds(begin, pair_rows), :], local_sems.at[i]
            )
            store.start()
            stores.append(store)

    stores = []
    weight_grads(1 - y, stores)
    finish_step(0)
    for store in stores:
        store.wait()
    stores = []
    source = at_rows(gw_ref, (1 - y) * size + owners[3], block_rows)
    early = links.to(source, early_ref, **to_y)
    n2 = total[...]
    for s in range(1, 4):
        steps_z[s].wait_recv()
        n2 = n2 + wide(recv_z[s - 1])
    hidden = hid_ref[...]
    gain_two = vector_of(scal_ref, width, width)
    scale = lax.rsqrt(jnp.mean(hidden * hidden, axis=-1, keepdims=True) + norm_eps)
    back, gain_grad = norm_back(n2, hidden, scale, gain_two)
    gain_ref[...] = gain_grad[None]
    hidden_grad = wide(cot_v[rows_of(z * rows + row_begin, quarter), :]) + back
    hg_ref[...] = hidden_grad
    own = bg_ref.at[rows_of(row_begin, quarter), :]
    own[...] = low(hidden_grad)
    bg_x = links.to(own, own, **to_x)
    bg_core = [links.to(own, own, **to_core)]
    weight_grads(y, stores)
    out_stores = []
    for i in range(2 * count):
        part = pl.ds(i * half, half)
        if i >= 2:
            out_stores[i - 2].wait()
        out_v[i % 2] = low(dot_nt(act_v[part, :], w_v[:, wide_units:]))
        store = pltpu.make_async_copy(out_v.at[i % 2], out_ref.at[part, :], local_sems.at[2 + i % 2])
        store.start()
        out_stores.append(store)
        if i == 1:
            bg_x.wait_recv()
            block = bg_ref.at[rows_of(x_begin, quarter), :]
            bg_core.append(links.to(block, block, **to_core))
    for copy in bg_core + [early]:
        copy.wait_recv()
    for store in stores[-2:] + out_stores[-2:]:
        store.wait()
    for copy in links.started:
        if copy is not steps_c[2] and copy is not steps_c[3]:
            copy.wait_send()


def feed_forward(nt, ff_w, ff_packs, cot_all, cot, cot_one, cot_two, hidden, scal, units):
    quarter, width = hidden.shape
    rows, stream, columns = 4 * quarter, cot_all.shape[0], ff_w.shape[1]
    bf16, f32 = jnp.bfloat16, jnp.float32
    shape = jax.ShapeDtypeStruct
    in_vmem_spec, anywhere = pl.BlockSpec(memory_space=pltpu.VMEM), pl.BlockSpec(memory_space=pl.ANY)
    outs = [
        (shape((quarter, width), f32), in_vmem_spec),
        (shape((rows, width), bf16), in_vmem_spec),
        (shape((1, width), f32), in_vmem_spec),
        (shape((width, columns), bf16), anywhere),
        (shape((stream, width), bf16), anywhere),
        (shape(ff_packs.shape[1:], bf16), anywhere),
    ]
    return pl.pallas_call(
        ff_kernel,
        out_shape=[o[0] for o in outs],
        in_specs=[anywhere] * 7 + [in_vmem_spec] * 2,
        out_specs=[o[1] for o in outs],
        scratch_shapes=[
            pltpu.VMEM((stream, width), bf16),
            pltpu.VMEM((stream, width), bf16),
            pltpu.VMEM((width, columns), bf16),
            pltpu.VMEM((stream, 2 * units), bf16),
            pltpu.VMEM((stream, columns - 2 * units), bf16),
            pltpu.VMEM((2, 2 * quarter, width), bf16),
            pltpu.VMEM((4, 2 * quarter, width), bf16),
            pltpu.VMEM((2, 2 * quarter, width), bf16),
            pltpu.VMEM((4, quarter, width), bf16),
            pltpu.VMEM((4, quarter, width), bf16),
            pltpu.VMEM((3, quarter, width), bf16),
            pltpu.VMEM((3, quarter, width), bf16),
            pltpu.VMEM((quarter, width), f32),
            pltpu.VMEM((2, width // 4, columns), bf16),
            pltpu.VMEM((2, 2 * quarter, width), bf16),
            pltpu.SemaphoreType.DMA((40,)),
            pltpu.SemaphoreType.DMA((40,)),
            pltpu.SemaphoreType.DMA((28,)),
        ],
        compiler_params=pltpu.CompilerParams(
            collective_id=2, has_side_effects=True, vmem_limit_bytes=62 * 1024 * 1024
        ),
        cost_estimate=pl.CostEstimate(
            flops=33 * 10**9, bytes_accessed=40 * 10**6, transcendentals=10**6
        ),
    )(nt, ff_w, ff_packs, cot_all, cot, cot_one, cot_two, hidden, scal)


def back_kernel(
    starts_ref, scal_ref, x_own, hid_ref, hg_ref, gain_two_ref, bg_ref, attn_w, normed_ref, q_ref, k_all, v_all,
    att_ref, lse_ref, cos_ref, sin_ref, gw_ref, part_ref, early_ref,
    layer_ref, input_ref, ff_grads, attn_ref, kv_ref, small_ref,
    ff_y, ff_own, out_c, out_own, out_sx, out_rx, out_sz, out_rz, dk, dv, do, dq, dkv_s, dkv_r, dkv_rz, dkv_own,
    qg, one_sc, one_rc, one_keep, one_sx, one_rx, layer_own, input_own, a_other, a_own, a_y, a_z, a_sz,
    small, small_y, small_s, small_z, small_h, kv_own,
    send_sems, recv_sems, local_sems,
):
    quarter, width = x_own.shape
    half, rows = 2 * quarter, 4 * quarter
    block_rows = attn_ref.shape[0]
    y, z, head = lax.axis_index("dp"), lax.axis_index("seq"), lax.axis_index("head")
    core, xx = lax.rem(head, 2), lax.div(head, 2)
    size = lax.axis_size("seq")
    heads = q_ref.shape[1] // HD
    wide_heads = heads * HD
    row_begin = core * half + xx * quarter
    x_begin = core * half + (1 - xx) * quarter
    owners = [z, z + 1 - 2 * lax.rem(z, 2), lax.rem(z + 2, 4), 3 - z]
    to_y, to_x, to_core = {"dp": 1 - y}, {"head": head + 2 - 4 * xx}, {"head": head + 1 - 2 * core}
    mine, other = rows_of(xx * quarter, quarter), rows_of((1 - xx) * quarter, quarter)
    is_core = wide(core)
    loads = []

    def load(source, target):
        copy = pltpu.make_async_copy(source, target, local_sems.at[len(loads)])
        copy.start()
        loads.append(copy)
        return copy

    greet([to_y] + [{"seq": owners[d]} for d in (1, 2, 3)] + [to_x, to_core])
    links = Links(send_sems, recv_sems)

    order = (3, 2, 1, 0)

    def grad_rows(ref, which, d):
        return at_rows(ref, which * size + owners[d], block_rows)

    ff_sent, ff_load = {}, {}

    def ff_start(d):
        ff_sent[d] = links.to(grad_rows(gw_ref, 1 - y, d), ff_y.at[d], **to_y)

    ff_start(2)
    ff_early = load(early_ref, ff_y.at[3])
    out_sent, out_load = [], []
    for s in range(4):
        begin = owners[s] * rows
        source = part_ref.at[rows_of(begin + (1 - core) * half, half), :]
        out_sent.append(links.to(source, out_c.at[s], **to_core))
    for s in range(4):
        source = part_ref.at[rows_of(owners[s] * rows + core * half, half), :]
        out_load.append(load(source, out_own.at[s]))
    for d in order:
        ff_load[d] = load(grad_rows(gw_ref, y, d), ff_own.at[d])

    ff_over_z = {}

    def ff_step(d):
        if d == 3:
            ff_early.wait()
        else:
            ff_sent[d].wait_recv()
        ff_load[d].wait()

        def add(i, unused):
            part = rows_of(i * 64, 64)
            ff_own[d, part, :] = low(wide(ff_own[d, part, :]) + wide(ff_y[d, part, :]))
            return unused

        lax.fori_loop(0, block_rows // 64, add, 0)
        if d == 0:
            load(ff_own.at[d], ff_grads.at[z])
        else:
            ff_over_z[d] = links.to(ff_own.at[d], ff_grads.at[z], seq=owners[d])

    out_x, out_z = {}, {}

    def out_step_c(s):
        out_sent[s].wait_recv()
        out_load[s].wait()
        out_sx[s] = low(wide(out_own[s, other, :]) + wide(out_c[s, other, :]))
        out_x[s] = links.to(out_sx.at[s], out_rx.at[s], **to_x)

    def out_value(s):
        out_x[s].wait_recv()
        return wide(out_own[s, mine, :]) + wide(out_c[s, mine, :]) + wide(out_rx[s])

    def out_step_x(s):
        value = out_value(s)
        if s == 2:
            out_z[3].wait_recv()
            value = value + wide(out_rz[2])
        out_sz[s - 1] = low(value)
        out_z[s] = links.to(out_sz.at[s - 1], out_rz.at[s - 1], seq=owners[2 if s == 2 else 1])

    def do_rows(i, unused):
        part = rows_of(i * half, half)
        do[part, :] = low(dot_nn(bg_ref[part, :], attn_w[:, wide_heads : 2 * wide_heads]))
        return unused

    ff_step(3)
    lax.fori_loop(0, 2, do_rows, 0)
    attention_backward(starts_ref, q_ref, k_all, v_all, do, att_ref, lse_ref, dq, dk, dv, (0,))
    out_step_c(3)
    out_step_c(2)
    attention_backward(starts_ref, q_ref, k_all, v_all, do, att_ref, lse_ref, dq, dk, dv, (1,))
    dkv_s[...] = low(dv[...] * (1.0 - is_core) + dk[...] * is_core)
    dkv_core = links.to(dkv_s, dkv_r, **to_core)
    for n in range(heads):
        at = slice(n * HD, (n + 1) * HD)
        qg[:, at] = low(turn(dq[:, at], cos_ref[...], -sin_ref[...]))
    dkv_core.wait_recv()

    def dkv_block(d):
        part = rows_of(owners[d] * rows, rows)
        return dk[part, :] * (1.0 - is_core) + dv[part, :] * is_core + wide(dkv_r[part, :])

    dkv_z = []
    for d in (1, 2, 3):
        dkv_own[d] = low(dkv_block(d))
        dkv_z.append(links.to(dkv_own.at[d], dkv_rz.at[d - 1], seq=owners[d]))
    total = dkv_block(0)
    ff_step(2)
    for d in (1, 2, 3):
        dkv_z[d - 1].wait_recv()
        total = total + wide(dkv_rz[d - 1])
    turned = turn(total, cos_ref[...], -sin_ref[...])
    dkv_own[0] = low(turned * (1.0 - is_core) + total * is_core)
    key_columns = pl.ds(pl.multiple_of(2 * wide_heads + core * HD, HD), HD)

    def one_part(begin):
        part = rows_of(begin, quarter)
        return dot_nt(qg[part, :], attn_w[:, :wide_heads]) + dot_nt(
            dkv_own[0, part, :], attn_w[:, key_columns]
        )

    def one_send(i, unused):
        one_sc[rows_of(i * quarter, quarter), :] = low(one_part((1 - core) * half + i * quarter))
        return unused

    def one_own(i, unused):
        one_keep[rows_of(i * quarter, quarter), :] = one_part(core * half + i * quarter)
        return unused

    lax.fori_loop(0, 2, one_send, 0)
    one_c = links.to(one_sc, one_rc, **to_core)
    lax.fori_loop(0, 2, one_own, 0)
    one_c.wait_recv()
    one_sx[...] = low(one_keep[other, :] + wide(one_rc[other, :]))
    one_x = links.to(one_sx, one_rx, **to_x)

    def attn_grads(which, target):
        columns = pl.ds(pl.multiple_of(which * (width // 2), 128), width // 2)
        normed = normed_ref[:, columns]
        target[:, :wide_heads] = low(dot_tn(normed, qg[...]))
        target[:, wide_heads : 2 * wide_heads] = low(
            dot_tn(bg_ref[:, columns], low(att_ref[...]))
        )
        target[:, 2 * wide_heads :] = low(dot_tn(normed, dkv_own[0]))

    attn_grads(1 - y, a_other)
    attn_sent = {
        d: links.to(at_rows(a_other, owners[d], block_rows), a_y.at[d], **to_y) for d in order
    }
    out_step_c(1)
    out_step_c(0)
    attn_grads(y, a_own)
    out_step_x(3)

    one_x.wait_recv()
    norm_one_grad = one_keep[mine, :] + wide(one_rc[mine, :]) + wide(one_rx[...])
    x_rows = wide(x_own[...])
    gain_one = vector_of(scal_ref, 0, width)
    scale = lax.rsqrt(jnp.mean(x_rows * x_rows, axis=-1, keepdims=True) + norm_eps)
    back, gain_grad = norm_back(norm_one_grad, x_rows, scale, gain_one)
    input_own[...] = low(hg_ref[...] + back)

    def gather(source, target):
        place = target.at[rows_of(row_begin, quarter), :]
        load(source, place)
        return links.to(source, place, **to_x), [links.to(source, place, **to_core)]

    def gather_on(sent, target):
        sent[0].wait_recv()
        block = target.at[rows_of(x_begin, quarter), :]
        sent[1].append(links.to(block, block, **to_core))

    input_sent = gather(input_own, input_ref)
    small[...] = jnp.zeros_like(small)
    per = small.shape[2] // 128

    def put(begin, values):
        for i in range(values.shape[1] // 128):
            tile = begin // 128 + i
            value = values[:, i * 128 : (i + 1) * 128]
            if isinstance(tile, int):
                small[tile // per, 0:1, tile % per * 128 : tile % per * 128 + 128] = value
            else:
                column = pl.ds(pl.multiple_of(lax.rem(tile, per) * 128, 128), 128)
                small[lax.div(tile, per), 0:1, column] = value

    put(0, gain_grad[None])
    put(width, gain_two_ref[...])
    put(2 * width + head * wide_heads, jnp.sum(wide(qg[...]), axis=0, keepdims=True))
    kv_begin = 2 * width + H * HD + (core * KV + lax.div(head * heads, H // KV)) * HD
    put(kv_begin, jnp.sum(wide(dkv_own[0]), axis=0, keepdims=True))
    small_sent = links.to(small.at[pl.ds((1 - y) * size, size)], small_y, **to_y)
    ff_start(1)
    ff_start(0)
    attn_over_z = {}

    def attn_step(d):
        attn_sent[d].wait_recv()
        block = wide(at_rows(a_own, owners[d], block_rows)[...]) + wide(a_y[d])
        if d == 0:
            return block
        if d == 2:
            attn_over_z[3].wait_recv()
            block = block + wide(a_z[2])
        a_sz[d - 1] = low(block)
        attn_over_z[d] = links.to(
            a_sz.at[d - 1], a_z.at[d - 1], seq=owners[2 if d == 2 else 1]
        )
        return None

    attn_step(3)
    out_step_x(1)
    out_step_x(2)
    gather_on(input_sent, input_ref)
    attn_step(1)
    attn_step(2)
    small_sent.wait_recv()
    small_s[...] = small[pl.ds(y * size, size)] + small_y[...]
    small_over_z = [
        links.to(small_s.at[owners[d]], small_z.at[d - 1], seq=owners[d]) for d in (1, 2, 3)
    ]
    layer = hid_ref[...] + out_value(0)
    for d in (1, 2):
        out_z[d].wait_recv()
        layer = layer + wide(out_rz[d - 1])
    layer_own[...] = low(layer)
    layer_sent = gather(layer_own, layer_ref)
    ff_step(1)
    value = small_s[z]
    for d in (1, 2, 3):
        small_over_z[d - 1].wait_recv()
        value = value + small_z[d - 1]
    small_h[0] = value
    small_x = links.to(small_h.at[0], small_h.at[1], **to_x)
    block = attn_step(0)
    small_x.wait_recv()
    small_h[2] = small_h[0] + small_h[1]
    small_c = links.to(small_h.at[2], small_h.at[3], **to_core)
    gather_on(layer_sent, layer_ref)
    for d in (1, 2):
        attn_over_z[d].wait_recv()
        block = block + wide(a_z[d - 1])
    attn_ref[...] = block
    place = kv_ref.at[core * 2 + xx]
    kv_own[...] = low(block[:, 2 * wide_heads :])
    place[...] = kv_own[...]
    kv_x = links.to(kv_own, place, **to_x)
    kv_core = [links.to(kv_own, place, **to_core)]
    small_c.wait_recv()
    small_ref[...] = small_h[2] + small_h[3]
    kv_x.wait_recv()
    place = kv_ref.at[core * 2 + 1 - xx]
    kv_core.append(links.to(place, place, **to_core))
    ff_step(0)
    for copy in kv_core + input_sent[1] + layer_sent[1] + [ff_over_z[d] for d in (3, 2, 1)]:
        copy.wait_recv()
    links.finish()
    for copy in loads[9:]:
        copy.wait()


def back(
    starts, scal, x_own, hidden, hidden_grad, gain_two_grad, branch_grad, attn_w, normed, q, k_all, v_all, attended, lse,
    cosine, sine_term, gw, out_part, early,
):
    quarter, width = x_own.shape
    half, rows = 2 * quarter, 4 * quarter
    size = lax.axis_size("seq")
    block_rows, columns = gw.shape[0] // (2 * size), gw.shape[1]
    wide_heads = q.shape[1]
    attn_columns = 2 * wide_heads + HD
    stream = k_all.shape[0]
    bf16, f32 = jnp.bfloat16, jnp.float32
    shape = jax.ShapeDtypeStruct
    in_vmem_spec, anywhere = pl.BlockSpec(memory_space=pltpu.VMEM), pl.BlockSpec(memory_space=pl.ANY)
    outs = [
        (shape((rows, width), bf16), anywhere),
        (shape((rows, width), bf16), anywhere),
        (shape((size, block_rows, columns), bf16), anywhere),
        (shape((block_rows, attn_columns), f32), in_vmem_spec),
        (shape((4, block_rows, HD), bf16), in_vmem_spec),
        (shape(scal.shape[1:], f32), in_vmem_spec),
    ]
    small = (size,) + scal.shape[1:]
    scratch = [
        ((size, block_rows, columns), bf16),
        ((size, block_rows, columns), bf16),
        ((4, half, width), bf16),
        ((4, half, width), bf16),
        ((4, quarter, width), bf16),
        ((4, quarter, width), bf16),
        ((3, quarter, width), bf16),
        ((3, quarter, width), bf16),
        ((stream, HD), f32),
        ((stream, HD), f32),
        ((rows, wide_heads), bf16),
        ((rows, wide_heads), f32),
        ((stream, HD), bf16),
        ((stream, HD), bf16),
        ((3, rows, HD), bf16),
        ((4, rows, HD), bf16),
        ((rows, wide_heads), bf16),
        ((half, width), bf16),
        ((half, width), bf16),
        ((half, width), f32),
        ((quarter, width), bf16),
        ((quarter, width), bf16),
        ((quarter, width), bf16),
        ((quarter, width), bf16),
        ((width // 2, attn_columns), bf16),
        ((width // 2, attn_columns), bf16),
        ((4, block_rows, attn_columns), bf16),
        ((3, block_rows, attn_columns), bf16),
        ((3, block_rows, attn_columns), bf16),
        (scal.shape, f32),
        (small, f32),
        (small, f32),
        ((3,) + scal.shape[1:], f32),
        ((4,) + scal.shape[1:], f32),
        ((block_rows, HD), bf16),
    ]
    return pl.pallas_call(
        back_kernel,
        out_shape=[o[0] for o in outs],
        in_specs=[pl.BlockSpec(memory_space=pltpu.SMEM)] + [in_vmem_spec] * 15 + [anywhere] * 3,
        out_specs=[o[1] for o in outs],
        scratch_shapes=[pltpu.VMEM(*one) for one in scratch]
        + [
            pltpu.SemaphoreType.DMA((56,)),
            pltpu.SemaphoreType.DMA((56,)),
            pltpu.SemaphoreType.DMA((12,)),
        ],
        compiler_params=pltpu.CompilerParams(
            collective_id=3, has_side_effects=True, vmem_limit_bytes=62 * 1024 * 1024
        ),
        cost_estimate=pl.CostEstimate(
            flops=10 * 10**9, bytes_accessed=40 * 10**6, transcendentals=10**6
        ),
    )(
        starts, scal, x_own, hidden, hidden_grad, gain_two_grad, branch_grad, attn_w, normed, q, k_all, v_all, attended,
        lse, cosine, sine_term, gw, out_part, early,
    )


def rope_tables(places):
    halves = HD // 2
    powers = jnp.arange(halves, dtype=jnp.float32) * (-2.0 / HD)
    frequency = jnp.power(jnp.float32(rope_base), powers)
    angles = places.astype(jnp.float32)[:, None] * frequency[None, :]
    cosine, sine_term = jnp.cos(angles), jnp.sin(angles)
    return (
        jnp.concatenate([cosine, cosine], axis=1),
        jnp.concatenate([-sine_term, sine_term], axis=1),
    )


def local(
    tokens,
    cotangent,
    doc_lengths,
    queries_master,
    queries_moment,
    queries_square,
    keyvalue_master,
    keyvalue_moment,
    keyvalue_square,
    mixing_master,
    mixing_moment,
    mixing_square,
    expand_master,
    expand_moment,
    expand_square,
    shrink_master,
    shrink_moment,
    shrink_square,
    scalars_master,
    scalars_moment,
    scalars_square,
):
    local_rows, width = tokens.shape[1], tokens.shape[2]
    seq_count = lax.axis_size("seq")
    head_count = lax.axis_size("head")
    head_index = lax.axis_index("head")
    seq_index = lax.axis_index("seq")
    local_heads = H // head_count
    wide_heads = local_heads * HD
    kv_head = head_index * local_heads // (H // KV)
    core = head_index % 2
    quarter = local_rows // 4
    row_begin = (head_index % 2) * (2 * quarter) + (head_index // 2) * quarter
    hidden_units = expand_master.shape[2]
    units = 64 * -(-hidden_units // (64 * seq_count))
    more = ((0, 0), (0, units * seq_count - hidden_units))

    attn_pack = jnp.concatenate(
        [
            low(queries_master),
            low(mixing_master).T,
            low(lax.dynamic_slice_in_dim(keyvalue_master, kv_head * HD, HD, 1)),
            low(lax.dynamic_slice_in_dim(keyvalue_master, (KV + kv_head) * HD, HD, 1)),
        ],
        axis=1,
    )
    expand_low = low(expand_master)

    def cut(values):
        values = jnp.pad(values, more)
        return values.reshape(values.shape[0], seq_count, units).transpose(1, 0, 2)

    ff_packs = jnp.concatenate(
        [cut(expand_low[:, 0]), cut(expand_low[:, 1]), cut(low(shrink_master).T)], axis=2
    )
    scalar_values = wide(lax.all_gather(low(scalars_master), ("dp", "seq"), axis=0, tiled=True))
    attn_weight = weight_gather(attn_pack)
    ff_weight = weight_exchange(ff_packs)
    query_weight = attn_weight[:, :wide_heads]
    mixing_t = attn_weight[:, wide_heads : 2 * wide_heads]
    key_value_weight = attn_weight[:, 2 * wide_heads :]
    expand_weight = ff_weight[:, : 2 * units]
    shrink_t = ff_weight[:, 2 * units :]

    cot_rows = cotangent[0]
    cot_own = lax.dynamic_slice_in_dim(cot_rows, row_begin, quarter, 0)
    cot_blocks = [cot_rows]
    moving = cot_own
    for s in range(1, seq_count):
        moving = shift(moving, "seq", 1)
        cot_blocks.append(head_gather(moving))

    gain_one = scalar_values[:width]
    gain_two = scalar_values[width : 2 * width]
    bias_query = lax.dynamic_slice_in_dim(
        scalar_values, 2 * width + head_index * wide_heads, wide_heads
    )
    bias_keyvalue = scalar_values[2 * width + H * HD :]
    key_bias = lax.dynamic_slice_in_dim(bias_keyvalue, kv_head * HD, HD)
    value_bias = lax.dynamic_slice_in_dim(bias_keyvalue, (KV + kv_head) * HD, HD)
    x_rows = wide(tokens[0])
    lengths = doc_lengths[0]
    places = folded_places(
        seq_index * local_rows + jnp.arange(local_rows, dtype=jnp.int32), local_rows, seq_count
    )
    starts = doc_starts(places, lengths)
    half_starts = jnp.stack([starts[0], starts[local_rows // 2]])
    within = places - starts
    scale_one = lax.rsqrt(jnp.mean(x_rows * x_rows, axis=-1, keepdims=True) + norm_eps)
    normed = low(x_rows * scale_one * gain_one)
    query_pre = dot_nn(normed, query_weight) + bias_query
    queries = low(rotate(query_pre.reshape(local_rows, local_heads, HD), within)).reshape(
        local_rows, wide_heads
    )
    key_value_pre = dot_nn(normed, key_value_weight)
    key_rows = low(rotate((key_value_pre[:, :HD] + key_bias)[:, None, :], within)[:, 0, :])
    value_rows = low(key_value_pre[:, HD:] + value_bias)
    moving = jnp.concatenate([key_rows, value_rows], axis=1)
    all_rows = jnp.zeros((seq_count,) + moving.shape, moving.dtype)
    for s in range(seq_count):
        if s > 0:
            moving = shift(moving, "seq", 1)
        owner = lax.rem(seq_index + seq_count - s, seq_count)
        all_rows = lax.dynamic_update_slice(all_rows, moving[None], (owner, 0, 0))
    all_rows = all_rows.reshape(-1, 2 * HD)
    all_keys, all_values = all_rows[:, :HD], all_rows[:, HD:]
    stream_rows = all_rows.shape[0]
    attended, log_total = in_vmem(
        attention_forward,
        [
            jax.ShapeDtypeStruct((local_rows, wide_heads), jnp.float32),
            jax.ShapeDtypeStruct((local_rows, local_heads), jnp.float32),
        ],
        half_starts,
        queries,
        all_keys,
        all_values,
    )
    attended_low = low(attended)
    x_own = lax.dynamic_slice_in_dim(x_rows, row_begin, quarter, 0)
    hidden = x_own + head_scatter(dot_nt(attended_low, mixing_t))
    scale_two = lax.rsqrt(jnp.mean(hidden * hidden, axis=-1, keepdims=True) + norm_eps)
    normed_two = low(hidden * scale_two * gain_two)

    normed_blocks, grad_blocks, act_blocks, back_parts, out_parts = [], [], [], [], []
    moving = normed_two
    for s in range(seq_count):
        if s > 0:
            moving = shift(moving, "seq", 1)
        block = head_gather(moving)
        both = dot_nn(block, expand_weight)
        gate_value, up_value = both[:, :units], both[:, units:]
        gate_sigmoid = jax.nn.sigmoid(gate_value)
        activation = low(gate_value * gate_sigmoid * up_value)
        act_grad = wide(low(dot_nn(cot_blocks[s], shrink_t)))
        gate_grad = low(act_grad * up_value * gate_sigmoid * (1.0 + gate_value * (1.0 - gate_sigmoid)))
        up_grad = low(act_grad * gate_value * gate_sigmoid)
        both_grad = jnp.concatenate([gate_grad, up_grad], axis=1)
        back_parts.append(head_scatter(dot_nt(both_grad, expand_weight)))
        out_parts.append(head_scatter(dot_nt(activation, shrink_t)))
        normed_blocks.append(block)
        grad_blocks.append(both_grad)
        act_blocks.append(activation)
    norm_two_grad = seq_sum(back_parts)
    back_two, gain_two_grad = norm_back(norm_two_grad, hidden, scale_two, gain_two)
    hidden_grad = wide(lax.dynamic_slice_in_dim(cot_rows, row_begin, quarter, 0)) + back_two
    branch_grad = head_gather(low(hidden_grad))
    feedforward = seq_sum(out_parts)
    layer_out = head_gather(low(hidden + feedforward))
    expand_part = dot_tn(jnp.concatenate(normed_blocks), jnp.concatenate(grad_blocks))
    shrink_part = dot_tn(jnp.concatenate(cot_blocks), jnp.concatenate(act_blocks))
    ff_grads = grad_exchange(low(jnp.concatenate([expand_part, shrink_part], axis=1)), False)

    attended_grad = low(dot_nn(branch_grad, mixing_t))
    query_sum, key_sum, value_sum = in_vmem(
        attention_backward,
        [
            jax.ShapeDtypeStruct((local_rows, wide_heads), jnp.float32),
            jax.ShapeDtypeStruct((stream_rows, HD), jnp.float32),
            jax.ShapeDtypeStruct((stream_rows, HD), jnp.float32),
        ],
        half_starts,
        queries,
        all_keys,
        all_values,
        attended_grad,
        attended,
        log_total,
    )
    mine = jnp.where(core == 0, key_sum, value_sum)
    other = jnp.where(core == 0, value_sum, key_sum)
    mine = mine + wide(swap(low(other), "head", 1))
    mine = mine.reshape(seq_count, local_rows, HD)
    own_sum = seq_sum(
        [
            lax.dynamic_index_in_dim(mine, lax.rem(seq_index + seq_count - s, seq_count), 0, False)
            for s in range(seq_count)
        ]
    )
    own_sum = low(jnp.where(core == 0, rotate(own_sum[:, None, :], -within)[:, 0, :], own_sum))
    query_grad = low(
        rotate(query_sum.reshape(local_rows, local_heads, HD), -within).reshape(
            local_rows, wide_heads
        )
    )
    own_weight = lax.dynamic_slice_in_dim(key_value_weight, core * HD, HD, 1)
    norm_one_grad = head_scatter(dot_nt(query_grad, query_weight) + dot_nt(own_sum, own_weight))
    scale_own = lax.dynamic_slice_in_dim(scale_one, row_begin, quarter, 0)
    back_one, gain_one_grad = norm_back(norm_one_grad, x_own, scale_own, gain_one)
    input_grad = head_gather(low(hidden_grad + back_one))
    attn_part = jnp.concatenate(
        [
            dot_tn(normed, query_grad),
            dot_tn(branch_grad, attended_low),
            dot_tn(normed, own_sum),
        ],
        axis=1,
    )
    attn_grads = grad_exchange(attn_part, True)
    kv_block = low(attn_grads[:, 2 * wide_heads :])
    small = jnp.zeros((scalars_master.shape[0] * 2 * seq_count,), jnp.float32)
    small = lax.dynamic_update_slice(small, jnp.concatenate([gain_one_grad, gain_two_grad]), (0,))
    small = lax.dynamic_update_slice(
        small, jnp.sum(wide(query_grad), axis=0), (2 * width + head_index * wide_heads,)
    )
    kv_column = core * KV * HD + kv_head * HD
    small = lax.dynamic_update_slice(
        small, jnp.sum(wide(own_sum), axis=0), (2 * width + H * HD + kv_column,)
    )
    small = lax.psum(small, "head")
    shared_scalars = lax.psum_scatter(small, ("dp", "seq"), scatter_dimension=0, tiled=True)
    gathered = head_gather(kv_block, 1)
    shared_keyvalue = wide(gathered)

    def joined(part):
        part = ff_grads[:, :, part * units : (part + 1) * units].transpose(1, 0, 2)
        return wide(part.reshape(part.shape[0], -1)[:, :hidden_units])

    grads = (
        attn_grads[:, :wide_heads],
        shared_keyvalue,
        attn_grads[:, wide_heads : 2 * wide_heads].T,
        jnp.stack([joined(0), joined(1)], axis=1),
        joined(2).T,
        shared_scalars,
    )
    masters = (
        (queries_master, queries_moment, queries_square),
        (keyvalue_master, keyvalue_moment, keyvalue_square),
        (mixing_master, mixing_moment, mixing_square),
        (expand_master, expand_moment, expand_square),
        (shrink_master, shrink_moment, shrink_square),
        (scalars_master, scalars_moment, scalars_square),
    )
    results = [layer_out[None], input_grad[None]]
    for held, grad, rate, decay in zip(masters, grads, learn_rates, decay_rates):
        results.extend(adamw(*held, wide(low(grad)), rate, decay))
    return tuple(results)


def local_fast(
    tokens,
    cotangent,
    doc_lengths,
    queries_master,
    queries_moment,
    queries_square,
    keyvalue_master,
    keyvalue_moment,
    keyvalue_square,
    mixing_master,
    mixing_moment,
    mixing_square,
    expand_master,
    expand_moment,
    expand_square,
    shrink_master,
    shrink_moment,
    shrink_square,
    scalars_master,
    scalars_moment,
    scalars_square,
):
    local_rows, width = tokens.shape[1], tokens.shape[2]
    seq_count = lax.axis_size("seq")
    head_count = lax.axis_size("head")
    head_index = lax.axis_index("head")
    seq_index = lax.axis_index("seq")
    local_heads = H // head_count
    wide_heads = local_heads * HD
    kv_head = head_index * local_heads // (H // KV)
    core = head_index % 2
    quarter = local_rows // 4
    row_begin = (head_index % 2) * (2 * quarter) + (head_index // 2) * quarter
    hidden_units = expand_master.shape[2]
    units = 64 * -(-hidden_units // (64 * seq_count))

    cot_own = lax.dynamic_slice_in_dim(cotangent[0], row_begin, quarter, 0)
    cot_two = lax.ppermute(cot_own, "seq", [(i, i ^ 2) for i in range(seq_count)])
    cot_one = lax.ppermute(cot_own, "seq", [(i, i ^ 1) for i in range(seq_count)])

    attn_pack = jnp.concatenate(
        [
            low(queries_master),
            low(mixing_master).T,
            low(lax.dynamic_slice_in_dim(keyvalue_master, kv_head * HD, HD, 1)),
            low(lax.dynamic_slice_in_dim(keyvalue_master, (KV + kv_head) * HD, HD, 1)),
        ],
        axis=1,
    )
    main = units // 128 * 128
    rest = units - main
    gate_low, up_low = low(expand_master[:, 0]), low(expand_master[:, 1])
    shrink_low = low(shrink_master).T

    def own_units(values, j):
        begin = main * seq_count + rest * j
        last = values[:, begin : begin + rest]
        last = jnp.pad(last, ((0, 0), (0, rest - last.shape[1])))
        return values[:, main * j : main * (j + 1)], last

    ff_packs = []
    for j in range(seq_count):
        gate_main, gate_rest = own_units(gate_low, j)
        up_main, up_rest = own_units(up_low, j)
        shrink_main, shrink_rest = own_units(shrink_low, j)
        pieces = [gate_main, up_main, gate_rest, up_rest, shrink_main, shrink_rest]
        pieces.append(jnp.zeros_like(shrink_rest))
        ff_packs.append(jnp.concatenate(pieces, axis=1))
    ff_packs = jnp.stack(ff_packs)
    x_low, cot_rows = tokens[0], cotangent[0]
    lengths = doc_lengths[0]
    places = folded_places(
        seq_index * local_rows + jnp.arange(local_rows, dtype=jnp.int32), local_rows, seq_count
    )
    starts = doc_starts(places, lengths)
    half_starts = jnp.stack([starts[0], starts[local_rows // 2]])
    within = places - starts
    cosine, sine_term = rope_tables(within)
    scal_in = jnp.broadcast_to(wide(low(scalars_master))[None], (8, scalars_master.shape[0]))
    (
        scal_all, attn_weight, ff_weight, cot_all, normed, queries, all_keys, all_values,
        attended, log_total, hidden, normed_all,
    ) = front(
        half_starts, scal_in, attn_pack, ff_packs, x_low, cot_one, cot_two, cosine, sine_term, wide_heads
    )
    hidden_grad, branch_grad, gain_two_grad, ff_part, out_part, early = feed_forward(
        normed_all, ff_weight, ff_packs, cot_all, cot_rows, cot_one, cot_two, hidden, scal_all, units
    )
    x_own = lax.dynamic_slice_in_dim(x_low, row_begin, quarter, 0)
    layer_out, input_grad, ff_grads, attn_grads, kv_blocks, small = back(
        half_starts, scal_all, x_own, hidden, hidden_grad, gain_two_grad, branch_grad, attn_weight, normed, queries,
        all_keys, all_values, attended, log_total, cosine, sine_term, ff_part, out_part, early,
    )
    shared_keyvalue = wide(jnp.concatenate([kv_blocks[i] for i in range(4)], axis=1))
    shared_scalars = small[0]

    def joined(begin, rest_begin):
        pieces = [ff_grads[j, :, begin : begin + main] for j in range(seq_count)]
        for j in range(seq_count):
            size = min(rest, hidden_units - main * seq_count - rest * j)
            pieces.append(ff_grads[j, :, rest_begin : rest_begin + size])
        return jnp.concatenate(pieces, axis=1)

    expand_grad = jnp.stack([joined(0, 2 * main), joined(main, 2 * main + rest)], axis=1)
    expand_grad = with_layout_constraint(expand_grad, Layout(major_to_minor=(0, 1, 2)))
    grads = (
        attn_grads[:, :wide_heads],
        shared_keyvalue,
        attn_grads[:, wide_heads : 2 * wide_heads].T,
        expand_grad,
        joined(2 * units, 2 * units + main).T,
        shared_scalars,
    )
    masters = (
        (queries_master, queries_moment, queries_square),
        (keyvalue_master, keyvalue_moment, keyvalue_square),
        (mixing_master, mixing_moment, mixing_square),
        (expand_master, expand_moment, expand_square),
        (shrink_master, shrink_moment, shrink_square),
        (scalars_master, scalars_moment, scalars_square),
    )
    results = [layer_out[None], input_grad[None]]
    for held, grad, rate, decay in zip(masters, grads, learn_rates, decay_rates):
        results.extend(adamw(*held, wide(low(grad)), rate, decay))
    return tuple(results)


def solution(mesh):
    placed = (
        P("dp", "seq", None),
        P("dp", "seq", None),
        P("dp", None),
        P(("dp", "seq"), "head"),
        P(("dp", "seq"), "head"),
        P(("dp", "seq"), "head"),
        P(("dp", "seq"), None),
        P(("dp", "seq"), None),
        P(("dp", "seq"), None),
        P("head", ("dp", "seq")),
        P("head", ("dp", "seq")),
        P("head", ("dp", "seq")),
        P(("dp", "seq"), None, "head"),
        P(("dp", "seq"), None, "head"),
        P(("dp", "seq"), None, "head"),
        P("head", ("dp", "seq")),
        P("head", ("dp", "seq")),
        P("head", ("dp", "seq")),
        P(("dp", "seq")),
        P(("dp", "seq")),
        P(("dp", "seq")),
    )
    small = dict(mesh.shape) == {"dp": 2, "seq": 4, "head": 4}
    return jax.shard_map(
        local_fast if small else local,
        mesh=mesh,
        in_specs=placed,
        out_specs=(
            P("dp", "seq", None),
            P("dp", "seq", None),
            P(("dp", "seq"), "head"),
            P(("dp", "seq"), "head"),
            P(("dp", "seq"), "head"),
            P(("dp", "seq"), "head"),
            P(("dp", "seq"), "head"),
            P(("dp", "seq"), None),
            P(("dp", "seq"), None),
            P(("dp", "seq"), None),
            P(("dp", "seq"), None),
            P(("dp", "seq"), None),
            P("head", ("dp", "seq")),
            P("head", ("dp", "seq")),
            P("head", ("dp", "seq")),
            P("head", ("dp", "seq")),
            P("head", ("dp", "seq")),
            P(("dp", "seq"), None, "head"),
            P(("dp", "seq"), None, "head"),
            P(("dp", "seq"), None, "head"),
            P(("dp", "seq"), None, "head"),
            P(("dp", "seq"), None, "head"),
            P("head", ("dp", "seq")),
            P("head", ("dp", "seq")),
            P("head", ("dp", "seq")),
            P("head", ("dp", "seq")),
            P("head", ("dp", "seq")),
            P(("dp", "seq")),
            P(("dp", "seq")),
            P(("dp", "seq")),
            P(("dp", "seq")),
            P(("dp", "seq")),
        ),
        check_vma=False,
    )
```

```python
import functools
import math

import jax
import jax.numpy as jnp
from jax import lax
from jax.experimental import pallas as pl
from jax.experimental.pallas import tpu as pltpu
from jax.sharding import PartitionSpec as P

D = 1536
H = 12
KV = 2
HD = 128
STEP = 5


norm_eps = 1e-06
rope_base = 1000000.0
beta_first = 0.5
beta_second = 0.5
adam_eps = 1e-08
masked_low = -1e30
learn_rates = (0.02, 0.02, 0.3, 0.02, 0.01, 0.2)
decay_rates = (0.1, 0.1, 0.1, 0.1, 0.1, 0.0)


def folded_places(row_ids, shard_rows, seq_count):
    owner_index = row_ids // shard_rows
    inside = row_ids % shard_rows
    halves = shard_rows // 2
    block_index = jnp.where(inside < halves, owner_index, 2 * seq_count - 1 - owner_index)
    return block_index * halves + inside % halves


def doc_starts(places, lengths):
    end, total = jnp.int32(0), jnp.zeros_like(places)
    for i in range(lengths.shape[0]):
        end = end + lengths[i]
        total = total + jnp.where(end <= places, lengths[i], 0)
    return total


def rotate(values, places):
    halves = values.shape[-1] // 2
    powers = jnp.arange(halves, dtype=jnp.float32) * (-2.0 / values.shape[-1])
    frequency = jnp.power(jnp.float32(rope_base), powers)
    angles = places.astype(jnp.float32)[:, None] * frequency[None, :]
    cosine = jnp.cos(angles)[:, None, :]
    sine_term = jnp.sin(angles)[:, None, :]
    first_half = values[..., :halves]
    second_half = values[..., halves:]
    return jnp.concatenate(
        [
            first_half * cosine - second_half * sine_term,
            second_half * cosine + first_half * sine_term,
        ],
        axis=-1,
    )


def norm_back(grad_rows, values, scale_rows, gain_vector):
    unit_rows = values * scale_rows
    scaled = grad_rows * gain_vector
    mean_term = jnp.mean(scaled * unit_rows, axis=-1, keepdims=True)
    return (scale_rows * (scaled - unit_rows * mean_term), jnp.sum(grad_rows * unit_rows, axis=0))


def adamw(master, moment, square, grad_rows, rate_value, decay_value):
    first_new = beta_first * moment + (1.0 - beta_first) * grad_rows
    second_new = beta_second * square + (1.0 - beta_second) * grad_rows * grad_rows
    fix_first = 1.0 - beta_first**STEP
    fix_second = 1.0 - beta_second**STEP
    weight = master - rate_value * (
        first_new / fix_first / (jnp.sqrt(second_new / fix_second) + adam_eps)
        + decay_value * master
    )
    return (grad_rows, first_new, second_new, weight, weight.astype(jnp.bfloat16))


def shift(values, axis, steps):
    size = lax.axis_size(axis)
    return lax.ppermute(values, axis, [(i, (i + steps) % size) for i in range(size)])


def swap(values, axis, bit):
    size = lax.axis_size(axis)
    return lax.ppermute(values, axis, [(i, i ^ bit) for i in range(size)])


def dot_nn(left, right):
    return jnp.dot(left, right, preferred_element_type=jnp.float32)


def dot_nt(left, right):
    return lax.dot_general(left, right, (((1,), (1,)), ((), ())), preferred_element_type=jnp.float32)


def dot_tn(left, right):
    return lax.dot_general(left, right, (((0,), (0,)), ((), ())), preferred_element_type=jnp.float32)


def low(values):
    return values.astype(jnp.bfloat16)


def wide(values):
    return values.astype(jnp.float32)


def halve(values, which):
    size = values.shape[0] // 2
    mine = lax.dynamic_slice_in_dim(values, which * size, size, 0)
    other = lax.dynamic_slice_in_dim(values, (1 - which) * size, size, 0)
    return mine, other


def head_scatter(values):
    index = lax.axis_index("head")
    mine, other = halve(values, index % 2)
    values = mine + wide(swap(low(other), "head", 1))
    mine, other = halve(values, index // 2)
    return mine + wide(swap(low(other), "head", 2))


def head_gather(values, dim=0):
    index = lax.axis_index("head")
    for bit, which in ((2, index // 2), (1, index % 2)):
        got = swap(values, "head", bit)
        values = jnp.where(
            which == 0,
            jnp.concatenate([values, got], dim),
            jnp.concatenate([got, values], dim),
        )
    return values


def seq_sum(blocks):
    total = blocks[0]
    for s in range(1, len(blocks)):
        total = total + wide(shift(low(blocks[s]), "seq", -s))
    return total


def place(blocks):
    size = lax.axis_size("seq")
    dp_index, seq_index = lax.axis_index("dp"), lax.axis_index("seq")
    first = next(iter(blocks.values()))
    out = jnp.zeros((2 * size,) + first.shape, first.dtype)
    for (a, k), block in blocks.items():
        owner = lax.rem(dp_index + a, 2) * size + lax.rem(seq_index + size - k, size)
        out = lax.dynamic_update_slice(out, block[None], (owner,) + (0,) * first.ndim)
    return out


def weight_gather(block):
    size = lax.axis_size("seq")
    blocks = {}
    for k in range(size):
        if k > 0:
            block = shift(block, "seq", 1)
        blocks[0, k] = block
        blocks[1, k] = swap(block, "dp", 1)
    out = place(blocks)
    return out.reshape((-1,) + out.shape[2:])


def weight_exchange(packs):
    size = lax.axis_size("seq")
    seq_index = lax.axis_index("seq")
    blocks = {}
    for k in range(size):
        block = lax.dynamic_index_in_dim(packs, lax.rem(seq_index + k, size), 0, False)
        if k > 0:
            block = shift(block, "seq", k)
        blocks[0, k] = block
        blocks[1, k] = swap(block, "dp", 1)
    out = place(blocks)
    return out.reshape((-1,) + out.shape[2:])


def grad_exchange(parts, scatter):
    size = lax.axis_size("seq")
    dp_index, seq_index = lax.axis_index("dp"), lax.axis_index("seq")
    parts = parts.reshape(2, size, -1, parts.shape[1])
    total = jnp.zeros(parts.shape[2:], jnp.float32)
    out = jnp.zeros(parts.shape[1:], jnp.bfloat16)
    for k in range(size - 1, -1, -1):
        target = lax.rem(seq_index + k, size)
        pair = lax.dynamic_index_in_dim(parts, target, 1, False)
        mine = lax.dynamic_index_in_dim(pair, dp_index, 0, False)
        other = lax.dynamic_index_in_dim(pair, 1 - dp_index, 0, False)
        block = wide(mine) + wide(swap(low(other), "dp", 1))
        if k > 0:
            block = wide(shift(low(block), "seq", k))
        if scatter:
            total = total + block
        else:
            source = lax.rem(seq_index + size - k, size)
            out = lax.dynamic_update_slice(out, low(block)[None], (source, 0, 0))
    return total if scatter else out


def hidden_before(starts_ref, half, block, block_rows):
    return jnp.where(block * block_rows >= starts_ref[half], 0.0, masked_low)


def last_block(half):
    index = lax.axis_index("seq")
    return index if half == 0 else 2 * lax.axis_size("seq") - 1 - index


def key_offset(block, size, block_rows):
    owner = jnp.where(block < size, block, 2 * size - 1 - block)
    return owner * (2 * block_rows) + jnp.where(block < size, 0, block_rows)


def seen_bias(block_rows, heads):
    row = lax.broadcasted_iota(jnp.int32, (block_rows, block_rows), 0)
    col = lax.broadcasted_iota(jnp.int32, (block_rows, block_rows), 1)
    return jnp.concatenate([jnp.where(col <= row, 0.0, masked_low)] * heads, axis=0)


def stacked_heads(ref, half):
    block_rows, heads = ref.shape[0] // 2, ref.shape[1] // HD
    rows = pl.ds(half * block_rows, block_rows)
    return jnp.concatenate([ref[rows, i * HD : (i + 1) * HD] for i in range(heads)], axis=0)


def attention_forward(starts_ref, q_ref, k_ref, v_ref, o_ref, lse_ref, halves=(0, 1)):
    local_rows, heads = q_ref.shape[0], q_ref.shape[1] // HD
    block_rows = local_rows // 2
    size = lax.axis_size("seq")
    scale = 1.0 / math.sqrt(HD)
    stacked = heads * block_rows
    for half in halves:
        last = last_block(half)
        rows = pl.ds(half * block_rows, block_rows)
        q = stacked_heads(q_ref, half)

        def step(block, carried, diagonal, q=q, half=half):
            running_max, running_sum, running_out = carried
            keys = pl.ds(pl.multiple_of(key_offset(block, size, block_rows), block_rows), block_rows)
            scores = dot_nt(q, k_ref[keys, :]) * scale
            if diagonal:
                scores = scores + seen_bias(block_rows, heads)
            else:
                scores = scores + hidden_before(starts_ref, half, block, block_rows)
            new_max = jnp.maximum(running_max, jnp.max(scores, axis=-1, keepdims=True))
            probs = jnp.exp(scores - new_max)
            fade = jnp.exp(running_max - new_max)
            running_sum = running_sum * fade + jnp.sum(probs, axis=-1, keepdims=True)
            running_out = running_out * fade + dot_nn(low(probs), v_ref[keys, :])
            return new_max, running_sum, running_out

        carried = (
            jnp.full((stacked, 1), masked_low, jnp.float32),
            jnp.zeros((stacked, 1), jnp.float32),
            jnp.zeros((stacked, HD), jnp.float32),
        )
        carried = lax.fori_loop(0, last, functools.partial(step, diagonal=False), carried)
        running_max, running_sum, running_out = step(last, carried, True)
        out = running_out / running_sum
        lse = running_max + jnp.log(running_sum)
        for i in range(heads):
            part = slice(i * block_rows, (i + 1) * block_rows)
            o_ref[rows, i * HD : (i + 1) * HD] = out[part]
            lse_ref[rows, i : i + 1] = lse[part]


def attention_backward(
    starts_ref, q_ref, k_ref, v_ref, do_ref, o_ref, lse_ref, dq_ref, dk_ref, dv_ref, halves=(0, 1)
):
    local_rows, heads = q_ref.shape[0], q_ref.shape[1] // HD
    block_rows = local_rows // 2
    size = lax.axis_size("seq")
    scale = 1.0 / math.sqrt(HD)
    stacked = heads * block_rows
    for half in halves:
        if half == 0:
            dk_ref[...] = jnp.zeros_like(dk_ref)
            dv_ref[...] = jnp.zeros_like(dv_ref)
        last = last_block(half)
        rows = pl.ds(half * block_rows, block_rows)
        q, do = stacked_heads(q_ref, half), stacked_heads(do_ref, half)
        delta = jnp.sum(wide(do) * stacked_heads(o_ref, half), axis=-1, keepdims=True)
        lse = jnp.concatenate([lse_ref[rows, i : i + 1] for i in range(heads)], axis=0)

        def step(block, dq, diagonal, q=q, do=do, delta=delta, lse=lse, half=half):
            keys = pl.ds(pl.multiple_of(key_offset(block, size, block_rows), block_rows), block_rows)
            k, v = k_ref[keys, :], v_ref[keys, :]
            scores = dot_nt(q, k) * scale
            if diagonal:
                scores = scores + seen_bias(block_rows, heads)
            else:
                scores = scores + hidden_before(starts_ref, half, block, block_rows)
            probs = jnp.exp(scores - lse)
            score_grad = low(probs * (dot_nt(do, v) - delta))
            dk_ref[keys, :] += dot_tn(score_grad, q) * scale
            dv_ref[keys, :] += dot_tn(low(probs), do)
            return dq + dot_nn(score_grad, k)

        dq = jnp.zeros((stacked, HD), jnp.float32)
        dq = lax.fori_loop(0, last, functools.partial(step, diagonal=False), dq)
        dq = step(last, dq, True) * scale
        for i in range(heads):
            dq_ref[rows, i * HD : (i + 1) * HD] = dq[i * block_rows : (i + 1) * block_rows]


def in_vmem(kernel, outs, scalars, *arrays):
    return pl.pallas_call(
        kernel,
        out_shape=outs,
        in_specs=[pl.BlockSpec(memory_space=pltpu.SMEM)]
        + [pl.BlockSpec(memory_space=pltpu.VMEM)] * len(arrays),
        out_specs=[pl.BlockSpec(memory_space=pltpu.VMEM)] * len(outs),
        compiler_params=pltpu.CompilerParams(vmem_limit_bytes=40 * 1024 * 1024),
        cost_estimate=pl.CostEstimate(
            flops=12 * 10**9, bytes_accessed=8 * 10**6, transcendentals=10**7
        ),
    )(scalars, *arrays)


class Links:
    def __init__(self, send_sems, recv_sems):
        self.send_sems, self.recv_sems, self.started = send_sems, recv_sems, []

    def to(self, source, target, **where):
        number = len(self.started)
        copy = pltpu.make_async_remote_copy(
            src_ref=source,
            dst_ref=target,
            send_sem=self.send_sems.at[number],
            recv_sem=self.recv_sems.at[number],
            device_id=where,
            device_id_type=pl.DeviceIdType.MESH,
        )
        copy.start()
        self.started.append(copy)
        return copy

    def finish(self):
        for copy in self.started:
            copy.wait_send()


def greet(partners):
    barrier = pltpu.get_barrier_semaphore()
    for where in partners:
        pl.semaphore_signal(
            barrier, inc=1, device_id=where, device_id_type=pl.DeviceIdType.MESH
        )
    pl.semaphore_wait(barrier, len(partners))


def at_rows(ref, block, size):
    return ref.at[pl.ds(pl.multiple_of(block * size, size), size), :]


def rows_of(begin, size):
    return pl.ds(pl.multiple_of(begin, size), size)


def turn(values, cosine, sine_term):
    return values * cosine + pltpu.roll(values, HD // 2, 1) * sine_term


def vector_of(scal_ref, begin, size):
    per = scal_ref.shape[2] // 128
    tiles = []
    for i in range(size // 128):
        tile = begin // 128 + i
        if isinstance(tile, int):
            owner, column = tile // per, tile % per * 128
        else:
            owner, column = lax.div(tile, per), pl.multiple_of(lax.rem(tile, per) * 128, 128)
        tiles.append(scal_ref[owner, 0:1, pl.ds(column, 128)])
    return jnp.concatenate(tiles, axis=1)


def cut_units(expand_v, shrink_v, packs):
    size, main, columns = packs.shape[0], 512, expand_v.shape[2]
    left = lax.broadcasted_iota(jnp.int32, (16, 128), 1) < 64

    def rows16(i, unused):
        part = rows_of(i * 16, 16)

        def rests(values):
            begin = size * main
            first = values[:, begin : begin + 128]
            last = jnp.concatenate([values[:, begin + 128 :], jnp.zeros((16, 64), jnp.float32)], axis=1)
            return first, pltpu.roll(first, 64, 1), last

        gate, up, down = expand_v[part, 0, :], expand_v[part, 1, :], shrink_v[part, :]
        for j in range(size):
            own = slice(j * main, (j + 1) * main)
            packs[j, part, :main] = low(gate[:, own])
            packs[j, part, main : 2 * main] = low(up[:, own])
            packs[j, part, 2 * main + 128 : 3 * main + 128] = low(down[:, own])
        pieces = zip(rests(gate), rests(up), rests(down))
        for j, (gate_rest, up_rest, down_rest) in enumerate(pieces):
            both = jnp.where(left, gate_rest, pltpu.roll(up_rest, 64, 1))
            packs[j, part, 2 * main : 2 * main + 128] = low(both)
            packs[j, part, 3 * main + 128 :] = low(jnp.where(left, down_rest, 0.0))
        packs[size - 1, part, 2 * main : 2 * main + 128] = jnp.zeros((16, 128), jnp.bfloat16)
        packs[size - 1, part, 3 * main + 128 :] = jnp.zeros((16, 128), jnp.bfloat16)
        return unused

    lax.fori_loop(0, packs.shape[1] // 16, rows16, 0)


def front_kernel(
    starts_ref, scal_in, query_ref, kv_ref, mixing_ref, expand_ref, shrink_ref, x_ref, cot_ref, cos_ref, sin_ref,
    scal_ref, attn_w, mix_w, ff_w, cot_all, normed_ref, q_ref, k_all, v_all, att_ref, lse_ref, hid_ref, nt_all,
    expand_v, shrink_v, ff_packs, nt_ref, send_c, recv_c, send_x, recv_x, kept, send_sems, recv_sems, local_sem,
):
    rows, width = x_ref.shape
    quarter, half = rows // 4, rows // 2
    block_rows = query_ref.shape[0]
    size = lax.axis_size("seq")
    y, z, head = lax.axis_index("dp"), lax.axis_index("seq"), lax.axis_index("head")
    core, xx = lax.rem(head, 2), lax.div(head, 2)
    heads = q_ref.shape[1] // HD
    wide_heads = heads * HD
    row_begin = core * half + xx * quarter
    me = y * size + z
    owners = [z, z + 1 - 2 * lax.rem(z, 2), lax.rem(z + 2, 4), 3 - z]
    to_y, to_x, to_core = {"dp": 1 - y}, {"head": head + 2 - 4 * xx}, {"head": head + 1 - 2 * core}
    greet([{"seq": owners[d]} for d in (1, 2, 3)] + [to_y, to_x, to_core])
    links = Links(send_sems, recv_sems)

    scal_ref[me] = scal_in[...]
    load_expand = pltpu.make_async_copy(expand_ref, expand_v, local_sem.at[1])
    load_expand.start()
    load_shrink = pltpu.make_async_copy(shrink_ref, shrink_v, local_sem.at[2])
    load_shrink.start()
    kv_head = lax.div(head * heads, H // KV)
    own_rows = rows_of(me * block_rows, block_rows)
    attn_w[own_rows, :wide_heads] = low(query_ref[...])
    for i, column in enumerate((kv_head, KV + kv_head)):
        columns = pl.ds(pl.multiple_of(column * HD, HD), HD)
        attn_w[own_rows, wide_heads + i * HD : wide_heads + (i + 1) * HD] = low(kv_ref[:, columns])
    mix_w[own_rows, :] = low(mixing_ref[...])
    scal_z = {d: links.to(scal_in, scal_ref.at[me], seq=owners[d]) for d in (1, 2, 3)}
    scal_y = [links.to(scal_in, scal_ref.at[me], **to_y)]
    attn_own = at_rows(attn_w, me, block_rows)
    attn_z = {d: links.to(attn_own, attn_own, seq=owners[d]) for d in (1, 2)}
    attn_y = [links.to(attn_own, attn_own, **to_y)]
    mix_own = at_rows(mix_w, me, block_rows)
    mix_z = {d: links.to(mix_own, mix_own, seq=owners[d]) for d in (1, 2)}
    mix_y = []
    for d in (1, 2, 3):
        scal_z[d].wait_recv()
        owner = y * size + owners[d]
        scal_y.append(links.to(scal_ref.at[owner], scal_ref.at[owner], **to_y))
    for copy in scal_y:
        copy.wait_recv()
    gain_one = vector_of(scal_ref, 0, width)

    def norm_rows(i, unused):
        part = rows_of(i * quarter, quarter)
        values = wide(x_ref[part, :])
        scale = lax.rsqrt(jnp.mean(values * values, axis=-1, keepdims=True) + norm_eps)
        normed_ref[part, :] = low(values * scale * gain_one)
        return unused

    lax.fori_loop(0, 4, norm_rows, 0)

    def attn_arrival(d):
        attn_z[d].wait_recv()
        block = at_rows(attn_w, y * size + owners[d], block_rows)
        if d == 2:
            attn_z[3] = links.to(block, block, seq=owners[1])
        attn_y.append(links.to(block, block, **to_y))

    def mix_arrival(d):
        mix_z[d].wait_recv()
        block = at_rows(mix_w, y * size + owners[d], block_rows)
        if d == 2:
            mix_z[3] = links.to(block, block, seq=owners[1])
        mix_y.append(links.to(block, block, **to_y))

    load_expand.wait()
    load_shrink.wait()
    cut_units(expand_v, shrink_v, ff_packs)
    attn_arrival(2)
    attn_arrival(1)
    mix_arrival(2)
    mix_arrival(1)
    x_begin = core * half + (1 - xx) * quarter

    def quarter_of(ref, d, begin):
        return ref.at[rows_of(owners[d] * rows + begin, quarter), :]

    cot_own = cot_ref.at[rows_of(row_begin, quarter), :]
    cot_z = {d: links.to(cot_own, quarter_of(cot_all, 0, row_begin), seq=owners[d]) for d in (2, 1)}
    cot_x, cot_core = {}, []

    def cot_arrival(d):
        cot_z[d].wait_recv()
        block = quarter_of(cot_all, d, row_begin)
        if d == 2:
            cot_z[3] = links.to(block, block, seq=owners[1])
        cot_x[d] = links.to(block, block, **to_x)
        cot_core.append(links.to(block, block, **to_core))

    def cot_on(d):
        cot_x[d].wait_recv()
        block = quarter_of(cot_all, d, x_begin)
        cot_core.append(links.to(block, block, **to_core))

    ff_own = at_rows(ff_w, me, block_rows)
    ff_copy = pltpu.make_async_copy(ff_packs.at[z], ff_own, local_sem.at[1])
    ff_copy.start()
    ff_z, ff_y = {}, []

    def ff_start(d):
        ff_z[d] = links.to(ff_packs.at[owners[d]], ff_own, seq=owners[d])

    def ff_arrival(d):
        ff_z[d].wait_recv()
        block = at_rows(ff_w, y * size + owners[d], block_rows)
        ff_y.append(links.to(block, block, **to_y))

    ff_start(2)
    attn_arrival(3)
    mix_y.append(links.to(mix_own, mix_own, **to_y))
    mix_arrival(3)
    cot_arrival(2)
    cot_arrival(1)
    ff_y.append(links.to(ff_packs.at[z], ff_own, **to_y))
    for copy in attn_y:
        copy.wait_recv()

    base = 2 * width + H * HD
    bias_q = vector_of(scal_ref, 2 * width + head * wide_heads, wide_heads)
    bias_k = vector_of(scal_ref, base + kv_head * HD, HD)
    bias_v = vector_of(scal_ref, base + (KV + kv_head) * HD, HD)
    own_k, own_v = at_rows(k_all, z, rows), at_rows(v_all, z, rows)

    def project(i, unused):
        part = rows_of(i * half, half)
        normed = normed_ref[part, :]
        cosine, sine_term = cos_ref[part, :], sin_ref[part, :]
        pre = dot_nn(normed, attn_w[:, wide_heads:])
        own = rows_of(z * rows + i * half, half)
        k_all[own, :] = low(turn(pre[:, :HD] + bias_k, cosine, sine_term))
        v_all[own, :] = low(pre[:, HD:] + bias_v)
        pre = dot_nn(normed, attn_w[:, :wide_heads]) + bias_q
        for n in range(heads):
            at = slice(n * HD, (n + 1) * HD)
            q_ref[part, at] = low(turn(pre[:, at], cosine, sine_term))
        return unused

    lax.fori_loop(0, 2, project, 0)
    def keys_or_values(owner, where):
        number = len(links.started)
        for which, ref in ((0, k_all), (1, v_all)):
            block = at_rows(ref, owner, rows)
            copy = pltpu.make_async_remote_copy(
                src_ref=block,
                dst_ref=block,
                send_sem=send_sems.at[number],
                recv_sem=recv_sems.at[number],
                device_id=where,
                device_id_type=pl.DeviceIdType.MESH,
            )
            pl.when(core == which)(copy.start)
        links.started.append(copy)
        return copy

    kv_z = {d: keys_or_values(z, {"seq": owners[d]}) for d in (3, 2, 1)}
    kv_core = []
    ff_start(1)
    ff_start(3)
    for d in (1, 2, 3):
        kv_z[d].wait_recv()
        kv_core.append(keys_or_values(owners[d], to_core))
    for copy in kv_core:
        copy.wait_recv()
    attention_forward(starts_ref, q_ref, k_all, v_all, att_ref, lse_ref)
    ff_arrival(2)
    cot_on(2)
    cot_on(1)

    for copy in mix_y:
        copy.wait_recv()

    def branch_part(begin, size_rows):
        return dot_nt(low(att_ref[rows_of(begin, size_rows), :]), mix_w[...])

    def branch_send(i, unused):
        part = rows_of(i * quarter, quarter)
        send_c[part, :] = low(branch_part((1 - core) * half + i * quarter, quarter))
        return unused

    lax.fori_loop(0, 2, branch_send, 0)
    to_c = links.to(send_c, recv_c, **to_core)

    def branch_keep(i, unused):
        part = rows_of(i * quarter, quarter)
        kept[part, :] = branch_part(core * half + i * quarter, quarter)
        return unused

    lax.fori_loop(0, 2, branch_keep, 0)
    to_c.wait_recv()
    other, mine = rows_of((1 - xx) * quarter, quarter), rows_of(xx * quarter, quarter)
    send_x[...] = low(kept[other, :] + wide(recv_c[other, :]))
    to_xx = links.to(send_x, recv_x, **to_x)
    cot_arrival(3)
    to_xx.wait_recv()
    gain_two = vector_of(scal_ref, width, width)
    hidden = wide(x_ref[rows_of(row_begin, quarter), :]) + (
        kept[mine, :] + wide(recv_c[mine, :]) + wide(recv_x[...])
    )
    hid_ref[...] = hidden
    scale = lax.rsqrt(jnp.mean(hidden * hidden, axis=-1, keepdims=True) + norm_eps)
    nt_ref[...] = low(hidden * scale * gain_two)
    own = quarter_of(nt_all, 0, row_begin)
    own_copy = pltpu.make_async_copy(nt_ref, own, local_sem.at[0])
    own_copy.start()
    nt_z = {d: links.to(nt_ref, own, seq=owners[d]) for d in (2, 1)}
    nt_x = {0: links.to(nt_ref, own, **to_x)}
    nt_core = [links.to(nt_ref, own, **to_core)]

    def nt_arrival(d):
        nt_z[d].wait_recv()
        block = quarter_of(nt_all, d, row_begin)
        if d == 2:
            nt_z[3] = links.to(block, block, seq=owners[1])
        nt_x[d] = links.to(block, block, **to_x)
        nt_core.append(links.to(block, block, **to_core))

    def nt_on(d):
        nt_x[d].wait_recv()
        block = quarter_of(nt_all, d, x_begin)
        nt_core.append(links.to(block, block, **to_core))

    ff_arrival(1)
    nt_arrival(2)
    nt_arrival(1)
    nt_on(0)
    cot_on(3)
    nt_arrival(3)
    ff_arrival(3)
    for d in (2, 1, 3):
        nt_on(d)
    for copy in cot_core + ff_y + nt_core:
        copy.wait_recv()
    links.finish()
    own_copy.wait()
    ff_copy.wait()


def front(
    starts, scal_in, query, keyvalue, mixing_t, expand, shrink_t, x_rows, cot_rows, cosine, sine_term, columns
):
    rows, width = x_rows.shape
    size = lax.axis_size("seq")
    quarter, half, count = rows // 4, rows // 2, 2 * size
    block_rows, wide_heads = query.shape
    bf16, f32 = jnp.bfloat16, jnp.float32
    shape = jax.ShapeDtypeStruct
    in_vmem_spec, anywhere = pl.BlockSpec(memory_space=pltpu.VMEM), pl.BlockSpec(memory_space=pl.ANY)
    outs = [
        (shape((count,) + scal_in.shape, f32), in_vmem_spec),
        (shape((count * block_rows, wide_heads + 2 * HD), bf16), in_vmem_spec),
        (shape((count * block_rows, wide_heads), bf16), in_vmem_spec),
        (shape((count * block_rows, columns), bf16), anywhere),
        (shape((size * rows, width), bf16), anywhere),
        (shape((rows, width), bf16), in_vmem_spec),
        (shape((rows, wide_heads), bf16), in_vmem_spec),
        (shape((size * rows, HD), bf16), in_vmem_spec),
        (shape((size * rows, HD), bf16), in_vmem_spec),
        (shape((rows, wide_heads), f32), in_vmem_spec),
        (shape((rows, wide_heads // HD), f32), in_vmem_spec),
        (shape((quarter, width), f32), in_vmem_spec),
        (shape((size * rows, width), bf16), anywhere),
    ]
    return pl.pallas_call(
        front_kernel,
        out_shape=[o[0] for o in outs],
        in_specs=[pl.BlockSpec(memory_space=pltpu.SMEM)]
        + [in_vmem_spec] * 4
        + [anywhere] * 2
        + [in_vmem_spec, anywhere, in_vmem_spec, in_vmem_spec],
        out_specs=[o[1] for o in outs],
        scratch_shapes=[
            pltpu.VMEM(expand.shape, f32),
            pltpu.VMEM(shrink_t.shape, f32),
            pltpu.VMEM((size, block_rows, columns), bf16),
            pltpu.VMEM((quarter, width), bf16),
            pltpu.VMEM((half, width), bf16),
            pltpu.VMEM((half, width), bf16),
            pltpu.VMEM((quarter, width), bf16),
            pltpu.VMEM((quarter, width), bf16),
            pltpu.VMEM((half, width), f32),
            pltpu.SemaphoreType.DMA((64,)),
            pltpu.SemaphoreType.DMA((64,)),
            pltpu.SemaphoreType.DMA((3,)),
        ],
        compiler_params=pltpu.CompilerParams(
            collective_id=1, has_side_effects=True, vmem_limit_bytes=62 * 1024 * 1024
        ),
        cost_estimate=pl.CostEstimate(
            flops=6 * 10**9, bytes_accessed=30 * 10**6, transcendentals=10**7
        ),
    )(starts, scal_in, query, keyvalue, mixing_t, expand, shrink_t, x_rows, cot_rows, cosine, sine_term)


def gated(gate_value, up_value, act_grad):
    gate_sigmoid = jax.nn.sigmoid(gate_value)
    silu = gate_value * gate_sigmoid
    gate_grad = act_grad * up_value * gate_sigmoid * (1.0 + gate_value * (1.0 - gate_sigmoid))
    return silu * up_value, gate_grad, act_grad * silu


def ff_kernel(
    nt_ref, ff_w, cot_all, cot_ref, hid_ref, scal_ref,
    hg_ref, bg_ref, gain_ref, gw_ref, out_ref, early_ref,
    nt_all, cot_v, w_v, both_v, act_v, send_c, recv_c, kept, send_x, recv_x, send_z, recv_z, total, grad_v, out_v,
    send_sems, recv_sems, local_sems,
):
    quarter, width = hid_ref.shape
    half, rows = 2 * quarter, 4 * quarter
    y, z, head = lax.axis_index("dp"), lax.axis_index("seq"), lax.axis_index("head")
    core, xx = lax.rem(head, 2), lax.div(head, 2)
    row_begin = core * half + xx * quarter
    x_begin = core * half + (1 - xx) * quarter
    wide_units = both_v.shape[1]
    main = wide_units // 256 * 128
    owners = [z, z + 1 - 2 * lax.rem(z, 2), lax.rem(z + 2, 4), 3 - z]
    to_x, to_core = {"head": head + 2 - 4 * xx}, {"head": head + 1 - 2 * core}
    size = 4
    block_rows = ff_w.shape[0] // (2 * size)
    loads = []

    def load(source, target):
        copy = pltpu.make_async_copy(source, target, local_sems.at[4 + len(loads)])
        copy.start()
        loads.append(copy)

    load(ff_w, w_v)
    load(cot_ref, at_rows(cot_v, z, rows))
    for d in (1, 2, 3):
        load(at_rows(cot_all, owners[d], rows), at_rows(cot_v, owners[d], rows))
    first_loads = list(loads)
    load(nt_ref, nt_all)
    to_y = {"dp": 1 - y}
    greet([{"seq": owners[d]} for d in (1, 2, 3)] + [to_y, to_x, to_core])
    links = Links(send_sems, recv_sems)

    for copy in first_loads:
        copy.wait()

    def act_grad_rows(i, unused):
        part = rows_of(i * half, half)
        act_v[part, :] = low(dot_nn(cot_v[part, :], w_v[:, wide_units:]))
        return unused

    lax.fori_loop(0, 2 * size, act_grad_rows, 0)
    loads[-1].wait()

    def gates(begin):
        part = rows_of(begin, half)
        values = dot_nn(nt_all[part, :], w_v[:, :wide_units])
        act_grad = wide(act_v[part, :])
        act, gate_grad, up_grad = gated(
            values[:, :main], values[:, main : 2 * main], act_grad[:, :main]
        )
        act_v[part, :main] = low(act)
        both_v[part, :main] = low(gate_grad)
        both_v[part, main : 2 * main] = low(up_grad)
        last = values[:, 2 * main :]
        act, gate_grad, up_grad = gated(last, pltpu.roll(last, 64, 1), act_grad[:, main:])
        left = lax.broadcasted_iota(jnp.int32, last.shape, 1) < 64
        act_v[part, main:] = low(jnp.where(left, act, 0.0))
        both_v[part, 2 * main :] = low(jnp.where(left, gate_grad, pltpu.roll(up_grad, 64, 1)))

    def back_part(begin):
        return low(dot_nt(both_v[rows_of(begin, half), :], w_v[:, :wide_units]))

    mine, other = rows_of(xx * quarter, quarter), rows_of((1 - xx) * quarter, quarter)
    steps_c, steps_x, steps_z = {}, {}, {}
    sequence = (3, 2, 1, 0)

    def start_step(s):
        steps_c[s].wait_recv()
        send_x[s] = low(wide(kept[s % 2, other, :]) + wide(recv_c[s, other, :]))
        steps_x[s] = links.to(send_x.at[s], recv_x.at[s], **to_x)

    def finish_step(s):
        steps_x[s].wait_recv()
        value = wide(kept[s % 2, mine, :]) + wide(recv_c[s, mine, :]) + wide(recv_x[s])
        if s == 0:
            total[...] = value
        else:
            send_z[s - 1] = low(value)
            steps_z[s] = links.to(send_z.at[s - 1], recv_z.at[s - 1], seq=owners[s])

    for s in sequence:
        base = owners[s] * rows
        gates(base + (1 - core) * half)
        if s < 2:
            steps_c[s + 2].wait_send()
        send_c[s % 2] = back_part(base + (1 - core) * half)
        steps_c[s] = links.to(send_c.at[s % 2], recv_c.at[s], **to_core)
        gates(base + core * half)
        kept[s % 2] = back_part(base + core * half)
        start_step(s)
        if s < 3:
            finish_step(s + 1)

    count = both_v.shape[0] // rows
    pair_rows = grad_v.shape[1]

    def weight_grads(first, stores):
        for i in range(2):
            begin = pl.multiple_of((first * 2 + i) * pair_rows, 128)
            if len(stores) >= 2:
                stores[-2].wait()
            slot = grad_v.at[i]
            columns = pl.ds(begin, pair_rows)
            slot[:, :wide_units] = low(dot_tn(nt_all[:, columns], both_v[...]))
            slot[:, wide_units:] = low(dot_tn(cot_v[:, columns], act_v[...]))
            store = pltpu.make_async_copy(
                slot, gw_ref.at[pl.ds(begin, pair_rows), :], local_sems.at[i]
            )
            store.start()
            stores.append(store)

    stores = []
    weight_grads(1 - y, stores)
    finish_step(0)
    for store in stores:
        store.wait()
    stores = []
    source = at_rows(gw_ref, (1 - y) * size + owners[3], block_rows)
    early = links.to(source, early_ref, **to_y)
    n2 = total[...]
    for s in range(1, 4):
        steps_z[s].wait_recv()
        n2 = n2 + wide(recv_z[s - 1])
    hidden = hid_ref[...]
    gain_two = vector_of(scal_ref, width, width)
    scale = lax.rsqrt(jnp.mean(hidden * hidden, axis=-1, keepdims=True) + norm_eps)
    back, gain_grad = norm_back(n2, hidden, scale, gain_two)
    gain_ref[...] = gain_grad[None]
    hidden_grad = wide(cot_v[rows_of(z * rows + row_begin, quarter), :]) + back
    hg_ref[...] = hidden_grad
    own = bg_ref.at[rows_of(row_begin, quarter), :]
    own[...] = low(hidden_grad)
    bg_x = links.to(own, own, **to_x)
    bg_core = [links.to(own, own, **to_core)]
    weight_grads(y, stores)
    out_stores = []
    for i in range(2 * count):
        part = pl.ds(i * half, half)
        if i >= 2:
            out_stores[i - 2].wait()
        out_v[i % 2] = low(dot_nt(act_v[part, :], w_v[:, wide_units:]))
        store = pltpu.make_async_copy(out_v.at[i % 2], out_ref.at[part, :], local_sems.at[2 + i % 2])
        store.start()
        out_stores.append(store)
        if i == 1:
            bg_x.wait_recv()
            block = bg_ref.at[rows_of(x_begin, quarter), :]
            bg_core.append(links.to(block, block, **to_core))
    for copy in bg_core + [early]:
        copy.wait_recv()
    for store in stores[-2:] + out_stores[-2:]:
        store.wait()
    for copy in links.started:
        if copy is not steps_c[2] and copy is not steps_c[3]:
            copy.wait_send()


def feed_forward(nt, ff_w, cot_all, cot, hidden, scal, units):
    quarter, width = hidden.shape
    rows, stream, columns = 4 * quarter, cot_all.shape[0], ff_w.shape[1]
    bf16, f32 = jnp.bfloat16, jnp.float32
    shape = jax.ShapeDtypeStruct
    in_vmem_spec, anywhere = pl.BlockSpec(memory_space=pltpu.VMEM), pl.BlockSpec(memory_space=pl.ANY)
    outs = [
        (shape((quarter, width), f32), in_vmem_spec),
        (shape((rows, width), bf16), in_vmem_spec),
        (shape((1, width), f32), in_vmem_spec),
        (shape((width, columns), bf16), anywhere),
        (shape((stream, width), bf16), anywhere),
        (shape((width // 8, columns), bf16), anywhere),
    ]
    return pl.pallas_call(
        ff_kernel,
        out_shape=[o[0] for o in outs],
        in_specs=[anywhere] * 4 + [in_vmem_spec] * 2,
        out_specs=[o[1] for o in outs],
        scratch_shapes=[
            pltpu.VMEM((stream, width), bf16),
            pltpu.VMEM((stream, width), bf16),
            pltpu.VMEM((width, columns), bf16),
            pltpu.VMEM((stream, 2 * units), bf16),
            pltpu.VMEM((stream, columns - 2 * units), bf16),
            pltpu.VMEM((2, 2 * quarter, width), bf16),
            pltpu.VMEM((4, 2 * quarter, width), bf16),
            pltpu.VMEM((2, 2 * quarter, width), bf16),
            pltpu.VMEM((4, quarter, width), bf16),
            pltpu.VMEM((4, quarter, width), bf16),
            pltpu.VMEM((3, quarter, width), bf16),
            pltpu.VMEM((3, quarter, width), bf16),
            pltpu.VMEM((quarter, width), f32),
            pltpu.VMEM((2, width // 4, columns), bf16),
            pltpu.VMEM((2, 2 * quarter, width), bf16),
            pltpu.SemaphoreType.DMA((40,)),
            pltpu.SemaphoreType.DMA((40,)),
            pltpu.SemaphoreType.DMA((28,)),
        ],
        compiler_params=pltpu.CompilerParams(
            collective_id=2, has_side_effects=True, vmem_limit_bytes=62 * 1024 * 1024
        ),
        cost_estimate=pl.CostEstimate(
            flops=33 * 10**9, bytes_accessed=40 * 10**6, transcendentals=10**6
        ),
    )(nt, ff_w, cot_all, cot, hidden, scal)


def back_kernel(
    starts_ref, scal_ref, x_ref, hid_ref, hg_ref, gain_two_ref, bg_ref, attn_w, mix_w, normed_ref, q_ref, k_all, v_all,
    att_ref, lse_ref, cos_ref, sin_ref, gw_ref, part_ref, early_ref,
    layer_ref, input_ref, ff_grads, attn_ref, kv_ref, small_ref,
    ff_y, ff_own, out_c, out_own, out_sx, out_rx, out_sz, out_rz, dk, dv, do, dq, dkv_s, dkv_r, dkv_rz, dkv_own,
    qg, one_sc, one_rc, one_keep, one_sx, one_rx, layer_own, input_own, a_other, a_own, a_y, a_z, a_sz,
    x_own, small, small_y, small_s, small_z, small_h, kv_own,
    send_sems, recv_sems, local_sems,
):
    quarter, width = x_own.shape
    half, rows = 2 * quarter, 4 * quarter
    block_rows = attn_ref.shape[0]
    y, z, head = lax.axis_index("dp"), lax.axis_index("seq"), lax.axis_index("head")
    core, xx = lax.rem(head, 2), lax.div(head, 2)
    size = lax.axis_size("seq")
    heads = q_ref.shape[1] // HD
    wide_heads = heads * HD
    row_begin = core * half + xx * quarter
    x_begin = core * half + (1 - xx) * quarter
    owners = [z, z + 1 - 2 * lax.rem(z, 2), lax.rem(z + 2, 4), 3 - z]
    to_y, to_x, to_core = {"dp": 1 - y}, {"head": head + 2 - 4 * xx}, {"head": head + 1 - 2 * core}
    mine, other = rows_of(xx * quarter, quarter), rows_of((1 - xx) * quarter, quarter)
    is_core = wide(core)
    loads = []

    def load(source, target):
        copy = pltpu.make_async_copy(source, target, local_sems.at[len(loads)])
        copy.start()
        loads.append(copy)
        return copy

    greet([to_y] + [{"seq": owners[d]} for d in (1, 2, 3)] + [to_x, to_core])
    links = Links(send_sems, recv_sems)

    order = (3, 2, 1, 0)

    def grad_rows(ref, which, d):
        return at_rows(ref, which * size + owners[d], block_rows)

    ff_sent, ff_load = {}, {}

    def ff_start(d):
        ff_sent[d] = links.to(grad_rows(gw_ref, 1 - y, d), ff_y.at[d], **to_y)

    ff_start(2)
    ff_early = load(early_ref, ff_y.at[3])
    x_load = load(x_ref.at[rows_of(row_begin, quarter), :], x_own)
    out_sent, out_load = [], []
    for s in range(4):
        begin = owners[s] * rows
        source = part_ref.at[rows_of(begin + (1 - core) * half, half), :]
        out_sent.append(links.to(source, out_c.at[s], **to_core))
    for s in range(4):
        source = part_ref.at[rows_of(owners[s] * rows + core * half, half), :]
        out_load.append(load(source, out_own.at[s]))
    for d in order:
        ff_load[d] = load(grad_rows(gw_ref, y, d), ff_own.at[d])

    ff_over_z = []

    def ff_add(d):
        if d == 3:
            ff_early.wait()
        else:
            ff_sent[d].wait_recv()
        ff_load[d].wait()

        def add(i, unused):
            part = rows_of(i * 64, 64)
            ff_own[d, part, :] = low(wide(ff_own[d, part, :]) + wide(ff_y[d, part, :]))
            return unused

        lax.fori_loop(0, block_rows // 64, add, 0)

    def ff_half(d, i):
        part = pl.ds(i * (block_rows // 2), block_rows // 2)
        ff_over_z.append(
            links.to(ff_own.at[d, part, :], ff_grads.at[z, part, :], seq=owners[d])
        )

    def ff_step(d):
        ff_add(d)
        if d == 0:
            load(ff_own.at[d], ff_grads.at[z])
        else:
            ff_half(d, 0)
            ff_half(d, 1)

    out_x, out_z = {}, {}

    def out_step_c(s):
        out_sent[s].wait_recv()
        out_load[s].wait()
        out_sx[s] = low(wide(out_own[s, other, :]) + wide(out_c[s, other, :]))
        out_x[s] = links.to(out_sx.at[s], out_rx.at[s], **to_x)

    def out_value(s):
        out_x[s].wait_recv()
        return wide(out_own[s, mine, :]) + wide(out_c[s, mine, :]) + wide(out_rx[s])

    def out_step_x(s):
        value = out_value(s)
        if s == 2:
            out_z[3].wait_recv()
            value = value + wide(out_rz[2])
        out_sz[s - 1] = low(value)
        out_z[s] = links.to(out_sz.at[s - 1], out_rz.at[s - 1], seq=owners[2 if s == 2 else 1])

    def do_rows(i, unused):
        part = rows_of(i * half, half)
        do[part, :] = low(dot_nn(bg_ref[part, :], mix_w[...]))
        return unused

    ff_add(3)
    ff_half(3, 0)
    lax.fori_loop(0, 2, do_rows, 0)
    attention_backward(starts_ref, q_ref, k_all, v_all, do, att_ref, lse_ref, dq, dk, dv, (0,))
    out_step_c(3)
    out_step_c(2)
    attention_backward(starts_ref, q_ref, k_all, v_all, do, att_ref, lse_ref, dq, dk, dv, (1,))
    dkv_s[...] = low(dv[...] * (1.0 - is_core) + dk[...] * is_core)
    dkv_core = links.to(dkv_s, dkv_r, **to_core)
    for n in range(heads):
        at = slice(n * HD, (n + 1) * HD)
        qg[:, at] = low(turn(dq[:, at], cos_ref[...], -sin_ref[...]))
    dkv_core.wait_recv()

    def dkv_block(d):
        part = rows_of(owners[d] * rows, rows)
        return dk[part, :] * (1.0 - is_core) + dv[part, :] * is_core + wide(dkv_r[part, :])

    dkv_z = []
    for d in (1, 2, 3):
        dkv_own[d] = low(dkv_block(d))
        dkv_z.append(links.to(dkv_own.at[d], dkv_rz.at[d - 1], seq=owners[d]))
    total = dkv_block(0)
    for d in (1, 2, 3):
        dkv_z[d - 1].wait_recv()
        total = total + wide(dkv_rz[d - 1])
    ff_half(3, 1)
    turned = turn(total, cos_ref[...], -sin_ref[...])
    dkv_own[0] = low(turned * (1.0 - is_core) + total * is_core)
    key_columns = pl.ds(pl.multiple_of(wide_heads + core * HD, HD), HD)

    def one_part(begin):
        part = rows_of(begin, quarter)
        return dot_nt(qg[part, :], attn_w[:, :wide_heads]) + dot_nt(
            dkv_own[0, part, :], attn_w[:, key_columns]
        )

    def one_send(i, unused):
        one_sc[rows_of(i * quarter, quarter), :] = low(one_part((1 - core) * half + i * quarter))
        return unused

    def one_own(i, unused):
        one_keep[rows_of(i * quarter, quarter), :] = one_part(core * half + i * quarter)
        return unused

    lax.fori_loop(0, 2, one_send, 0)
    one_c = links.to(one_sc, one_rc, **to_core)
    lax.fori_loop(0, 2, one_own, 0)
    one_c.wait_recv()
    one_sx[...] = low(one_keep[other, :] + wide(one_rc[other, :]))
    one_x = links.to(one_sx, one_rx, **to_x)

    def attn_grads(which, target):
        columns = pl.ds(pl.multiple_of(which * (width // 2), 128), width // 2)
        normed = normed_ref[:, columns]
        target[:, :wide_heads] = low(dot_tn(normed, qg[...]))
        target[:, wide_heads : 2 * wide_heads] = low(
            dot_tn(bg_ref[:, columns], low(att_ref[...]))
        )
        target[:, 2 * wide_heads :] = low(dot_tn(normed, dkv_own[0]))

    attn_grads(1 - y, a_other)
    attn_sent = {
        d: links.to(at_rows(a_other, owners[d], block_rows), a_y.at[d], **to_y) for d in order
    }
    ff_step(2)
    out_step_c(1)
    out_step_c(0)
    attn_grads(y, a_own)
    out_step_x(3)

    one_x.wait_recv()
    norm_one_grad = one_keep[mine, :] + wide(one_rc[mine, :]) + wide(one_rx[...])
    x_load.wait()
    x_rows = wide(x_own[...])
    gain_one = vector_of(scal_ref, 0, width)
    scale = lax.rsqrt(jnp.mean(x_rows * x_rows, axis=-1, keepdims=True) + norm_eps)
    back, gain_grad = norm_back(norm_one_grad, x_rows, scale, gain_one)
    input_own[...] = low(hg_ref[...] + back)

    def gather(source, target):
        place = target.at[rows_of(row_begin, quarter), :]
        load(source, place)
        return links.to(source, place, **to_x), [links.to(source, place, **to_core)]

    def gather_on(sent, target):
        sent[0].wait_recv()
        block = target.at[rows_of(x_begin, quarter), :]
        sent[1].append(links.to(block, block, **to_core))

    input_sent = gather(input_own, input_ref)
    small[...] = jnp.zeros_like(small)
    per = small.shape[2] // 128

    def put(begin, values):
        for i in range(values.shape[1] // 128):
            tile = begin // 128 + i
            value = values[:, i * 128 : (i + 1) * 128]
            if isinstance(tile, int):
                small[tile // per, 0:1, tile % per * 128 : tile % per * 128 + 128] = value
            else:
                column = pl.ds(pl.multiple_of(lax.rem(tile, per) * 128, 128), 128)
                small[lax.div(tile, per), 0:1, column] = value

    put(0, gain_grad[None])
    put(width, gain_two_ref[...])
    put(2 * width + head * wide_heads, jnp.sum(wide(qg[...]), axis=0, keepdims=True))
    kv_begin = 2 * width + H * HD + (core * KV + lax.div(head * heads, H // KV)) * HD
    put(kv_begin, jnp.sum(wide(dkv_own[0]), axis=0, keepdims=True))
    small_sent = links.to(small.at[pl.ds((1 - y) * size, size)], small_y, **to_y)
    ff_start(1)
    ff_start(0)
    attn_over_z = {}

    def attn_step(d):
        attn_sent[d].wait_recv()
        block = wide(at_rows(a_own, owners[d], block_rows)[...]) + wide(a_y[d])
        if d == 0:
            return block
        if d == 2:
            attn_over_z[3].wait_recv()
            block = block + wide(a_z[2])
        a_sz[d - 1] = low(block)
        attn_over_z[d] = links.to(
            a_sz.at[d - 1], a_z.at[d - 1], seq=owners[2 if d == 2 else 1]
        )
        return None

    attn_step(3)
    out_step_x(1)
    out_step_x(2)
    gather_on(input_sent, input_ref)
    attn_step(1)
    attn_step(2)
    small_sent.wait_recv()
    small_s[...] = small[pl.ds(y * size, size)] + small_y[...]
    small_over_z = [
        links.to(small_s.at[owners[d]], small_z.at[d - 1], seq=owners[d]) for d in (1, 2, 3)
    ]
    layer = hid_ref[...] + out_value(0)
    for d in (1, 2):
        out_z[d].wait_recv()
        layer = layer + wide(out_rz[d - 1])
    layer_own[...] = low(layer)
    layer_sent = gather(layer_own, layer_ref)
    ff_step(1)
    block = attn_step(0)
    for d in (1, 2):
        attn_over_z[d].wait_recv()
        block = block + wide(a_z[d - 1])
    attn_ref[...] = block
    place = kv_ref.at[core * 2 + xx]
    kv_own[...] = low(block[:, 2 * wide_heads :])
    place[...] = kv_own[...]
    kv_x = links.to(kv_own, place, **to_x)
    kv_core = [links.to(kv_own, place, **to_core)]
    gather_on(layer_sent, layer_ref)
    value = small_s[z]
    for d in (1, 2, 3):
        small_over_z[d - 1].wait_recv()
        value = value + small_z[d - 1]
    small_h[0] = value
    small_x = links.to(small_h.at[0], small_h.at[1], **to_x)
    small_x.wait_recv()
    small_h[2] = small_h[0] + small_h[1]
    small_c = links.to(small_h.at[2], small_h.at[3], **to_core)
    small_c.wait_recv()
    small_ref[...] = small_h[2] + small_h[3]
    kv_x.wait_recv()
    place = kv_ref.at[core * 2 + 1 - xx]
    kv_core.append(links.to(place, place, **to_core))
    ff_step(0)
    for copy in kv_core + input_sent[1] + layer_sent[1] + ff_over_z:
        copy.wait_recv()
    links.finish()
    for copy in loads[10:]:
        copy.wait()


def back(
    starts, scal, x_rows, hidden, hidden_grad, gain_two_grad, branch_grad, attn_w, mix_w, normed, q, k_all, v_all, attended, lse,
    cosine, sine_term, gw, out_part, early,
):
    quarter, width = hidden.shape
    half, rows = 2 * quarter, 4 * quarter
    size = lax.axis_size("seq")
    block_rows, columns = gw.shape[0] // (2 * size), gw.shape[1]
    wide_heads = q.shape[1]
    attn_columns = 2 * wide_heads + HD
    stream = k_all.shape[0]
    bf16, f32 = jnp.bfloat16, jnp.float32
    shape = jax.ShapeDtypeStruct
    in_vmem_spec, anywhere = pl.BlockSpec(memory_space=pltpu.VMEM), pl.BlockSpec(memory_space=pl.ANY)
    outs = [
        (shape((rows, width), bf16), anywhere),
        (shape((rows, width), bf16), anywhere),
        (shape((size, block_rows, columns), bf16), anywhere),
        (shape((block_rows, attn_columns), f32), in_vmem_spec),
        (shape((4, block_rows, HD), bf16), in_vmem_spec),
        (shape(scal.shape[1:], f32), in_vmem_spec),
    ]
    small = (size,) + scal.shape[1:]
    scratch = [
        ((size, block_rows, columns), bf16),
        ((size, block_rows, columns), bf16),
        ((4, half, width), bf16),
        ((4, half, width), bf16),
        ((4, quarter, width), bf16),
        ((4, quarter, width), bf16),
        ((3, quarter, width), bf16),
        ((3, quarter, width), bf16),
        ((stream, HD), f32),
        ((stream, HD), f32),
        ((rows, wide_heads), bf16),
        ((rows, wide_heads), f32),
        ((stream, HD), bf16),
        ((stream, HD), bf16),
        ((3, rows, HD), bf16),
        ((4, rows, HD), bf16),
        ((rows, wide_heads), bf16),
        ((half, width), bf16),
        ((half, width), bf16),
        ((half, width), f32),
        ((quarter, width), bf16),
        ((quarter, width), bf16),
        ((quarter, width), bf16),
        ((quarter, width), bf16),
        ((width // 2, attn_columns), bf16),
        ((width // 2, attn_columns), bf16),
        ((4, block_rows, attn_columns), bf16),
        ((3, block_rows, attn_columns), bf16),
        ((3, block_rows, attn_columns), bf16),
        ((quarter, width), bf16),
        (scal.shape, f32),
        (small, f32),
        (small, f32),
        ((3,) + scal.shape[1:], f32),
        ((4,) + scal.shape[1:], f32),
        ((block_rows, HD), bf16),
    ]
    return pl.pallas_call(
        back_kernel,
        out_shape=[o[0] for o in outs],
        in_specs=[pl.BlockSpec(memory_space=pltpu.SMEM), in_vmem_spec, anywhere]
        + [in_vmem_spec] * 14
        + [anywhere] * 3,
        out_specs=[o[1] for o in outs],
        scratch_shapes=[pltpu.VMEM(*one) for one in scratch]
        + [
            pltpu.SemaphoreType.DMA((56,)),
            pltpu.SemaphoreType.DMA((56,)),
            pltpu.SemaphoreType.DMA((14,)),
        ],
        compiler_params=pltpu.CompilerParams(
            collective_id=3, has_side_effects=True, vmem_limit_bytes=62 * 1024 * 1024
        ),
        cost_estimate=pl.CostEstimate(
            flops=10 * 10**9, bytes_accessed=40 * 10**6, transcendentals=10**6
        ),
    )(
        starts, scal, x_rows, hidden, hidden_grad, gain_two_grad, branch_grad, attn_w, mix_w, normed, q, k_all, v_all, attended,
        lse, cosine, sine_term, gw, out_part, early,
    )


def optimizer_kernel(*refs):
    ff_grads, attn_grads, kv_blocks = refs[:3]
    held, outs = refs[3:18], refs[18:]
    size, wide_heads = ff_grads.shape[0], held[0].shape[1]
    main = 512

    def joined(begin, rest_begin, width):
        pieces = [ff_grads[j, :, begin : begin + main] for j in range(size)]
        pieces += [
            ff_grads[j, :, rest_begin : rest_begin + 64] for j in range((width - size * main) // 64)
        ]
        return wide(jnp.concatenate(pieces, axis=1))

    def update(number, grad, at=slice(None)):
        master, moment, square = (ref[at] for ref in held[3 * number : 3 * number + 3])
        results = adamw(master, moment, square, grad, learn_rates[number], decay_rates[number])
        for ref, value in zip(outs[5 * number : 5 * number + 4], results):
            ref[at] = value
        if at == slice(None):
            outs[5 * number + 4][...] = results[4]

    update(0, wide(low(attn_grads[:, :wide_heads])))
    update(1, wide(jnp.concatenate([kv_blocks[i] for i in range(4)], axis=1)))
    update(2, wide(low(attn_grads[:, wide_heads : 2 * wide_heads])))
    every = slice(None)
    hidden_units = held[9].shape[2]
    update(3, joined(0, 2 * main, hidden_units), (every, 0, every))
    update(3, joined(main, 2 * main + 64, hidden_units), (every, 1, every))
    outs[19][...] = low(outs[18][...])
    update(4, joined(2 * main + 128, 3 * main + 128, hidden_units))


def optimizer(ff_grads, attn_grads, kv_blocks, held):
    rows, step = attn_grads.shape[0], 16

    def block(array):
        if array.ndim == 3 and array.shape[0] == 4:
            return pl.BlockSpec((4, step) + array.shape[2:], lambda i: (0, i, 0))
        rest = array.shape[1:]
        return pl.BlockSpec((step,) + rest, lambda i: (i,) + (0,) * len(rest))

    outs, flat = [], []
    for three in held:
        flat.extend(three)
        outs += [jax.ShapeDtypeStruct(three[0].shape, jnp.float32)] * 4
        outs.append(jax.ShapeDtypeStruct(three[0].shape, jnp.bfloat16))
    operands = [ff_grads, attn_grads, kv_blocks] + flat
    return pl.pallas_call(
        optimizer_kernel,
        grid=(rows // step,),
        out_shape=outs,
        in_specs=[block(one) for one in operands],
        out_specs=[block(one) for one in outs],
        compiler_params=pltpu.CompilerParams(vmem_limit_bytes=62 * 1024 * 1024),
        cost_estimate=pl.CostEstimate(
            flops=3 * 10**7, bytes_accessed=50 * 10**6, transcendentals=2 * 10**6
        ),
    )(*operands)


def rope_tables(places):
    halves = HD // 2
    powers = jnp.arange(halves, dtype=jnp.float32) * (-2.0 / HD)
    frequency = jnp.power(jnp.float32(rope_base), powers)
    angles = places.astype(jnp.float32)[:, None] * frequency[None, :]
    cosine, sine_term = jnp.cos(angles), jnp.sin(angles)
    return (
        jnp.concatenate([cosine, cosine], axis=1),
        jnp.concatenate([-sine_term, sine_term], axis=1),
    )


def local(
    tokens,
    cotangent,
    doc_lengths,
    queries_master,
    queries_moment,
    queries_square,
    keyvalue_master,
    keyvalue_moment,
    keyvalue_square,
    mixing_master,
    mixing_moment,
    mixing_square,
    expand_master,
    expand_moment,
    expand_square,
    shrink_master,
    shrink_moment,
    shrink_square,
    scalars_master,
    scalars_moment,
    scalars_square,
):
    local_rows, width = tokens.shape[1], tokens.shape[2]
    seq_count = lax.axis_size("seq")
    head_count = lax.axis_size("head")
    head_index = lax.axis_index("head")
    seq_index = lax.axis_index("seq")
    local_heads = H // head_count
    wide_heads = local_heads * HD
    kv_head = head_index * local_heads // (H // KV)
    core = head_index % 2
    quarter = local_rows // 4
    row_begin = (head_index % 2) * (2 * quarter) + (head_index // 2) * quarter
    hidden_units = expand_master.shape[2]
    units = 64 * -(-hidden_units // (64 * seq_count))
    more = ((0, 0), (0, units * seq_count - hidden_units))

    attn_pack = jnp.concatenate(
        [
            low(queries_master),
            low(mixing_master).T,
            low(lax.dynamic_slice_in_dim(keyvalue_master, kv_head * HD, HD, 1)),
            low(lax.dynamic_slice_in_dim(keyvalue_master, (KV + kv_head) * HD, HD, 1)),
        ],
        axis=1,
    )
    expand_low = low(expand_master)

    def cut(values):
        values = jnp.pad(values, more)
        return values.reshape(values.shape[0], seq_count, units).transpose(1, 0, 2)

    ff_packs = jnp.concatenate(
        [cut(expand_low[:, 0]), cut(expand_low[:, 1]), cut(low(shrink_master).T)], axis=2
    )
    scalar_values = wide(lax.all_gather(low(scalars_master), ("dp", "seq"), axis=0, tiled=True))
    attn_weight = weight_gather(attn_pack)
    ff_weight = weight_exchange(ff_packs)
    query_weight = attn_weight[:, :wide_heads]
    mixing_t = attn_weight[:, wide_heads : 2 * wide_heads]
    key_value_weight = attn_weight[:, 2 * wide_heads :]
    expand_weight = ff_weight[:, : 2 * units]
    shrink_t = ff_weight[:, 2 * units :]

    cot_rows = cotangent[0]
    cot_own = lax.dynamic_slice_in_dim(cot_rows, row_begin, quarter, 0)
    cot_blocks = [cot_rows]
    moving = cot_own
    for s in range(1, seq_count):
        moving = shift(moving, "seq", 1)
        cot_blocks.append(head_gather(moving))

    gain_one = scalar_values[:width]
    gain_two = scalar_values[width : 2 * width]
    bias_query = lax.dynamic_slice_in_dim(
        scalar_values, 2 * width + head_index * wide_heads, wide_heads
    )
    bias_keyvalue = scalar_values[2 * width + H * HD :]
    key_bias = lax.dynamic_slice_in_dim(bias_keyvalue, kv_head * HD, HD)
    value_bias = lax.dynamic_slice_in_dim(bias_keyvalue, (KV + kv_head) * HD, HD)
    x_rows = wide(tokens[0])
    lengths = doc_lengths[0]
    places = folded_places(
        seq_index * local_rows + jnp.arange(local_rows, dtype=jnp.int32), local_rows, seq_count
    )
    starts = doc_starts(places, lengths)
    half_starts = jnp.stack([starts[0], starts[local_rows // 2]])
    within = places - starts
    scale_one = lax.rsqrt(jnp.mean(x_rows * x_rows, axis=-1, keepdims=True) + norm_eps)
    normed = low(x_rows * scale_one * gain_one)
    query_pre = dot_nn(normed, query_weight) + bias_query
    queries = low(rotate(query_pre.reshape(local_rows, local_heads, HD), within)).reshape(
        local_rows, wide_heads
    )
    key_value_pre = dot_nn(normed, key_value_weight)
    key_rows = low(rotate((key_value_pre[:, :HD] + key_bias)[:, None, :], within)[:, 0, :])
    value_rows = low(key_value_pre[:, HD:] + value_bias)
    moving = jnp.concatenate([key_rows, value_rows], axis=1)
    all_rows = jnp.zeros((seq_count,) + moving.shape, moving.dtype)
    for s in range(seq_count):
        if s > 0:
            moving = shift(moving, "seq", 1)
        owner = lax.rem(seq_index + seq_count - s, seq_count)
        all_rows = lax.dynamic_update_slice(all_rows, moving[None], (owner, 0, 0))
    all_rows = all_rows.reshape(-1, 2 * HD)
    all_keys, all_values = all_rows[:, :HD], all_rows[:, HD:]
    stream_rows = all_rows.shape[0]
    attended, log_total = in_vmem(
        attention_forward,
        [
            jax.ShapeDtypeStruct((local_rows, wide_heads), jnp.float32),
            jax.ShapeDtypeStruct((local_rows, local_heads), jnp.float32),
        ],
        half_starts,
        queries,
        all_keys,
        all_values,
    )
    attended_low = low(attended)
    x_own = lax.dynamic_slice_in_dim(x_rows, row_begin, quarter, 0)
    hidden = x_own + head_scatter(dot_nt(attended_low, mixing_t))
    scale_two = lax.rsqrt(jnp.mean(hidden * hidden, axis=-1, keepdims=True) + norm_eps)
    normed_two = low(hidden * scale_two * gain_two)

    normed_blocks, grad_blocks, act_blocks, back_parts, out_parts = [], [], [], [], []
    moving = normed_two
    for s in range(seq_count):
        if s > 0:
            moving = shift(moving, "seq", 1)
        block = head_gather(moving)
        both = dot_nn(block, expand_weight)
        gate_value, up_value = both[:, :units], both[:, units:]
        gate_sigmoid = jax.nn.sigmoid(gate_value)
        activation = low(gate_value * gate_sigmoid * up_value)
        act_grad = wide(low(dot_nn(cot_blocks[s], shrink_t)))
        gate_grad = low(act_grad * up_value * gate_sigmoid * (1.0 + gate_value * (1.0 - gate_sigmoid)))
        up_grad = low(act_grad * gate_value * gate_sigmoid)
        both_grad = jnp.concatenate([gate_grad, up_grad], axis=1)
        back_parts.append(head_scatter(dot_nt(both_grad, expand_weight)))
        out_parts.append(head_scatter(dot_nt(activation, shrink_t)))
        normed_blocks.append(block)
        grad_blocks.append(both_grad)
        act_blocks.append(activation)
    norm_two_grad = seq_sum(back_parts)
    back_two, gain_two_grad = norm_back(norm_two_grad, hidden, scale_two, gain_two)
    hidden_grad = wide(lax.dynamic_slice_in_dim(cot_rows, row_begin, quarter, 0)) + back_two
    branch_grad = head_gather(low(hidden_grad))
    feedforward = seq_sum(out_parts)
    layer_out = head_gather(low(hidden + feedforward))
    expand_part = dot_tn(jnp.concatenate(normed_blocks), jnp.concatenate(grad_blocks))
    shrink_part = dot_tn(jnp.concatenate(cot_blocks), jnp.concatenate(act_blocks))
    ff_grads = grad_exchange(low(jnp.concatenate([expand_part, shrink_part], axis=1)), False)

    attended_grad = low(dot_nn(branch_grad, mixing_t))
    query_sum, key_sum, value_sum = in_vmem(
        attention_backward,
        [
            jax.ShapeDtypeStruct((local_rows, wide_heads), jnp.float32),
            jax.ShapeDtypeStruct((stream_rows, HD), jnp.float32),
            jax.ShapeDtypeStruct((stream_rows, HD), jnp.float32),
        ],
        half_starts,
        queries,
        all_keys,
        all_values,
        attended_grad,
        attended,
        log_total,
    )
    mine = jnp.where(core == 0, key_sum, value_sum)
    other = jnp.where(core == 0, value_sum, key_sum)
    mine = mine + wide(swap(low(other), "head", 1))
    mine = mine.reshape(seq_count, local_rows, HD)
    own_sum = seq_sum(
        [
            lax.dynamic_index_in_dim(mine, lax.rem(seq_index + seq_count - s, seq_count), 0, False)
            for s in range(seq_count)
        ]
    )
    own_sum = low(jnp.where(core == 0, rotate(own_sum[:, None, :], -within)[:, 0, :], own_sum))
    query_grad = low(
        rotate(query_sum.reshape(local_rows, local_heads, HD), -within).reshape(
            local_rows, wide_heads
        )
    )
    own_weight = lax.dynamic_slice_in_dim(key_value_weight, core * HD, HD, 1)
    norm_one_grad = head_scatter(dot_nt(query_grad, query_weight) + dot_nt(own_sum, own_weight))
    scale_own = lax.dynamic_slice_in_dim(scale_one, row_begin, quarter, 0)
    back_one, gain_one_grad = norm_back(norm_one_grad, x_own, scale_own, gain_one)
    input_grad = head_gather(low(hidden_grad + back_one))
    attn_part = jnp.concatenate(
        [
            dot_tn(normed, query_grad),
            dot_tn(branch_grad, attended_low),
            dot_tn(normed, own_sum),
        ],
        axis=1,
    )
    attn_grads = grad_exchange(attn_part, True)
    kv_block = low(attn_grads[:, 2 * wide_heads :])
    small = jnp.zeros((scalars_master.shape[0] * 2 * seq_count,), jnp.float32)
    small = lax.dynamic_update_slice(small, jnp.concatenate([gain_one_grad, gain_two_grad]), (0,))
    small = lax.dynamic_update_slice(
        small, jnp.sum(wide(query_grad), axis=0), (2 * width + head_index * wide_heads,)
    )
    kv_column = core * KV * HD + kv_head * HD
    small = lax.dynamic_update_slice(
        small, jnp.sum(wide(own_sum), axis=0), (2 * width + H * HD + kv_column,)
    )
    small = lax.psum(small, "head")
    shared_scalars = lax.psum_scatter(small, ("dp", "seq"), scatter_dimension=0, tiled=True)
    gathered = head_gather(kv_block, 1)
    shared_keyvalue = wide(gathered)

    def joined(part):
        part = ff_grads[:, :, part * units : (part + 1) * units].transpose(1, 0, 2)
        return wide(part.reshape(part.shape[0], -1)[:, :hidden_units])

    grads = (
        attn_grads[:, :wide_heads],
        shared_keyvalue,
        attn_grads[:, wide_heads : 2 * wide_heads].T,
        jnp.stack([joined(0), joined(1)], axis=1),
        joined(2).T,
        shared_scalars,
    )
    masters = (
        (queries_master, queries_moment, queries_square),
        (keyvalue_master, keyvalue_moment, keyvalue_square),
        (mixing_master, mixing_moment, mixing_square),
        (expand_master, expand_moment, expand_square),
        (shrink_master, shrink_moment, shrink_square),
        (scalars_master, scalars_moment, scalars_square),
    )
    results = [layer_out[None], input_grad[None]]
    for held, grad, rate, decay in zip(masters, grads, learn_rates, decay_rates):
        results.extend(adamw(*held, wide(low(grad)), rate, decay))
    return tuple(results)


def local_fast(
    tokens,
    cotangent,
    doc_lengths,
    queries_master,
    queries_moment,
    queries_square,
    keyvalue_master,
    keyvalue_moment,
    keyvalue_square,
    mixing_master,
    mixing_moment,
    mixing_square,
    expand_master,
    expand_moment,
    expand_square,
    shrink_master,
    shrink_moment,
    shrink_square,
    scalars_master,
    scalars_moment,
    scalars_square,
):
    local_rows = tokens.shape[1]
    seq_count = lax.axis_size("seq")
    seq_index = lax.axis_index("seq")
    hidden_units = expand_master.shape[2]

    units = 64 * -(-hidden_units // (64 * seq_count))
    x_low, cot_rows = tokens[0], cotangent[0]
    lengths = doc_lengths[0]
    places = folded_places(
        seq_index * local_rows + jnp.arange(local_rows, dtype=jnp.int32), local_rows, seq_count
    )
    starts = doc_starts(places, lengths)
    half_starts = jnp.stack([starts[0], starts[local_rows // 2]])
    within = places - starts
    cosine, sine_term = rope_tables(within)
    scal_in = jnp.broadcast_to(wide(low(scalars_master))[None], (8, scalars_master.shape[0]))
    (
        scal_all, attn_weight, mix_weight, ff_weight, cot_all, normed, queries, all_keys, all_values,
        attended, log_total, hidden, normed_all,
    ) = front(
        half_starts, scal_in, queries_master, keyvalue_master, mixing_master.T, expand_master, shrink_master.T,
        x_low, cot_rows, cosine, sine_term, 3 * units + 64,
    )
    hidden_grad, branch_grad, gain_two_grad, ff_part, out_part, early = feed_forward(
        normed_all, ff_weight, cot_all, cot_rows, hidden, scal_all, units
    )
    layer_out, input_grad, ff_grads, attn_grads, kv_blocks, small = back(
        half_starts, scal_all, x_low, hidden, hidden_grad, gain_two_grad, branch_grad, attn_weight, mix_weight, normed, queries,
        all_keys, all_values, attended, log_total, cosine, sine_term, ff_part, out_part, early,
    )
    held = (
        (queries_master, queries_moment, queries_square),
        (keyvalue_master, keyvalue_moment, keyvalue_square),
        tuple(one.T for one in (mixing_master, mixing_moment, mixing_square)),
        (expand_master, expand_moment, expand_square),
        tuple(one.T for one in (shrink_master, shrink_moment, shrink_square)),
    )
    updated = optimizer(ff_grads, attn_grads, kv_blocks, held)
    results = [layer_out[None], input_grad[None]]
    for i in range(5):
        results.extend(one.T if i in (2, 4) else one for one in updated[5 * i : 5 * i + 5])
    results.extend(
        adamw(
            scalars_master, scalars_moment, scalars_square, wide(low(small[0])), learn_rates[5], decay_rates[5]
        )
    )
    return tuple(results)


def solution(mesh):
    placed = (
        P("dp", "seq", None),
        P("dp", "seq", None),
        P("dp", None),
        P(("dp", "seq"), "head"),
        P(("dp", "seq"), "head"),
        P(("dp", "seq"), "head"),
        P(("dp", "seq"), None),
        P(("dp", "seq"), None),
        P(("dp", "seq"), None),
        P("head", ("dp", "seq")),
        P("head", ("dp", "seq")),
        P("head", ("dp", "seq")),
        P(("dp", "seq"), None, "head"),
        P(("dp", "seq"), None, "head"),
        P(("dp", "seq"), None, "head"),
        P("head", ("dp", "seq")),
        P("head", ("dp", "seq")),
        P("head", ("dp", "seq")),
        P(("dp", "seq")),
        P(("dp", "seq")),
        P(("dp", "seq")),
    )
    small = dict(mesh.shape) == {"dp": 2, "seq": 4, "head": 4}
    return jax.shard_map(
        local_fast if small else local,
        mesh=mesh,
        in_specs=placed,
        out_specs=(
            P("dp", "seq", None),
            P("dp", "seq", None),
            P(("dp", "seq"), "head"),
            P(("dp", "seq"), "head"),
            P(("dp", "seq"), "head"),
            P(("dp", "seq"), "head"),
            P(("dp", "seq"), "head"),
            P(("dp", "seq"), None),
            P(("dp", "seq"), None),
            P(("dp", "seq"), None),
            P(("dp", "seq"), None),
            P(("dp", "seq"), None),
            P("head", ("dp", "seq")),
            P("head", ("dp", "seq")),
            P("head", ("dp", "seq")),
            P("head", ("dp", "seq")),
            P("head", ("dp", "seq")),
            P(("dp", "seq"), None, "head"),
            P(("dp", "seq"), None, "head"),
            P(("dp", "seq"), None, "head"),
            P(("dp", "seq"), None, "head"),
            P(("dp", "seq"), None, "head"),
            P("head", ("dp", "seq")),
            P("head", ("dp", "seq")),
            P("head", ("dp", "seq")),
            P("head", ("dp", "seq")),
            P("head", ("dp", "seq")),
            P(("dp", "seq")),
            P(("dp", "seq")),
            P(("dp", "seq")),
            P(("dp", "seq")),
            P(("dp", "seq")),
        ),
        check_vma=False,
    )
```

```python
import functools
import math

import jax
import jax.numpy as jnp
from jax import lax
from jax.experimental import pallas as pl
from jax.experimental.pallas import tpu as pltpu
from jax.sharding import PartitionSpec as P

D = 1536
H = 12
KV = 2
HD = 128
STEP = 5


norm_eps = 1e-06
rope_base = 1000000.0
beta_first = 0.5
beta_second = 0.5
adam_eps = 1e-08
masked_low = -1e30
learn_rates = (0.02, 0.02, 0.3, 0.02, 0.01, 0.2)
decay_rates = (0.1, 0.1, 0.1, 0.1, 0.1, 0.0)


def folded_places(row_ids, shard_rows, seq_count):
    owner_index = row_ids // shard_rows
    inside = row_ids % shard_rows
    halves = shard_rows // 2
    block_index = jnp.where(inside < halves, owner_index, 2 * seq_count - 1 - owner_index)
    return block_index * halves + inside % halves


def doc_starts(places, lengths):
    end, total = jnp.int32(0), jnp.zeros_like(places)
    for i in range(lengths.shape[0]):
        end = end + lengths[i]
        total = total + jnp.where(end <= places, lengths[i], 0)
    return total


def rotate(values, places):
    halves = values.shape[-1] // 2
    powers = jnp.arange(halves, dtype=jnp.float32) * (-2.0 / values.shape[-1])
    frequency = jnp.power(jnp.float32(rope_base), powers)
    angles = places.astype(jnp.float32)[:, None] * frequency[None, :]
    cosine = jnp.cos(angles)[:, None, :]
    sine_term = jnp.sin(angles)[:, None, :]
    first_half = values[..., :halves]
    second_half = values[..., halves:]
    return jnp.concatenate(
        [
            first_half * cosine - second_half * sine_term,
            second_half * cosine + first_half * sine_term,
        ],
        axis=-1,
    )


def norm_back(grad_rows, values, scale_rows, gain_vector):
    unit_rows = values * scale_rows
    scaled = grad_rows * gain_vector
    mean_term = jnp.mean(scaled * unit_rows, axis=-1, keepdims=True)
    return (scale_rows * (scaled - unit_rows * mean_term), jnp.sum(grad_rows * unit_rows, axis=0))


def adamw(master, moment, square, grad_rows, rate_value, decay_value):
    first_new = beta_first * moment + (1.0 - beta_first) * grad_rows
    second_new = beta_second * square + (1.0 - beta_second) * grad_rows * grad_rows
    fix_first = 1.0 - beta_first**STEP
    fix_second = 1.0 - beta_second**STEP
    weight = master - rate_value * (
        first_new / fix_first / (jnp.sqrt(second_new / fix_second) + adam_eps)
        + decay_value * master
    )
    return (grad_rows, first_new, second_new, weight, weight.astype(jnp.bfloat16))


def shift(values, axis, steps):
    size = lax.axis_size(axis)
    return lax.ppermute(values, axis, [(i, (i + steps) % size) for i in range(size)])


def swap(values, axis, bit):
    size = lax.axis_size(axis)
    return lax.ppermute(values, axis, [(i, i ^ bit) for i in range(size)])


def dot_nn(left, right):
    return jnp.dot(left, right, preferred_element_type=jnp.float32)


def dot_nt(left, right):
    return lax.dot_general(left, right, (((1,), (1,)), ((), ())), preferred_element_type=jnp.float32)


def dot_tn(left, right):
    return lax.dot_general(left, right, (((0,), (0,)), ((), ())), preferred_element_type=jnp.float32)


def low(values):
    return values.astype(jnp.bfloat16)


def wide(values):
    return values.astype(jnp.float32)


def halve(values, which):
    size = values.shape[0] // 2
    mine = lax.dynamic_slice_in_dim(values, which * size, size, 0)
    other = lax.dynamic_slice_in_dim(values, (1 - which) * size, size, 0)
    return mine, other


def head_scatter(values):
    index = lax.axis_index("head")
    mine, other = halve(values, index % 2)
    values = mine + wide(swap(low(other), "head", 1))
    mine, other = halve(values, index // 2)
    return mine + wide(swap(low(other), "head", 2))


def head_gather(values, dim=0):
    index = lax.axis_index("head")
    for bit, which in ((2, index // 2), (1, index % 2)):
        got = swap(values, "head", bit)
        values = jnp.where(
            which == 0,
            jnp.concatenate([values, got], dim),
            jnp.concatenate([got, values], dim),
        )
    return values


def seq_sum(blocks):
    total = blocks[0]
    for s in range(1, len(blocks)):
        total = total + wide(shift(low(blocks[s]), "seq", -s))
    return total


def place(blocks):
    size = lax.axis_size("seq")
    dp_index, seq_index = lax.axis_index("dp"), lax.axis_index("seq")
    first = next(iter(blocks.values()))
    out = jnp.zeros((2 * size,) + first.shape, first.dtype)
    for (a, k), block in blocks.items():
        owner = lax.rem(dp_index + a, 2) * size + lax.rem(seq_index + size - k, size)
        out = lax.dynamic_update_slice(out, block[None], (owner,) + (0,) * first.ndim)
    return out


def weight_gather(block):
    size = lax.axis_size("seq")
    blocks = {}
    for k in range(size):
        if k > 0:
            block = shift(block, "seq", 1)
        blocks[0, k] = block
        blocks[1, k] = swap(block, "dp", 1)
    out = place(blocks)
    return out.reshape((-1,) + out.shape[2:])


def weight_exchange(packs):
    size = lax.axis_size("seq")
    seq_index = lax.axis_index("seq")
    blocks = {}
    for k in range(size):
        block = lax.dynamic_index_in_dim(packs, lax.rem(seq_index + k, size), 0, False)
        if k > 0:
            block = shift(block, "seq", k)
        blocks[0, k] = block
        blocks[1, k] = swap(block, "dp", 1)
    out = place(blocks)
    return out.reshape((-1,) + out.shape[2:])


def grad_exchange(parts, scatter):
    size = lax.axis_size("seq")
    dp_index, seq_index = lax.axis_index("dp"), lax.axis_index("seq")
    parts = parts.reshape(2, size, -1, parts.shape[1])
    total = jnp.zeros(parts.shape[2:], jnp.float32)
    out = jnp.zeros(parts.shape[1:], jnp.bfloat16)
    for k in range(size - 1, -1, -1):
        target = lax.rem(seq_index + k, size)
        pair = lax.dynamic_index_in_dim(parts, target, 1, False)
        mine = lax.dynamic_index_in_dim(pair, dp_index, 0, False)
        other = lax.dynamic_index_in_dim(pair, 1 - dp_index, 0, False)
        block = wide(mine) + wide(swap(low(other), "dp", 1))
        if k > 0:
            block = wide(shift(low(block), "seq", k))
        if scatter:
            total = total + block
        else:
            source = lax.rem(seq_index + size - k, size)
            out = lax.dynamic_update_slice(out, low(block)[None], (source, 0, 0))
    return total if scatter else out


def hidden_before(lengths_ref, half, block, block_rows):
    first_place = last_block(half) * block_rows
    end, start = jnp.int32(0), jnp.int32(0)
    for i in range(lengths_ref.shape[1]):
        end = end + lengths_ref[0, i]
        start = start + jnp.where(end <= first_place, lengths_ref[0, i], 0)
    return jnp.where(block * block_rows >= start, 0.0, masked_low)


def last_block(half):
    index = lax.axis_index("seq")
    return index if half == 0 else 2 * lax.axis_size("seq") - 1 - index


def key_offset(block, size, block_rows):
    owner = jnp.where(block < size, block, 2 * size - 1 - block)
    return owner * (2 * block_rows) + jnp.where(block < size, 0, block_rows)


def seen_bias(block_rows, heads):
    row = lax.broadcasted_iota(jnp.int32, (block_rows, block_rows), 0)
    col = lax.broadcasted_iota(jnp.int32, (block_rows, block_rows), 1)
    return jnp.concatenate([jnp.where(col <= row, 0.0, masked_low)] * heads, axis=0)


def stacked_heads(ref, half):
    block_rows, heads = ref.shape[0] // 2, ref.shape[1] // HD
    rows = pl.ds(half * block_rows, block_rows)
    return jnp.concatenate([ref[rows, i * HD : (i + 1) * HD] for i in range(heads)], axis=0)


def attention_forward(lengths_ref, q_ref, k_ref, v_ref, o_ref, lse_ref, halves=(0, 1)):
    local_rows, heads = q_ref.shape[0], q_ref.shape[1] // HD
    block_rows = local_rows // 2
    size = lax.axis_size("seq")
    scale = 1.0 / math.sqrt(HD)
    stacked = heads * block_rows
    for half in halves:
        last = last_block(half)
        rows = pl.ds(half * block_rows, block_rows)
        q = stacked_heads(q_ref, half)

        def step(block, carried, diagonal, q=q, half=half):
            running_max, running_sum, running_out = carried
            keys = pl.ds(pl.multiple_of(key_offset(block, size, block_rows), block_rows), block_rows)
            scores = dot_nt(q, k_ref[keys, :]) * scale
            if diagonal:
                scores = scores + seen_bias(block_rows, heads)
            else:
                scores = scores + hidden_before(lengths_ref, half, block, block_rows)
            new_max = jnp.maximum(running_max, jnp.max(scores, axis=-1, keepdims=True))
            probs = jnp.exp(scores - new_max)
            fade = jnp.exp(running_max - new_max)
            running_sum = running_sum * fade + jnp.sum(probs, axis=-1, keepdims=True)
            running_out = running_out * fade + dot_nn(low(probs), v_ref[keys, :])
            return new_max, running_sum, running_out

        carried = (
            jnp.full((stacked, 1), masked_low, jnp.float32),
            jnp.zeros((stacked, 1), jnp.float32),
            jnp.zeros((stacked, HD), jnp.float32),
        )
        carried = lax.fori_loop(0, last, functools.partial(step, diagonal=False), carried)
        running_max, running_sum, running_out = step(last, carried, True)
        out = running_out / running_sum
        lse = running_max + jnp.log(running_sum)
        for i in range(heads):
            part = slice(i * block_rows, (i + 1) * block_rows)
            o_ref[rows, i * HD : (i + 1) * HD] = out[part]
            lse_ref[rows, i : i + 1] = lse[part]


def attention_backward(
    lengths_ref, q_ref, k_ref, v_ref, do_ref, o_ref, lse_ref, dq_ref, dk_ref, dv_ref, halves=(0, 1)
):
    local_rows, heads = q_ref.shape[0], q_ref.shape[1] // HD
    block_rows = local_rows // 2
    size = lax.axis_size("seq")
    scale = 1.0 / math.sqrt(HD)
    stacked = heads * block_rows
    for half in halves:
        if half == 0:
            dk_ref[...] = jnp.zeros_like(dk_ref)
            dv_ref[...] = jnp.zeros_like(dv_ref)
        last = last_block(half)
        rows = pl.ds(half * block_rows, block_rows)
        q, do = stacked_heads(q_ref, half), stacked_heads(do_ref, half)
        delta = jnp.sum(wide(do) * stacked_heads(o_ref, half), axis=-1, keepdims=True)
        lse = jnp.concatenate([lse_ref[rows, i : i + 1] for i in range(heads)], axis=0)

        def step(block, dq, diagonal, q=q, do=do, delta=delta, lse=lse, half=half):
            keys = pl.ds(pl.multiple_of(key_offset(block, size, block_rows), block_rows), block_rows)
            k, v = k_ref[keys, :], v_ref[keys, :]
            scores = dot_nt(q, k) * scale
            if diagonal:
                scores = scores + seen_bias(block_rows, heads)
            else:
                scores = scores + hidden_before(lengths_ref, half, block, block_rows)
            probs = jnp.exp(scores - lse)
            score_grad = low(probs * (dot_nt(do, v) - delta))
            dk_ref[keys, :] += dot_tn(score_grad, q) * scale
            dv_ref[keys, :] += dot_tn(low(probs), do)
            return dq + dot_nn(score_grad, k)

        dq = jnp.zeros((stacked, HD), jnp.float32)
        dq = lax.fori_loop(0, last, functools.partial(step, diagonal=False), dq)
        dq = step(last, dq, True) * scale
        for i in range(heads):
            dq_ref[rows, i * HD : (i + 1) * HD] = dq[i * block_rows : (i + 1) * block_rows]


def in_vmem(kernel, outs, scalars, *arrays):
    return pl.pallas_call(
        kernel,
        out_shape=outs,
        in_specs=[pl.BlockSpec(memory_space=pltpu.SMEM)]
        + [pl.BlockSpec(memory_space=pltpu.VMEM)] * len(arrays),
        out_specs=[pl.BlockSpec(memory_space=pltpu.VMEM)] * len(outs),
        compiler_params=pltpu.CompilerParams(vmem_limit_bytes=40 * 1024 * 1024),
        cost_estimate=pl.CostEstimate(
            flops=12 * 10**9, bytes_accessed=8 * 10**6, transcendentals=10**7
        ),
    )(scalars, *arrays)


class Links:
    def __init__(self, send_sems, recv_sems):
        self.send_sems, self.recv_sems, self.started = send_sems, recv_sems, []

    def to(self, source, target, **where):
        number = len(self.started)
        copy = pltpu.make_async_remote_copy(
            src_ref=source,
            dst_ref=target,
            send_sem=self.send_sems.at[number],
            recv_sem=self.recv_sems.at[number],
            device_id=where,
            device_id_type=pl.DeviceIdType.MESH,
        )
        copy.start()
        self.started.append(copy)
        return copy

    def finish(self):
        for copy in self.started:
            copy.wait_send()


def greet(partners):
    barrier = pltpu.get_barrier_semaphore()
    for where in partners:
        pl.semaphore_signal(
            barrier, inc=1, device_id=where, device_id_type=pl.DeviceIdType.MESH
        )
    pl.semaphore_wait(barrier, len(partners))


def at_rows(ref, block, size):
    return ref.at[pl.ds(pl.multiple_of(block * size, size), size), :]


def rows_of(begin, size):
    return pl.ds(pl.multiple_of(begin, size), size)


def turn(values, cosine, sine_term):
    return values * cosine + pltpu.roll(values, HD // 2, 1) * sine_term


def vector_of(scal_ref, begin, size):
    per = scal_ref.shape[2] // 128
    tiles = []
    for i in range(size // 128):
        tile = begin // 128 + i
        if isinstance(tile, int):
            owner, column = tile // per, tile % per * 128
        else:
            owner, column = lax.div(tile, per), pl.multiple_of(lax.rem(tile, per) * 128, 128)
        tiles.append(scal_ref[owner, 0:1, pl.ds(column, 128)])
    return jnp.concatenate(tiles, axis=1)


def cut_units(expand_v, shrink_v, packs):
    size, main, columns = packs.shape[0], 512, expand_v.shape[2]
    left = lax.broadcasted_iota(jnp.int32, (16, 128), 1) < 64

    def rows16(i, unused):
        part = rows_of(i * 16, 16)

        def rests(values):
            begin = size * main
            first = values[:, begin : begin + 128]
            last = jnp.concatenate([values[:, begin + 128 :], jnp.zeros((16, 64), jnp.float32)], axis=1)
            return first, pltpu.roll(first, 64, 1), last

        gate, up, down = expand_v[part, 0, :], expand_v[part, 1, :], shrink_v[part, :]
        for j in range(size):
            own = slice(j * main, (j + 1) * main)
            packs[j, part, :main] = low(gate[:, own])
            packs[j, part, main : 2 * main] = low(up[:, own])
            packs[j, part, 2 * main + 128 : 3 * main + 128] = low(down[:, own])
        pieces = zip(rests(gate), rests(up), rests(down))
        for j, (gate_rest, up_rest, down_rest) in enumerate(pieces):
            both = jnp.where(left, gate_rest, pltpu.roll(up_rest, 64, 1))
            packs[j, part, 2 * main : 2 * main + 128] = low(both)
            packs[j, part, 3 * main + 128 :] = low(jnp.where(left, down_rest, 0.0))
        packs[size - 1, part, 2 * main : 2 * main + 128] = jnp.zeros((16, 128), jnp.bfloat16)
        packs[size - 1, part, 3 * main + 128 :] = jnp.zeros((16, 128), jnp.bfloat16)
        return unused

    lax.fori_loop(0, packs.shape[1] // 16, rows16, 0)


def front_kernel(
    lengths_ref, scal_own, query_ref, kv_ref, mixing_ref, expand_ref, shrink_ref, x_ref, cot_ref, cos_half, sin_half,
    scal_ref, attn_out, mix_out, ff_w, cot_all, normed_out, q_out, k_out, v_out, att_out, lse_out, hid_out, nt_all,
    cos_out, sin_out, scal_in, cos_ref, sin_ref, attn_w, mix_w, normed_ref, q_ref, k_all, v_all, att_ref, lse_ref, hid_ref, expand_v, shrink_v, ff_packs, nt_ref, send_c, recv_c, send_x, recv_x, kept, send_sems, recv_sems, local_sem, store_sems,
):
    rows, width = x_ref.shape
    quarter, half = rows // 4, rows // 2
    block_rows = query_ref.shape[0]
    size = lax.axis_size("seq")
    y, z, head = lax.axis_index("dp"), lax.axis_index("seq"), lax.axis_index("head")
    core, xx = lax.rem(head, 2), lax.div(head, 2)
    heads = q_ref.shape[1] // HD
    wide_heads = heads * HD
    row_begin = core * half + xx * quarter
    me = y * size + z
    owners = [z, z + 1 - 2 * lax.rem(z, 2), lax.rem(z + 2, 4), 3 - z]
    to_y, to_x, to_core = {"dp": 1 - y}, {"head": head + 2 - 4 * xx}, {"head": head + 1 - 2 * core}
    greet([{"seq": owners[d]} for d in (1, 2, 3)] + [to_y, to_x, to_core])
    links = Links(send_sems, recv_sems)
    stores = []

    def store(source, target):
        copy = pltpu.make_async_copy(source, target, store_sems.at[len(stores)])
        copy.start()
        stores.append(copy)


    scal_in[...] = jnp.broadcast_to(wide(low(scal_own[...])), scal_in.shape)
    scal_ref[me] = scal_in[...]
    load_expand = pltpu.make_async_copy(expand_ref, expand_v, local_sem.at[1])
    load_expand.start()
    load_shrink = pltpu.make_async_copy(shrink_ref, shrink_v, local_sem.at[2])
    load_shrink.start()
    kv_head = lax.div(head * heads, H // KV)
    own_rows = rows_of(me * block_rows, block_rows)
    attn_w[own_rows, :wide_heads] = low(query_ref[...])
    for i, column in enumerate((kv_head, KV + kv_head)):
        columns = pl.ds(pl.multiple_of(column * HD, HD), HD)
        attn_w[own_rows, wide_heads + i * HD : wide_heads + (i + 1) * HD] = low(kv_ref[:, columns])
    mix_w[own_rows, :] = low(mixing_ref[...])
    scal_z = {d: links.to(scal_in, scal_ref.at[me], seq=owners[d]) for d in (1, 2, 3)}
    scal_y = [links.to(scal_in, scal_ref.at[me], **to_y)]
    attn_own = at_rows(attn_w, me, block_rows)
    attn_z = {d: links.to(attn_own, attn_own, seq=owners[d]) for d in (1, 2)}
    attn_y = [links.to(attn_own, attn_own, **to_y)]
    mix_own = at_rows(mix_w, me, block_rows)
    mix_z = {d: links.to(mix_own, mix_own, seq=owners[d]) for d in (1, 2)}
    mix_y = []
    for d in (1, 2, 3):
        scal_z[d].wait_recv()
        owner = y * size + owners[d]
        scal_y.append(links.to(scal_ref.at[owner], scal_ref.at[owner], **to_y))
    for copy in scal_y:
        copy.wait_recv()
    gain_one = vector_of(scal_ref, 0, width)

    def norm_rows(i, unused):
        part = rows_of(i * quarter, quarter)
        values = wide(x_ref[part, :])
        scale = lax.rsqrt(jnp.mean(values * values, axis=-1, keepdims=True) + norm_eps)
        normed_ref[part, :] = low(values * scale * gain_one)
        return unused

    lax.fori_loop(0, 4, norm_rows, 0)
    cos_ref[...] = jnp.concatenate([cos_half[...], cos_half[...]], axis=1)
    sin_ref[...] = jnp.concatenate([-sin_half[...], sin_half[...]], axis=1)
    store(cos_ref, cos_out)
    store(sin_ref, sin_out)

    def attn_arrival(d):
        attn_z[d].wait_recv()
        block = at_rows(attn_w, y * size + owners[d], block_rows)
        if d == 2:
            attn_z[3] = links.to(block, block, seq=owners[1])
        attn_y.append(links.to(block, block, **to_y))

    def mix_arrival(d):
        mix_z[d].wait_recv()
        block = at_rows(mix_w, y * size + owners[d], block_rows)
        if d == 2:
            mix_z[3] = links.to(block, block, seq=owners[1])
        mix_y.append(links.to(block, block, **to_y))

    load_expand.wait()
    load_shrink.wait()
    cut_units(expand_v, shrink_v, ff_packs)
    attn_arrival(2)
    attn_arrival(1)
    mix_arrival(2)
    mix_arrival(1)
    x_begin = core * half + (1 - xx) * quarter

    def quarter_of(ref, d, begin):
        return ref.at[rows_of(owners[d] * rows + begin, quarter), :]

    cot_own = cot_ref.at[rows_of(row_begin, quarter), :]
    cot_z = {d: links.to(cot_own, quarter_of(cot_all, 0, row_begin), seq=owners[d]) for d in (2, 1)}
    cot_x, cot_core = {}, []

    def cot_arrival(d):
        cot_z[d].wait_recv()
        block = quarter_of(cot_all, d, row_begin)
        if d == 2:
            cot_z[3] = links.to(block, block, seq=owners[1])
        cot_x[d] = links.to(block, block, **to_x)
        cot_core.append(links.to(block, block, **to_core))

    def cot_on(d):
        cot_x[d].wait_recv()
        block = quarter_of(cot_all, d, x_begin)
        cot_core.append(links.to(block, block, **to_core))

    ff_own = at_rows(ff_w, me, block_rows)
    ff_copy = pltpu.make_async_copy(ff_packs.at[z], ff_own, local_sem.at[1])
    ff_copy.start()
    ff_z, ff_y = {}, []

    half_block = block_rows // 2

    def ff_start(d, part):
        rows_there = rows_of(me * block_rows + part * half_block, half_block)
        source = ff_packs.at[owners[d], pl.ds(part * half_block, half_block), :]
        ff_z[d, part] = links.to(source, ff_w.at[rows_there, :], seq=owners[d])

    def ff_arrival(d, part):
        ff_z[d, part].wait_recv()
        begin = (y * size + owners[d]) * block_rows + part * half_block
        block = ff_w.at[rows_of(begin, half_block), :]
        ff_y.append(links.to(block, block, **to_y))

    ff_start(2, 0)
    ff_start(2, 1)
    attn_arrival(3)
    mix_y.append(links.to(mix_own, mix_own, **to_y))
    mix_arrival(3)
    cot_arrival(2)
    cot_arrival(1)
    ff_y.append(links.to(ff_packs.at[z], ff_own, **to_y))
    for copy in attn_y:
        copy.wait_recv()

    base = 2 * width + H * HD
    bias_q = vector_of(scal_ref, 2 * width + head * wide_heads, wide_heads)
    bias_k = vector_of(scal_ref, base + kv_head * HD, HD)
    bias_v = vector_of(scal_ref, base + (KV + kv_head) * HD, HD)
    own_k, own_v = at_rows(k_all, z, rows), at_rows(v_all, z, rows)

    def project(i, unused):
        part = rows_of(i * half, half)
        normed = normed_ref[part, :]
        cosine, sine_term = cos_ref[part, :], sin_ref[part, :]
        pre = dot_nn(normed, attn_w[:, wide_heads:])
        own = rows_of(z * rows + i * half, half)
        k_all[own, :] = low(turn(pre[:, :HD] + bias_k, cosine, sine_term))
        v_all[own, :] = low(pre[:, HD:] + bias_v)
        pre = dot_nn(normed, attn_w[:, :wide_heads]) + bias_q
        for n in range(heads):
            at = slice(n * HD, (n + 1) * HD)
            q_ref[part, at] = low(turn(pre[:, at], cosine, sine_term))
        return unused

    lax.fori_loop(0, 2, project, 0)
    def keys_or_values(owner, where):
        number = len(links.started)
        for which, ref in ((0, k_all), (1, v_all)):
            block = at_rows(ref, owner, rows)
            copy = pltpu.make_async_remote_copy(
                src_ref=block,
                dst_ref=block,
                send_sem=send_sems.at[number],
                recv_sem=recv_sems.at[number],
                device_id=where,
                device_id_type=pl.DeviceIdType.MESH,
            )
            pl.when(core == which)(copy.start)
        links.started.append(copy)
        return copy

    kv_z = {d: keys_or_values(z, {"seq": owners[d]}) for d in (3, 2, 1)}
    kv_core = []
    ff_start(1, 0)
    ff_start(1, 1)
    ff_start(3, 0)
    ff_start(3, 1)
    for d in (1, 2, 3):
        kv_z[d].wait_recv()
        kv_core.append(keys_or_values(owners[d], to_core))
    for copy in kv_core:
        copy.wait_recv()
    store(attn_w, attn_out)
    store(normed_ref, normed_out)
    store(q_ref, q_out)
    store(k_all, k_out)
    store(v_all, v_out)
    attention_forward(lengths_ref, q_ref, k_all, v_all, att_ref, lse_ref)
    store(att_ref, att_out)
    store(lse_ref, lse_out)
    ff_arrival(2, 0)
    ff_arrival(2, 1)
    cot_on(2)
    cot_on(1)

    for copy in mix_y:
        copy.wait_recv()
    store(mix_w, mix_out)

    def branch_part(begin, size_rows):
        return dot_nt(low(att_ref[rows_of(begin, size_rows), :]), mix_w[...])

    def branch_send(i, unused):
        part = rows_of(i * quarter, quarter)
        send_c[part, :] = low(branch_part((1 - core) * half + i * quarter, quarter))
        return unused

    lax.fori_loop(0, 2, branch_send, 0)
    to_c = links.to(send_c, recv_c, **to_core)

    def branch_keep(i, unused):
        part = rows_of(i * quarter, quarter)
        kept[part, :] = branch_part(core * half + i * quarter, quarter)
        return unused

    lax.fori_loop(0, 2, branch_keep, 0)
    to_c.wait_recv()
    other, mine = rows_of((1 - xx) * quarter, quarter), rows_of(xx * quarter, quarter)
    send_x[...] = low(kept[other, :] + wide(recv_c[other, :]))
    to_xx = links.to(send_x, recv_x, **to_x)
    cot_arrival(3)
    to_xx.wait_recv()
    gain_two = vector_of(scal_ref, width, width)
    hidden = wide(x_ref[rows_of(row_begin, quarter), :]) + (
        kept[mine, :] + wide(recv_c[mine, :]) + wide(recv_x[...])
    )
    hid_ref[...] = hidden
    store(hid_ref, hid_out)
    scale = lax.rsqrt(jnp.mean(hidden * hidden, axis=-1, keepdims=True) + norm_eps)
    nt_ref[...] = low(hidden * scale * gain_two)
    own = quarter_of(nt_all, 0, row_begin)
    own_copy = pltpu.make_async_copy(nt_ref, own, local_sem.at[0])
    own_copy.start()
    nt_z = {d: links.to(nt_ref, own, seq=owners[d]) for d in (2, 1)}
    nt_x = {0: links.to(nt_ref, own, **to_x)}
    nt_core = [links.to(nt_ref, own, **to_core)]

    def nt_arrival(d):
        nt_z[d].wait_recv()
        block = quarter_of(nt_all, d, row_begin)
        if d == 2:
            nt_z[3] = links.to(block, block, seq=owners[1])
        nt_x[d] = links.to(block, block, **to_x)
        nt_core.append(links.to(block, block, **to_core))

    def nt_on(d):
        nt_x[d].wait_recv()
        block = quarter_of(nt_all, d, x_begin)
        nt_core.append(links.to(block, block, **to_core))

    ff_arrival(1, 0)
    ff_arrival(1, 1)
    nt_arrival(2)
    nt_arrival(1)
    nt_on(0)
    cot_on(3)
    nt_arrival(3)
    ff_arrival(3, 0)
    ff_arrival(3, 1)
    for d in (2, 1, 3):
        nt_on(d)
    for copy in cot_core + ff_y + nt_core:
        copy.wait_recv()
    links.finish()
    own_copy.wait()
    ff_copy.wait()
    for copy in stores:
        copy.wait()


def front(
    lengths, scal_own, query, keyvalue, mixing_t, expand, shrink_t, x_rows, cot_rows, cosine, sine_term, columns
):
    rows, width = x_rows.shape
    size = lax.axis_size("seq")
    quarter, half, count = rows // 4, rows // 2, 2 * size
    block_rows, wide_heads = query.shape
    bf16, f32 = jnp.bfloat16, jnp.float32
    shape = jax.ShapeDtypeStruct
    in_vmem_spec, anywhere = pl.BlockSpec(memory_space=pltpu.VMEM), pl.BlockSpec(memory_space=pl.ANY)
    staged = [
        shape((count * block_rows, wide_heads + 2 * HD), bf16),
        shape((count * block_rows, wide_heads), bf16),
        shape((rows, width), bf16),
        shape((rows, wide_heads), bf16),
        shape((size * rows, HD), bf16),
        shape((size * rows, HD), bf16),
        shape((rows, wide_heads), f32),
        shape((rows, wide_heads // HD), f32),
        shape((quarter, width), f32),
    ]
    table = shape((rows, HD), f32)
    outs = [(shape((count, 8, scal_own.shape[1]), f32), in_vmem_spec)]
    outs += [(one, anywhere) for one in staged[:2]]
    outs += [
        (shape((count * block_rows, columns), bf16), anywhere),
        (shape((size * rows, width), bf16), anywhere),
    ]
    outs += [(one, anywhere) for one in staged[2:]]
    outs.append((shape((size * rows, width), bf16), anywhere))
    outs += [(table, anywhere)] * 2
    return pl.pallas_call(
        front_kernel,
        out_shape=[o[0] for o in outs],
        in_specs=[pl.BlockSpec(memory_space=pltpu.SMEM)]
        + [in_vmem_spec] * 4
        + [anywhere] * 2
        + [in_vmem_spec, anywhere, in_vmem_spec, in_vmem_spec],
        out_specs=[o[1] for o in outs],
        scratch_shapes=[
            pltpu.VMEM((8, scal_own.shape[1]), f32),
            pltpu.VMEM(table.shape, f32),
            pltpu.VMEM(table.shape, f32),
        ]
        + [pltpu.VMEM(one.shape, one.dtype) for one in staged]
        + [
            pltpu.VMEM(expand.shape, f32),
            pltpu.VMEM(shrink_t.shape, f32),
            pltpu.VMEM((size, block_rows, columns), bf16),
            pltpu.VMEM((quarter, width), bf16),
            pltpu.VMEM((half, width), bf16),
            pltpu.VMEM((half, width), bf16),
            pltpu.VMEM((quarter, width), bf16),
            pltpu.VMEM((quarter, width), bf16),
            pltpu.VMEM((half, width), f32),
            pltpu.SemaphoreType.DMA((72,)),
            pltpu.SemaphoreType.DMA((72,)),
            pltpu.SemaphoreType.DMA((3,)),
            pltpu.SemaphoreType.DMA((11,)),
        ],
        compiler_params=pltpu.CompilerParams(
            collective_id=1, has_side_effects=True, vmem_limit_bytes=62 * 1024 * 1024
        ),
        cost_estimate=pl.CostEstimate(
            flops=6 * 10**9, bytes_accessed=30 * 10**6, transcendentals=10**7
        ),
    )(lengths, scal_own, query, keyvalue, mixing_t, expand, shrink_t, x_rows, cot_rows, cosine, sine_term)


def gated(gate_value, up_value, act_grad):
    gate_sigmoid = jax.nn.sigmoid(gate_value)
    silu = gate_value * gate_sigmoid
    gate_grad = act_grad * up_value * gate_sigmoid * (1.0 + gate_value * (1.0 - gate_sigmoid))
    return silu * up_value, gate_grad, act_grad * silu


def ff_kernel(
    nt_ref, ff_w, cot_all, cot_ref, hid_ref, scal_ref,
    hg_ref, bg_ref, gain_ref, gw_ref, out_ref, early_ref,
    nt_all, cot_v, w_v, both_v, act_v, send_c, recv_c, kept, send_x, recv_x, send_z, recv_z, total, grad_v, out_v,
    send_sems, recv_sems, local_sems,
):
    quarter, width = hid_ref.shape
    half, rows = 2 * quarter, 4 * quarter
    y, z, head = lax.axis_index("dp"), lax.axis_index("seq"), lax.axis_index("head")
    core, xx = lax.rem(head, 2), lax.div(head, 2)
    row_begin = core * half + xx * quarter
    x_begin = core * half + (1 - xx) * quarter
    wide_units = both_v.shape[1]
    main = wide_units // 256 * 128
    owners = [z, z + 1 - 2 * lax.rem(z, 2), lax.rem(z + 2, 4), 3 - z]
    to_x, to_core = {"head": head + 2 - 4 * xx}, {"head": head + 1 - 2 * core}
    size = 4
    block_rows = ff_w.shape[0] // (2 * size)
    loads = []

    def load(source, target):
        copy = pltpu.make_async_copy(source, target, local_sems.at[4 + len(loads)])
        copy.start()
        loads.append(copy)

    load(ff_w, w_v)
    for d in (3, 2, 1, 0):
        if d > 0:
            load(at_rows(cot_all, owners[d], rows), at_rows(cot_v, owners[d], rows))
        else:
            load(cot_ref, at_rows(cot_v, z, rows))
        load(at_rows(nt_ref, owners[d], rows), at_rows(nt_all, owners[d], rows))
    to_y = {"dp": 1 - y}
    greet([{"seq": owners[d]} for d in (1, 2, 3)] + [to_y, to_x, to_core])
    links = Links(send_sems, recv_sems)

    loads[0].wait()

    def act_grad_rows(begin):
        part = rows_of(begin, half)
        act_v[part, :] = low(dot_nn(cot_v[part, :], w_v[:, wide_units:]))

    def gates(begin):
        part = rows_of(begin, half)
        values = dot_nn(nt_all[part, :], w_v[:, :wide_units])
        act_grad = wide(act_v[part, :])
        act, gate_grad, up_grad = gated(
            values[:, :main], values[:, main : 2 * main], act_grad[:, :main]
        )
        act_v[part, :main] = low(act)
        both_v[part, :main] = low(gate_grad)
        both_v[part, main : 2 * main] = low(up_grad)
        last = values[:, 2 * main :]
        act, gate_grad, up_grad = gated(last, pltpu.roll(last, 64, 1), act_grad[:, main:])
        left = lax.broadcasted_iota(jnp.int32, last.shape, 1) < 64
        act_v[part, main:] = low(jnp.where(left, act, 0.0))
        both_v[part, 2 * main :] = low(jnp.where(left, gate_grad, pltpu.roll(up_grad, 64, 1)))

    def back_part(begin):
        return low(dot_nt(both_v[rows_of(begin, half), :], w_v[:, :wide_units]))

    mine, other = rows_of(xx * quarter, quarter), rows_of((1 - xx) * quarter, quarter)
    steps_c, steps_x, steps_z = {}, {}, {}
    sequence = (3, 2, 1, 0)

    def start_step(s):
        steps_c[s].wait_recv()
        send_x[s] = low(wide(kept[s % 2, other, :]) + wide(recv_c[s, other, :]))
        steps_x[s] = links.to(send_x.at[s], recv_x.at[s], **to_x)

    def finish_step(s):
        steps_x[s].wait_recv()
        value = wide(kept[s % 2, mine, :]) + wide(recv_c[s, mine, :]) + wide(recv_x[s])
        if s == 0:
            total[...] = value
        else:
            send_z[s - 1] = low(value)
            steps_z[s] = links.to(send_z.at[s - 1], recv_z.at[s - 1], seq=owners[s])

    for s in sequence:
        base = owners[s] * rows
        loads[7 - 2 * s].wait()
        loads[8 - 2 * s].wait()
        act_grad_rows(base + (1 - core) * half)
        gates(base + (1 - core) * half)
        if s < 2:
            steps_c[s + 2].wait_send()
        send_c[s % 2] = back_part(base + (1 - core) * half)
        steps_c[s] = links.to(send_c.at[s % 2], recv_c.at[s], **to_core)
        act_grad_rows(base + core * half)
        gates(base + core * half)
        kept[s % 2] = back_part(base + core * half)
        start_step(s)
        if s < 3:
            finish_step(s + 1)

    count = both_v.shape[0] // rows
    pair_rows = grad_v.shape[1]

    def weight_grads(first, stores):
        for i in range(2):
            begin = pl.multiple_of((first * 2 + i) * pair_rows, 128)
            if len(stores) >= 2:
                stores[-2].wait()
            slot = grad_v.at[i]
            columns = pl.ds(begin, pair_rows)
            slot[:, :wide_units] = low(dot_tn(nt_all[:, columns], both_v[...]))
            slot[:, wide_units:] = low(dot_tn(cot_v[:, columns], act_v[...]))
            store = pltpu.make_async_copy(
                slot, gw_ref.at[pl.ds(begin, pair_rows), :], local_sems.at[i]
            )
            store.start()
            stores.append(store)

    stores = []
    weight_grads(1 - y, stores)
    finish_step(0)
    for store in stores:
        store.wait()
    stores = []
    source = at_rows(gw_ref, (1 - y) * size + owners[3], block_rows)
    early = links.to(source, early_ref, **to_y)
    n2 = total[...]
    for s in range(1, 4):
        steps_z[s].wait_recv()
        n2 = n2 + wide(recv_z[s - 1])
    hidden = hid_ref[...]
    gain_two = vector_of(scal_ref, width, width)
    scale = lax.rsqrt(jnp.mean(hidden * hidden, axis=-1, keepdims=True) + norm_eps)
    back, gain_grad = norm_back(n2, hidden, scale, gain_two)
    gain_ref[...] = gain_grad[None]
    hidden_grad = wide(cot_v[rows_of(z * rows + row_begin, quarter), :]) + back
    hg_ref[...] = hidden_grad
    own = bg_ref.at[rows_of(row_begin, quarter), :]
    own[...] = low(hidden_grad)
    bg_x = links.to(own, own, **to_x)
    bg_core = [links.to(own, own, **to_core)]
    weight_grads(y, stores)
    out_stores = []
    for i in range(2 * count):
        part = pl.ds(i * half, half)
        if i >= 2:
            out_stores[i - 2].wait()
        out_v[i % 2] = low(dot_nt(act_v[part, :], w_v[:, wide_units:]))
        store = pltpu.make_async_copy(out_v.at[i % 2], out_ref.at[part, :], local_sems.at[2 + i % 2])
        store.start()
        out_stores.append(store)
        if i == 1:
            bg_x.wait_recv()
            block = bg_ref.at[rows_of(x_begin, quarter), :]
            bg_core.append(links.to(block, block, **to_core))
    for copy in bg_core + [early]:
        copy.wait_recv()
    for store in stores[-2:] + out_stores[-2:]:
        store.wait()
    for copy in links.started:
        if copy is not steps_c[2] and copy is not steps_c[3]:
            copy.wait_send()


def feed_forward(nt, ff_w, cot_all, cot, hidden, scal, units):
    quarter, width = hidden.shape
    rows, stream, columns = 4 * quarter, cot_all.shape[0], ff_w.shape[1]
    bf16, f32 = jnp.bfloat16, jnp.float32
    shape = jax.ShapeDtypeStruct
    in_vmem_spec, anywhere = pl.BlockSpec(memory_space=pltpu.VMEM), pl.BlockSpec(memory_space=pl.ANY)
    outs = [
        (shape((quarter, width), f32), in_vmem_spec),
        (shape((rows, width), bf16), in_vmem_spec),
        (shape((1, width), f32), in_vmem_spec),
        (shape((width, columns), bf16), anywhere),
        (shape((stream, width), bf16), anywhere),
        (shape((width // 8, columns), bf16), anywhere),
    ]
    return pl.pallas_call(
        ff_kernel,
        out_shape=[o[0] for o in outs],
        in_specs=[anywhere] * 4 + [in_vmem_spec] * 2,
        out_specs=[o[1] for o in outs],
        scratch_shapes=[
            pltpu.VMEM((stream, width), bf16),
            pltpu.VMEM((stream, width), bf16),
            pltpu.VMEM((width, columns), bf16),
            pltpu.VMEM((stream, 2 * units), bf16),
            pltpu.VMEM((stream, columns - 2 * units), bf16),
            pltpu.VMEM((2, 2 * quarter, width), bf16),
            pltpu.VMEM((4, 2 * quarter, width), bf16),
            pltpu.VMEM((2, 2 * quarter, width), bf16),
            pltpu.VMEM((4, quarter, width), bf16),
            pltpu.VMEM((4, quarter, width), bf16),
            pltpu.VMEM((3, quarter, width), bf16),
            pltpu.VMEM((3, quarter, width), bf16),
            pltpu.VMEM((quarter, width), f32),
            pltpu.VMEM((2, width // 4, columns), bf16),
            pltpu.VMEM((2, 2 * quarter, width), bf16),
            pltpu.SemaphoreType.DMA((40,)),
            pltpu.SemaphoreType.DMA((40,)),
            pltpu.SemaphoreType.DMA((28,)),
        ],
        compiler_params=pltpu.CompilerParams(
            collective_id=2, has_side_effects=True, vmem_limit_bytes=62 * 1024 * 1024
        ),
        cost_estimate=pl.CostEstimate(
            flops=33 * 10**9, bytes_accessed=40 * 10**6, transcendentals=10**6
        ),
    )(nt, ff_w, cot_all, cot, hidden, scal)


def back_kernel(
    lengths_ref, scal_ref, x_ref, gain_two_ref, gw_ref, part_ref, early_ref,
    bg_in, mix_in, q_in, k_in, v_in, att_in, lse_in, cos_in, sin_in, attn_in, normed_in, hid_in, hg_in,
    layer_ref, input_ref, ff_grads, attn_ref, kv_ref, small_ref,
    bg_ref, mix_w, q_ref, k_all, v_all, att_ref, lse_ref, cos_ref, sin_ref, attn_w, normed_ref, hid_ref, hg_ref,
    ff_y, ff_own, out_c, out_own, out_sx, out_rx, out_sz, out_rz, dk, dv, do, dq, dkv_s, dkv_r, dkv_rz, dkv_own,
    qg, one_sc, one_rc, one_keep, one_sx, one_rx, layer_own, input_own, a_other, a_own, a_y, a_z, a_sz,
    x_own, small, small_y, small_s, small_z, small_h, kv_own,
    send_sems, recv_sems, local_sems, stage_sems,
):
    quarter, width = x_own.shape
    half, rows = 2 * quarter, 4 * quarter
    block_rows = attn_ref.shape[0]
    y, z, head = lax.axis_index("dp"), lax.axis_index("seq"), lax.axis_index("head")
    core, xx = lax.rem(head, 2), lax.div(head, 2)
    size = lax.axis_size("seq")
    heads = q_ref.shape[1] // HD
    wide_heads = heads * HD
    row_begin = core * half + xx * quarter
    x_begin = core * half + (1 - xx) * quarter
    owners = [z, z + 1 - 2 * lax.rem(z, 2), lax.rem(z + 2, 4), 3 - z]
    to_y, to_x, to_core = {"dp": 1 - y}, {"head": head + 2 - 4 * xx}, {"head": head + 1 - 2 * core}
    mine, other = rows_of(xx * quarter, quarter), rows_of((1 - xx) * quarter, quarter)
    is_core = wide(core)
    staged = {}
    for name, source, target in (
        ("bg", bg_in, bg_ref), ("mix", mix_in, mix_w), ("q", q_in, q_ref), ("k", k_in, k_all), ("v", v_in, v_all),
        ("att", att_in, att_ref), ("lse", lse_in, lse_ref), ("cos", cos_in, cos_ref), ("sin", sin_in, sin_ref),
        ("attn", attn_in, attn_w), ("normed", normed_in, normed_ref), ("hid", hid_in, hid_ref), ("hg", hg_in, hg_ref),
    ):
        staged[name] = pltpu.make_async_copy(source, target, stage_sems.at[len(staged)])
        staged[name].start()
    loads = []

    def load(source, target):
        copy = pltpu.make_async_copy(source, target, local_sems.at[len(loads)])
        copy.start()
        loads.append(copy)
        return copy

    greet([to_y] + [{"seq": owners[d]} for d in (1, 2, 3)] + [to_x, to_core])
    links = Links(send_sems, recv_sems)

    order = (3, 2, 1, 0)

    def grad_rows(ref, which, d):
        return at_rows(ref, which * size + owners[d], block_rows)

    ff_sent, ff_load = {}, {}

    def ff_start(d):
        ff_sent[d] = links.to(grad_rows(gw_ref, 1 - y, d), ff_y.at[d], **to_y)

    ff_start(2)
    ff_early = load(early_ref, ff_y.at[3])
    x_load = load(x_ref.at[rows_of(row_begin, quarter), :], x_own)
    out_sent, out_load = [], []
    for s in range(4):
        begin = owners[s] * rows
        source = part_ref.at[rows_of(begin + (1 - core) * half, half), :]
        out_sent.append(links.to(source, out_c.at[s], **to_core))
    for s in range(4):
        source = part_ref.at[rows_of(owners[s] * rows + core * half, half), :]
        out_load.append(load(source, out_own.at[s]))
    for d in order:
        ff_load[d] = load(grad_rows(gw_ref, y, d), ff_own.at[d])

    ff_over_z = []

    def ff_add(d):
        if d == 3:
            ff_early.wait()
        else:
            ff_sent[d].wait_recv()
        ff_load[d].wait()

        def add(i, unused):
            part = rows_of(i * 64, 64)
            ff_own[d, part, :] = low(wide(ff_own[d, part, :]) + wide(ff_y[d, part, :]))
            return unused

        lax.fori_loop(0, block_rows // 64, add, 0)

    def ff_half(d, i):
        part = pl.ds(i * (block_rows // 2), block_rows // 2)
        ff_over_z.append(
            links.to(ff_own.at[d, part, :], ff_grads.at[z, part, :], seq=owners[d])
        )

    def ff_step(d):
        ff_add(d)
        if d == 0:
            load(ff_own.at[d], ff_grads.at[z])
        else:
            ff_half(d, 0)
            ff_half(d, 1)

    out_x, out_z = {}, {}

    def out_step_c(s):
        out_sent[s].wait_recv()
        out_load[s].wait()
        out_sx[s] = low(wide(out_own[s, other, :]) + wide(out_c[s, other, :]))
        out_x[s] = links.to(out_sx.at[s], out_rx.at[s], **to_x)

    def out_value(s):
        out_x[s].wait_recv()
        return wide(out_own[s, mine, :]) + wide(out_c[s, mine, :]) + wide(out_rx[s])

    def out_step_x(s):
        value = out_value(s)
        if s == 2:
            out_z[3].wait_recv()
            value = value + wide(out_rz[2])
        out_sz[s - 1] = low(value)
        out_z[s] = links.to(out_sz.at[s - 1], out_rz.at[s - 1], seq=owners[2 if s == 2 else 1])

    def do_rows(i, unused):
        part = rows_of(i * half, half)
        do[part, :] = low(dot_nn(bg_ref[part, :], mix_w[...]))
        return unused

    ff_add(3)
    ff_half(3, 0)
    for name in ("bg", "mix"):
        staged[name].wait()
    lax.fori_loop(0, 2, do_rows, 0)
    for name in ("q", "k", "v", "att", "lse"):
        staged[name].wait()
    attention_backward(lengths_ref, q_ref, k_all, v_all, do, att_ref, lse_ref, dq, dk, dv, (0,))
    out_step_c(3)
    out_step_c(2)
    attention_backward(lengths_ref, q_ref, k_all, v_all, do, att_ref, lse_ref, dq, dk, dv, (1,))
    dkv_s[...] = low(dv[...] * (1.0 - is_core) + dk[...] * is_core)
    dkv_core = links.to(dkv_s, dkv_r, **to_core)
    for name in ("cos", "sin", "attn", "normed", "hid", "hg"):
        staged[name].wait()
    for n in range(heads):
        at = slice(n * HD, (n + 1) * HD)
        qg[:, at] = low(turn(dq[:, at], cos_ref[...], -sin_ref[...]))
    dkv_core.wait_recv()

    def dkv_block(d):
        part = rows_of(owners[d] * rows, rows)
        return dk[part, :] * (1.0 - is_core) + dv[part, :] * is_core + wide(dkv_r[part, :])

    dkv_z = []
    for d in (1, 2, 3):
        dkv_own[d] = low(dkv_block(d))
        dkv_z.append(links.to(dkv_own.at[d], dkv_rz.at[d - 1], seq=owners[d]))
    total = dkv_block(0)
    for d in (1, 2, 3):
        dkv_z[d - 1].wait_recv()
        total = total + wide(dkv_rz[d - 1])
    ff_half(3, 1)
    turned = turn(total, cos_ref[...], -sin_ref[...])
    dkv_own[0] = low(turned * (1.0 - is_core) + total * is_core)
    key_columns = pl.ds(pl.multiple_of(wide_heads + core * HD, HD), HD)

    def one_part(begin):
        part = rows_of(begin, quarter)
        return dot_nt(qg[part, :], attn_w[:, :wide_heads]) + dot_nt(
            dkv_own[0, part, :], attn_w[:, key_columns]
        )

    def one_send(i, unused):
        one_sc[rows_of(i * quarter, quarter), :] = low(one_part((1 - core) * half + i * quarter))
        return unused

    def one_own(i, unused):
        one_keep[rows_of(i * quarter, quarter), :] = one_part(core * half + i * quarter)
        return unused

    lax.fori_loop(0, 2, one_send, 0)
    one_c = links.to(one_sc, one_rc, **to_core)
    lax.fori_loop(0, 2, one_own, 0)
    one_c.wait_recv()
    one_sx[...] = low(one_keep[other, :] + wide(one_rc[other, :]))
    one_x = links.to(one_sx, one_rx, **to_x)

    def attn_grads(which, target):
        columns = pl.ds(pl.multiple_of(which * (width // 2), 128), width // 2)
        normed = normed_ref[:, columns]
        target[:, :wide_heads] = low(dot_tn(normed, qg[...]))
        target[:, wide_heads : 2 * wide_heads] = low(
            dot_tn(bg_ref[:, columns], low(att_ref[...]))
        )
        target[:, 2 * wide_heads :] = low(dot_tn(normed, dkv_own[0]))

    attn_grads(1 - y, a_other)
    attn_sent = {
        d: links.to(at_rows(a_other, owners[d], block_rows), a_y.at[d], **to_y) for d in order
    }
    ff_step(2)
    out_step_c(1)
    out_step_c(0)
    attn_grads(y, a_own)
    out_step_x(3)

    one_x.wait_recv()
    norm_one_grad = one_keep[mine, :] + wide(one_rc[mine, :]) + wide(one_rx[...])
    x_load.wait()
    x_rows = wide(x_own[...])
    gain_one = vector_of(scal_ref, 0, width)
    scale = lax.rsqrt(jnp.mean(x_rows * x_rows, axis=-1, keepdims=True) + norm_eps)
    back, gain_grad = norm_back(norm_one_grad, x_rows, scale, gain_one)
    input_own[...] = low(hg_ref[...] + back)

    def gather(source, target):
        place = target.at[rows_of(row_begin, quarter), :]
        load(source, place)
        return links.to(source, place, **to_x), [links.to(source, place, **to_core)]

    def gather_on(sent, target):
        sent[0].wait_recv()
        block = target.at[rows_of(x_begin, quarter), :]
        sent[1].append(links.to(block, block, **to_core))

    input_sent = gather(input_own, input_ref)
    small[...] = jnp.zeros_like(small)
    per = small.shape[2] // 128

    def put(begin, values):
        for i in range(values.shape[1] // 128):
            tile = begin // 128 + i
            value = values[:, i * 128 : (i + 1) * 128]
            if isinstance(tile, int):
                small[tile // per, 0:1, tile % per * 128 : tile % per * 128 + 128] = value
            else:
                column = pl.ds(pl.multiple_of(lax.rem(tile, per) * 128, 128), 128)
                small[lax.div(tile, per), 0:1, column] = value

    put(0, gain_grad[None])
    put(width, gain_two_ref[...])
    put(2 * width + head * wide_heads, jnp.sum(wide(qg[...]), axis=0, keepdims=True))
    kv_begin = 2 * width + H * HD + (core * KV + lax.div(head * heads, H // KV)) * HD
    put(kv_begin, jnp.sum(wide(dkv_own[0]), axis=0, keepdims=True))
    small_sent = links.to(small.at[pl.ds((1 - y) * size, size)], small_y, **to_y)
    ff_start(1)
    ff_start(0)
    attn_over_z = {}

    def attn_step(d):
        attn_sent[d].wait_recv()
        block = wide(at_rows(a_own, owners[d], block_rows)[...]) + wide(a_y[d])
        if d == 0:
            return block
        if d == 2:
            attn_over_z[3].wait_recv()
            block = block + wide(a_z[2])
        a_sz[d - 1] = low(block)
        attn_over_z[d] = links.to(
            a_sz.at[d - 1], a_z.at[d - 1], seq=owners[2 if d == 2 else 1]
        )
        return None

    attn_step(3)
    out_step_x(1)
    out_step_x(2)
    gather_on(input_sent, input_ref)
    attn_step(1)
    attn_step(2)
    small_sent.wait_recv()
    small_s[...] = small[pl.ds(y * size, size)] + small_y[...]
    small_over_z = [
        links.to(small_s.at[owners[d]], small_z.at[d - 1], seq=owners[d]) for d in (1, 2, 3)
    ]
    layer = hid_ref[...] + out_value(0)
    for d in (1, 2):
        out_z[d].wait_recv()
        layer = layer + wide(out_rz[d - 1])
    layer_own[...] = low(layer)
    layer_sent = gather(layer_own, layer_ref)
    ff_step(1)
    block = attn_step(0)
    for d in (1, 2):
        attn_over_z[d].wait_recv()
        block = block + wide(a_z[d - 1])
    attn_ref[...] = block
    place = kv_ref.at[core * 2 + xx]
    kv_own[...] = low(block[:, 2 * wide_heads :])
    place[...] = kv_own[...]
    kv_x = links.to(kv_own, place, **to_x)
    kv_core = [links.to(kv_own, place, **to_core)]
    gather_on(layer_sent, layer_ref)
    value = small_s[z]
    for d in (1, 2, 3):
        small_over_z[d - 1].wait_recv()
        value = value + small_z[d - 1]
    small_h[0] = value
    small_x = links.to(small_h.at[0], small_h.at[1], **to_x)
    small_x.wait_recv()
    small_h[2] = small_h[0] + small_h[1]
    small_c = links.to(small_h.at[2], small_h.at[3], **to_core)
    small_c.wait_recv()
    small_ref[...] = small_h[2] + small_h[3]
    kv_x.wait_recv()
    place = kv_ref.at[core * 2 + 1 - xx]
    kv_core.append(links.to(place, place, **to_core))
    ff_step(0)
    for copy in kv_core + input_sent[1] + layer_sent[1] + ff_over_z:
        copy.wait_recv()
    links.finish()
    for copy in loads[10:]:
        copy.wait()


def back(
    lengths, scal, x_rows, hidden, hidden_grad, gain_two_grad, branch_grad, attn_w, mix_w, normed, q, k_all, v_all, attended, lse,
    cosine, sine_term, gw, out_part, early,
):
    quarter, width = hidden.shape
    half, rows = 2 * quarter, 4 * quarter
    size = lax.axis_size("seq")
    block_rows, columns = gw.shape[0] // (2 * size), gw.shape[1]
    wide_heads = q.shape[1]
    attn_columns = 2 * wide_heads + HD
    stream = k_all.shape[0]
    bf16, f32 = jnp.bfloat16, jnp.float32
    shape = jax.ShapeDtypeStruct
    in_vmem_spec, anywhere = pl.BlockSpec(memory_space=pltpu.VMEM), pl.BlockSpec(memory_space=pl.ANY)
    outs = [
        (shape((rows, width), bf16), anywhere),
        (shape((rows, width), bf16), anywhere),
        (shape((size, block_rows, columns), bf16), anywhere),
        (shape((block_rows, attn_columns), f32), in_vmem_spec),
        (shape((4, block_rows, HD), bf16), in_vmem_spec),
        (shape(scal.shape[1:], f32), in_vmem_spec),
    ]
    small = (size,) + scal.shape[1:]
    scratch = [
        ((rows, width), bf16),
        (mix_w.shape, bf16),
        (q.shape, bf16),
        (k_all.shape, bf16),
        (v_all.shape, bf16),
        (attended.shape, f32),
        (lse.shape, f32),
        (cosine.shape, f32),
        (sine_term.shape, f32),
        (attn_w.shape, bf16),
        (normed.shape, bf16),
        (hidden.shape, f32),
        (hidden.shape, f32),
        ((size, block_rows, columns), bf16),
        ((size, block_rows, columns), bf16),
        ((4, half, width), bf16),
        ((4, half, width), bf16),
        ((4, quarter, width), bf16),
        ((4, quarter, width), bf16),
        ((3, quarter, width), bf16),
        ((3, quarter, width), bf16),
        ((stream, HD), f32),
        ((stream, HD), f32),
        ((rows, wide_heads), bf16),
        ((rows, wide_heads), f32),
        ((stream, HD), bf16),
        ((stream, HD), bf16),
        ((3, rows, HD), bf16),
        ((4, rows, HD), bf16),
        ((rows, wide_heads), bf16),
        ((half, width), bf16),
        ((half, width), bf16),
        ((half, width), f32),
        ((quarter, width), bf16),
        ((quarter, width), bf16),
        ((quarter, width), bf16),
        ((quarter, width), bf16),
        ((width // 2, attn_columns), bf16),
        ((width // 2, attn_columns), bf16),
        ((4, block_rows, attn_columns), bf16),
        ((3, block_rows, attn_columns), bf16),
        ((3, block_rows, attn_columns), bf16),
        ((quarter, width), bf16),
        (scal.shape, f32),
        (small, f32),
        (small, f32),
        ((3,) + scal.shape[1:], f32),
        ((4,) + scal.shape[1:], f32),
        ((block_rows, HD), bf16),
    ]
    return pl.pallas_call(
        back_kernel,
        out_shape=[o[0] for o in outs],
        in_specs=[pl.BlockSpec(memory_space=pltpu.SMEM), in_vmem_spec, anywhere, in_vmem_spec]
        + [anywhere] * 16,
        out_specs=[o[1] for o in outs],
        scratch_shapes=[pltpu.VMEM(*one) for one in scratch]
        + [
            pltpu.SemaphoreType.DMA((56,)),
            pltpu.SemaphoreType.DMA((56,)),
            pltpu.SemaphoreType.DMA((14,)),
            pltpu.SemaphoreType.DMA((13,)),
        ],
        compiler_params=pltpu.CompilerParams(
            collective_id=3, has_side_effects=True, vmem_limit_bytes=62 * 1024 * 1024
        ),
        cost_estimate=pl.CostEstimate(
            flops=10 * 10**9, bytes_accessed=40 * 10**6, transcendentals=10**6
        ),
    )(
        lengths, scal, x_rows, gain_two_grad, gw, out_part, early, branch_grad, mix_w, q, k_all, v_all, attended, lse,
        cosine, sine_term, attn_w, normed, hidden, hidden_grad,
    )


def optimizer_kernel(*refs):
    ff_grads, attn_grads, kv_blocks = refs[:3]
    held, outs = refs[3:18], refs[18:]
    size, wide_heads = ff_grads.shape[0], held[0].shape[1]
    main = 512

    def joined(begin, rest_begin, width):
        pieces = [ff_grads[j, :, begin : begin + main] for j in range(size)]
        pieces += [
            ff_grads[j, :, rest_begin : rest_begin + 64] for j in range((width - size * main) // 64)
        ]
        return wide(jnp.concatenate(pieces, axis=1))

    def update(number, grad, at=slice(None)):
        master, moment, square = (ref[at] for ref in held[3 * number : 3 * number + 3])
        results = adamw(master, moment, square, grad, learn_rates[number], decay_rates[number])
        for ref, value in zip(outs[5 * number : 5 * number + 4], results):
            ref[at] = value
        if at == slice(None):
            outs[5 * number + 4][...] = results[4]

    update(0, wide(low(attn_grads[:, :wide_heads])))
    update(1, wide(jnp.concatenate([kv_blocks[i] for i in range(4)], axis=1)))
    update(2, wide(low(attn_grads[:, wide_heads : 2 * wide_heads])))
    every = slice(None)
    hidden_units = held[9].shape[2]
    update(3, joined(0, 2 * main, hidden_units), (every, 0, every))
    update(3, joined(main, 2 * main + 64, hidden_units), (every, 1, every))
    outs[19][...] = low(outs[18][...])
    update(4, joined(2 * main + 128, 3 * main + 128, hidden_units))


def optimizer(ff_grads, attn_grads, kv_blocks, held):
    rows, step = attn_grads.shape[0], 32

    def block(array):
        if array.ndim == 3 and array.shape[0] == 4:
            return pl.BlockSpec((4, step) + array.shape[2:], lambda i: (0, i, 0))
        rest = array.shape[1:]
        return pl.BlockSpec((step,) + rest, lambda i: (i,) + (0,) * len(rest))

    outs, flat = [], []
    for three in held:
        flat.extend(three)
        outs += [jax.ShapeDtypeStruct(three[0].shape, jnp.float32)] * 4
        outs.append(jax.ShapeDtypeStruct(three[0].shape, jnp.bfloat16))
    operands = [ff_grads, attn_grads, kv_blocks] + flat
    return pl.pallas_call(
        optimizer_kernel,
        grid=(rows // step,),
        out_shape=outs,
        in_specs=[block(one) for one in operands],
        out_specs=[block(one) for one in outs],
        compiler_params=pltpu.CompilerParams(vmem_limit_bytes=62 * 1024 * 1024),
        cost_estimate=pl.CostEstimate(
            flops=3 * 10**7, bytes_accessed=50 * 10**6, transcendentals=2 * 10**6
        ),
    )(*operands)


def rope_tables(places):
    halves = HD // 2
    powers = jnp.arange(halves, dtype=jnp.float32) * (-2.0 / HD)
    frequency = jnp.power(jnp.float32(rope_base), powers)
    angles = places.astype(jnp.float32)[:, None] * frequency[None, :]
    return jnp.cos(angles), jnp.sin(angles)


def local(
    tokens,
    cotangent,
    doc_lengths,
    queries_master,
    queries_moment,
    queries_square,
    keyvalue_master,
    keyvalue_moment,
    keyvalue_square,
    mixing_master,
    mixing_moment,
    mixing_square,
    expand_master,
    expand_moment,
    expand_square,
    shrink_master,
    shrink_moment,
    shrink_square,
    scalars_master,
    scalars_moment,
    scalars_square,
):
    local_rows, width = tokens.shape[1], tokens.shape[2]
    seq_count = lax.axis_size("seq")
    head_count = lax.axis_size("head")
    head_index = lax.axis_index("head")
    seq_index = lax.axis_index("seq")
    local_heads = H // head_count
    wide_heads = local_heads * HD
    kv_head = head_index * local_heads // (H // KV)
    core = head_index % 2
    quarter = local_rows // 4
    row_begin = (head_index % 2) * (2 * quarter) + (head_index // 2) * quarter
    hidden_units = expand_master.shape[2]
    units = 64 * -(-hidden_units // (64 * seq_count))
    more = ((0, 0), (0, units * seq_count - hidden_units))

    attn_pack = jnp.concatenate(
        [
            low(queries_master),
            low(mixing_master).T,
            low(lax.dynamic_slice_in_dim(keyvalue_master, kv_head * HD, HD, 1)),
            low(lax.dynamic_slice_in_dim(keyvalue_master, (KV + kv_head) * HD, HD, 1)),
        ],
        axis=1,
    )
    expand_low = low(expand_master)

    def cut(values):
        values = jnp.pad(values, more)
        return values.reshape(values.shape[0], seq_count, units).transpose(1, 0, 2)

    ff_packs = jnp.concatenate(
        [cut(expand_low[:, 0]), cut(expand_low[:, 1]), cut(low(shrink_master).T)], axis=2
    )
    scalar_values = wide(lax.all_gather(low(scalars_master), ("dp", "seq"), axis=0, tiled=True))
    attn_weight = weight_gather(attn_pack)
    ff_weight = weight_exchange(ff_packs)
    query_weight = attn_weight[:, :wide_heads]
    mixing_t = attn_weight[:, wide_heads : 2 * wide_heads]
    key_value_weight = attn_weight[:, 2 * wide_heads :]
    expand_weight = ff_weight[:, : 2 * units]
    shrink_t = ff_weight[:, 2 * units :]

    cot_rows = cotangent[0]
    cot_own = lax.dynamic_slice_in_dim(cot_rows, row_begin, quarter, 0)
    cot_blocks = [cot_rows]
    moving = cot_own
    for s in range(1, seq_count):
        moving = shift(moving, "seq", 1)
        cot_blocks.append(head_gather(moving))

    gain_one = scalar_values[:width]
    gain_two = scalar_values[width : 2 * width]
    bias_query = lax.dynamic_slice_in_dim(
        scalar_values, 2 * width + head_index * wide_heads, wide_heads
    )
    bias_keyvalue = scalar_values[2 * width + H * HD :]
    key_bias = lax.dynamic_slice_in_dim(bias_keyvalue, kv_head * HD, HD)
    value_bias = lax.dynamic_slice_in_dim(bias_keyvalue, (KV + kv_head) * HD, HD)
    x_rows = wide(tokens[0])
    lengths = doc_lengths[0]
    places = folded_places(
        seq_index * local_rows + jnp.arange(local_rows, dtype=jnp.int32), local_rows, seq_count
    )
    starts = doc_starts(places, lengths)
    within = places - starts
    scale_one = lax.rsqrt(jnp.mean(x_rows * x_rows, axis=-1, keepdims=True) + norm_eps)
    normed = low(x_rows * scale_one * gain_one)
    query_pre = dot_nn(normed, query_weight) + bias_query
    queries = low(rotate(query_pre.reshape(local_rows, local_heads, HD), within)).reshape(
        local_rows, wide_heads
    )
    key_value_pre = dot_nn(normed, key_value_weight)
    key_rows = low(rotate((key_value_pre[:, :HD] + key_bias)[:, None, :], within)[:, 0, :])
    value_rows = low(key_value_pre[:, HD:] + value_bias)
    moving = jnp.concatenate([key_rows, value_rows], axis=1)
    all_rows = jnp.zeros((seq_count,) + moving.shape, moving.dtype)
    for s in range(seq_count):
        if s > 0:
            moving = shift(moving, "seq", 1)
        owner = lax.rem(seq_index + seq_count - s, seq_count)
        all_rows = lax.dynamic_update_slice(all_rows, moving[None], (owner, 0, 0))
    all_rows = all_rows.reshape(-1, 2 * HD)
    all_keys, all_values = all_rows[:, :HD], all_rows[:, HD:]
    stream_rows = all_rows.shape[0]
    attended, log_total = in_vmem(
        attention_forward,
        [
            jax.ShapeDtypeStruct((local_rows, wide_heads), jnp.float32),
            jax.ShapeDtypeStruct((local_rows, local_heads), jnp.float32),
        ],
        doc_lengths,
        queries,
        all_keys,
        all_values,
    )
    attended_low = low(attended)
    x_own = lax.dynamic_slice_in_dim(x_rows, row_begin, quarter, 0)
    hidden = x_own + head_scatter(dot_nt(attended_low, mixing_t))
    scale_two = lax.rsqrt(jnp.mean(hidden * hidden, axis=-1, keepdims=True) + norm_eps)
    normed_two = low(hidden * scale_two * gain_two)

    normed_blocks, grad_blocks, act_blocks, back_parts, out_parts = [], [], [], [], []
    moving = normed_two
    for s in range(seq_count):
        if s > 0:
            moving = shift(moving, "seq", 1)
        block = head_gather(moving)
        both = dot_nn(block, expand_weight)
        gate_value, up_value = both[:, :units], both[:, units:]
        gate_sigmoid = jax.nn.sigmoid(gate_value)
        activation = low(gate_value * gate_sigmoid * up_value)
        act_grad = wide(low(dot_nn(cot_blocks[s], shrink_t)))
        gate_grad = low(act_grad * up_value * gate_sigmoid * (1.0 + gate_value * (1.0 - gate_sigmoid)))
        up_grad = low(act_grad * gate_value * gate_sigmoid)
        both_grad = jnp.concatenate([gate_grad, up_grad], axis=1)
        back_parts.append(head_scatter(dot_nt(both_grad, expand_weight)))
        out_parts.append(head_scatter(dot_nt(activation, shrink_t)))
        normed_blocks.append(block)
        grad_blocks.append(both_grad)
        act_blocks.append(activation)
    norm_two_grad = seq_sum(back_parts)
    back_two, gain_two_grad = norm_back(norm_two_grad, hidden, scale_two, gain_two)
    hidden_grad = wide(lax.dynamic_slice_in_dim(cot_rows, row_begin, quarter, 0)) + back_two
    branch_grad = head_gather(low(hidden_grad))
    feedforward = seq_sum(out_parts)
    layer_out = head_gather(low(hidden + feedforward))
    expand_part = dot_tn(jnp.concatenate(normed_blocks), jnp.concatenate(grad_blocks))
    shrink_part = dot_tn(jnp.concatenate(cot_blocks), jnp.concatenate(act_blocks))
    ff_grads = grad_exchange(low(jnp.concatenate([expand_part, shrink_part], axis=1)), False)

    attended_grad = low(dot_nn(branch_grad, mixing_t))
    query_sum, key_sum, value_sum = in_vmem(
        attention_backward,
        [
            jax.ShapeDtypeStruct((local_rows, wide_heads), jnp.float32),
            jax.ShapeDtypeStruct((stream_rows, HD), jnp.float32),
            jax.ShapeDtypeStruct((stream_rows, HD), jnp.float32),
        ],
        doc_lengths,
        queries,
        all_keys,
        all_values,
        attended_grad,
        attended,
        log_total,
    )
    mine = jnp.where(core == 0, key_sum, value_sum)
    other = jnp.where(core == 0, value_sum, key_sum)
    mine = mine + wide(swap(low(other), "head", 1))
    mine = mine.reshape(seq_count, local_rows, HD)
    own_sum = seq_sum(
        [
            lax.dynamic_index_in_dim(mine, lax.rem(seq_index + seq_count - s, seq_count), 0, False)
            for s in range(seq_count)
        ]
    )
    own_sum = low(jnp.where(core == 0, rotate(own_sum[:, None, :], -within)[:, 0, :], own_sum))
    query_grad = low(
        rotate(query_sum.reshape(local_rows, local_heads, HD), -within).reshape(
            local_rows, wide_heads
        )
    )
    own_weight = lax.dynamic_slice_in_dim(key_value_weight, core * HD, HD, 1)
    norm_one_grad = head_scatter(dot_nt(query_grad, query_weight) + dot_nt(own_sum, own_weight))
    scale_own = lax.dynamic_slice_in_dim(scale_one, row_begin, quarter, 0)
    back_one, gain_one_grad = norm_back(norm_one_grad, x_own, scale_own, gain_one)
    input_grad = head_gather(low(hidden_grad + back_one))
    attn_part = jnp.concatenate(
        [
            dot_tn(normed, query_grad),
            dot_tn(branch_grad, attended_low),
            dot_tn(normed, own_sum),
        ],
        axis=1,
    )
    attn_grads = grad_exchange(attn_part, True)
    kv_block = low(attn_grads[:, 2 * wide_heads :])
    small = jnp.zeros((scalars_master.shape[0] * 2 * seq_count,), jnp.float32)
    small = lax.dynamic_update_slice(small, jnp.concatenate([gain_one_grad, gain_two_grad]), (0,))
    small = lax.dynamic_update_slice(
        small, jnp.sum(wide(query_grad), axis=0), (2 * width + head_index * wide_heads,)
    )
    kv_column = core * KV * HD + kv_head * HD
    small = lax.dynamic_update_slice(
        small, jnp.sum(wide(own_sum), axis=0), (2 * width + H * HD + kv_column,)
    )
    small = lax.psum(small, "head")
    shared_scalars = lax.psum_scatter(small, ("dp", "seq"), scatter_dimension=0, tiled=True)
    gathered = head_gather(kv_block, 1)
    shared_keyvalue = wide(gathered)

    def joined(part):
        part = ff_grads[:, :, part * units : (part + 1) * units].transpose(1, 0, 2)
        return wide(part.reshape(part.shape[0], -1)[:, :hidden_units])

    grads = (
        attn_grads[:, :wide_heads],
        shared_keyvalue,
        attn_grads[:, wide_heads : 2 * wide_heads].T,
        jnp.stack([joined(0), joined(1)], axis=1),
        joined(2).T,
        shared_scalars,
    )
    masters = (
        (queries_master, queries_moment, queries_square),
        (keyvalue_master, keyvalue_moment, keyvalue_square),
        (mixing_master, mixing_moment, mixing_square),
        (expand_master, expand_moment, expand_square),
        (shrink_master, shrink_moment, shrink_square),
        (scalars_master, scalars_moment, scalars_square),
    )
    results = [layer_out[None], input_grad[None]]
    for held, grad, rate, decay in zip(masters, grads, learn_rates, decay_rates):
        results.extend(adamw(*held, wide(low(grad)), rate, decay))
    return tuple(results)


def local_fast(
    tokens,
    cotangent,
    doc_lengths,
    queries_master,
    queries_moment,
    queries_square,
    keyvalue_master,
    keyvalue_moment,
    keyvalue_square,
    mixing_master,
    mixing_moment,
    mixing_square,
    expand_master,
    expand_moment,
    expand_square,
    shrink_master,
    shrink_moment,
    shrink_square,
    scalars_master,
    scalars_moment,
    scalars_square,
):
    local_rows = tokens.shape[1]
    seq_count = lax.axis_size("seq")
    seq_index = lax.axis_index("seq")
    hidden_units = expand_master.shape[2]

    units = 64 * -(-hidden_units // (64 * seq_count))
    x_low, cot_rows = tokens[0], cotangent[0]
    lengths = doc_lengths[0]
    places = folded_places(
        seq_index * local_rows + jnp.arange(local_rows, dtype=jnp.int32), local_rows, seq_count
    )
    starts = doc_starts(places, lengths)
    within = places - starts
    cos_half, sin_half = rope_tables(within)
    (
        scal_all, attn_weight, mix_weight, ff_weight, cot_all, normed, queries, all_keys, all_values,
        attended, log_total, hidden, normed_all, cosine, sine_term,
    ) = front(
        doc_lengths, scalars_master[None], queries_master, keyvalue_master, mixing_master.T, expand_master, shrink_master.T,
        x_low, cot_rows, cos_half, sin_half, 3 * units + 64,
    )
    hidden_grad, branch_grad, gain_two_grad, ff_part, out_part, early = feed_forward(
        normed_all, ff_weight, cot_all, cot_rows, hidden, scal_all, units
    )
    layer_out, input_grad, ff_grads, attn_grads, kv_blocks, small = back(
        doc_lengths, scal_all, x_low, hidden, hidden_grad, gain_two_grad, branch_grad, attn_weight, mix_weight, normed, queries,
        all_keys, all_values, attended, log_total, cosine, sine_term, ff_part, out_part, early,
    )
    held = (
        (queries_master, queries_moment, queries_square),
        (keyvalue_master, keyvalue_moment, keyvalue_square),
        tuple(one.T for one in (mixing_master, mixing_moment, mixing_square)),
        (expand_master, expand_moment, expand_square),
        tuple(one.T for one in (shrink_master, shrink_moment, shrink_square)),
    )
    updated = optimizer(ff_grads, attn_grads, kv_blocks, held)
    results = [layer_out[None], input_grad[None]]
    for i in range(5):
        results.extend(one.T if i in (2, 4) else one for one in updated[5 * i : 5 * i + 5])
    results.extend(
        adamw(
            scalars_master, scalars_moment, scalars_square, wide(low(small[0])), learn_rates[5], decay_rates[5]
        )
    )
    return tuple(results)


def solution(mesh):
    placed = (
        P("dp", "seq", None),
        P("dp", "seq", None),
        P("dp", None),
        P(("dp", "seq"), "head"),
        P(("dp", "seq"), "head"),
        P(("dp", "seq"), "head"),
        P(("dp", "seq"), None),
        P(("dp", "seq"), None),
        P(("dp", "seq"), None),
        P("head", ("dp", "seq")),
        P("head", ("dp", "seq")),
        P("head", ("dp", "seq")),
        P(("dp", "seq"), None, "head"),
        P(("dp", "seq"), None, "head"),
        P(("dp", "seq"), None, "head"),
        P("head", ("dp", "seq")),
        P("head", ("dp", "seq")),
        P("head", ("dp", "seq")),
        P(("dp", "seq")),
        P(("dp", "seq")),
        P(("dp", "seq")),
    )
    small = dict(mesh.shape) == {"dp": 2, "seq": 4, "head": 4}
    return jax.shard_map(
        local_fast if small else local,
        mesh=mesh,
        in_specs=placed,
        out_specs=(
            P("dp", "seq", None),
            P("dp", "seq", None),
            P(("dp", "seq"), "head"),
            P(("dp", "seq"), "head"),
            P(("dp", "seq"), "head"),
            P(("dp", "seq"), "head"),
            P(("dp", "seq"), "head"),
            P(("dp", "seq"), None),
            P(("dp", "seq"), None),
            P(("dp", "seq"), None),
            P(("dp", "seq"), None),
            P(("dp", "seq"), None),
            P("head", ("dp", "seq")),
            P("head", ("dp", "seq")),
            P("head", ("dp", "seq")),
            P("head", ("dp", "seq")),
            P("head", ("dp", "seq")),
            P(("dp", "seq"), None, "head"),
            P(("dp", "seq"), None, "head"),
            P(("dp", "seq"), None, "head"),
            P(("dp", "seq"), None, "head"),
            P(("dp", "seq"), None, "head"),
            P("head", ("dp", "seq")),
            P("head", ("dp", "seq")),
            P("head", ("dp", "seq")),
            P("head", ("dp", "seq")),
            P("head", ("dp", "seq")),
            P(("dp", "seq")),
            P(("dp", "seq")),
            P(("dp", "seq")),
            P(("dp", "seq")),
            P(("dp", "seq")),
        ),
        check_vma=False,
    )
```

```python
import functools
import math

import jax
import jax.numpy as jnp
from jax import lax
from jax.experimental import pallas as pl
from jax.experimental.pallas import tpu as pltpu
from jax.sharding import PartitionSpec as P

D = 1536
H = 12
KV = 2
HD = 128
STEP = 5


norm_eps = 1e-06
rope_base = 1000000.0
beta_first = 0.5
beta_second = 0.5
adam_eps = 1e-08
masked_low = -1e30
learn_rates = (0.02, 0.02, 0.3, 0.02, 0.01, 0.2)
decay_rates = (0.1, 0.1, 0.1, 0.1, 0.1, 0.0)


def folded_places(row_ids, shard_rows, seq_count):
    owner_index = row_ids // shard_rows
    inside = row_ids % shard_rows
    halves = shard_rows // 2
    block_index = jnp.where(inside < halves, owner_index, 2 * seq_count - 1 - owner_index)
    return block_index * halves + inside % halves


def doc_starts(places, lengths):
    end, total = jnp.int32(0), jnp.zeros_like(places)
    for i in range(lengths.shape[0]):
        end = end + lengths[i]
        total = total + jnp.where(end <= places, lengths[i], 0)
    return total


def rotate(values, places):
    halves = values.shape[-1] // 2
    powers = jnp.arange(halves, dtype=jnp.float32) * (-2.0 / values.shape[-1])
    frequency = jnp.power(jnp.float32(rope_base), powers)
    angles = places.astype(jnp.float32)[:, None] * frequency[None, :]
    cosine = jnp.cos(angles)[:, None, :]
    sine_term = jnp.sin(angles)[:, None, :]
    first_half = values[..., :halves]
    second_half = values[..., halves:]
    return jnp.concatenate(
        [
            first_half * cosine - second_half * sine_term,
            second_half * cosine + first_half * sine_term,
        ],
        axis=-1,
    )


def norm_back(grad_rows, values, scale_rows, gain_vector):
    unit_rows = values * scale_rows
    scaled = grad_rows * gain_vector
    mean_term = jnp.mean(scaled * unit_rows, axis=-1, keepdims=True)
    return (scale_rows * (scaled - unit_rows * mean_term), jnp.sum(grad_rows * unit_rows, axis=0))


def adamw(master, moment, square, grad_rows, rate_value, decay_value):
    first_new = beta_first * moment + (1.0 - beta_first) * grad_rows
    second_new = beta_second * square + (1.0 - beta_second) * grad_rows * grad_rows
    fix_first = 1.0 - beta_first**STEP
    fix_second = 1.0 - beta_second**STEP
    weight = master - rate_value * (
        first_new / fix_first / (jnp.sqrt(second_new / fix_second) + adam_eps)
        + decay_value * master
    )
    return (grad_rows, first_new, second_new, weight, weight.astype(jnp.bfloat16))


def shift(values, axis, steps):
    size = lax.axis_size(axis)
    return lax.ppermute(values, axis, [(i, (i + steps) % size) for i in range(size)])


def swap(values, axis, bit):
    size = lax.axis_size(axis)
    return lax.ppermute(values, axis, [(i, i ^ bit) for i in range(size)])


def dot_nn(left, right):
    return jnp.dot(left, right, preferred_element_type=jnp.float32)


def dot_nt(left, right):
    return lax.dot_general(left, right, (((1,), (1,)), ((), ())), preferred_element_type=jnp.float32)


def dot_tn(left, right):
    return lax.dot_general(left, right, (((0,), (0,)), ((), ())), preferred_element_type=jnp.float32)


def low(values):
    return values.astype(jnp.bfloat16)


def wide(values):
    return values.astype(jnp.float32)


def halve(values, which):
    size = values.shape[0] // 2
    mine = lax.dynamic_slice_in_dim(values, which * size, size, 0)
    other = lax.dynamic_slice_in_dim(values, (1 - which) * size, size, 0)
    return mine, other


def head_scatter(values):
    index = lax.axis_index("head")
    mine, other = halve(values, index % 2)
    values = mine + wide(swap(low(other), "head", 1))
    mine, other = halve(values, index // 2)
    return mine + wide(swap(low(other), "head", 2))


def head_gather(values, dim=0):
    index = lax.axis_index("head")
    for bit, which in ((2, index // 2), (1, index % 2)):
        got = swap(values, "head", bit)
        values = jnp.where(
            which == 0,
            jnp.concatenate([values, got], dim),
            jnp.concatenate([got, values], dim),
        )
    return values


def seq_sum(blocks):
    total = blocks[0]
    for s in range(1, len(blocks)):
        total = total + wide(shift(low(blocks[s]), "seq", -s))
    return total


def place(blocks):
    size = lax.axis_size("seq")
    dp_index, seq_index = lax.axis_index("dp"), lax.axis_index("seq")
    first = next(iter(blocks.values()))
    out = jnp.zeros((2 * size,) + first.shape, first.dtype)
    for (a, k), block in blocks.items():
        owner = lax.rem(dp_index + a, 2) * size + lax.rem(seq_index + size - k, size)
        out = lax.dynamic_update_slice(out, block[None], (owner,) + (0,) * first.ndim)
    return out


def weight_gather(block):
    size = lax.axis_size("seq")
    blocks = {}
    for k in range(size):
        if k > 0:
            block = shift(block, "seq", 1)
        blocks[0, k] = block
        blocks[1, k] = swap(block, "dp", 1)
    out = place(blocks)
    return out.reshape((-1,) + out.shape[2:])


def weight_exchange(packs):
    size = lax.axis_size("seq")
    seq_index = lax.axis_index("seq")
    blocks = {}
    for k in range(size):
        block = lax.dynamic_index_in_dim(packs, lax.rem(seq_index + k, size), 0, False)
        if k > 0:
            block = shift(block, "seq", k)
        blocks[0, k] = block
        blocks[1, k] = swap(block, "dp", 1)
    out = place(blocks)
    return out.reshape((-1,) + out.shape[2:])


def grad_exchange(parts, scatter):
    size = lax.axis_size("seq")
    dp_index, seq_index = lax.axis_index("dp"), lax.axis_index("seq")
    parts = parts.reshape(2, size, -1, parts.shape[1])
    total = jnp.zeros(parts.shape[2:], jnp.float32)
    out = jnp.zeros(parts.shape[1:], jnp.bfloat16)
    for k in range(size - 1, -1, -1):
        target = lax.rem(seq_index + k, size)
        pair = lax.dynamic_index_in_dim(parts, target, 1, False)
        mine = lax.dynamic_index_in_dim(pair, dp_index, 0, False)
        other = lax.dynamic_index_in_dim(pair, 1 - dp_index, 0, False)
        block = wide(mine) + wide(swap(low(other), "dp", 1))
        if k > 0:
            block = wide(shift(low(block), "seq", k))
        if scatter:
            total = total + block
        else:
            source = lax.rem(seq_index + size - k, size)
            out = lax.dynamic_update_slice(out, low(block)[None], (source, 0, 0))
    return total if scatter else out


def hidden_before(lengths_ref, half, block, block_rows):
    first_place = last_block(half) * block_rows
    end, start = jnp.int32(0), jnp.int32(0)
    for i in range(lengths_ref.shape[1]):
        end = end + lengths_ref[0, i]
        start = start + jnp.where(end <= first_place, lengths_ref[0, i], 0)
    return jnp.where(block * block_rows >= start, 0.0, masked_low)


def last_block(half):
    index = lax.axis_index("seq")
    return index if half == 0 else 2 * lax.axis_size("seq") - 1 - index


def key_offset(block, size, block_rows):
    owner = jnp.where(block < size, block, 2 * size - 1 - block)
    return owner * (2 * block_rows) + jnp.where(block < size, 0, block_rows)


def seen_bias(block_rows, heads):
    row = lax.broadcasted_iota(jnp.int32, (block_rows, block_rows), 0)
    col = lax.broadcasted_iota(jnp.int32, (block_rows, block_rows), 1)
    return jnp.concatenate([jnp.where(col <= row, 0.0, masked_low)] * heads, axis=0)


def stacked_heads(ref, half):
    block_rows, heads = ref.shape[0] // 2, ref.shape[1] // HD
    rows = pl.ds(half * block_rows, block_rows)
    return jnp.concatenate([ref[rows, i * HD : (i + 1) * HD] for i in range(heads)], axis=0)


def attention_forward(lengths_ref, q_ref, k_ref, v_ref, o_ref, lse_ref, halves=(0, 1)):
    local_rows, heads = q_ref.shape[0], q_ref.shape[1] // HD
    block_rows = local_rows // 2
    size = lax.axis_size("seq")
    scale = 1.0 / math.sqrt(HD)
    stacked = heads * block_rows
    for half in halves:
        last = last_block(half)
        rows = pl.ds(half * block_rows, block_rows)
        q = stacked_heads(q_ref, half)

        def step(block, carried, diagonal, q=q, half=half):
            running_max, running_sum, running_out = carried
            keys = pl.ds(pl.multiple_of(key_offset(block, size, block_rows), block_rows), block_rows)
            scores = dot_nt(q, k_ref[keys, :]) * scale
            if diagonal:
                scores = scores + seen_bias(block_rows, heads)
            else:
                scores = scores + hidden_before(lengths_ref, half, block, block_rows)
            new_max = jnp.maximum(running_max, jnp.max(scores, axis=-1, keepdims=True))
            probs = jnp.exp(scores - new_max)
            fade = jnp.exp(running_max - new_max)
            running_sum = running_sum * fade + jnp.sum(probs, axis=-1, keepdims=True)
            running_out = running_out * fade + dot_nn(low(probs), v_ref[keys, :])
            return new_max, running_sum, running_out

        carried = (
            jnp.full((stacked, 1), masked_low, jnp.float32),
            jnp.zeros((stacked, 1), jnp.float32),
            jnp.zeros((stacked, HD), jnp.float32),
        )
        carried = lax.fori_loop(0, last, functools.partial(step, diagonal=False), carried)
        running_max, running_sum, running_out = step(last, carried, True)
        out = running_out / running_sum
        lse = running_max + jnp.log(running_sum)
        for i in range(heads):
            part = slice(i * block_rows, (i + 1) * block_rows)
            o_ref[rows, i * HD : (i + 1) * HD] = out[part]
            lse_ref[rows, i : i + 1] = lse[part]


def attention_backward(
    lengths_ref, q_ref, k_ref, v_ref, do_ref, o_ref, lse_ref, dq_ref, dk_ref, dv_ref, halves=(0, 1)
):
    local_rows, heads = q_ref.shape[0], q_ref.shape[1] // HD
    block_rows = local_rows // 2
    size = lax.axis_size("seq")
    scale = 1.0 / math.sqrt(HD)
    stacked = heads * block_rows
    for half in halves:
        if half == 0:
            dk_ref[...] = jnp.zeros_like(dk_ref)
            dv_ref[...] = jnp.zeros_like(dv_ref)
        last = last_block(half)
        rows = pl.ds(half * block_rows, block_rows)
        q, do = stacked_heads(q_ref, half), stacked_heads(do_ref, half)
        delta = jnp.sum(wide(do) * stacked_heads(o_ref, half), axis=-1, keepdims=True)
        lse = jnp.concatenate([lse_ref[rows, i : i + 1] for i in range(heads)], axis=0)

        def step(block, dq, diagonal, q=q, do=do, delta=delta, lse=lse, half=half):
            keys = pl.ds(pl.multiple_of(key_offset(block, size, block_rows), block_rows), block_rows)
            k, v = k_ref[keys, :], v_ref[keys, :]
            scores = dot_nt(q, k) * scale
            if diagonal:
                scores = scores + seen_bias(block_rows, heads)
            else:
                scores = scores + hidden_before(lengths_ref, half, block, block_rows)
            probs = jnp.exp(scores - lse)
            score_grad = low(probs * (dot_nt(do, v) - delta))
            dk_ref[keys, :] += dot_tn(score_grad, q) * scale
            dv_ref[keys, :] += dot_tn(low(probs), do)
            return dq + dot_nn(score_grad, k)

        dq = jnp.zeros((stacked, HD), jnp.float32)
        dq = lax.fori_loop(0, last, functools.partial(step, diagonal=False), dq)
        dq = step(last, dq, True) * scale
        for i in range(heads):
            dq_ref[rows, i * HD : (i + 1) * HD] = dq[i * block_rows : (i + 1) * block_rows]


def in_vmem(kernel, outs, scalars, *arrays):
    return pl.pallas_call(
        kernel,
        out_shape=outs,
        in_specs=[pl.BlockSpec(memory_space=pltpu.SMEM)]
        + [pl.BlockSpec(memory_space=pltpu.VMEM)] * len(arrays),
        out_specs=[pl.BlockSpec(memory_space=pltpu.VMEM)] * len(outs),
        compiler_params=pltpu.CompilerParams(vmem_limit_bytes=40 * 1024 * 1024),
        cost_estimate=pl.CostEstimate(
            flops=12 * 10**9, bytes_accessed=8 * 10**6, transcendentals=10**7
        ),
    )(scalars, *arrays)


class Links:
    def __init__(self, send_sems, recv_sems):
        self.send_sems, self.recv_sems, self.started = send_sems, recv_sems, []

    def to(self, source, target, **where):
        number = len(self.started)
        copy = pltpu.make_async_remote_copy(
            src_ref=source,
            dst_ref=target,
            send_sem=self.send_sems.at[number],
            recv_sem=self.recv_sems.at[number],
            device_id=where,
            device_id_type=pl.DeviceIdType.MESH,
        )
        copy.start()
        self.started.append(copy)
        return copy

    def finish(self):
        for copy in self.started:
            copy.wait_send()


def greet(partners):
    barrier = pltpu.get_barrier_semaphore()
    for where in partners:
        pl.semaphore_signal(
            barrier, inc=1, device_id=where, device_id_type=pl.DeviceIdType.MESH
        )
    pl.semaphore_wait(barrier, len(partners))


def at_rows(ref, block, size):
    return ref.at[pl.ds(pl.multiple_of(block * size, size), size), :]


def rows_of(begin, size):
    return pl.ds(pl.multiple_of(begin, size), size)


def turn(values, cosine, sine_term):
    return values * cosine + pltpu.roll(values, HD // 2, 1) * sine_term


def vector_of(scal_ref, begin, size):
    per = scal_ref.shape[2] // 128
    tiles = []
    for i in range(size // 128):
        tile = begin // 128 + i
        if isinstance(tile, int):
            owner, column = tile // per, tile % per * 128
        else:
            owner, column = lax.div(tile, per), pl.multiple_of(lax.rem(tile, per) * 128, 128)
        tiles.append(scal_ref[owner, 0:1, pl.ds(column, 128)])
    return jnp.concatenate(tiles, axis=1)


def cut_units(expand_v, shrink_v, packs):
    size, main, columns = packs.shape[0], 512, expand_v.shape[2]
    left = lax.broadcasted_iota(jnp.int32, (16, 128), 1) < 64

    def rows16(i, unused):
        part = rows_of(i * 16, 16)

        def rests(values):
            begin = size * main
            first = values[:, begin : begin + 128]
            last = jnp.concatenate([values[:, begin + 128 :], jnp.zeros((16, 64), jnp.float32)], axis=1)
            return first, pltpu.roll(first, 64, 1), last

        gate, up, down = expand_v[part, 0, :], expand_v[part, 1, :], shrink_v[part, :]
        for j in range(size):
            own = slice(j * main, (j + 1) * main)
            packs[j, part, :main] = low(gate[:, own])
            packs[j, part, main : 2 * main] = low(up[:, own])
            packs[j, part, 2 * main + 128 : 3 * main + 128] = low(down[:, own])
        pieces = zip(rests(gate), rests(up), rests(down))
        for j, (gate_rest, up_rest, down_rest) in enumerate(pieces):
            both = jnp.where(left, gate_rest, pltpu.roll(up_rest, 64, 1))
            packs[j, part, 2 * main : 2 * main + 128] = low(both)
            packs[j, part, 3 * main + 128 :] = low(jnp.where(left, down_rest, 0.0))
        packs[size - 1, part, 2 * main : 2 * main + 128] = jnp.zeros((16, 128), jnp.bfloat16)
        packs[size - 1, part, 3 * main + 128 :] = jnp.zeros((16, 128), jnp.bfloat16)
        return unused

    lax.fori_loop(0, packs.shape[1] // 16, rows16, 0)


def front_kernel(
    lengths_ref, scal_own, query_ref, kv_ref, mixing_ref, expand_ref, shrink_ref, x_ref, cot_ref, cos_half, sin_half,
    scal_ref, attn_out, mix_out, ff_w, cot_all, normed_out, q_out, k_out, v_out, att_out, lse_out, hid_out, nt_all,
    cos_out, sin_out, scal_in, cos_ref, sin_ref, attn_w, mix_w, normed_ref, q_ref, k_all, v_all, att_ref, lse_ref, hid_ref, expand_v, shrink_v, ff_packs, nt_ref, send_c, recv_c, send_x, recv_x, kept, send_sems, recv_sems, local_sem, store_sems,
):
    rows, width = x_ref.shape
    quarter, half = rows // 4, rows // 2
    block_rows = query_ref.shape[0]
    size = lax.axis_size("seq")
    y, z, head = lax.axis_index("dp"), lax.axis_index("seq"), lax.axis_index("head")
    core, xx = lax.rem(head, 2), lax.div(head, 2)
    heads = q_ref.shape[1] // HD
    wide_heads = heads * HD
    row_begin = core * half + xx * quarter
    me = y * size + z
    owners = [z, z + 1 - 2 * lax.rem(z, 2), lax.rem(z + 2, 4), 3 - z]
    to_y, to_x, to_core = {"dp": 1 - y}, {"head": head + 2 - 4 * xx}, {"head": head + 1 - 2 * core}
    greet([{"seq": owners[d]} for d in (1, 2, 3)] + [to_y, to_x, to_core])
    links = Links(send_sems, recv_sems)
    stores = []

    def store(source, target):
        copy = pltpu.make_async_copy(source, target, store_sems.at[len(stores)])
        copy.start()
        stores.append(copy)


    scal_in[...] = jnp.broadcast_to(wide(low(scal_own[...])), scal_in.shape)
    scal_ref[me] = scal_in[...]
    load_expand = pltpu.make_async_copy(expand_ref, expand_v, local_sem.at[1])
    load_expand.start()
    load_shrink = pltpu.make_async_copy(shrink_ref, shrink_v, local_sem.at[2])
    load_shrink.start()
    kv_head = lax.div(head * heads, H // KV)
    own_rows = rows_of(me * block_rows, block_rows)
    attn_w[own_rows, :wide_heads] = low(query_ref[...])
    kv_columns = pl.ds(pl.multiple_of((core * KV + kv_head) * HD, HD), HD)
    attn_w[own_rows, wide_heads:] = low(kv_ref[:, kv_columns])
    mix_w[own_rows, :] = low(mixing_ref[...])
    scal_z = {d: links.to(scal_in, scal_ref.at[me], seq=owners[d]) for d in (1, 2, 3)}
    scal_y = [links.to(scal_in, scal_ref.at[me], **to_y)]
    attn_own = at_rows(attn_w, me, block_rows)
    attn_z = {d: links.to(attn_own, attn_own, seq=owners[d]) for d in (1, 2)}
    attn_y = [links.to(attn_own, attn_own, **to_y)]
    mix_own = at_rows(mix_w, me, block_rows)
    mix_z = {d: links.to(mix_own, mix_own, seq=owners[d]) for d in (1, 2)}
    mix_y = []
    for d in (1, 2, 3):
        scal_z[d].wait_recv()
        owner = y * size + owners[d]
        scal_y.append(links.to(scal_ref.at[owner], scal_ref.at[owner], **to_y))
    for copy in scal_y:
        copy.wait_recv()
    gain_one = vector_of(scal_ref, 0, width)

    def norm_rows(i, unused):
        part = rows_of(i * quarter, quarter)
        values = wide(x_ref[part, :])
        scale = lax.rsqrt(jnp.mean(values * values, axis=-1, keepdims=True) + norm_eps)
        normed_ref[part, :] = low(values * scale * gain_one)
        return unused

    lax.fori_loop(0, 4, norm_rows, 0)
    cos_ref[...] = jnp.concatenate([cos_half[...], cos_half[...]], axis=1)
    sin_ref[...] = jnp.concatenate([-sin_half[...], sin_half[...]], axis=1)
    store(cos_ref, cos_out)
    store(sin_ref, sin_out)

    def attn_arrival(d):
        attn_z[d].wait_recv()
        block = at_rows(attn_w, y * size + owners[d], block_rows)
        if d == 2:
            attn_z[3] = links.to(block, block, seq=owners[1])
        attn_y.append(links.to(block, block, **to_y))

    def mix_arrival(d):
        mix_z[d].wait_recv()
        block = at_rows(mix_w, y * size + owners[d], block_rows)
        if d == 2:
            mix_z[3] = links.to(block, block, seq=owners[1])
        mix_y.append(links.to(block, block, **to_y))

    load_expand.wait()
    load_shrink.wait()
    cut_units(expand_v, shrink_v, ff_packs)
    attn_arrival(2)
    attn_arrival(1)
    mix_arrival(2)
    mix_arrival(1)
    x_begin = core * half + (1 - xx) * quarter

    def quarter_of(ref, d, begin):
        return ref.at[rows_of(owners[d] * rows + begin, quarter), :]

    cot_own = cot_ref.at[rows_of(row_begin, quarter), :]
    cot_z = {d: links.to(cot_own, quarter_of(cot_all, 0, row_begin), seq=owners[d]) for d in (2, 1)}
    cot_x, cot_core = {}, []

    def cot_arrival(d):
        cot_z[d].wait_recv()
        block = quarter_of(cot_all, d, row_begin)
        if d == 2:
            cot_z[3] = links.to(block, block, seq=owners[1])
        cot_x[d] = links.to(block, block, **to_x)
        cot_core.append(links.to(block, block, **to_core))

    def cot_on(d):
        cot_x[d].wait_recv()
        block = quarter_of(cot_all, d, x_begin)
        cot_core.append(links.to(block, block, **to_core))

    ff_own = at_rows(ff_w, me, block_rows)
    ff_copy = pltpu.make_async_copy(ff_packs.at[z], ff_own, local_sem.at[1])
    ff_copy.start()
    ff_z, ff_y = {}, []

    half_block = block_rows // 2

    def ff_start(d, part):
        rows_there = rows_of(me * block_rows + part * half_block, half_block)
        source = ff_packs.at[owners[d], pl.ds(part * half_block, half_block), :]
        ff_z[d, part] = links.to(source, ff_w.at[rows_there, :], seq=owners[d])

    def ff_arrival(d, part):
        ff_z[d, part].wait_recv()
        begin = (y * size + owners[d]) * block_rows + part * half_block
        block = ff_w.at[rows_of(begin, half_block), :]
        ff_y.append(links.to(block, block, **to_y))

    ff_start(2, 0)
    ff_start(2, 1)
    attn_arrival(3)
    mix_y.append(links.to(mix_own, mix_own, **to_y))
    mix_arrival(3)
    cot_arrival(2)
    cot_arrival(1)
    ff_y.append(links.to(ff_packs.at[z], ff_own, **to_y))
    for copy in attn_y:
        copy.wait_recv()

    base = 2 * width + H * HD
    bias_q = vector_of(scal_ref, 2 * width + head * wide_heads, wide_heads)
    bias_kv = vector_of(scal_ref, base + (core * KV + kv_head) * HD, HD)

    def project(i, unused):
        part = rows_of(i * half, half)
        normed = normed_ref[part, :]
        cosine, sine_term = cos_ref[part, :], sin_ref[part, :]
        pre = dot_nn(normed, attn_w[:, wide_heads:]) + bias_kv
        own = rows_of(z * rows + i * half, half)

        @pl.when(core == 0)
        def _():
            k_all[own, :] = low(turn(pre, cosine, sine_term))

        @pl.when(core == 1)
        def _():
            v_all[own, :] = low(pre)

        pre = dot_nn(normed, attn_w[:, :wide_heads]) + bias_q
        for n in range(heads):
            at = slice(n * HD, (n + 1) * HD)
            q_ref[part, at] = low(turn(pre[:, at], cosine, sine_term))
        return unused

    lax.fori_loop(0, 2, project, 0)
    def keys_or_values(owner, where):
        number = len(links.started)
        for which, ref in ((0, k_all), (1, v_all)):
            block = at_rows(ref, owner, rows)
            copy = pltpu.make_async_remote_copy(
                src_ref=block,
                dst_ref=block,
                send_sem=send_sems.at[number],
                recv_sem=recv_sems.at[number],
                device_id=where,
                device_id_type=pl.DeviceIdType.MESH,
            )
            pl.when(core == which)(copy.start)
        links.started.append(copy)
        return copy

    kv_z = {d: keys_or_values(z, {"seq": owners[d]}) for d in (3, 2, 1)}
    kv_core = [keys_or_values(z, to_core)]
    ff_start(1, 0)
    ff_start(1, 1)
    ff_start(3, 0)
    ff_start(3, 1)
    for d in (1, 2, 3):
        kv_z[d].wait_recv()
        kv_core.append(keys_or_values(owners[d], to_core))
    for copy in kv_core:
        copy.wait_recv()
    store(attn_w, attn_out)
    store(normed_ref, normed_out)
    store(q_ref, q_out)
    store(k_all, k_out)
    store(v_all, v_out)
    attention_forward(lengths_ref, q_ref, k_all, v_all, att_ref, lse_ref)
    store(att_ref, att_out)
    store(lse_ref, lse_out)
    ff_arrival(2, 0)
    ff_arrival(2, 1)
    cot_on(2)
    cot_on(1)

    for copy in mix_y:
        copy.wait_recv()
    store(mix_w, mix_out)

    def branch_part(begin, size_rows):
        return dot_nt(low(att_ref[rows_of(begin, size_rows), :]), mix_w[...])

    def branch_send(i, unused):
        part = rows_of(i * quarter, quarter)
        send_c[part, :] = low(branch_part((1 - core) * half + i * quarter, quarter))
        return unused

    lax.fori_loop(0, 2, branch_send, 0)
    to_c = links.to(send_c, recv_c, **to_core)

    def branch_keep(i, unused):
        part = rows_of(i * quarter, quarter)
        kept[part, :] = branch_part(core * half + i * quarter, quarter)
        return unused

    lax.fori_loop(0, 2, branch_keep, 0)
    to_c.wait_recv()
    other, mine = rows_of((1 - xx) * quarter, quarter), rows_of(xx * quarter, quarter)
    send_x[...] = low(kept[other, :] + wide(recv_c[other, :]))
    to_xx = links.to(send_x, recv_x, **to_x)
    cot_arrival(3)
    to_xx.wait_recv()
    gain_two = vector_of(scal_ref, width, width)
    hidden = wide(x_ref[rows_of(row_begin, quarter), :]) + (
        kept[mine, :] + wide(recv_c[mine, :]) + wide(recv_x[...])
    )
    hid_ref[...] = hidden
    store(hid_ref, hid_out)
    scale = lax.rsqrt(jnp.mean(hidden * hidden, axis=-1, keepdims=True) + norm_eps)
    nt_ref[...] = low(hidden * scale * gain_two)
    own = quarter_of(nt_all, 0, row_begin)
    own_copy = pltpu.make_async_copy(nt_ref, own, local_sem.at[0])
    own_copy.start()
    nt_z = {d: links.to(nt_ref, own, seq=owners[d]) for d in (2, 1)}
    nt_x = {0: links.to(nt_ref, own, **to_x)}
    nt_core = [links.to(nt_ref, own, **to_core)]

    def nt_arrival(d):
        nt_z[d].wait_recv()
        block = quarter_of(nt_all, d, row_begin)
        if d == 2:
            nt_z[3] = links.to(block, block, seq=owners[1])
        nt_x[d] = links.to(block, block, **to_x)
        nt_core.append(links.to(block, block, **to_core))

    def nt_on(d):
        nt_x[d].wait_recv()
        block = quarter_of(nt_all, d, x_begin)
        nt_core.append(links.to(block, block, **to_core))

    ff_arrival(1, 0)
    ff_arrival(1, 1)
    nt_arrival(2)
    nt_arrival(1)
    nt_on(0)
    cot_on(3)
    nt_arrival(3)
    ff_arrival(3, 0)
    ff_arrival(3, 1)
    for d in (2, 1, 3):
        nt_on(d)
    for copy in cot_core + ff_y + nt_core:
        copy.wait_recv()
    links.finish()
    own_copy.wait()
    ff_copy.wait()
    for copy in stores:
        copy.wait()


def front(
    lengths, scal_own, query, keyvalue, mixing_t, expand, shrink_t, x_rows, cot_rows, cosine, sine_term, columns
):
    rows, width = x_rows.shape
    size = lax.axis_size("seq")
    quarter, half, count = rows // 4, rows // 2, 2 * size
    block_rows, wide_heads = query.shape
    bf16, f32 = jnp.bfloat16, jnp.float32
    shape = jax.ShapeDtypeStruct
    in_vmem_spec, anywhere = pl.BlockSpec(memory_space=pltpu.VMEM), pl.BlockSpec(memory_space=pl.ANY)
    staged = [
        shape((count * block_rows, wide_heads + HD), bf16),
        shape((count * block_rows, wide_heads), bf16),
        shape((rows, width), bf16),
        shape((rows, wide_heads), bf16),
        shape((size * rows, HD), bf16),
        shape((size * rows, HD), bf16),
        shape((rows, wide_heads), f32),
        shape((rows, wide_heads // HD), f32),
        shape((quarter, width), f32),
    ]
    table = shape((rows, HD), f32)
    outs = [(shape((count, 8, scal_own.shape[1]), f32), in_vmem_spec)]
    outs += [(one, anywhere) for one in staged[:2]]
    outs += [
        (shape((count * block_rows, columns), bf16), anywhere),
        (shape((size * rows, width), bf16), anywhere),
    ]
    outs += [(one, anywhere) for one in staged[2:]]
    outs.append((shape((size * rows, width), bf16), anywhere))
    outs += [(table, anywhere)] * 2
    return pl.pallas_call(
        front_kernel,
        out_shape=[o[0] for o in outs],
        in_specs=[pl.BlockSpec(memory_space=pltpu.SMEM)]
        + [in_vmem_spec] * 4
        + [anywhere] * 2
        + [in_vmem_spec, anywhere, in_vmem_spec, in_vmem_spec],
        out_specs=[o[1] for o in outs],
        scratch_shapes=[
            pltpu.VMEM((8, scal_own.shape[1]), f32),
            pltpu.VMEM(table.shape, f32),
            pltpu.VMEM(table.shape, f32),
        ]
        + [pltpu.VMEM(one.shape, one.dtype) for one in staged]
        + [
            pltpu.VMEM(expand.shape, f32),
            pltpu.VMEM(shrink_t.shape, f32),
            pltpu.VMEM((size, block_rows, columns), bf16),
            pltpu.VMEM((quarter, width), bf16),
            pltpu.VMEM((half, width), bf16),
            pltpu.VMEM((half, width), bf16),
            pltpu.VMEM((quarter, width), bf16),
            pltpu.VMEM((quarter, width), bf16),
            pltpu.VMEM((half, width), f32),
            pltpu.SemaphoreType.DMA((72,)),
            pltpu.SemaphoreType.DMA((72,)),
            pltpu.SemaphoreType.DMA((3,)),
            pltpu.SemaphoreType.DMA((11,)),
        ],
        compiler_params=pltpu.CompilerParams(
            collective_id=1, has_side_effects=True, vmem_limit_bytes=62 * 1024 * 1024
        ),
        cost_estimate=pl.CostEstimate(
            flops=6 * 10**9, bytes_accessed=30 * 10**6, transcendentals=10**7
        ),
    )(lengths, scal_own, query, keyvalue, mixing_t, expand, shrink_t, x_rows, cot_rows, cosine, sine_term)


def gated(gate_value, up_value, act_grad):
    gate_sigmoid = jax.nn.sigmoid(gate_value)
    silu = gate_value * gate_sigmoid
    gate_grad = act_grad * up_value * gate_sigmoid * (1.0 + gate_value * (1.0 - gate_sigmoid))
    return silu * up_value, gate_grad, act_grad * silu


def ff_kernel(
    nt_ref, ff_w, cot_all, cot_ref, hid_ref, scal_ref,
    hg_ref, bg_ref, gain_ref, gw_ref, out_ref, early_ref,
    nt_all, cot_v, w_v, both_v, act_v, send_c, recv_c, kept, send_x, recv_x, send_z, recv_z, total, grad_v, out_v,
    send_sems, recv_sems, local_sems,
):
    quarter, width = hid_ref.shape
    half, rows = 2 * quarter, 4 * quarter
    y, z, head = lax.axis_index("dp"), lax.axis_index("seq"), lax.axis_index("head")
    core, xx = lax.rem(head, 2), lax.div(head, 2)
    row_begin = core * half + xx * quarter
    x_begin = core * half + (1 - xx) * quarter
    wide_units = both_v.shape[1]
    main = wide_units // 256 * 128
    owners = [z, z + 1 - 2 * lax.rem(z, 2), lax.rem(z + 2, 4), 3 - z]
    to_x, to_core = {"head": head + 2 - 4 * xx}, {"head": head + 1 - 2 * core}
    size = 4
    block_rows = ff_w.shape[0] // (2 * size)
    loads = []

    def load(source, target):
        copy = pltpu.make_async_copy(source, target, local_sems.at[4 + len(loads)])
        copy.start()
        loads.append(copy)

    load(ff_w, w_v)
    for d in (3, 2, 1, 0):
        if d > 0:
            load(at_rows(cot_all, owners[d], rows), at_rows(cot_v, owners[d], rows))
        else:
            load(cot_ref, at_rows(cot_v, z, rows))
        load(at_rows(nt_ref, owners[d], rows), at_rows(nt_all, owners[d], rows))
    to_y = {"dp": 1 - y}
    greet([{"seq": owners[d]} for d in (1, 2, 3)] + [to_y, to_x, to_core])
    links = Links(send_sems, recv_sems)

    loads[0].wait()

    def act_grad_rows(begin):
        part = rows_of(begin, half)
        act_v[part, :] = low(dot_nn(cot_v[part, :], w_v[:, wide_units:]))

    def gates(begin):
        part = rows_of(begin, half)
        values = dot_nn(nt_all[part, :], w_v[:, :wide_units])
        act_grad = wide(act_v[part, :])
        act, gate_grad, up_grad = gated(
            values[:, :main], values[:, main : 2 * main], act_grad[:, :main]
        )
        act_v[part, :main] = low(act)
        both_v[part, :main] = low(gate_grad)
        both_v[part, main : 2 * main] = low(up_grad)
        last = values[:, 2 * main :]
        act, gate_grad, up_grad = gated(last, pltpu.roll(last, 64, 1), act_grad[:, main:])
        left = lax.broadcasted_iota(jnp.int32, last.shape, 1) < 64
        act_v[part, main:] = low(jnp.where(left, act, 0.0))
        both_v[part, 2 * main :] = low(jnp.where(left, gate_grad, pltpu.roll(up_grad, 64, 1)))

    def back_part(begin):
        return low(dot_nt(both_v[rows_of(begin, half), :], w_v[:, :wide_units]))

    mine, other = rows_of(xx * quarter, quarter), rows_of((1 - xx) * quarter, quarter)
    steps_c, steps_x, steps_z = {}, {}, {}
    sequence = (3, 2, 1, 0)

    def start_step(s):
        steps_c[s].wait_recv()
        send_x[s] = low(wide(kept[s % 2, other, :]) + wide(recv_c[s, other, :]))
        steps_x[s] = links.to(send_x.at[s], recv_x.at[s], **to_x)

    def finish_step(s):
        steps_x[s].wait_recv()
        value = wide(kept[s % 2, mine, :]) + wide(recv_c[s, mine, :]) + wide(recv_x[s])
        if s == 0:
            total[...] = value
        else:
            send_z[s - 1] = low(value)
            steps_z[s] = links.to(send_z.at[s - 1], recv_z.at[s - 1], seq=owners[s])

    for s in sequence:
        base = owners[s] * rows
        loads[7 - 2 * s].wait()
        loads[8 - 2 * s].wait()
        act_grad_rows(base + (1 - core) * half)
        gates(base + (1 - core) * half)
        if s < 2:
            steps_c[s + 2].wait_send()
        send_c[s % 2] = back_part(base + (1 - core) * half)
        steps_c[s] = links.to(send_c.at[s % 2], recv_c.at[s], **to_core)
        act_grad_rows(base + core * half)
        gates(base + core * half)
        kept[s % 2] = back_part(base + core * half)
        start_step(s)
        if s < 3:
            finish_step(s + 1)

    count = both_v.shape[0] // rows
    pair_rows = grad_v.shape[1]

    def weight_grads(first, stores):
        for i in range(2):
            begin = pl.multiple_of((first * 2 + i) * pair_rows, 128)
            if len(stores) >= 2:
                stores[-2].wait()
            slot = grad_v.at[i]
            columns = pl.ds(begin, pair_rows)
            slot[:, :wide_units] = low(dot_tn(nt_all[:, columns], both_v[...]))
            slot[:, wide_units:] = low(dot_tn(cot_v[:, columns], act_v[...]))
            store = pltpu.make_async_copy(
                slot, gw_ref.at[pl.ds(begin, pair_rows), :], local_sems.at[i]
            )
            store.start()
            stores.append(store)

    stores = []
    weight_grads(1 - y, stores)
    finish_step(0)
    for store in stores:
        store.wait()
    stores = []
    source = at_rows(gw_ref, (1 - y) * size + owners[3], block_rows)
    early = links.to(source, early_ref, **to_y)
    n2 = total[...]
    for s in range(1, 4):
        steps_z[s].wait_recv()
        n2 = n2 + wide(recv_z[s - 1])
    hidden = hid_ref[...]
    gain_two = vector_of(scal_ref, width, width)
    scale = lax.rsqrt(jnp.mean(hidden * hidden, axis=-1, keepdims=True) + norm_eps)
    back, gain_grad = norm_back(n2, hidden, scale, gain_two)
    gain_ref[...] = gain_grad[None]
    hidden_grad = wide(cot_v[rows_of(z * rows + row_begin, quarter), :]) + back
    hg_ref[...] = hidden_grad
    own = bg_ref.at[rows_of(row_begin, quarter), :]
    own[...] = low(hidden_grad)
    bg_x = links.to(own, own, **to_x)
    bg_core = [links.to(own, own, **to_core)]
    weight_grads(y, stores)
    out_stores = []
    for i in range(2 * count):
        part = pl.ds(i * half, half)
        if i >= 2:
            out_stores[i - 2].wait()
        out_v[i % 2] = low(dot_nt(act_v[part, :], w_v[:, wide_units:]))
        store = pltpu.make_async_copy(out_v.at[i % 2], out_ref.at[part, :], local_sems.at[2 + i % 2])
        store.start()
        out_stores.append(store)
        if i == 1:
            bg_x.wait_recv()
            block = bg_ref.at[rows_of(x_begin, quarter), :]
            bg_core.append(links.to(block, block, **to_core))
    for copy in bg_core + [early]:
        copy.wait_recv()
    for store in stores[-2:] + out_stores[-2:]:
        store.wait()
    for copy in links.started:
        if copy is not steps_c[2] and copy is not steps_c[3]:
            copy.wait_send()


def feed_forward(nt, ff_w, cot_all, cot, hidden, scal, units):
    quarter, width = hidden.shape
    rows, stream, columns = 4 * quarter, cot_all.shape[0], ff_w.shape[1]
    bf16, f32 = jnp.bfloat16, jnp.float32
    shape = jax.ShapeDtypeStruct
    in_vmem_spec, anywhere = pl.BlockSpec(memory_space=pltpu.VMEM), pl.BlockSpec(memory_space=pl.ANY)
    outs = [
        (shape((quarter, width), f32), in_vmem_spec),
        (shape((rows, width), bf16), in_vmem_spec),
        (shape((1, width), f32), in_vmem_spec),
        (shape((width, columns), bf16), anywhere),
        (shape((stream, width), bf16), anywhere),
        (shape((width // 8, columns), bf16), anywhere),
    ]
    return pl.pallas_call(
        ff_kernel,
        out_shape=[o[0] for o in outs],
        in_specs=[anywhere] * 4 + [in_vmem_spec] * 2,
        out_specs=[o[1] for o in outs],
        scratch_shapes=[
            pltpu.VMEM((stream, width), bf16),
            pltpu.VMEM((stream, width), bf16),
            pltpu.VMEM((width, columns), bf16),
            pltpu.VMEM((stream, 2 * units), bf16),
            pltpu.VMEM((stream, columns - 2 * units), bf16),
            pltpu.VMEM((2, 2 * quarter, width), bf16),
            pltpu.VMEM((4, 2 * quarter, width), bf16),
            pltpu.VMEM((2, 2 * quarter, width), bf16),
            pltpu.VMEM((4, quarter, width), bf16),
            pltpu.VMEM((4, quarter, width), bf16),
            pltpu.VMEM((3, quarter, width), bf16),
            pltpu.VMEM((3, quarter, width), bf16),
            pltpu.VMEM((quarter, width), f32),
            pltpu.VMEM((2, width // 4, columns), bf16),
            pltpu.VMEM((2, 2 * quarter, width), bf16),
            pltpu.SemaphoreType.DMA((40,)),
            pltpu.SemaphoreType.DMA((40,)),
            pltpu.SemaphoreType.DMA((28,)),
        ],
        compiler_params=pltpu.CompilerParams(
            collective_id=2, has_side_effects=True, vmem_limit_bytes=62 * 1024 * 1024
        ),
        cost_estimate=pl.CostEstimate(
            flops=33 * 10**9, bytes_accessed=40 * 10**6, transcendentals=10**6
        ),
    )(nt, ff_w, cot_all, cot, hidden, scal)


def back_kernel(
    lengths_ref, scal_ref, x_ref, gain_two_ref, gw_ref, part_ref, early_ref,
    bg_in, mix_in, q_in, k_in, v_in, att_in, lse_in, cos_in, sin_in, attn_in, normed_in, hid_in, hg_in,
    layer_ref, input_ref, ff_grads, attn_ref, kv_ref, small_ref,
    bg_ref, mix_w, q_ref, k_all, v_all, att_ref, lse_ref, cos_ref, sin_ref, attn_w, normed_ref, hid_ref, hg_ref,
    ff_y, ff_own, out_c, out_own, out_sx, out_rx, out_sz, out_rz, dk, dv, do, dq, dkv_s, dkv_r, dkv_rz, dkv_own,
    qg, one_sc, one_rc, one_keep, one_sx, one_rx, layer_own, input_own, a_other, a_own, a_y, a_z, a_sz,
    x_own, small, small_y, small_s, small_z, small_h, kv_own,
    send_sems, recv_sems, local_sems, stage_sems,
):
    quarter, width = x_own.shape
    half, rows = 2 * quarter, 4 * quarter
    block_rows = attn_ref.shape[0]
    y, z, head = lax.axis_index("dp"), lax.axis_index("seq"), lax.axis_index("head")
    core, xx = lax.rem(head, 2), lax.div(head, 2)
    size = lax.axis_size("seq")
    heads = q_ref.shape[1] // HD
    wide_heads = heads * HD
    row_begin = core * half + xx * quarter
    x_begin = core * half + (1 - xx) * quarter
    owners = [z, z + 1 - 2 * lax.rem(z, 2), lax.rem(z + 2, 4), 3 - z]
    to_y, to_x, to_core = {"dp": 1 - y}, {"head": head + 2 - 4 * xx}, {"head": head + 1 - 2 * core}
    mine, other = rows_of(xx * quarter, quarter), rows_of((1 - xx) * quarter, quarter)
    is_core = wide(core)
    staged = {}
    for name, source, target in (
        ("bg", bg_in, bg_ref), ("mix", mix_in, mix_w), ("q", q_in, q_ref), ("k", k_in, k_all), ("v", v_in, v_all),
        ("att", att_in, att_ref), ("lse", lse_in, lse_ref), ("cos", cos_in, cos_ref), ("sin", sin_in, sin_ref),
        ("attn", attn_in, attn_w), ("normed", normed_in, normed_ref), ("hid", hid_in, hid_ref), ("hg", hg_in, hg_ref),
    ):
        staged[name] = pltpu.make_async_copy(source, target, stage_sems.at[len(staged)])
        staged[name].start()
    loads = []

    def load(source, target):
        copy = pltpu.make_async_copy(source, target, local_sems.at[len(loads)])
        copy.start()
        loads.append(copy)
        return copy

    greet([to_y] + [{"seq": owners[d]} for d in (1, 2, 3)] + [to_x, to_core])
    links = Links(send_sems, recv_sems)

    order = (3, 2, 1, 0)

    def grad_rows(ref, which, d):
        return at_rows(ref, which * size + owners[d], block_rows)

    ff_sent, ff_load = {}, {}

    def ff_start(d):
        ff_sent[d] = links.to(grad_rows(gw_ref, 1 - y, d), ff_y.at[d], **to_y)

    ff_start(2)
    ff_early = load(early_ref, ff_y.at[3])
    x_load = load(x_ref.at[rows_of(row_begin, quarter), :], x_own)
    out_sent, out_load = [], []
    for s in range(4):
        begin = owners[s] * rows
        source = part_ref.at[rows_of(begin + (1 - core) * half, half), :]
        out_sent.append(links.to(source, out_c.at[s], **to_core))
    for s in range(4):
        source = part_ref.at[rows_of(owners[s] * rows + core * half, half), :]
        out_load.append(load(source, out_own.at[s]))
    for d in order:
        ff_load[d] = load(grad_rows(gw_ref, y, d), ff_own.at[d])

    ff_over_z = []

    def ff_add(d):
        if d == 3:
            ff_early.wait()
        else:
            ff_sent[d].wait_recv()
        ff_load[d].wait()

        def add(i, unused):
            part = rows_of(i * 64, 64)
            ff_own[d, part, :] = low(wide(ff_own[d, part, :]) + wide(ff_y[d, part, :]))
            return unused

        lax.fori_loop(0, block_rows // 64, add, 0)

    def ff_half(d, i):
        part = pl.ds(i * (block_rows // 2), block_rows // 2)
        ff_over_z.append(
            links.to(ff_own.at[d, part, :], ff_grads.at[z, part, :], seq=owners[d])
        )

    def ff_step(d):
        ff_add(d)
        if d == 0:
            load(ff_own.at[d], ff_grads.at[z])
        else:
            ff_half(d, 0)
            ff_half(d, 1)

    out_x, out_z = {}, {}

    def out_step_c(s):
        out_sent[s].wait_recv()
        out_load[s].wait()
        out_sx[s] = low(wide(out_own[s, other, :]) + wide(out_c[s, other, :]))
        out_x[s] = links.to(out_sx.at[s], out_rx.at[s], **to_x)

    def out_value(s):
        out_x[s].wait_recv()
        return wide(out_own[s, mine, :]) + wide(out_c[s, mine, :]) + wide(out_rx[s])

    def out_step_x(s):
        value = out_value(s)
        if s == 2:
            out_z[3].wait_recv()
            value = value + wide(out_rz[2])
        out_sz[s - 1] = low(value)
        out_z[s] = links.to(out_sz.at[s - 1], out_rz.at[s - 1], seq=owners[2 if s == 2 else 1])

    def do_rows(i, unused):
        part = rows_of(i * half, half)
        do[part, :] = low(dot_nn(bg_ref[part, :], mix_w[...]))
        return unused

    ff_add(3)
    ff_half(3, 0)
    for name in ("bg", "mix"):
        staged[name].wait()
    lax.fori_loop(0, 2, do_rows, 0)
    for name in ("q", "k", "v", "att", "lse"):
        staged[name].wait()
    attention_backward(lengths_ref, q_ref, k_all, v_all, do, att_ref, lse_ref, dq, dk, dv, (0,))
    out_step_c(3)
    out_step_c(2)
    attention_backward(lengths_ref, q_ref, k_all, v_all, do, att_ref, lse_ref, dq, dk, dv, (1,))
    dkv_s[...] = low(dv[...] * (1.0 - is_core) + dk[...] * is_core)
    dkv_core = links.to(dkv_s, dkv_r, **to_core)
    for name in ("cos", "sin", "attn", "normed", "hid", "hg"):
        staged[name].wait()
    for n in range(heads):
        at = slice(n * HD, (n + 1) * HD)
        qg[:, at] = low(turn(dq[:, at], cos_ref[...], -sin_ref[...]))
    dkv_core.wait_recv()

    def dkv_block(d):
        part = rows_of(owners[d] * rows, rows)
        return dk[part, :] * (1.0 - is_core) + dv[part, :] * is_core + wide(dkv_r[part, :])

    dkv_z = []
    for d in (1, 2, 3):
        dkv_own[d] = low(dkv_block(d))
        dkv_z.append(links.to(dkv_own.at[d], dkv_rz.at[d - 1], seq=owners[d]))
    total = dkv_block(0)
    for d in (1, 2, 3):
        dkv_z[d - 1].wait_recv()
        total = total + wide(dkv_rz[d - 1])
    ff_half(3, 1)
    turned = turn(total, cos_ref[...], -sin_ref[...])
    dkv_own[0] = low(turned * (1.0 - is_core) + total * is_core)

    def one_part(begin):
        part = rows_of(begin, quarter)
        return dot_nt(qg[part, :], attn_w[:, :wide_heads]) + dot_nt(
            dkv_own[0, part, :], attn_w[:, wide_heads:]
        )

    def one_send(i, unused):
        one_sc[rows_of(i * quarter, quarter), :] = low(one_part((1 - core) * half + i * quarter))
        return unused

    def one_own(i, unused):
        one_keep[rows_of(i * quarter, quarter), :] = one_part(core * half + i * quarter)
        return unused

    lax.fori_loop(0, 2, one_send, 0)
    one_c = links.to(one_sc, one_rc, **to_core)
    lax.fori_loop(0, 2, one_own, 0)
    one_c.wait_recv()
    one_sx[...] = low(one_keep[other, :] + wide(one_rc[other, :]))
    one_x = links.to(one_sx, one_rx, **to_x)

    def attn_grads(which, target):
        columns = pl.ds(pl.multiple_of(which * (width // 2), 128), width // 2)
        normed = normed_ref[:, columns]
        target[:, :wide_heads] = low(dot_tn(normed, qg[...]))
        target[:, wide_heads : 2 * wide_heads] = low(
            dot_tn(bg_ref[:, columns], low(att_ref[...]))
        )
        target[:, 2 * wide_heads :] = low(dot_tn(normed, dkv_own[0]))

    attn_grads(1 - y, a_other)
    attn_sent = {
        d: links.to(at_rows(a_other, owners[d], block_rows), a_y.at[d], **to_y) for d in order
    }
    ff_step(2)
    out_step_c(1)
    out_step_c(0)
    attn_grads(y, a_own)
    out_step_x(3)

    one_x.wait_recv()
    norm_one_grad = one_keep[mine, :] + wide(one_rc[mine, :]) + wide(one_rx[...])
    x_load.wait()
    x_rows = wide(x_own[...])
    gain_one = vector_of(scal_ref, 0, width)
    scale = lax.rsqrt(jnp.mean(x_rows * x_rows, axis=-1, keepdims=True) + norm_eps)
    back, gain_grad = norm_back(norm_one_grad, x_rows, scale, gain_one)
    input_own[...] = low(hg_ref[...] + back)

    def gather(source, target):
        place = target.at[rows_of(row_begin, quarter), :]
        load(source, place)
        return links.to(source, place, **to_x), [links.to(source, place, **to_core)]

    def gather_on(sent, target):
        sent[0].wait_recv()
        block = target.at[rows_of(x_begin, quarter), :]
        sent[1].append(links.to(block, block, **to_core))

    input_sent = gather(input_own, input_ref)
    small[...] = jnp.zeros_like(small)
    per = small.shape[2] // 128

    def put(begin, values):
        for i in range(values.shape[1] // 128):
            tile = begin // 128 + i
            value = values[:, i * 128 : (i + 1) * 128]
            if isinstance(tile, int):
                small[tile // per, 0:1, tile % per * 128 : tile % per * 128 + 128] = value
            else:
                column = pl.ds(pl.multiple_of(lax.rem(tile, per) * 128, 128), 128)
                small[lax.div(tile, per), 0:1, column] = value

    put(0, gain_grad[None])
    put(width, gain_two_ref[...])
    put(2 * width + head * wide_heads, jnp.sum(wide(qg[...]), axis=0, keepdims=True))
    kv_begin = 2 * width + H * HD + (core * KV + lax.div(head * heads, H // KV)) * HD
    put(kv_begin, jnp.sum(wide(dkv_own[0]), axis=0, keepdims=True))
    small_sent = links.to(small.at[pl.ds((1 - y) * size, size)], small_y, **to_y)
    ff_start(1)
    ff_start(0)
    attn_over_z = {}

    def attn_step(d):
        attn_sent[d].wait_recv()
        block = wide(at_rows(a_own, owners[d], block_rows)[...]) + wide(a_y[d])
        if d == 0:
            return block
        if d == 2:
            attn_over_z[3].wait_recv()
            block = block + wide(a_z[2])
        a_sz[d - 1] = low(block)
        attn_over_z[d] = links.to(
            a_sz.at[d - 1], a_z.at[d - 1], seq=owners[2 if d == 2 else 1]
        )
        return None

    attn_step(3)
    out_step_x(1)
    out_step_x(2)
    gather_on(input_sent, input_ref)
    attn_step(1)
    attn_step(2)
    small_sent.wait_recv()
    small_s[...] = small[pl.ds(y * size, size)] + small_y[...]
    small_over_z = [
        links.to(small_s.at[owners[d]], small_z.at[d - 1], seq=owners[d]) for d in (1, 2, 3)
    ]
    layer = hid_ref[...] + out_value(0)
    for d in (1, 2):
        out_z[d].wait_recv()
        layer = layer + wide(out_rz[d - 1])
    layer_own[...] = low(layer)
    layer_sent = gather(layer_own, layer_ref)
    ff_step(1)
    block = attn_step(0)
    for d in (1, 2):
        attn_over_z[d].wait_recv()
        block = block + wide(a_z[d - 1])
    attn_ref[...] = block
    place = kv_ref.at[core * 2 + xx]
    kv_own[...] = low(block[:, 2 * wide_heads :])
    place[...] = kv_own[...]
    kv_x = links.to(kv_own, place, **to_x)
    kv_core = [links.to(kv_own, place, **to_core)]
    gather_on(layer_sent, layer_ref)
    value = small_s[z]
    for d in (1, 2, 3):
        small_over_z[d - 1].wait_recv()
        value = value + small_z[d - 1]
    small_h[0] = value
    small_x = links.to(small_h.at[0], small_h.at[1], **to_x)
    small_x.wait_recv()
    small_h[2] = small_h[0] + small_h[1]
    small_c = links.to(small_h.at[2], small_h.at[3], **to_core)
    small_c.wait_recv()
    small_ref[...] = small_h[2] + small_h[3]
    kv_x.wait_recv()
    place = kv_ref.at[core * 2 + 1 - xx]
    kv_core.append(links.to(place, place, **to_core))
    ff_step(0)
    for copy in kv_core + input_sent[1] + layer_sent[1] + ff_over_z:
        copy.wait_recv()
    links.finish()
    for copy in loads[10:]:
        copy.wait()


def back(
    lengths, scal, x_rows, hidden, hidden_grad, gain_two_grad, branch_grad, attn_w, mix_w, normed, q, k_all, v_all, attended, lse,
    cosine, sine_term, gw, out_part, early,
):
    quarter, width = hidden.shape
    half, rows = 2 * quarter, 4 * quarter
    size = lax.axis_size("seq")
    block_rows, columns = gw.shape[0] // (2 * size), gw.shape[1]
    wide_heads = q.shape[1]
    attn_columns = 2 * wide_heads + HD
    stream = k_all.shape[0]
    bf16, f32 = jnp.bfloat16, jnp.float32
    shape = jax.ShapeDtypeStruct
    in_vmem_spec, anywhere = pl.BlockSpec(memory_space=pltpu.VMEM), pl.BlockSpec(memory_space=pl.ANY)
    outs = [
        (shape((rows, width), bf16), anywhere),
        (shape((rows, width), bf16), anywhere),
        (shape((size, block_rows, columns), bf16), anywhere),
        (shape((block_rows, attn_columns), f32), in_vmem_spec),
        (shape((4, block_rows, HD), bf16), in_vmem_spec),
        (shape(scal.shape[1:], f32), in_vmem_spec),
    ]
    small = (size,) + scal.shape[1:]
    scratch = [
        ((rows, width), bf16),
        (mix_w.shape, bf16),
        (q.shape, bf16),
        (k_all.shape, bf16),
        (v_all.shape, bf16),
        (attended.shape, f32),
        (lse.shape, f32),
        (cosine.shape, f32),
        (sine_term.shape, f32),
        (attn_w.shape, bf16),
        (normed.shape, bf16),
        (hidden.shape, f32),
        (hidden.shape, f32),
        ((size, block_rows, columns), bf16),
        ((size, block_rows, columns), bf16),
        ((4, half, width), bf16),
        ((4, half, width), bf16),
        ((4, quarter, width), bf16),
        ((4, quarter, width), bf16),
        ((3, quarter, width), bf16),
        ((3, quarter, width), bf16),
        ((stream, HD), f32),
        ((stream, HD), f32),
        ((rows, wide_heads), bf16),
        ((rows, wide_heads), f32),
        ((stream, HD), bf16),
        ((stream, HD), bf16),
        ((3, rows, HD), bf16),
        ((4, rows, HD), bf16),
        ((rows, wide_heads), bf16),
        ((half, width), bf16),
        ((half, width), bf16),
        ((half, width), f32),
        ((quarter, width), bf16),
        ((quarter, width), bf16),
        ((quarter, width), bf16),
        ((quarter, width), bf16),
        ((width // 2, attn_columns), bf16),
        ((width // 2, attn_columns), bf16),
        ((4, block_rows, attn_columns), bf16),
        ((3, block_rows, attn_columns), bf16),
        ((3, block_rows, attn_columns), bf16),
        ((quarter, width), bf16),
        (scal.shape, f32),
        (small, f32),
        (small, f32),
        ((3,) + scal.shape[1:], f32),
        ((4,) + scal.shape[1:], f32),
        ((block_rows, HD), bf16),
    ]
    return pl.pallas_call(
        back_kernel,
        out_shape=[o[0] for o in outs],
        in_specs=[pl.BlockSpec(memory_space=pltpu.SMEM), in_vmem_spec, anywhere, in_vmem_spec]
        + [anywhere] * 16,
        out_specs=[o[1] for o in outs],
        scratch_shapes=[pltpu.VMEM(*one) for one in scratch]
        + [
            pltpu.SemaphoreType.DMA((56,)),
            pltpu.SemaphoreType.DMA((56,)),
            pltpu.SemaphoreType.DMA((14,)),
            pltpu.SemaphoreType.DMA((13,)),
        ],
        compiler_params=pltpu.CompilerParams(
            collective_id=3, has_side_effects=True, vmem_limit_bytes=62 * 1024 * 1024
        ),
        cost_estimate=pl.CostEstimate(
            flops=10 * 10**9, bytes_accessed=40 * 10**6, transcendentals=10**6
        ),
    )(
        lengths, scal, x_rows, gain_two_grad, gw, out_part, early, branch_grad, mix_w, q, k_all, v_all, attended, lse,
        cosine, sine_term, attn_w, normed, hidden, hidden_grad,
    )


def optimizer_kernel(*refs):
    ff_grads, attn_grads, kv_blocks = refs[:3]
    held, outs = refs[3:18], refs[18:]
    size, wide_heads = ff_grads.shape[0], held[0].shape[1]
    main = 512

    def joined(begin, rest_begin, width):
        pieces = [ff_grads[j, :, begin : begin + main] for j in range(size)]
        pieces += [
            ff_grads[j, :, rest_begin : rest_begin + 64] for j in range((width - size * main) // 64)
        ]
        return wide(jnp.concatenate(pieces, axis=1))

    def update(number, grad, at=slice(None)):
        master, moment, square = (ref[at] for ref in held[3 * number : 3 * number + 3])
        results = adamw(master, moment, square, grad, learn_rates[number], decay_rates[number])
        for ref, value in zip(outs[5 * number : 5 * number + 4], results):
            ref[at] = value
        if at == slice(None):
            outs[5 * number + 4][...] = results[4]

    update(0, wide(low(attn_grads[:, :wide_heads])))
    update(1, wide(jnp.concatenate([kv_blocks[i] for i in range(4)], axis=1)))
    update(2, wide(low(attn_grads[:, wide_heads : 2 * wide_heads])))
    every = slice(None)
    hidden_units = held[9].shape[2]
    update(3, joined(0, 2 * main, hidden_units), (every, 0, every))
    update(3, joined(main, 2 * main + 64, hidden_units), (every, 1, every))
    outs[19][...] = low(outs[18][...])
    update(4, joined(2 * main + 128, 3 * main + 128, hidden_units))


def optimizer(ff_grads, attn_grads, kv_blocks, held):
    rows, step = attn_grads.shape[0], 32

    def block(array):
        if array.ndim == 3 and array.shape[0] == 4:
            return pl.BlockSpec((4, step) + array.shape[2:], lambda i: (0, i, 0))
        rest = array.shape[1:]
        return pl.BlockSpec((step,) + rest, lambda i: (i,) + (0,) * len(rest))

    outs, flat = [], []
    for three in held:
        flat.extend(three)
        outs += [jax.ShapeDtypeStruct(three[0].shape, jnp.float32)] * 4
        outs.append(jax.ShapeDtypeStruct(three[0].shape, jnp.bfloat16))
    operands = [ff_grads, attn_grads, kv_blocks] + flat
    return pl.pallas_call(
        optimizer_kernel,
        grid=(rows // step,),
        out_shape=outs,
        in_specs=[block(one) for one in operands],
        out_specs=[block(one) for one in outs],
        compiler_params=pltpu.CompilerParams(vmem_limit_bytes=62 * 1024 * 1024),
        cost_estimate=pl.CostEstimate(
            flops=3 * 10**7, bytes_accessed=50 * 10**6, transcendentals=2 * 10**6
        ),
    )(*operands)


def rope_tables(places):
    halves = HD // 2
    powers = jnp.arange(halves, dtype=jnp.float32) * (-2.0 / HD)
    frequency = jnp.power(jnp.float32(rope_base), powers)
    angles = places.astype(jnp.float32)[:, None] * frequency[None, :]
    return jnp.cos(angles), jnp.sin(angles)


def local(
    tokens,
    cotangent,
    doc_lengths,
    queries_master,
    queries_moment,
    queries_square,
    keyvalue_master,
    keyvalue_moment,
    keyvalue_square,
    mixing_master,
    mixing_moment,
    mixing_square,
    expand_master,
    expand_moment,
    expand_square,
    shrink_master,
    shrink_moment,
    shrink_square,
    scalars_master,
    scalars_moment,
    scalars_square,
):
    local_rows, width = tokens.shape[1], tokens.shape[2]
    seq_count = lax.axis_size("seq")
    head_count = lax.axis_size("head")
    head_index = lax.axis_index("head")
    seq_index = lax.axis_index("seq")
    local_heads = H // head_count
    wide_heads = local_heads * HD
    kv_head = head_index * local_heads // (H // KV)
    core = head_index % 2
    quarter = local_rows // 4
    row_begin = (head_index % 2) * (2 * quarter) + (head_index // 2) * quarter
    hidden_units = expand_master.shape[2]
    units = 64 * -(-hidden_units // (64 * seq_count))
    more = ((0, 0), (0, units * seq_count - hidden_units))

    attn_pack = jnp.concatenate(
        [
            low(queries_master),
            low(mixing_master).T,
            low(lax.dynamic_slice_in_dim(keyvalue_master, kv_head * HD, HD, 1)),
            low(lax.dynamic_slice_in_dim(keyvalue_master, (KV + kv_head) * HD, HD, 1)),
        ],
        axis=1,
    )
    expand_low = low(expand_master)

    def cut(values):
        values = jnp.pad(values, more)
        return values.reshape(values.shape[0], seq_count, units).transpose(1, 0, 2)

    ff_packs = jnp.concatenate(
        [cut(expand_low[:, 0]), cut(expand_low[:, 1]), cut(low(shrink_master).T)], axis=2
    )
    scalar_values = wide(lax.all_gather(low(scalars_master), ("dp", "seq"), axis=0, tiled=True))
    attn_weight = weight_gather(attn_pack)
    ff_weight = weight_exchange(ff_packs)
    query_weight = attn_weight[:, :wide_heads]
    mixing_t = attn_weight[:, wide_heads : 2 * wide_heads]
    key_value_weight = attn_weight[:, 2 * wide_heads :]
    expand_weight = ff_weight[:, : 2 * units]
    shrink_t = ff_weight[:, 2 * units :]

    cot_rows = cotangent[0]
    cot_own = lax.dynamic_slice_in_dim(cot_rows, row_begin, quarter, 0)
    cot_blocks = [cot_rows]
    moving = cot_own
    for s in range(1, seq_count):
        moving = shift(moving, "seq", 1)
        cot_blocks.append(head_gather(moving))

    gain_one = scalar_values[:width]
    gain_two = scalar_values[width : 2 * width]
    bias_query = lax.dynamic_slice_in_dim(
        scalar_values, 2 * width + head_index * wide_heads, wide_heads
    )
    bias_keyvalue = scalar_values[2 * width + H * HD :]
    key_bias = lax.dynamic_slice_in_dim(bias_keyvalue, kv_head * HD, HD)
    value_bias = lax.dynamic_slice_in_dim(bias_keyvalue, (KV + kv_head) * HD, HD)
    x_rows = wide(tokens[0])
    lengths = doc_lengths[0]
    places = folded_places(
        seq_index * local_rows + jnp.arange(local_rows, dtype=jnp.int32), local_rows, seq_count
    )
    starts = doc_starts(places, lengths)
    within = places - starts
    scale_one = lax.rsqrt(jnp.mean(x_rows * x_rows, axis=-1, keepdims=True) + norm_eps)
    normed = low(x_rows * scale_one * gain_one)
    query_pre = dot_nn(normed, query_weight) + bias_query
    queries = low(rotate(query_pre.reshape(local_rows, local_heads, HD), within)).reshape(
        local_rows, wide_heads
    )
    key_value_pre = dot_nn(normed, key_value_weight)
    key_rows = low(rotate((key_value_pre[:, :HD] + key_bias)[:, None, :], within)[:, 0, :])
    value_rows = low(key_value_pre[:, HD:] + value_bias)
    moving = jnp.concatenate([key_rows, value_rows], axis=1)
    all_rows = jnp.zeros((seq_count,) + moving.shape, moving.dtype)
    for s in range(seq_count):
        if s > 0:
            moving = shift(moving, "seq", 1)
        owner = lax.rem(seq_index + seq_count - s, seq_count)
        all_rows = lax.dynamic_update_slice(all_rows, moving[None], (owner, 0, 0))
    all_rows = all_rows.reshape(-1, 2 * HD)
    all_keys, all_values = all_rows[:, :HD], all_rows[:, HD:]
    stream_rows = all_rows.shape[0]
    attended, log_total = in_vmem(
        attention_forward,
        [
            jax.ShapeDtypeStruct((local_rows, wide_heads), jnp.float32),
            jax.ShapeDtypeStruct((local_rows, local_heads), jnp.float32),
        ],
        doc_lengths,
        queries,
        all_keys,
        all_values,
    )
    attended_low = low(attended)
    x_own = lax.dynamic_slice_in_dim(x_rows, row_begin, quarter, 0)
    hidden = x_own + head_scatter(dot_nt(attended_low, mixing_t))
    scale_two = lax.rsqrt(jnp.mean(hidden * hidden, axis=-1, keepdims=True) + norm_eps)
    normed_two = low(hidden * scale_two * gain_two)

    normed_blocks, grad_blocks, act_blocks, back_parts, out_parts = [], [], [], [], []
    moving = normed_two
    for s in range(seq_count):
        if s > 0:
            moving = shift(moving, "seq", 1)
        block = head_gather(moving)
        both = dot_nn(block, expand_weight)
        gate_value, up_value = both[:, :units], both[:, units:]
        gate_sigmoid = jax.nn.sigmoid(gate_value)
        activation = low(gate_value * gate_sigmoid * up_value)
        act_grad = wide(low(dot_nn(cot_blocks[s], shrink_t)))
        gate_grad = low(act_grad * up_value * gate_sigmoid * (1.0 + gate_value * (1.0 - gate_sigmoid)))
        up_grad = low(act_grad * gate_value * gate_sigmoid)
        both_grad = jnp.concatenate([gate_grad, up_grad], axis=1)
        back_parts.append(head_scatter(dot_nt(both_grad, expand_weight)))
        out_parts.append(head_scatter(dot_nt(activation, shrink_t)))
        normed_blocks.append(block)
        grad_blocks.append(both_grad)
        act_blocks.append(activation)
    norm_two_grad = seq_sum(back_parts)
    back_two, gain_two_grad = norm_back(norm_two_grad, hidden, scale_two, gain_two)
    hidden_grad = wide(lax.dynamic_slice_in_dim(cot_rows, row_begin, quarter, 0)) + back_two
    branch_grad = head_gather(low(hidden_grad))
    feedforward = seq_sum(out_parts)
    layer_out = head_gather(low(hidden + feedforward))
    expand_part = dot_tn(jnp.concatenate(normed_blocks), jnp.concatenate(grad_blocks))
    shrink_part = dot_tn(jnp.concatenate(cot_blocks), jnp.concatenate(act_blocks))
    ff_grads = grad_exchange(low(jnp.concatenate([expand_part, shrink_part], axis=1)), False)

    attended_grad = low(dot_nn(branch_grad, mixing_t))
    query_sum, key_sum, value_sum = in_vmem(
        attention_backward,
        [
            jax.ShapeDtypeStruct((local_rows, wide_heads), jnp.float32),
            jax.ShapeDtypeStruct((stream_rows, HD), jnp.float32),
            jax.ShapeDtypeStruct((stream_rows, HD), jnp.float32),
        ],
        doc_lengths,
        queries,
        all_keys,
        all_values,
        attended_grad,
        attended,
        log_total,
    )
    mine = jnp.where(core == 0, key_sum, value_sum)
    other = jnp.where(core == 0, value_sum, key_sum)
    mine = mine + wide(swap(low(other), "head", 1))
    mine = mine.reshape(seq_count, local_rows, HD)
    own_sum = seq_sum(
        [
            lax.dynamic_index_in_dim(mine, lax.rem(seq_index + seq_count - s, seq_count), 0, False)
            for s in range(seq_count)
        ]
    )
    own_sum = low(jnp.where(core == 0, rotate(own_sum[:, None, :], -within)[:, 0, :], own_sum))
    query_grad = low(
        rotate(query_sum.reshape(local_rows, local_heads, HD), -within).reshape(
            local_rows, wide_heads
        )
    )
    own_weight = lax.dynamic_slice_in_dim(key_value_weight, core * HD, HD, 1)
    norm_one_grad = head_scatter(dot_nt(query_grad, query_weight) + dot_nt(own_sum, own_weight))
    scale_own = lax.dynamic_slice_in_dim(scale_one, row_begin, quarter, 0)
    back_one, gain_one_grad = norm_back(norm_one_grad, x_own, scale_own, gain_one)
    input_grad = head_gather(low(hidden_grad + back_one))
    attn_part = jnp.concatenate(
        [
            dot_tn(normed, query_grad),
            dot_tn(branch_grad, attended_low),
            dot_tn(normed, own_sum),
        ],
        axis=1,
    )
    attn_grads = grad_exchange(attn_part, True)
    kv_block = low(attn_grads[:, 2 * wide_heads :])
    small = jnp.zeros((scalars_master.shape[0] * 2 * seq_count,), jnp.float32)
    small = lax.dynamic_update_slice(small, jnp.concatenate([gain_one_grad, gain_two_grad]), (0,))
    small = lax.dynamic_update_slice(
        small, jnp.sum(wide(query_grad), axis=0), (2 * width + head_index * wide_heads,)
    )
    kv_column = core * KV * HD + kv_head * HD
    small = lax.dynamic_update_slice(
        small, jnp.sum(wide(own_sum), axis=0), (2 * width + H * HD + kv_column,)
    )
    small = lax.psum(small, "head")
    shared_scalars = lax.psum_scatter(small, ("dp", "seq"), scatter_dimension=0, tiled=True)
    gathered = head_gather(kv_block, 1)
    shared_keyvalue = wide(gathered)

    def joined(part):
        part = ff_grads[:, :, part * units : (part + 1) * units].transpose(1, 0, 2)
        return wide(part.reshape(part.shape[0], -1)[:, :hidden_units])

    grads = (
        attn_grads[:, :wide_heads],
        shared_keyvalue,
        attn_grads[:, wide_heads : 2 * wide_heads].T,
        jnp.stack([joined(0), joined(1)], axis=1),
        joined(2).T,
        shared_scalars,
    )
    masters = (
        (queries_master, queries_moment, queries_square),
        (keyvalue_master, keyvalue_moment, keyvalue_square),
        (mixing_master, mixing_moment, mixing_square),
        (expand_master, expand_moment, expand_square),
        (shrink_master, shrink_moment, shrink_square),
        (scalars_master, scalars_moment, scalars_square),
    )
    results = [layer_out[None], input_grad[None]]
    for held, grad, rate, decay in zip(masters, grads, learn_rates, decay_rates):
        results.extend(adamw(*held, wide(low(grad)), rate, decay))
    return tuple(results)


def local_fast(
    tokens,
    cotangent,
    doc_lengths,
    queries_master,
    queries_moment,
    queries_square,
    keyvalue_master,
    keyvalue_moment,
    keyvalue_square,
    mixing_master,
    mixing_moment,
    mixing_square,
    expand_master,
    expand_moment,
    expand_square,
    shrink_master,
    shrink_moment,
    shrink_square,
    scalars_master,
    scalars_moment,
    scalars_square,
):
    local_rows = tokens.shape[1]
    seq_count = lax.axis_size("seq")
    seq_index = lax.axis_index("seq")
    hidden_units = expand_master.shape[2]

    units = 64 * -(-hidden_units // (64 * seq_count))
    x_low, cot_rows = tokens[0], cotangent[0]
    lengths = doc_lengths[0]
    places = folded_places(
        seq_index * local_rows + jnp.arange(local_rows, dtype=jnp.int32), local_rows, seq_count
    )
    starts = doc_starts(places, lengths)
    within = places - starts
    cos_half, sin_half = rope_tables(within)
    (
        scal_all, attn_weight, mix_weight, ff_weight, cot_all, normed, queries, all_keys, all_values,
        attended, log_total, hidden, normed_all, cosine, sine_term,
    ) = front(
        doc_lengths, scalars_master[None], queries_master, keyvalue_master, mixing_master.T, expand_master, shrink_master.T,
        x_low, cot_rows, cos_half, sin_half, 3 * units + 64,
    )
    hidden_grad, branch_grad, gain_two_grad, ff_part, out_part, early = feed_forward(
        normed_all, ff_weight, cot_all, cot_rows, hidden, scal_all, units
    )
    layer_out, input_grad, ff_grads, attn_grads, kv_blocks, small = back(
        doc_lengths, scal_all, x_low, hidden, hidden_grad, gain_two_grad, branch_grad, attn_weight, mix_weight, normed, queries,
        all_keys, all_values, attended, log_total, cosine, sine_term, ff_part, out_part, early,
    )
    held = (
        (queries_master, queries_moment, queries_square),
        (keyvalue_master, keyvalue_moment, keyvalue_square),
        tuple(one.T for one in (mixing_master, mixing_moment, mixing_square)),
        (expand_master, expand_moment, expand_square),
        tuple(one.T for one in (shrink_master, shrink_moment, shrink_square)),
    )
    updated = optimizer(ff_grads, attn_grads, kv_blocks, held)
    results = [layer_out[None], input_grad[None]]
    for i in range(5):
        results.extend(one.T if i in (2, 4) else one for one in updated[5 * i : 5 * i + 5])
    results.extend(
        adamw(
            scalars_master, scalars_moment, scalars_square, wide(low(small[0])), learn_rates[5], decay_rates[5]
        )
    )
    return tuple(results)


def solution(mesh):
    placed = (
        P("dp", "seq", None),
        P("dp", "seq", None),
        P("dp", None),
        P(("dp", "seq"), "head"),
        P(("dp", "seq"), "head"),
        P(("dp", "seq"), "head"),
        P(("dp", "seq"), None),
        P(("dp", "seq"), None),
        P(("dp", "seq"), None),
        P("head", ("dp", "seq")),
        P("head", ("dp", "seq")),
        P("head", ("dp", "seq")),
        P(("dp", "seq"), None, "head"),
        P(("dp", "seq"), None, "head"),
        P(("dp", "seq"), None, "head"),
        P("head", ("dp", "seq")),
        P("head", ("dp", "seq")),
        P("head", ("dp", "seq")),
        P(("dp", "seq")),
        P(("dp", "seq")),
        P(("dp", "seq")),
    )
    small = dict(mesh.shape) == {"dp": 2, "seq": 4, "head": 4}
    return jax.shard_map(
        local_fast if small else local,
        mesh=mesh,
        in_specs=placed,
        out_specs=(
            P("dp", "seq", None),
            P("dp", "seq", None),
            P(("dp", "seq"), "head"),
            P(("dp", "seq"), "head"),
            P(("dp", "seq"), "head"),
            P(("dp", "seq"), "head"),
            P(("dp", "seq"), "head"),
            P(("dp", "seq"), None),
            P(("dp", "seq"), None),
            P(("dp", "seq"), None),
            P(("dp", "seq"), None),
            P(("dp", "seq"), None),
            P("head", ("dp", "seq")),
            P("head", ("dp", "seq")),
            P("head", ("dp", "seq")),
            P("head", ("dp", "seq")),
            P("head", ("dp", "seq")),
            P(("dp", "seq"), None, "head"),
            P(("dp", "seq"), None, "head"),
            P(("dp", "seq"), None, "head"),
            P(("dp", "seq"), None, "head"),
            P(("dp", "seq"), None, "head"),
            P("head", ("dp", "seq")),
            P("head", ("dp", "seq")),
            P("head", ("dp", "seq")),
            P("head", ("dp", "seq")),
            P("head", ("dp", "seq")),
            P(("dp", "seq")),
            P(("dp", "seq")),
            P(("dp", "seq")),
            P(("dp", "seq")),
            P(("dp", "seq")),
        ),
        check_vma=False,
    )
```
